32 devices in a mesh: groups: 2 (over y), expert: 8 (over z, x), ffn: 2 (over core).
Axes of the slice: x: 2, y: 2, z: 4, core: 2. Of those that a mesh axis runs over, the one named last changes fastest.
Arguments:
- tokens: bfloat16 [2048, 4096], P(('groups', 'expert'), 'ffn'), parts along dimension 0, may hold values from -6 to 6
- grad_out: bfloat16 [2048, 4096], P(('groups', 'expert'), 'ffn'), parts along dimension 0, may hold values from -6 to 6
- route_ids: int32 [2048, 8], P(('groups', 'expert')), parts along dimension 0, may hold values from 0 to 127, all different within a row; in each aligned block of 128 rows (0 to 127, 128 to 255, ...) at most 9 rows name the same one
- route_weight: float32 [2048, 8], P(('groups', 'expert')), parts along dimension 0, may hold values from 0.05 to 1
- gate_weight: bfloat16 [8, 4096, 1536], P('expert', None, 'ffn'), may hold values from -0.09375 to 0.09375
- up_weight: bfloat16 [8, 4096, 1536], P('expert', None, 'ffn'), may hold values from -0.09375 to 0.09375
- down_weight: bfloat16 [8, 1536, 4096], P('expert', 'ffn'), may hold values from -0.15625 to 0.15625
Outputs:
- out_tokens: bfloat16 [2048, 4096], P(('groups', 'expert'), 'ffn'), parts along dimension 0
- grad_tokens: bfloat16 [2048, 4096], P(('groups', 'expert'), 'ffn'), parts along dimension 0
- grad_gate: bfloat16 [16, 4096, 1536], P(('groups', 'expert'), None, 'ffn'), parts along dimension 0
- grad_up: bfloat16 [16, 4096, 1536], P(('groups', 'expert'), None, 'ffn'), parts along dimension 0
- grad_down: bfloat16 [16, 1536, 4096], P(('groups', 'expert'), 'ffn'), parts along dimension 0
The draws below stay inside these ranges and needn't reach their ends.
There are 2 independent parts, one for each index of `groups`. The reference program is written for one: setup_inputs(seed, part) draws one part's arguments, and reference() takes and returns one part's arrays. A program takes and returns all parts, laid end to end along the dimension named above; an argument that names none is the same for every part. Nothing has to cross between parts.
Inputs may be any that keep to these rules, and one draw needn't show every extreme that they name: `route_ids`: each token names 8 different experts. Among the tokens of one index of expert (aligned blocks of 128 tokens) no expert is named more than 9 times.
All inputs are finite; a program needn't handle non-finite values.
Results may differ from the reference program's by a relative error of at most 0.014.
Values may be sent and summed in bfloat16 or wider, within the bound.
No kernel may reach another device: no remote copies, remote signals or barrier semaphores. Data moves between devices by JAX's collectives and lax.ppermute only.
A program may use at most 128 MiB of HBM per device.

```python
import math
import jax
import jax.numpy as jnp
import numpy as np
from jax import lax

D = 4096
FF = 1536
EXPERTS = 128
TOP = 8
FLIGHT = 8
TOK_DEV = 128
PIECES = 1
CAP = 9
TOKENS = 1024
N_FFN = 2


def steps_of(own_key, shape, pieces, least, high):
    def one(dim, parts):
        heights = jax.random.uniform(jax.random.fold_in(jax.random.fold_in(own_key, 6), dim), (parts,), jnp.float32, least / len(pieces), high / len(pieces))
        return jnp.repeat(jnp.exp(heights), shape[dim] // parts).reshape((-1,) + (1,) * (len(shape) - dim - 1))

    gain = one(*pieces[0])
    for cut in pieces[1:]:
        gain = gain * one(*cut)
    return gain


def deal_out(key, own, number, rows, count, top, most, skew):
    sequence = jax.random.permutation(key, count)
    crowded, common = portions_of(count, rows * top, most, skew, True), portions_of(count, rows * top, most, skew, False)
    places = jnp.arange(count)

    def named(lengths, offset_by):
        used = int((lengths > 0).sum())
        fixed = max(1, used // 4)
        moved = fixed + (places - fixed + offset_by * (used - fixed)) % max(1, count - fixed)
        return jnp.zeros((count,), jnp.int32).at[sequence[jnp.where(places < fixed, places, moved)]].set(jnp.asarray(lengths, jnp.int32))

    lengths = jnp.where(number % 4 == 0, named(crowded, number // 4), named(common, number - number // 4 - 1))
    mixed = jax.random.permutation(jax.random.fold_in(own, 3), count)
    source_of, taker = mixed[0:count // 2 * 2:2], mixed[1:count // 2 * 2:2]
    margin = jnp.minimum(lengths[source_of] - 1, most - lengths[taker]) // 2
    margin = jnp.where((source_of == sequence[0]) | (taker == sequence[0]) | (lengths[taker] == 0), 0, jnp.maximum(margin, 0))
    moved = jax.random.randint(jax.random.fold_in(own, 4), (count // 2,), 0, 1 << 20) % (margin + 1)
    lengths = lengths.at[source_of].add(-moved).at[taker].add(moved)
    items = jnp.searchsorted(jnp.cumsum(lengths), jnp.arange(rows * top), side="right").astype(jnp.int32)
    listing = items.reshape(top, rows).T
    listing = listing[jax.random.permutation(jax.random.fold_in(own, 1), rows)]
    offset_by = jax.random.randint(jax.random.fold_in(own, 2), (rows, 1), 0, top)
    return jnp.take_along_axis(listing, (jnp.arange(top)[None, :] + offset_by) % top, axis=1)


def portions_of(count, total, bound, skew, full):
    portions = [(1 << 20) // math.isqrt(grade ** skew) + 1 for grade in range(1, count + 1)]
    largest = bound if full else min(bound, max(-(-total // count), total * portions[0] // sum(portions)))
    least = 1 if total - largest >= count - 1 else 0
    holding, spare = [largest] + [least] * (count - 1), total - largest - least * (count - 1)
    while spare > 0:
        candidates = [i for i in range(1, count) if holding[i] < largest] or [i for i in range(1, count) if holding[i] < bound]
        mass, budget = sum([portions[i] for i in candidates]), spare
        for i in candidates:
            extra = min(bound - holding[i], max(1, budget * portions[i] // mass), spare)
            holding[i] = holding[i] + extra
            spare = spare - extra
    return np.array(holding)


def centred(rng, dims, deviation, reach, cuts=(), held_as=jnp.bfloat16):
    drawn = deviation * jax.random.normal(rng, dims, jnp.float32)
    if cuts:
        drawn = drawn * steps_of(rng, dims, cuts, -0.22, 0.18)
    return jnp.clip(drawn, -reach, reach).astype(held_as)


def setup_inputs(seed: int = 0, part: int = 0) -> dict:
    seeds = jax.random.split(jax.random.key(seed), 8)
    part_splits = jax.random.split(jax.random.fold_in(seeds[7], part), 8)
    tokens = centred(part_splits[0], (TOKENS, D), 1.0, 6.0, ((0, 8), (1, 2)))
    grad_out = centred(part_splits[1], (TOKENS, D), 1.0, 6.0, ((0, 8), (1, 2)))
    route_ids_keys = jax.random.split(jax.random.fold_in(part_splits[2], 1), TOKENS // TOK_DEV)
    route_ids_turns = jax.random.permutation(jax.random.fold_in(part_splits[2], 3), TOKENS // TOK_DEV)
    route_ids = jax.vmap(lambda own, number: deal_out(jax.random.fold_in(part_splits[2], 2), own, number, TOK_DEV, EXPERTS, TOP, CAP, 1))(route_ids_keys, route_ids_turns).reshape((TOKENS, TOP))
    route_weight = jnp.clip(jnp.exp(math.log(1.0) - 2.9957323 * jax.random.uniform(part_splits[3], (TOKENS, TOP), jnp.float32) ** steps_of(part_splits[3], (TOKENS, TOP), ((0, 8),), -0.2, 0.2)), 0.05, 1.0)
    gate_weight = centred(seeds[4], (FLIGHT * PIECES, D // PIECES, FF), D ** -0.5, 0.09375, ((0, 8), (2, 2)))
    up_weight = centred(seeds[5], (FLIGHT * PIECES, D // PIECES, FF), D ** -0.5, 0.09375, ((0, 8), (2, 2)))
    down_weight = centred(seeds[6], (FLIGHT * PIECES, FF, D // PIECES), FF ** -0.5, 0.15625, ((0, 8), (1, 2)))
    return {"tokens": tokens, "grad_out": grad_out, "route_ids": route_ids, "route_weight": route_weight, "gate_weight": gate_weight, "up_weight": up_weight, "down_weight": down_weight}


def to_bf16_f32(value):
    return lax.optimization_barrier(value.astype(jnp.bfloat16)).astype(jnp.float32)


def reference(tokens, grad_out, route_ids, route_weight, gate_weight, up_weight, down_weight):
    halves = N_FFN
    piece_width = D // PIECES
    sub_width = piece_width // halves
    blocks = TOKENS // TOK_DEV
    rows = blocks * CAP
    ids = route_ids.reshape(blocks, TOK_DEV, TOP)
    onehot = (ids[..., None] == jnp.arange(FLIGHT, dtype=jnp.int32)).astype(jnp.float32)
    member = onehot.sum(axis=2)
    mixing = (onehot * route_weight.reshape(blocks, TOK_DEV, TOP)[..., None].astype(jnp.float32)).sum(axis=2)
    slots = jnp.cumsum(member, axis=1) - member
    place = member[..., None] * (slots[..., None] == jnp.arange(CAP, dtype=jnp.float32)).astype(jnp.float32)
    x_five = tokens.reshape(blocks, TOK_DEV, halves, PIECES, sub_width).astype(jnp.float32)
    g_five = grad_out.reshape(blocks, TOK_DEV, halves, PIECES, sub_width).astype(jnp.float32)
    x_rows = jnp.einsum("bTec,bThjr->ejbchr", place, x_five).astype(jnp.bfloat16).reshape(FLIGHT, PIECES, rows, piece_width)
    g_rows = jnp.einsum("bTec,bThjr->ejbchr", place * mixing[..., None], g_five).astype(jnp.bfloat16).reshape(FLIGHT, PIECES, rows, piece_width)
    w_gate = gate_weight.reshape(FLIGHT, PIECES, piece_width, FF)
    w_up = up_weight.reshape(FLIGHT, PIECES, piece_width, FF)
    w_down = down_weight.reshape(FLIGHT, PIECES, FF, piece_width)

    def one_expert(items):
        x_e, g_e, wg_e, wu_e, wd_e = items
        x_f = x_e.astype(jnp.float32)
        g_f = g_e.astype(jnp.float32)
        wg_f = wg_e.astype(jnp.float32)
        wu_f = wu_e.astype(jnp.float32)
        wd_f = wd_e.astype(jnp.float32)
        gate = to_bf16_f32(jnp.einsum("jrd,jdf->jrf", x_f, wg_f)).sum(axis=0)
        up = to_bf16_f32(jnp.einsum("jrd,jdf->jrf", x_f, wu_f)).sum(axis=0)
        sig = jax.nn.sigmoid(gate)
        act = gate * sig
        hidden = (act * up).astype(jnp.bfloat16)
        h_f = hidden.astype(jnp.float32)
        out_part = jnp.einsum("rf,jfd->jrd", h_f, wd_f)
        d_down = jnp.einsum("rf,jrd->jfd", h_f, g_f).astype(jnp.bfloat16)
        d_hidden = to_bf16_f32(jnp.einsum("jrd,jfd->jrf", g_f, wd_f)).sum(axis=0)
        d_gate_pre = (d_hidden * up * sig * (1.0 + gate * (1.0 - sig))).astype(jnp.bfloat16).astype(jnp.float32)
        d_up_pre = (d_hidden * act).astype(jnp.bfloat16).astype(jnp.float32)
        d_gate = jnp.einsum("jrd,rf->jdf", x_f, d_gate_pre).astype(jnp.bfloat16)
        d_up = jnp.einsum("jrd,rf->jdf", x_f, d_up_pre).astype(jnp.bfloat16)
        d_x = jnp.einsum("rf,jdf->jrd", d_gate_pre, wg_f) + jnp.einsum("rf,jdf->jrd", d_up_pre, wu_f)
        return out_part, d_x, d_gate, d_up, d_down

    out_part, d_x, d_gate, d_up, d_down = lax.map(one_expert, (x_rows, g_rows, w_gate, w_up, w_down))
    out_six = out_part.reshape(FLIGHT, PIECES, blocks, CAP, halves, sub_width)
    dx_six = d_x.reshape(FLIGHT, PIECES, blocks, CAP, halves, sub_width)
    out_tokens = jnp.einsum("bTec,ejbchr->bThjr", place * mixing[..., None], out_six).reshape(TOKENS, D).astype(jnp.bfloat16)
    grad_tokens = jnp.einsum("bTec,ejbchr->bThjr", place, dx_six).reshape(TOKENS, D).astype(jnp.bfloat16)
    grad_gate = d_gate.reshape(FLIGHT * PIECES, piece_width, FF)
    grad_up = d_up.reshape(FLIGHT * PIECES, piece_width, FF)
    grad_down = d_down.reshape(FLIGHT * PIECES, FF, piece_width)
    return (out_tokens, grad_tokens, grad_gate, grad_up, grad_down)
```

```python
import functools

import jax
import jax.numpy as jnp
from jax import lax
from jax.experimental import pallas as pl
from jax.experimental.pallas import tpu as pltpu
from jax.sharding import PartitionSpec as P

EXPERTS = 128
LANES = 128
MIB = 1024 * 1024


def contract_rows(left, right):
    return lax.dot_general(
        left, right, (((0,), (0,)), ((), ())), preferred_element_type=jnp.float32
    )


def contract_cols(left, right):
    return lax.dot_general(
        left, right, (((1,), (1,)), ((), ())), preferred_element_type=jnp.float32
    )


def general_shards(tokens, grad_out, route_ids, route_weight, gate_weight, up_weight, down_weight):
    tokens, grad_out = (
        lax.all_gather(tokens, "ffn", axis=1, tiled=True),
        lax.all_gather(grad_out, "ffn", axis=1, tiled=True),
    )
    tok_dev, width = tokens.shape
    top_count = route_ids.shape[1]
    piece_width = gate_weight.shape[1]
    hidden_half = gate_weight.shape[2]
    pieces = width // piece_width
    devices = lax.axis_size("expert")
    flight = devices // pieces
    halves = lax.axis_size("ffn")
    sub_width = piece_width // halves
    capacity = max(2, min(tok_dev, (9 * tok_dev * top_count + 8 * EXPERTS - 1) // (8 * EXPERTS)))
    total_rows = devices * capacity
    expert_ids = jnp.arange(flight, dtype=jnp.int32)
    member = jnp.zeros((tok_dev, flight), jnp.float32)
    mixing = jnp.zeros((tok_dev, flight), jnp.float32)
    for route in range(top_count):
        hit = (route_ids[:, route : route + 1] == expert_ids[None, :]).astype(jnp.float32)
        member = member + hit
        mixing = mixing + hit * route_weight[:, route : route + 1]
    slots = jnp.cumsum(member, axis=0) - member
    place = member[:, :, None] * (
        slots[:, :, None] == jnp.arange(capacity, dtype=jnp.float32)
    ).astype(jnp.float32)
    weighted = place * mixing[:, :, None]
    place_low = place.astype(jnp.bfloat16)
    x_four = tokens.reshape(tok_dev, halves, pieces, sub_width)
    g_four = grad_out.reshape(tok_dev, halves, pieces, sub_width)
    x_parts = []
    g_parts = []
    for half in range(halves):
        x_parts.append(
            jnp.einsum(
                "Tec,Tjr->ejcr", place_low, x_four[:, half], preferred_element_type=jnp.float32
            )
        )
        g_parts.append(jnp.einsum("Tec,Tjr->ejcr", weighted, g_four[:, half].astype(jnp.float32)))
    x_send = jnp.concatenate(x_parts, axis=3).astype(jnp.bfloat16).reshape(total_rows, piece_width)
    g_send = jnp.concatenate(g_parts, axis=3).astype(jnp.bfloat16).reshape(total_rows, piece_width)

    def return_parts(values):
        arrived = lax.all_to_all(values, "expert", split_axis=0, concat_axis=0, tiled=True)
        lanes = arrived.shape[1]
        return arrived.astype(jnp.float32).reshape(flight, pieces, capacity, lanes).sum(axis=1)

    def spread_rows(values):
        lanes = values.shape[2]
        copies = jnp.broadcast_to(values[:, None], (flight, pieces, capacity, lanes)).reshape(
            total_rows, lanes
        )
        return lax.all_to_all(copies, "expert", split_axis=0, concat_axis=0, tiled=True)

    def finish(term, mix):
        summed = lax.psum_scatter(term, "ffn", scatter_dimension=1, tiled=True)
        back = lax.all_to_all(summed, "expert", split_axis=0, concat_axis=0, tiled=True)
        back = back.reshape(flight, pieces, capacity, sub_width)
        joined = jnp.einsum("Tec,ejcr->Tjr", mix, back)
        return joined.reshape(tok_dev, pieces * sub_width).astype(jnp.bfloat16)

    rows = lax.all_to_all(x_send, "expert", split_axis=0, concat_axis=0, tiled=True)
    w_gate = gate_weight[0]
    w_up = up_weight[0]
    w_down = down_weight[0]
    partial_value = jnp.concatenate(
        [
            jnp.dot(rows, w_gate, preferred_element_type=jnp.float32),
            jnp.dot(rows, w_up, preferred_element_type=jnp.float32),
        ],
        axis=1,
    )
    summed = return_parts(partial_value.astype(jnp.bfloat16))
    gate = summed[:, :, :hidden_half]
    up = summed[:, :, hidden_half:]
    sig = jax.nn.sigmoid(gate)
    act = gate * sig
    hidden = (act * up).astype(jnp.bfloat16)
    h_rows = spread_rows(hidden)
    out_term = jnp.dot(h_rows, w_down, preferred_element_type=jnp.float32)
    out_tokens = finish(out_term, weighted)
    grads = lax.all_to_all(g_send, "expert", split_axis=0, concat_axis=0, tiled=True)
    grad_down = contract_rows(h_rows, grads).astype(jnp.bfloat16)
    hidden_part = contract_cols(grads, w_down).astype(jnp.bfloat16)
    grad_hidden = return_parts(hidden_part)
    pre_gate = (grad_hidden * up * sig * (1.0 + gate * (1.0 - sig))).astype(jnp.bfloat16)
    pre_up = (grad_hidden * act).astype(jnp.bfloat16)
    both = spread_rows(jnp.concatenate([pre_gate, pre_up], axis=2))
    d_gate_rows = both[:, :hidden_half]
    d_up_rows = both[:, hidden_half:]
    grad_gate = contract_rows(rows, d_gate_rows).astype(jnp.bfloat16)
    grad_up = contract_rows(rows, d_up_rows).astype(jnp.bfloat16)
    x_term = contract_cols(d_gate_rows, w_gate) + contract_cols(d_up_rows, w_up)
    grad_tokens = finish(x_term, place)
    return (out_tokens, grad_tokens, grad_gate[None], grad_up[None], grad_down[None])


def vmem(shape, dtype):
    return pltpu.VMEM(shape, dtype)


def call(kernel, out_shape, args, in_spaces=None, out_spaces=None, flops=0, traffic=0, scratch=(), limit=16):
    spaces = in_spaces or [pltpu.VMEM] * len(args)
    outs = out_spaces or [pltpu.VMEM] * len(out_shape)
    return pl.pallas_call(
        kernel,
        out_shape=tuple(out_shape),
        in_specs=[pl.BlockSpec(memory_space=space) for space in spaces],
        out_specs=tuple(pl.BlockSpec(memory_space=space) for space in outs),
        scratch_shapes=list(scratch),
        compiler_params=pltpu.CompilerParams(vmem_limit_bytes=limit * MIB),
        cost_estimate=pl.CostEstimate(flops=flops, bytes_accessed=traffic, transcendentals=0),
    )(*args)


def rows_to_blocks(scratch, outs, take, rows, capacity, subs):
    for sub in range(subs):
        scratch[pl.ds(sub, rows, stride=subs), :] = take(sub)
    size = capacity * subs
    for place, out in enumerate(outs):
        out[...] = scratch[place * size : (place + 1) * size, :].astype(out.dtype)


def blocks_to_rows(scratch, blocks, put, rows, capacity, subs):
    size = capacity * subs
    for place, block in enumerate(blocks):
        scratch[place * size : (place + 1) * size, :] = block[...].astype(jnp.float32)
    for sub in range(subs):
        put(sub, scratch[pl.ds(sub, rows, stride=subs), :])


def route_kernel(devices, capacity, subs, ids, weight, x, g, *refs):
    x_outs, g_outs = refs[:devices], refs[devices : 2 * devices]
    place_out, mix_out, scratch = refs[2 * devices :]
    top, tok = ids.shape
    rows = devices * capacity
    me = lax.axis_index("expert")
    order = lax.broadcasted_iota(jnp.int32, (devices, tok), 0)
    expert = order ^ me
    member = jnp.zeros((devices, tok), jnp.float32)
    mixing = jnp.zeros((devices, tok), jnp.float32)
    for route in range(top):
        hit = ids[route : route + 1, :] == expert
        member = jnp.where(hit, 1.0, member)
        mixing = jnp.where(hit, weight[route : route + 1, :], mixing)
    before = lax.broadcasted_iota(jnp.int32, (tok, tok), 0) < lax.broadcasted_iota(jnp.int32, (tok, tok), 1)
    slots = jnp.dot(
        member.astype(jnp.bfloat16),
        jnp.where(before, 1.0, 0.0).astype(jnp.bfloat16),
        preferred_element_type=jnp.float32,
    )
    target = jnp.where(member > 0, slots + capacity * order.astype(jnp.float32), -1.0)
    row = lax.broadcasted_iota(jnp.int32, (rows, tok), 0).astype(jnp.float32)
    place = jnp.zeros((rows, tok), jnp.float32)
    mix = jnp.zeros((rows, tok), jnp.float32)
    for k in range(devices):
        equal = target[k : k + 1, :] == row
        place = jnp.where(equal, 1.0, place)
        mix = jnp.where(equal, mixing[k : k + 1, :], mix)
    row_weight = jnp.broadcast_to(jnp.sum(mix, axis=1, keepdims=True), (rows, LANES))
    low = place.astype(jnp.bfloat16)
    place_out[...] = low
    mix_out[...] = row_weight

    def x_part(sub):
        return jnp.dot(low, x[:, sub * LANES : (sub + 1) * LANES], preferred_element_type=jnp.float32)

    def g_part(sub):
        part = jnp.dot(low, g[:, sub * LANES : (sub + 1) * LANES], preferred_element_type=jnp.float32)
        return part * row_weight

    rows_to_blocks(scratch, x_outs, x_part, rows, capacity, subs)
    rows_to_blocks(scratch, g_outs, g_part, rows, capacity, subs)


def hold_kernel(count, *refs):
    sems = refs[2 * count]
    copies = [pltpu.make_async_copy(refs[i], refs[count + i], sems.at[i]) for i in range(count)]
    for copy in copies:
        copy.start()
    for copy in copies:
        copy.wait()


def arrive_kernel(devices, capacity, subs, *refs):
    blocks, out, scratch = refs[:devices], refs[devices], refs[devices + 1]

    def put(sub, value):
        out[:, sub * LANES : (sub + 1) * LANES] = value.astype(out.dtype)

    blocks_to_rows(scratch, blocks, put, devices * capacity, capacity, subs)


def leave_kernel(devices, capacity, subs, own, other, *refs):
    outs, scratch = refs[:devices], refs[devices]

    def take(sub):
        cols = slice(sub * LANES, (sub + 1) * LANES)
        return own[:, cols] + other[:, cols].astype(jnp.float32)

    rows_to_blocks(scratch, outs, take, devices * capacity, capacity, subs)


def forward_kernel(step, x_own, x_other, w_gate, w_up, w_down, x_full, gate, up, hidden, out_own, out_other):
    half_width = x_own.shape[1]
    lanes = gate.shape[1]
    half = lax.axis_index("ffn")
    own_at = pl.multiple_of(half * half_width, half_width)
    other_at = pl.multiple_of((1 - half) * half_width, half_width)
    x_full[:, pl.ds(own_at, half_width)] = x_own[...]
    x_full[:, pl.ds(other_at, half_width)] = x_other[...]

    def project(i, carry):
        cols = pl.ds(pl.multiple_of(i * step, step), step)
        gate_low = jnp.dot(x_full[...], w_gate[0, :, cols], preferred_element_type=jnp.float32).astype(jnp.bfloat16)
        up_low = jnp.dot(x_full[...], w_up[0, :, cols], preferred_element_type=jnp.float32).astype(jnp.bfloat16)
        gate[:, cols] = gate_low
        up[:, cols] = up_low
        gate_val = gate_low.astype(jnp.float32)
        hidden[:, cols] = (gate_val * jax.nn.sigmoid(gate_val) * up_low.astype(jnp.float32)).astype(jnp.bfloat16)
        return carry

    lax.fori_loop(0, lanes // step, project, 0)

    def spread(i, carry):
        at = pl.multiple_of(i * step, step)
        here = pl.ds(at, step)
        other = jnp.dot(hidden[...], w_down[0, :, pl.ds(other_at + at, step)], preferred_element_type=jnp.float32)
        out_other[:, here] = other.astype(jnp.bfloat16)
        out_own[:, here] = jnp.dot(hidden[...], w_down[0, :, pl.ds(own_at + at, step)], preferred_element_type=jnp.float32)
        return carry

    lax.fori_loop(0, half_width // step, spread, 0)


def backward_kernel(
    step, g_own, g_other, gate, up, w_gate, w_up, w_down, g_full, pre_gate, pre_up, dx_own, dx_other
):
    half_width = g_own.shape[1]
    lanes = gate.shape[1]
    half = lax.axis_index("ffn")
    own_at = pl.multiple_of(half * half_width, half_width)
    other_at = pl.multiple_of((1 - half) * half_width, half_width)
    g_full[:, pl.ds(own_at, half_width)] = g_own[...]
    g_full[:, pl.ds(other_at, half_width)] = g_other[...]

    def pull(i, carry):
        cols = pl.ds(pl.multiple_of(i * step, step), step)
        part = contract_cols(g_full[...], w_down[0, cols, :]).astype(jnp.bfloat16)
        grad_hidden = part.astype(jnp.float32)
        gate_val = gate[:, cols].astype(jnp.float32)
        up_val = up[:, cols].astype(jnp.float32)
        sig = jax.nn.sigmoid(gate_val)
        pre_gate[:, cols] = (grad_hidden * up_val * sig * (1.0 + gate_val * (1.0 - sig))).astype(jnp.bfloat16)
        pre_up[:, cols] = (grad_hidden * gate_val * sig).astype(jnp.bfloat16)
        return carry

    lax.fori_loop(0, lanes // step, pull, 0)

    def spread(i, carry):
        at = pl.multiple_of(i * step, step)
        here = pl.ds(at, step)

        def term(base):
            there = pl.ds(base + at, step)
            return contract_cols(pre_gate[...], w_gate[0, there, :]) + contract_cols(pre_up[...], w_up[0, there, :])

        dx_other[:, here] = term(other_at).astype(jnp.bfloat16)
        dx_own[:, here] = term(own_at)
        return carry

    lax.fori_loop(0, half_width // step, spread, 0)


def outer_kernel(left, *refs):
    count = len(refs) // 2
    for right, out in zip(refs[:count], refs[count:]):
        out[0] = contract_rows(left[...], right[...]).astype(out.dtype)


def outer(left, rights, step):
    rows, height = left.shape
    width = rights[0].shape[1]
    return pl.pallas_call(
        outer_kernel,
        grid=(height // step,),
        out_shape=tuple(jax.ShapeDtypeStruct((1, height, width), jnp.bfloat16) for _ in rights),
        in_specs=[pl.BlockSpec((rows, step), lambda i: (0, i))]
        + [pl.BlockSpec((rows, width), lambda i: (0, 0)) for _ in rights],
        out_specs=tuple(pl.BlockSpec((1, step, width), lambda i: (0, i, 0)) for _ in rights),
        compiler_params=pltpu.CompilerParams(vmem_limit_bytes=24 * MIB),
        cost_estimate=pl.CostEstimate(
            flops=2 * rows * height * width * len(rights),
            bytes_accessed=2 * height * width * len(rights),
            transcendentals=0,
        ),
    )(left, *rights)


def join_kernel(weighted, devices, capacity, subs, place, mix, *refs):
    blocks, out, scratch = refs[:devices], refs[devices], refs[devices + 1]

    def put(sub, value):
        if weighted:
            value = value * mix[...]
        out[:, sub * LANES : (sub + 1) * LANES] = contract_rows(place[...], value.astype(jnp.bfloat16)).astype(out.dtype)

    blocks_to_rows(scratch, blocks, put, devices * capacity, capacity, subs)


def exchange(blocks, devices):
    arrived = [blocks[0]]
    for k in range(1, devices):
        arrived.append(lax.ppermute(blocks[k], "expert", [(i, i ^ k) for i in range(devices)]))
    return arrived


def swap(value):
    return lax.ppermute(value, "ffn", [(0, 1), (1, 0)])


def one_piece_shards(tokens, grad_out, route_ids, route_weight, gate_weight, up_weight, down_weight):
    tok_dev, sub_width = tokens.shape
    top_count = route_ids.shape[1]
    width = gate_weight.shape[1]
    lanes = gate_weight.shape[2]
    devices = lax.axis_size("expert")
    capacity = max(2, min(tok_dev, (9 * tok_dev * top_count + 8 * EXPERTS - 1) // (8 * EXPERTS)))
    rows = devices * capacity
    subs = sub_width // LANES
    low = jnp.bfloat16
    block = jax.ShapeDtypeStruct((capacity * subs, LANES), low)
    spread_scratch = [pltpu.VMEM((rows * subs, LANES), jnp.float32)]
    sizes = (devices, capacity, subs)

    routed = call(
        functools.partial(route_kernel, *sizes),
        [block] * (2 * devices)
        + [jax.ShapeDtypeStruct((rows, tok_dev), low), jax.ShapeDtypeStruct((rows, LANES), jnp.float32)],
        (route_ids.T, route_weight.T, tokens, grad_out),
        scratch=spread_scratch,
        traffic=4 * tok_dev * sub_width,
    )
    place, mix = routed[2 * devices :]
    x_blocks = exchange(routed[:devices], devices)
    g_blocks = exchange(routed[devices : 2 * devices], devices)

    weights = (gate_weight, up_weight, down_weight)
    w_gate, w_up, w_down = call(
        functools.partial(hold_kernel, 3),
        [vmem(w.shape, w.dtype) for w in weights],
        weights,
        in_spaces=[pl.ANY] * 3,
        scratch=[pltpu.SemaphoreType.DMA((3,))],
        traffic=sum(w.size * 2 for w in weights),
    )

    def arrive(blocks):
        return call(
            functools.partial(arrive_kernel, *sizes),
            [vmem((rows, sub_width), low)],
            blocks,
            scratch=spread_scratch,
            traffic=4 * rows * sub_width,
        )[0]

    x_own = arrive(x_blocks)
    x_other = swap(x_own)
    step = 256
    x_full, gate, up, hidden, out_own, out_other = call(
        functools.partial(forward_kernel, step),
        [
            vmem((rows, width), low),
            vmem((rows, lanes), low),
            vmem((rows, lanes), low),
            vmem((rows, lanes), low),
            vmem((rows, sub_width), jnp.float32),
            vmem((rows, sub_width), low),
        ],
        (x_own, x_other, w_gate, w_up, w_down),
        flops=6 * rows * width * lanes,
    )
    out_arrived = swap(out_other)
    g_own = arrive(g_blocks)
    g_other = swap(g_own)
    g_full, pre_gate, pre_up, dx_own, dx_other = call(
        functools.partial(backward_kernel, step),
        [
            vmem((rows, width), low),
            vmem((rows, lanes), low),
            vmem((rows, lanes), low),
            vmem((rows, sub_width), jnp.float32),
            vmem((rows, sub_width), low),
        ],
        (g_own, g_other, gate, up, w_gate, w_up, w_down),
        flops=6 * rows * width * lanes,
    )
    dx_arrived = swap(dx_other)

    def leave(own, other):
        return call(
            functools.partial(leave_kernel, *sizes),
            [block] * devices,
            (own, other),
            scratch=spread_scratch,
            traffic=8 * rows * sub_width,
        )

    out_blocks = exchange(leave(out_own, out_arrived), devices)
    dx_blocks = exchange(leave(dx_own, dx_arrived), devices)
    (grad_down,) = outer(hidden, [g_full], 128)
    grad_gate, grad_up = outer(x_full, [pre_gate, pre_up], 512)

    def join(weighted, blocks):
        return call(
            functools.partial(join_kernel, weighted, *sizes),
            [jax.ShapeDtypeStruct((tok_dev, sub_width), low)],
            (place, mix, *blocks),
            scratch=spread_scratch,
            traffic=4 * tok_dev * sub_width,
        )[0]

    return join(True, out_blocks), join(False, dx_blocks), grad_gate, grad_up, grad_down


def shards(*args):
    tokens, gate_weight = args[0], args[4]
    halves = lax.axis_size("ffn")
    devices = lax.axis_size("expert")
    if halves == 2 and devices & (devices - 1) == 0 and tokens.shape[1] * halves == gate_weight.shape[1]:
        return one_piece_shards(*args)
    return general_shards(*args)


def solution(mesh):
    in_specs = (
        P(("groups", "expert"), "ffn"),
        P(("groups", "expert"), "ffn"),
        P(("groups", "expert"), None),
        P(("groups", "expert"), None),
        P("expert", None, "ffn"),
        P("expert", None, "ffn"),
        P("expert", "ffn", None),
    )
    out_specs = (
        P(("groups", "expert"), "ffn"),
        P(("groups", "expert"), "ffn"),
        P(("groups", "expert"), None, "ffn"),
        P(("groups", "expert"), None, "ffn"),
        P(("groups", "expert"), "ffn", None),
    )
    return jax.shard_map(shards, mesh=mesh, in_specs=in_specs, out_specs=out_specs, check_vma=False)
```

```python
import functools

import jax
import jax.numpy as jnp
from jax import lax
from jax.experimental import pallas as pl
from jax.experimental.pallas import tpu as pltpu
from jax.sharding import PartitionSpec as P

EXPERTS = 128
LANES = 128
MIB = 1024 * 1024


def contract_rows(left, right):
    return lax.dot_general(
        left, right, (((0,), (0,)), ((), ())), preferred_element_type=jnp.float32
    )


def contract_cols(left, right):
    return lax.dot_general(
        left, right, (((1,), (1,)), ((), ())), preferred_element_type=jnp.float32
    )


def general_shards(tokens, grad_out, route_ids, route_weight, gate_weight, up_weight, down_weight):
    tokens, grad_out = (
        lax.all_gather(tokens, "ffn", axis=1, tiled=True),
        lax.all_gather(grad_out, "ffn", axis=1, tiled=True),
    )
    tok_dev, width = tokens.shape
    top_count = route_ids.shape[1]
    piece_width = gate_weight.shape[1]
    hidden_half = gate_weight.shape[2]
    pieces = width // piece_width
    devices = lax.axis_size("expert")
    flight = devices // pieces
    halves = lax.axis_size("ffn")
    sub_width = piece_width // halves
    capacity = max(2, min(tok_dev, (9 * tok_dev * top_count + 8 * EXPERTS - 1) // (8 * EXPERTS)))
    total_rows = devices * capacity
    expert_ids = jnp.arange(flight, dtype=jnp.int32)
    member = jnp.zeros((tok_dev, flight), jnp.float32)
    mixing = jnp.zeros((tok_dev, flight), jnp.float32)
    for route in range(top_count):
        hit = (route_ids[:, route : route + 1] == expert_ids[None, :]).astype(jnp.float32)
        member = member + hit
        mixing = mixing + hit * route_weight[:, route : route + 1]
    slots = jnp.cumsum(member, axis=0) - member
    place = member[:, :, None] * (
        slots[:, :, None] == jnp.arange(capacity, dtype=jnp.float32)
    ).astype(jnp.float32)
    weighted = place * mixing[:, :, None]
    place_low = place.astype(jnp.bfloat16)
    x_four = tokens.reshape(tok_dev, halves, pieces, sub_width)
    g_four = grad_out.reshape(tok_dev, halves, pieces, sub_width)
    x_parts = []
    g_parts = []
    for half in range(halves):
        x_parts.append(
            jnp.einsum(
                "Tec,Tjr->ejcr", place_low, x_four[:, half], preferred_element_type=jnp.float32
            )
        )
        g_parts.append(jnp.einsum("Tec,Tjr->ejcr", weighted, g_four[:, half].astype(jnp.float32)))
    x_send = jnp.concatenate(x_parts, axis=3).astype(jnp.bfloat16).reshape(total_rows, piece_width)
    g_send = jnp.concatenate(g_parts, axis=3).astype(jnp.bfloat16).reshape(total_rows, piece_width)

    def return_parts(values):
        arrived = lax.all_to_all(values, "expert", split_axis=0, concat_axis=0, tiled=True)
        lanes = arrived.shape[1]
        return arrived.astype(jnp.float32).reshape(flight, pieces, capacity, lanes).sum(axis=1)

    def spread_rows(values):
        lanes = values.shape[2]
        copies = jnp.broadcast_to(values[:, None], (flight, pieces, capacity, lanes)).reshape(
            total_rows, lanes
        )
        return lax.all_to_all(copies, "expert", split_axis=0, concat_axis=0, tiled=True)

    def finish(term, mix):
        summed = lax.psum_scatter(term, "ffn", scatter_dimension=1, tiled=True)
        back = lax.all_to_all(summed, "expert", split_axis=0, concat_axis=0, tiled=True)
        back = back.reshape(flight, pieces, capacity, sub_width)
        joined = jnp.einsum("Tec,ejcr->Tjr", mix, back)
        return joined.reshape(tok_dev, pieces * sub_width).astype(jnp.bfloat16)

    rows = lax.all_to_all(x_send, "expert", split_axis=0, concat_axis=0, tiled=True)
    w_gate = gate_weight[0]
    w_up = up_weight[0]
    w_down = down_weight[0]
    partial_value = jnp.concatenate(
        [
            jnp.dot(rows, w_gate, preferred_element_type=jnp.float32),
            jnp.dot(rows, w_up, preferred_element_type=jnp.float32),
        ],
        axis=1,
    )
    summed = return_parts(partial_value.astype(jnp.bfloat16))
    gate = summed[:, :, :hidden_half]
    up = summed[:, :, hidden_half:]
    sig = jax.nn.sigmoid(gate)
    act = gate * sig
    hidden = (act * up).astype(jnp.bfloat16)
    h_rows = spread_rows(hidden)
    out_term = jnp.dot(h_rows, w_down, preferred_element_type=jnp.float32)
    out_tokens = finish(out_term, weighted)
    grads = lax.all_to_all(g_send, "expert", split_axis=0, concat_axis=0, tiled=True)
    grad_down = contract_rows(h_rows, grads).astype(jnp.bfloat16)
    hidden_part = contract_cols(grads, w_down).astype(jnp.bfloat16)
    grad_hidden = return_parts(hidden_part)
    pre_gate = (grad_hidden * up * sig * (1.0 + gate * (1.0 - sig))).astype(jnp.bfloat16)
    pre_up = (grad_hidden * act).astype(jnp.bfloat16)
    both = spread_rows(jnp.concatenate([pre_gate, pre_up], axis=2))
    d_gate_rows = both[:, :hidden_half]
    d_up_rows = both[:, hidden_half:]
    grad_gate = contract_rows(rows, d_gate_rows).astype(jnp.bfloat16)
    grad_up = contract_rows(rows, d_up_rows).astype(jnp.bfloat16)
    x_term = contract_cols(d_gate_rows, w_gate) + contract_cols(d_up_rows, w_up)
    grad_tokens = finish(x_term, place)
    return (out_tokens, grad_tokens, grad_gate[None], grad_up[None], grad_down[None])


def vmem(shape, dtype):
    return pltpu.VMEM(shape, dtype)


def call(kernel, out_shape, args, in_spaces=None, out_spaces=None, flops=0, traffic=0, scratch=(), limit=16):
    spaces = in_spaces or [pltpu.VMEM] * len(args)
    outs = out_spaces or [pltpu.VMEM] * len(out_shape)
    return pl.pallas_call(
        kernel,
        out_shape=tuple(out_shape),
        in_specs=[pl.BlockSpec(memory_space=space) for space in spaces],
        out_specs=tuple(pl.BlockSpec(memory_space=space) for space in outs),
        scratch_shapes=list(scratch),
        compiler_params=pltpu.CompilerParams(vmem_limit_bytes=limit * MIB),
        cost_estimate=pl.CostEstimate(flops=flops, bytes_accessed=traffic, transcendentals=0),
    )(*args)


def rows_to_blocks(scratch, out, take, subs):
    devices, size, _ = out.shape
    for sub in range(subs):
        scratch[pl.ds(sub, devices * size // subs, stride=subs), :] = take(sub)
    for place in range(devices):
        out[place] = scratch[place * size : (place + 1) * size, :].astype(out.dtype)


def blocks_to_rows(scratch, blocks, put, subs):
    devices, size, _ = blocks.shape
    for place in range(devices):
        scratch[place * size : (place + 1) * size, :] = blocks[place].astype(jnp.float32)
    for sub in range(subs):
        put(sub, scratch[pl.ds(sub, devices * size // subs, stride=subs), :])


def route_kernel(
    devices, capacity, subs, ids_in, weight_in, x_in, g_in, x_out, g_out, place_out, mix_out, scratch, ids, weight, x, g, sems
):
    pairs = ((ids_in, ids), (weight_in, weight), (x_in, x), (g_in, g))
    copies = [pltpu.make_async_copy(src, dst, sems.at[i]) for i, (src, dst) in enumerate(pairs)]
    for copy in copies:
        copy.start()
    top, tok = ids.shape
    rows = devices * capacity
    expert = lax.broadcasted_iota(jnp.int32, (devices, tok), 0)
    member = jnp.zeros((devices, tok), jnp.float32)
    mixing = jnp.zeros((devices, tok), jnp.float32)
    copies[0].wait()
    copies[1].wait()
    for route in range(top):
        hit = ids[route : route + 1, :] == expert
        member = jnp.where(hit, 1.0, member)
        mixing = jnp.where(hit, weight[route : route + 1, :], mixing)
    before = lax.broadcasted_iota(jnp.int32, (tok, tok), 0) < lax.broadcasted_iota(jnp.int32, (tok, tok), 1)
    slots = jnp.dot(
        member.astype(jnp.bfloat16),
        jnp.where(before, 1.0, 0.0).astype(jnp.bfloat16),
        preferred_element_type=jnp.float32,
    )
    target = jnp.where(member > 0, slots + capacity * expert.astype(jnp.float32), -1.0)
    row = lax.broadcasted_iota(jnp.int32, (rows, tok), 0).astype(jnp.float32)
    place = jnp.zeros((rows, tok), jnp.float32)
    mix = jnp.zeros((rows, tok), jnp.float32)
    for k in range(devices):
        equal = target[k : k + 1, :] == row
        place = jnp.where(equal, 1.0, place)
        mix = jnp.where(equal, mixing[k : k + 1, :], mix)
    row_weight = jnp.broadcast_to(jnp.sum(mix, axis=1, keepdims=True), (rows, LANES))
    low = place.astype(jnp.bfloat16)
    place_out[...] = low
    mix_out[...] = row_weight

    def x_part(sub):
        return jnp.dot(low, x[:, sub * LANES : (sub + 1) * LANES], preferred_element_type=jnp.float32)

    def g_part(sub):
        part = jnp.dot(low, g[:, sub * LANES : (sub + 1) * LANES], preferred_element_type=jnp.float32)
        return part * row_weight

    copies[2].wait()
    rows_to_blocks(scratch, x_out, x_part, subs)
    copies[3].wait()
    rows_to_blocks(scratch, g_out, g_part, subs)


def hold_kernel(count, *refs):
    sems = refs[2 * count]
    copies = [pltpu.make_async_copy(refs[i], refs[count + i], sems.at[i]) for i in range(count)]
    for copy in copies:
        copy.start()
    for copy in copies:
        copy.wait()


def arrive_kernel(subs, blocks, out, scratch):
    def put(sub, value):
        out[:, sub * LANES : (sub + 1) * LANES] = value.astype(out.dtype)

    blocks_to_rows(scratch, blocks, put, subs)


def leave_kernel(subs, own, other, out, scratch):
    def take(sub):
        cols = slice(sub * LANES, (sub + 1) * LANES)
        return own[:, cols] + other[:, cols].astype(jnp.float32)

    rows_to_blocks(scratch, out, take, subs)


def forward_kernel(step, x_own, x_other, w_gate, w_up, w_down, x_full, gate, up, hidden, out_own, out_other):
    half_width = x_own.shape[1]
    lanes = gate.shape[1]
    half = lax.axis_index("ffn")
    own_at = pl.multiple_of(half * half_width, half_width)
    other_at = pl.multiple_of((1 - half) * half_width, half_width)
    x_full[:, pl.ds(own_at, half_width)] = x_own[...]
    x_full[:, pl.ds(other_at, half_width)] = x_other[...]

    def project(i, carry):
        cols = pl.ds(pl.multiple_of(i * step, step), step)
        gate_low = jnp.dot(x_full[...], w_gate[0, :, cols], preferred_element_type=jnp.float32).astype(jnp.bfloat16)
        up_low = jnp.dot(x_full[...], w_up[0, :, cols], preferred_element_type=jnp.float32).astype(jnp.bfloat16)
        gate[:, cols] = gate_low
        up[:, cols] = up_low
        gate_val = gate_low.astype(jnp.float32)
        hidden[:, cols] = (gate_val * jax.nn.sigmoid(gate_val) * up_low.astype(jnp.float32)).astype(jnp.bfloat16)
        return carry

    lax.fori_loop(0, lanes // step, project, 0)

    def spread(i, carry):
        at = pl.multiple_of(i * step, step)
        here = pl.ds(at, step)
        other = jnp.dot(hidden[...], w_down[0, :, pl.ds(other_at + at, step)], preferred_element_type=jnp.float32)
        out_other[:, here] = other.astype(jnp.bfloat16)
        out_own[:, here] = jnp.dot(hidden[...], w_down[0, :, pl.ds(own_at + at, step)], preferred_element_type=jnp.float32)
        return carry

    lax.fori_loop(0, half_width // step, spread, 0)


def backward_kernel(
    step, g_own, g_other, gate, up, w_gate, w_up, w_down, g_full, pre_gate, pre_up, dx_own, dx_other
):
    half_width = g_own.shape[1]
    lanes = gate.shape[1]
    half = lax.axis_index("ffn")
    own_at = pl.multiple_of(half * half_width, half_width)
    other_at = pl.multiple_of((1 - half) * half_width, half_width)
    g_full[:, pl.ds(own_at, half_width)] = g_own[...]
    g_full[:, pl.ds(other_at, half_width)] = g_other[...]

    def pull(i, carry):
        cols = pl.ds(pl.multiple_of(i * step, step), step)
        part = contract_cols(g_full[...], w_down[0, cols, :]).astype(jnp.bfloat16)
        grad_hidden = part.astype(jnp.float32)
        gate_val = gate[:, cols].astype(jnp.float32)
        up_val = up[:, cols].astype(jnp.float32)
        sig = jax.nn.sigmoid(gate_val)
        pre_gate[:, cols] = (grad_hidden * up_val * sig * (1.0 + gate_val * (1.0 - sig))).astype(jnp.bfloat16)
        pre_up[:, cols] = (grad_hidden * gate_val * sig).astype(jnp.bfloat16)
        return carry

    lax.fori_loop(0, lanes // step, pull, 0)

    def spread(i, carry):
        at = pl.multiple_of(i * step, step)
        here = pl.ds(at, step)

        def term(base):
            there = pl.ds(base + at, step)
            return contract_cols(pre_gate[...], w_gate[0, there, :]) + contract_cols(pre_up[...], w_up[0, there, :])

        dx_other[:, here] = term(other_at).astype(jnp.bfloat16)
        dx_own[:, here] = term(own_at)
        return carry

    lax.fori_loop(0, half_width // step, spread, 0)


def tall_outer_kernel(left, *refs):
    count = len(refs) // 2
    for right, out in zip(refs[:count], refs[count:]):
        out[0] = contract_rows(left[...], right[...]).astype(out.dtype)


def tall_outer(left, rights, step):
    rows, height = left.shape
    width = rights[0].shape[1]
    return pl.pallas_call(
        tall_outer_kernel,
        grid=(height // step,),
        out_shape=tuple(jax.ShapeDtypeStruct((1, height, width), jnp.bfloat16) for _ in rights),
        in_specs=[pl.BlockSpec((rows, step), lambda i: (0, i))]
        + [pl.BlockSpec((rows, width), lambda i: (0, 0)) for _ in rights],
        out_specs=tuple(pl.BlockSpec((1, step, width), lambda i: (0, i, 0)) for _ in rights),
        compiler_params=pltpu.CompilerParams(vmem_limit_bytes=24 * MIB),
        cost_estimate=pl.CostEstimate(
            flops=2 * rows * height * width * len(rights),
            bytes_accessed=2 * height * width * len(rights),
            transcendentals=0,
        ),
    )(left, *rights)


def wide_outer_kernel(left, right, out, flipped):
    @pl.when(pl.program_id(0) == 0)
    def _():
        flipped[...] = left[...].astype(jnp.float32).T.astype(flipped.dtype)

    out[0] = jnp.dot(flipped[...], right[...], preferred_element_type=jnp.float32).astype(out.dtype)


def wide_outer(left, right, step):
    rows, height = left.shape
    width = right.shape[1]
    return pl.pallas_call(
        wide_outer_kernel,
        grid=(width // step,),
        out_shape=jax.ShapeDtypeStruct((1, height, width), jnp.bfloat16),
        in_specs=[pl.BlockSpec((rows, height), lambda i: (0, 0)), pl.BlockSpec((rows, step), lambda i: (0, i))],
        out_specs=pl.BlockSpec((1, height, step), lambda i: (0, 0, i)),
        scratch_shapes=[pltpu.VMEM((height, rows), jnp.bfloat16)],
        compiler_params=pltpu.CompilerParams(vmem_limit_bytes=24 * MIB),
        cost_estimate=pl.CostEstimate(
            flops=2 * rows * height * width, bytes_accessed=2 * height * width, transcendentals=0
        ),
    )(left, right)


def join_kernel(weighted, subs, place, mix, blocks, out, scratch):
    def put(sub, value):
        if weighted:
            value = value * mix[...]
        out[:, sub * LANES : (sub + 1) * LANES] = contract_rows(place[...], value.astype(jnp.bfloat16)).astype(out.dtype)

    blocks_to_rows(scratch, blocks, put, subs)


def exchange(blocks):
    return lax.all_to_all(blocks, "expert", split_axis=0, concat_axis=0, tiled=True)


def swap(value):
    return lax.ppermute(value, "ffn", [(0, 1), (1, 0)])


def one_piece_shards(tokens, grad_out, route_ids, route_weight, gate_weight, up_weight, down_weight):
    tok_dev, sub_width = tokens.shape
    top_count = route_ids.shape[1]
    width = gate_weight.shape[1]
    lanes = gate_weight.shape[2]
    devices = lax.axis_size("expert")
    capacity = max(2, min(tok_dev, (9 * tok_dev * top_count + 8 * EXPERTS - 1) // (8 * EXPERTS)))
    rows = devices * capacity
    subs = sub_width // LANES
    low = jnp.bfloat16
    blocks = jax.ShapeDtypeStruct((devices, capacity * subs, LANES), low)
    spread_scratch = [pltpu.VMEM((rows * subs, LANES), jnp.float32)]

    sources = (route_ids.T, route_weight.T, tokens, grad_out)
    x_sent, g_sent, place, mix = call(
        functools.partial(route_kernel, devices, capacity, subs),
        [blocks, blocks, jax.ShapeDtypeStruct((rows, tok_dev), low), jax.ShapeDtypeStruct((rows, LANES), jnp.float32)],
        [pltpu.with_memory_space_constraint(value, pltpu.HBM) for value in sources],
        in_spaces=[pl.ANY] * 4,
        scratch=spread_scratch
        + [pltpu.VMEM(value.shape, value.dtype) for value in sources]
        + [pltpu.SemaphoreType.DMA((4,))],
        traffic=4 * tok_dev * sub_width,
    )
    x_blocks = exchange(x_sent)
    g_blocks = exchange(g_sent)

    weights = (gate_weight, up_weight, down_weight)
    w_gate, w_up, w_down = call(
        functools.partial(hold_kernel, 3),
        [vmem(w.shape, w.dtype) for w in weights],
        [pltpu.with_memory_space_constraint(w, pltpu.HBM) for w in weights],
        in_spaces=[pl.ANY] * 3,
        scratch=[pltpu.SemaphoreType.DMA((3,))],
        traffic=sum(w.size * 2 for w in weights),
    )

    def arrive(blocks):
        return call(
            functools.partial(arrive_kernel, subs),
            [vmem((rows, sub_width), low)],
            (blocks,),
            scratch=spread_scratch,
            traffic=4 * rows * sub_width,
        )[0]

    x_own = arrive(x_blocks)
    x_other = swap(x_own)
    step = 256
    x_full, gate, up, hidden, out_own, out_other = call(
        functools.partial(forward_kernel, step),
        [
            vmem((rows, width), low),
            vmem((rows, lanes), low),
            vmem((rows, lanes), low),
            vmem((rows, lanes), low),
            vmem((rows, sub_width), jnp.float32),
            vmem((rows, sub_width), low),
        ],
        (x_own, x_other, w_gate, w_up, w_down),
        flops=6 * rows * width * lanes,
    )
    out_arrived = swap(out_other)
    g_own = arrive(g_blocks)
    g_other = swap(g_own)
    g_full, pre_gate, pre_up, dx_own, dx_other = call(
        functools.partial(backward_kernel, step),
        [
            vmem((rows, width), low),
            vmem((rows, lanes), low),
            vmem((rows, lanes), low),
            vmem((rows, sub_width), jnp.float32),
            vmem((rows, sub_width), low),
        ],
        (g_own, g_other, gate, up, w_gate, w_up, w_down),
        flops=6 * rows * width * lanes,
    )
    dx_arrived = swap(dx_other)

    def leave(own, other):
        return call(
            functools.partial(leave_kernel, subs),
            [blocks],
            (own, other),
            scratch=spread_scratch,
            traffic=8 * rows * sub_width,
        )[0]

    out_blocks = exchange(leave(out_own, out_arrived))
    dx_blocks = exchange(leave(dx_own, dx_arrived))
    grad_down = wide_outer(hidden, g_full, 512)
    grad_gate, grad_up = tall_outer(x_full, [pre_gate, pre_up], 1024)

    def join(weighted, blocks):
        return call(
            functools.partial(join_kernel, weighted, subs),
            [jax.ShapeDtypeStruct((tok_dev, sub_width), low)],
            (place, mix, blocks),
            scratch=spread_scratch,
            traffic=4 * tok_dev * sub_width,
        )[0]

    return join(True, out_blocks), join(False, dx_blocks), grad_gate, grad_up, grad_down


def shards(*args):
    tokens, gate_weight = args[0], args[4]
    halves = lax.axis_size("ffn")
    if halves == 2 and tokens.shape[1] * halves == gate_weight.shape[1]:
        return one_piece_shards(*args)
    return general_shards(*args)


def solution(mesh):
    in_specs = (
        P(("groups", "expert"), "ffn"),
        P(("groups", "expert"), "ffn"),
        P(("groups", "expert"), None),
        P(("groups", "expert"), None),
        P("expert", None, "ffn"),
        P("expert", None, "ffn"),
        P("expert", "ffn", None),
    )
    out_specs = (
        P(("groups", "expert"), "ffn"),
        P(("groups", "expert"), "ffn"),
        P(("groups", "expert"), None, "ffn"),
        P(("groups", "expert"), None, "ffn"),
        P(("groups", "expert"), "ffn", None),
    )
    return jax.shard_map(shards, mesh=mesh, in_specs=in_specs, out_specs=out_specs, check_vma=False)
```

```python
import functools

import jax
import jax.numpy as jnp
from jax import lax
from jax.experimental import pallas as pl
from jax.experimental.pallas import tpu as pltpu
from jax.sharding import PartitionSpec as P

EXPERTS = 128
LANES = 128
MIB = 1024 * 1024


def contract_rows(left, right):
    return lax.dot_general(
        left, right, (((0,), (0,)), ((), ())), preferred_element_type=jnp.float32
    )


def contract_cols(left, right):
    return lax.dot_general(
        left, right, (((1,), (1,)), ((), ())), preferred_element_type=jnp.float32
    )


def general_shards(tokens, grad_out, route_ids, route_weight, gate_weight, up_weight, down_weight):
    tokens, grad_out = (
        lax.all_gather(tokens, "ffn", axis=1, tiled=True),
        lax.all_gather(grad_out, "ffn", axis=1, tiled=True),
    )
    tok_dev, width = tokens.shape
    top_count = route_ids.shape[1]
    piece_width = gate_weight.shape[1]
    hidden_half = gate_weight.shape[2]
    pieces = width // piece_width
    devices = lax.axis_size("expert")
    flight = devices // pieces
    halves = lax.axis_size("ffn")
    sub_width = piece_width // halves
    capacity = max(2, min(tok_dev, (9 * tok_dev * top_count + 8 * EXPERTS - 1) // (8 * EXPERTS)))
    total_rows = devices * capacity
    expert_ids = jnp.arange(flight, dtype=jnp.int32)
    member = jnp.zeros((tok_dev, flight), jnp.float32)
    mixing = jnp.zeros((tok_dev, flight), jnp.float32)
    for route in range(top_count):
        hit = (route_ids[:, route : route + 1] == expert_ids[None, :]).astype(jnp.float32)
        member = member + hit
        mixing = mixing + hit * route_weight[:, route : route + 1]
    slots = jnp.cumsum(member, axis=0) - member
    place = member[:, :, None] * (
        slots[:, :, None] == jnp.arange(capacity, dtype=jnp.float32)
    ).astype(jnp.float32)
    weighted = place * mixing[:, :, None]
    place_low = place.astype(jnp.bfloat16)
    x_four = tokens.reshape(tok_dev, halves, pieces, sub_width)
    g_four = grad_out.reshape(tok_dev, halves, pieces, sub_width)
    x_parts = []
    g_parts = []
    for half in range(halves):
        x_parts.append(
            jnp.einsum(
                "Tec,Tjr->ejcr", place_low, x_four[:, half], preferred_element_type=jnp.float32
            )
        )
        g_parts.append(jnp.einsum("Tec,Tjr->ejcr", weighted, g_four[:, half].astype(jnp.float32)))
    x_send = jnp.concatenate(x_parts, axis=3).astype(jnp.bfloat16).reshape(total_rows, piece_width)
    g_send = jnp.concatenate(g_parts, axis=3).astype(jnp.bfloat16).reshape(total_rows, piece_width)

    def return_parts(values):
        arrived = lax.all_to_all(values, "expert", split_axis=0, concat_axis=0, tiled=True)
        lanes = arrived.shape[1]
        return arrived.astype(jnp.float32).reshape(flight, pieces, capacity, lanes).sum(axis=1)

    def spread_rows(values):
        lanes = values.shape[2]
        copies = jnp.broadcast_to(values[:, None], (flight, pieces, capacity, lanes)).reshape(
            total_rows, lanes
        )
        return lax.all_to_all(copies, "expert", split_axis=0, concat_axis=0, tiled=True)

    def finish(term, mix):
        summed = lax.psum_scatter(term, "ffn", scatter_dimension=1, tiled=True)
        back = lax.all_to_all(summed, "expert", split_axis=0, concat_axis=0, tiled=True)
        back = back.reshape(flight, pieces, capacity, sub_width)
        joined = jnp.einsum("Tec,ejcr->Tjr", mix, back)
        return joined.reshape(tok_dev, pieces * sub_width).astype(jnp.bfloat16)

    rows = lax.all_to_all(x_send, "expert", split_axis=0, concat_axis=0, tiled=True)
    w_gate = gate_weight[0]
    w_up = up_weight[0]
    w_down = down_weight[0]
    partial_value = jnp.concatenate(
        [
            jnp.dot(rows, w_gate, preferred_element_type=jnp.float32),
            jnp.dot(rows, w_up, preferred_element_type=jnp.float32),
        ],
        axis=1,
    )
    summed = return_parts(partial_value.astype(jnp.bfloat16))
    gate = summed[:, :, :hidden_half]
    up = summed[:, :, hidden_half:]
    sig = jax.nn.sigmoid(gate)
    act = gate * sig
    hidden = (act * up).astype(jnp.bfloat16)
    h_rows = spread_rows(hidden)
    out_term = jnp.dot(h_rows, w_down, preferred_element_type=jnp.float32)
    out_tokens = finish(out_term, weighted)
    grads = lax.all_to_all(g_send, "expert", split_axis=0, concat_axis=0, tiled=True)
    grad_down = contract_rows(h_rows, grads).astype(jnp.bfloat16)
    hidden_part = contract_cols(grads, w_down).astype(jnp.bfloat16)
    grad_hidden = return_parts(hidden_part)
    pre_gate = (grad_hidden * up * sig * (1.0 + gate * (1.0 - sig))).astype(jnp.bfloat16)
    pre_up = (grad_hidden * act).astype(jnp.bfloat16)
    both = spread_rows(jnp.concatenate([pre_gate, pre_up], axis=2))
    d_gate_rows = both[:, :hidden_half]
    d_up_rows = both[:, hidden_half:]
    grad_gate = contract_rows(rows, d_gate_rows).astype(jnp.bfloat16)
    grad_up = contract_rows(rows, d_up_rows).astype(jnp.bfloat16)
    x_term = contract_cols(d_gate_rows, w_gate) + contract_cols(d_up_rows, w_up)
    grad_tokens = finish(x_term, place)
    return (out_tokens, grad_tokens, grad_gate[None], grad_up[None], grad_down[None])


def vmem(shape, dtype):
    return pltpu.VMEM(shape, dtype)


def call(kernel, out_shape, args, in_spaces=None, out_spaces=None, flops=0, traffic=0, scratch=(), limit=16):
    spaces = in_spaces or [pltpu.VMEM] * len(args)
    outs = out_spaces or [pltpu.VMEM] * len(out_shape)
    return pl.pallas_call(
        kernel,
        out_shape=tuple(out_shape),
        in_specs=[pl.BlockSpec(memory_space=space) for space in spaces],
        out_specs=tuple(pl.BlockSpec(memory_space=space) for space in outs),
        scratch_shapes=list(scratch),
        compiler_params=pltpu.CompilerParams(vmem_limit_bytes=limit * MIB),
        cost_estimate=pl.CostEstimate(flops=flops, bytes_accessed=traffic, transcendentals=0),
    )(*args)


def rows_to_blocks(scratch, outs, at, take, subs):
    total = scratch.shape[0]
    size = total // len(outs)
    for sub in range(subs):
        scratch[pl.ds(sub, total // subs, stride=subs), :] = take(sub)
    for k, out in enumerate(outs):
        out[at : at + size, :] = scratch[k * size : (k + 1) * size, :].astype(out.dtype)


def blocks_to_rows(scratch, blocks, at, put, subs):
    total = scratch.shape[0]
    size = total // len(blocks)
    for k, block in enumerate(blocks):
        scratch[k * size : (k + 1) * size, :] = block[at : at + size, :].astype(jnp.float32)
    for sub in range(subs):
        put(sub, scratch[pl.ds(sub, total // subs, stride=subs), :])


def lanes_of(sub):
    return slice(sub * LANES, (sub + 1) * LANES)


def route_kernel(devices, capacity, subs, ids_in, weight_in, x_in, g_in, *refs):
    outs, (place_out, mix_out, scratch, ids, weight, x, g, sems) = refs[:devices], refs[devices:]
    pairs = ((ids_in, ids), (weight_in, weight), (x_in, x), (g_in, g))
    copies = [pltpu.make_async_copy(src, dst, sems.at[i]) for i, (src, dst) in enumerate(pairs)]
    for copy in copies:
        copy.start()
    top, tok = ids.shape
    rows = devices * capacity
    order = lax.broadcasted_iota(jnp.int32, (devices, tok), 0)
    expert = order ^ lax.axis_index("expert")
    member = jnp.zeros((devices, tok), jnp.float32)
    mixing = jnp.zeros((devices, tok), jnp.float32)
    copies[0].wait()
    copies[1].wait()
    for route in range(top):
        hit = ids[route : route + 1, :] == expert
        member = jnp.where(hit, 1.0, member)
        mixing = jnp.where(hit, weight[route : route + 1, :], mixing)
    before = lax.broadcasted_iota(jnp.int32, (tok, tok), 0) < lax.broadcasted_iota(jnp.int32, (tok, tok), 1)
    slots = jnp.dot(
        member.astype(jnp.bfloat16),
        jnp.where(before, 1.0, 0.0).astype(jnp.bfloat16),
        preferred_element_type=jnp.float32,
    )
    target = jnp.where(member > 0, slots + capacity * order.astype(jnp.float32), -1.0)
    row = lax.broadcasted_iota(jnp.int32, (rows, tok), 0).astype(jnp.float32)
    place = jnp.zeros((rows, tok), jnp.float32)
    mix = jnp.zeros((rows, tok), jnp.float32)
    for k in range(devices):
        equal = target[k : k + 1, :] == row
        place = jnp.where(equal, 1.0, place)
        mix = jnp.where(equal, mixing[k : k + 1, :], mix)
    row_weight = jnp.broadcast_to(jnp.sum(mix, axis=1, keepdims=True), (rows, LANES))
    low = place.astype(jnp.bfloat16)
    place_out[...] = low
    mix_out[...] = row_weight

    def x_part(sub):
        return jnp.dot(low, x[:, lanes_of(sub)], preferred_element_type=jnp.float32)

    def g_part(sub):
        return jnp.dot(low, g[:, lanes_of(sub)], preferred_element_type=jnp.float32) * row_weight

    copies[2].wait()
    rows_to_blocks(scratch, outs, 0, x_part, subs)
    copies[3].wait()
    rows_to_blocks(scratch, outs, capacity * subs, g_part, subs)


def hold_kernel(count, *refs):
    held, sems = refs[2 * count :]
    held[...] = jnp.zeros_like(held)
    copies = [pltpu.make_async_copy(refs[i], refs[count + i], sems.at[i]) for i in range(count)]
    for copy in copies:
        copy.start()
    for copy in copies:
        copy.wait()


def arrive_kernel(devices, capacity, subs, *refs):
    blocks, (_, x_own, g_own, scratch) = refs[:devices], refs[devices:]

    def put_into(out):
        def put(sub, value):
            out[:, lanes_of(sub)] = value.astype(out.dtype)

        return put

    blocks_to_rows(scratch, blocks, 0, put_into(x_own), subs)
    blocks_to_rows(scratch, blocks, capacity * subs, put_into(g_own), subs)


def leave_kernel(capacity, subs, out_own, out_other, dx_own, dx_other, *refs):
    outs, scratch = refs[:-1], refs[-1]

    def sum_of(own, other):
        def take(sub):
            return own[:, lanes_of(sub)] + other[:, lanes_of(sub)].astype(jnp.float32)

        return take

    rows_to_blocks(scratch, outs, 0, sum_of(out_own, out_other), subs)
    rows_to_blocks(scratch, outs, capacity * subs, sum_of(dx_own, dx_other), subs)


def join_kernel(devices, capacity, subs, place, mix, *refs):
    blocks, (out_tokens, grad_tokens, scratch) = refs[:devices], refs[devices:]

    def put_out(sub, value):
        low = (value * mix[...]).astype(jnp.bfloat16)
        out_tokens[:, lanes_of(sub)] = contract_rows(place[...], low).astype(out_tokens.dtype)

    def put_grad(sub, value):
        grad_tokens[:, lanes_of(sub)] = contract_rows(place[...], value.astype(jnp.bfloat16)).astype(grad_tokens.dtype)

    blocks_to_rows(scratch, blocks, 0, put_out, subs)
    blocks_to_rows(scratch, blocks, capacity * subs, put_grad, subs)


def half_starts(half_width):
    half = lax.axis_index("ffn")
    own = pl.multiple_of(half * half_width, half_width)
    other = pl.multiple_of((1 - half) * half_width, half_width)
    return own, other


def chunk(i, step, base=0):
    return pl.ds(base + pl.multiple_of(i * step, step), step)


def dot(left, right):
    return jnp.dot(left, right, preferred_element_type=jnp.float32)


def project_own_kernel(step, x_own, w_gate, w_up, gate_part, up_part):
    half_width = x_own.shape[1]
    own, _ = half_starts(half_width)
    rows = pl.ds(own, half_width)

    def project(i, carry):
        cols = chunk(i, step)
        gate_part[:, cols] = dot(x_own[...], w_gate[0, rows, cols])
        up_part[:, cols] = dot(x_own[...], w_up[0, rows, cols])
        return carry

    lax.fori_loop(0, gate_part.shape[1] // step, project, 0)


def forward_kernel(
    step, x_own, x_other, gate_part, up_part, w_gate, w_up, w_down, x_full, gate, up, hidden, out_own, out_other
):
    half_width = x_own.shape[1]
    own, other = half_starts(half_width)
    x_full[:, pl.ds(own, half_width)] = x_own[...]
    x_full[:, pl.ds(other, half_width)] = x_other[...]
    rows = pl.ds(other, half_width)

    def project(i, carry):
        cols = chunk(i, step)
        gate_low = (gate_part[:, cols] + dot(x_other[...], w_gate[0, rows, cols])).astype(jnp.bfloat16)
        up_low = (up_part[:, cols] + dot(x_other[...], w_up[0, rows, cols])).astype(jnp.bfloat16)
        gate[:, cols] = gate_low
        up[:, cols] = up_low
        value = gate_low.astype(jnp.float32)
        hidden[:, cols] = (value * jax.nn.sigmoid(value) * up_low.astype(jnp.float32)).astype(jnp.bfloat16)
        return carry

    lax.fori_loop(0, gate.shape[1] // step, project, 0)

    def spread(i, carry):
        here = chunk(i, step)
        out_other[:, here] = dot(hidden[...], w_down[0, :, chunk(i, step, other)]).astype(jnp.bfloat16)
        out_own[:, here] = dot(hidden[...], w_down[0, :, chunk(i, step, own)])
        return carry

    lax.fori_loop(0, half_width // step, spread, 0)


def input_term(pre_gate, pre_up, w_gate, w_up, there):
    return contract_cols(pre_gate[...], w_gate[0, there, :]) + contract_cols(pre_up[...], w_up[0, there, :])


def backward_kernel(step, g_own, g_other, gate, up, w_gate, w_up, w_down, g_full, pre_gate, pre_up, dx_other):
    half_width = g_own.shape[1]
    own, other = half_starts(half_width)
    g_full[:, pl.ds(own, half_width)] = g_own[...]
    g_full[:, pl.ds(other, half_width)] = g_other[...]

    def pull(i, carry):
        cols = chunk(i, step)
        part = contract_cols(g_full[...], w_down[0, cols, :]).astype(jnp.bfloat16)
        grad_hidden = part.astype(jnp.float32)
        value = gate[:, cols].astype(jnp.float32)
        sig = jax.nn.sigmoid(value)
        pre_gate[:, cols] = (
            grad_hidden * up[:, cols].astype(jnp.float32) * sig * (1.0 + value * (1.0 - sig))
        ).astype(jnp.bfloat16)
        pre_up[:, cols] = (grad_hidden * value * sig).astype(jnp.bfloat16)
        return carry

    lax.fori_loop(0, gate.shape[1] // step, pull, 0)

    def spread(i, carry):
        dx_other[:, chunk(i, step)] = input_term(pre_gate, pre_up, w_gate, w_up, chunk(i, step, other)).astype(
            jnp.bfloat16
        )
        return carry

    lax.fori_loop(0, half_width // step, spread, 0)


def backward_own_kernel(step, pre_gate, pre_up, w_gate, w_up, dx_own):
    half_width = dx_own.shape[1]
    own, _ = half_starts(half_width)

    def spread(i, carry):
        dx_own[:, chunk(i, step)] = input_term(pre_gate, pre_up, w_gate, w_up, chunk(i, step, own))
        return carry

    lax.fori_loop(0, half_width // step, spread, 0)


def gradient_kernel(
    step, x, g, hidden, pre_gate, pre_up, grad_gate, grad_up, grad_down, flipped, tall, wide, tall_sems, wide_sems
):
    width, lanes = x.shape[1], hidden.shape[1]
    count = width // step
    flipped[...] = hidden[...].astype(jnp.float32).T.astype(flipped.dtype)

    def wide_copy(i, slot):
        return pltpu.make_async_copy(wide.at[slot], grad_down.at[0, :, chunk(i, step)], wide_sems.at[slot])

    def tall_copy(which, out, i, slot):
        return pltpu.make_async_copy(tall.at[which, slot], out.at[0, chunk(i, step), :], tall_sems.at[which, slot])

    def down(i, carry):
        slot = i % 2

        @pl.when(i >= 2)
        def _():
            wide_copy(i - 2, slot).wait()

        wide[slot] = dot(flipped[...], g[:, chunk(i, step)]).astype(wide.dtype)
        wide_copy(i, slot).start()
        return carry

    lax.fori_loop(0, count, down, 0)

    def inputs(i, carry):
        slot = i % 2
        for which, (right, out) in enumerate(((pre_gate, grad_gate), (pre_up, grad_up))):

            @pl.when(i >= 2)
            def _():
                tall_copy(which, out, i - 2, slot).wait()

            tall[which, slot] = contract_rows(x[:, chunk(i, step)], right[...]).astype(tall.dtype)
            tall_copy(which, out, i, slot).start()
        return carry

    lax.fori_loop(0, count, inputs, 0)
    for i in range(max(0, count - 2), count):
        wide_copy(i, i % 2).wait()
        tall_copy(0, grad_gate, i, i % 2).wait()
        tall_copy(1, grad_up, i, i % 2).wait()


def exchange(blocks):
    pairs = [[(i, i ^ k) for i in range(len(blocks))] for k in range(len(blocks))]
    return [blocks[0]] + [lax.ppermute(blocks[k], "expert", pairs[k]) for k in range(1, len(blocks))]


def swap(value):
    return lax.ppermute(value, "ffn", [(0, 1), (1, 0)])


def in_hbm(values):
    return [pltpu.with_memory_space_constraint(value, pltpu.HBM) for value in values]


def one_piece_shards(tokens, grad_out, route_ids, route_weight, gate_weight, up_weight, down_weight):
    tok_dev, sub_width = tokens.shape
    top_count = route_ids.shape[1]
    width, lanes = gate_weight.shape[1:]
    devices = lax.axis_size("expert")
    capacity = max(2, min(tok_dev, (9 * tok_dev * top_count + 8 * EXPERTS - 1) // (8 * EXPERTS)))
    rows = devices * capacity
    subs = sub_width // LANES
    low, full = jnp.bfloat16, jnp.float32
    blocks = [jax.ShapeDtypeStruct((2 * capacity * subs, LANES), low)] * devices
    spread_scratch = [pltpu.VMEM((rows * subs, LANES), full)]
    sizes = (devices, capacity, subs)
    step = 256
    half_flops = 2 * rows * width * lanes // 2

    sources = (route_ids.T, route_weight.T, tokens, grad_out)
    routed = call(
        functools.partial(route_kernel, *sizes),
        blocks + [jax.ShapeDtypeStruct((rows, tok_dev), low), jax.ShapeDtypeStruct((rows, LANES), full)],
        in_hbm(sources),
        in_spaces=[pl.ANY] * 4,
        scratch=spread_scratch
        + [pltpu.VMEM(value.shape, value.dtype) for value in sources]
        + [pltpu.SemaphoreType.DMA((4,))],
        traffic=4 * tok_dev * sub_width,
    )
    place, mix = routed[devices:]
    arrived = exchange(routed[:devices])

    weights = (gate_weight, up_weight, down_weight)
    w_gate, w_up, w_down, held = call(
        functools.partial(hold_kernel, 3),
        [vmem(w.shape, w.dtype) for w in weights] + [vmem((8, LANES), full)],
        in_hbm(weights),
        in_spaces=[pl.ANY] * 3,
        scratch=[pltpu.SemaphoreType.DMA((3,))],
        traffic=sum(w.size * 2 for w in weights),
    )
    x_own, g_own = call(
        functools.partial(arrive_kernel, *sizes),
        [vmem((rows, sub_width), low)] * 2,
        (*arrived, held),
        scratch=spread_scratch,
        traffic=8 * rows * sub_width,
    )
    x_other = swap(x_own)
    g_other = swap(g_own)
    gate_part, up_part = call(
        functools.partial(project_own_kernel, step),
        [vmem((rows, lanes), full)] * 2,
        (x_own, w_gate, w_up),
        flops=2 * half_flops,
    )
    x_full, gate, up, hidden, out_own, out_other = call(
        functools.partial(forward_kernel, step),
        [vmem((rows, width), low)]
        + [vmem((rows, lanes), low)] * 3
        + [vmem((rows, sub_width), full), vmem((rows, sub_width), low)],
        (x_own, x_other, gate_part, up_part, w_gate, w_up, w_down),
        flops=4 * half_flops,
    )
    out_arrived = swap(out_other)
    g_full, pre_gate, pre_up, dx_other = call(
        functools.partial(backward_kernel, step),
        [vmem((rows, width), low)] + [vmem((rows, lanes), low)] * 2 + [vmem((rows, sub_width), low)],
        (g_own, g_other, gate, up, w_gate, w_up, w_down),
        flops=4 * half_flops,
    )
    dx_arrived = swap(dx_other)
    (dx_own,) = call(
        functools.partial(backward_own_kernel, step),
        [vmem((rows, sub_width), full)],
        (pre_gate, pre_up, w_gate, w_up),
        flops=2 * half_flops,
    )
    returned = exchange(
        call(
            functools.partial(leave_kernel, capacity, subs),
            blocks,
            (out_own, out_arrived, dx_own, dx_arrived),
            scratch=spread_scratch,
            traffic=16 * rows * sub_width,
        )
    )
    cut = 1024 if width % 1024 == 0 else width
    grad_gate, grad_up, grad_down = call(
        functools.partial(gradient_kernel, cut),
        [jax.ShapeDtypeStruct(w.shape, low) for w in weights],
        (x_full, g_full, hidden, pre_gate, pre_up),
        out_spaces=[pl.ANY] * 3,
        scratch=[
            pltpu.VMEM((lanes, rows), low),
            pltpu.VMEM((2, 2, cut, lanes), low),
            pltpu.VMEM((2, lanes, cut), low),
            pltpu.SemaphoreType.DMA((2, 2)),
            pltpu.SemaphoreType.DMA((2,)),
        ],
        flops=6 * half_flops,
        traffic=sum(w.size * 2 for w in weights),
        limit=32,
    )
    out_tokens, grad_tokens = call(
        functools.partial(join_kernel, *sizes),
        [jax.ShapeDtypeStruct((tok_dev, sub_width), low)] * 2,
        (place, mix, *returned),
        scratch=spread_scratch,
        traffic=8 * tok_dev * sub_width,
    )
    return out_tokens, grad_tokens, grad_gate, grad_up, grad_down


def shards(*args):
    tokens, gate_weight = args[0], args[4]
    halves = lax.axis_size("ffn")
    devices = lax.axis_size("expert")
    if halves == 2 and devices & (devices - 1) == 0 and tokens.shape[1] * halves == gate_weight.shape[1]:
        return one_piece_shards(*args)
    return general_shards(*args)


def solution(mesh):
    in_specs = (
        P(("groups", "expert"), "ffn"),
        P(("groups", "expert"), "ffn"),
        P(("groups", "expert"), None),
        P(("groups", "expert"), None),
        P("expert", None, "ffn"),
        P("expert", None, "ffn"),
        P("expert", "ffn", None),
    )
    out_specs = (
        P(("groups", "expert"), "ffn"),
        P(("groups", "expert"), "ffn"),
        P(("groups", "expert"), None, "ffn"),
        P(("groups", "expert"), None, "ffn"),
        P(("groups", "expert"), "ffn", None),
    )
    return jax.shard_map(shards, mesh=mesh, in_specs=in_specs, out_specs=out_specs, check_vma=False)
```

```python
import functools

import jax
import jax.numpy as jnp
from jax import lax
from jax.experimental import pallas as pl
from jax.experimental.pallas import tpu as pltpu
from jax.sharding import PartitionSpec as P

EXPERTS = 128
LANES = 128
MIB = 1024 * 1024


def contract_rows(left, right):
    return lax.dot_general(
        left, right, (((0,), (0,)), ((), ())), preferred_element_type=jnp.float32
    )


def contract_cols(left, right):
    return lax.dot_general(
        left, right, (((1,), (1,)), ((), ())), preferred_element_type=jnp.float32
    )


def general_shards(tokens, grad_out, route_ids, route_weight, gate_weight, up_weight, down_weight):
    tokens, grad_out = (
        lax.all_gather(tokens, "ffn", axis=1, tiled=True),
        lax.all_gather(grad_out, "ffn", axis=1, tiled=True),
    )
    tok_dev, width = tokens.shape
    top_count = route_ids.shape[1]
    piece_width = gate_weight.shape[1]
    hidden_half = gate_weight.shape[2]
    pieces = width // piece_width
    devices = lax.axis_size("expert")
    flight = devices // pieces
    halves = lax.axis_size("ffn")
    sub_width = piece_width // halves
    capacity = max(2, min(tok_dev, (9 * tok_dev * top_count + 8 * EXPERTS - 1) // (8 * EXPERTS)))
    total_rows = devices * capacity
    expert_ids = jnp.arange(flight, dtype=jnp.int32)
    member = jnp.zeros((tok_dev, flight), jnp.float32)
    mixing = jnp.zeros((tok_dev, flight), jnp.float32)
    for route in range(top_count):
        hit = (route_ids[:, route : route + 1] == expert_ids[None, :]).astype(jnp.float32)
        member = member + hit
        mixing = mixing + hit * route_weight[:, route : route + 1]
    slots = jnp.cumsum(member, axis=0) - member
    place = member[:, :, None] * (
        slots[:, :, None] == jnp.arange(capacity, dtype=jnp.float32)
    ).astype(jnp.float32)
    weighted = place * mixing[:, :, None]
    place_low = place.astype(jnp.bfloat16)
    x_four = tokens.reshape(tok_dev, halves, pieces, sub_width)
    g_four = grad_out.reshape(tok_dev, halves, pieces, sub_width)
    x_parts = []
    g_parts = []
    for half in range(halves):
        x_parts.append(
            jnp.einsum(
                "Tec,Tjr->ejcr", place_low, x_four[:, half], preferred_element_type=jnp.float32
            )
        )
        g_parts.append(jnp.einsum("Tec,Tjr->ejcr", weighted, g_four[:, half].astype(jnp.float32)))
    x_send = jnp.concatenate(x_parts, axis=3).astype(jnp.bfloat16).reshape(total_rows, piece_width)
    g_send = jnp.concatenate(g_parts, axis=3).astype(jnp.bfloat16).reshape(total_rows, piece_width)

    def return_parts(values):
        arrived = lax.all_to_all(values, "expert", split_axis=0, concat_axis=0, tiled=True)
        lanes = arrived.shape[1]
        return arrived.astype(jnp.float32).reshape(flight, pieces, capacity, lanes).sum(axis=1)

    def spread_rows(values):
        lanes = values.shape[2]
        copies = jnp.broadcast_to(values[:, None], (flight, pieces, capacity, lanes)).reshape(
            total_rows, lanes
        )
        return lax.all_to_all(copies, "expert", split_axis=0, concat_axis=0, tiled=True)

    def finish(term, mix):
        summed = lax.psum_scatter(term, "ffn", scatter_dimension=1, tiled=True)
        back = lax.all_to_all(summed, "expert", split_axis=0, concat_axis=0, tiled=True)
        back = back.reshape(flight, pieces, capacity, sub_width)
        joined = jnp.einsum("Tec,ejcr->Tjr", mix, back)
        return joined.reshape(tok_dev, pieces * sub_width).astype(jnp.bfloat16)

    rows = lax.all_to_all(x_send, "expert", split_axis=0, concat_axis=0, tiled=True)
    w_gate = gate_weight[0]
    w_up = up_weight[0]
    w_down = down_weight[0]
    partial_value = jnp.concatenate(
        [
            jnp.dot(rows, w_gate, preferred_element_type=jnp.float32),
            jnp.dot(rows, w_up, preferred_element_type=jnp.float32),
        ],
        axis=1,
    )
    summed = return_parts(partial_value.astype(jnp.bfloat16))
    gate = summed[:, :, :hidden_half]
    up = summed[:, :, hidden_half:]
    sig = jax.nn.sigmoid(gate)
    act = gate * sig
    hidden = (act * up).astype(jnp.bfloat16)
    h_rows = spread_rows(hidden)
    out_term = jnp.dot(h_rows, w_down, preferred_element_type=jnp.float32)
    out_tokens = finish(out_term, weighted)
    grads = lax.all_to_all(g_send, "expert", split_axis=0, concat_axis=0, tiled=True)
    grad_down = contract_rows(h_rows, grads).astype(jnp.bfloat16)
    hidden_part = contract_cols(grads, w_down).astype(jnp.bfloat16)
    grad_hidden = return_parts(hidden_part)
    pre_gate = (grad_hidden * up * sig * (1.0 + gate * (1.0 - sig))).astype(jnp.bfloat16)
    pre_up = (grad_hidden * act).astype(jnp.bfloat16)
    both = spread_rows(jnp.concatenate([pre_gate, pre_up], axis=2))
    d_gate_rows = both[:, :hidden_half]
    d_up_rows = both[:, hidden_half:]
    grad_gate = contract_rows(rows, d_gate_rows).astype(jnp.bfloat16)
    grad_up = contract_rows(rows, d_up_rows).astype(jnp.bfloat16)
    x_term = contract_cols(d_gate_rows, w_gate) + contract_cols(d_up_rows, w_up)
    grad_tokens = finish(x_term, place)
    return (out_tokens, grad_tokens, grad_gate[None], grad_up[None], grad_down[None])


def vmem(shape, dtype):
    return pltpu.VMEM(shape, dtype)


def call(kernel, out_shape, args, in_spaces=None, out_spaces=None, flops=0, traffic=0, scratch=(), limit=16):
    spaces = in_spaces or [pltpu.VMEM] * len(args)
    outs = out_spaces or [pltpu.VMEM] * len(out_shape)
    return pl.pallas_call(
        kernel,
        out_shape=tuple(out_shape),
        in_specs=[pl.BlockSpec(memory_space=space) for space in spaces],
        out_specs=tuple(pl.BlockSpec(memory_space=space) for space in outs),
        scratch_shapes=list(scratch),
        compiler_params=pltpu.CompilerParams(vmem_limit_bytes=limit * MIB),
        cost_estimate=pl.CostEstimate(flops=flops, bytes_accessed=traffic, transcendentals=0),
    )(*args)


def rows_to_blocks(scratch, outs, at, take, subs):
    total = scratch.shape[0]
    size = total // len(outs)
    for sub in range(subs):
        scratch[pl.ds(sub, total // subs, stride=subs), :] = take(sub)
    for k, out in enumerate(outs):
        out[at : at + size, :] = scratch[k * size : (k + 1) * size, :].astype(out.dtype)


def blocks_to_rows(scratch, blocks, at, put, subs):
    total = scratch.shape[0]
    size = total // len(blocks)
    for k, block in enumerate(blocks):
        scratch[k * size : (k + 1) * size, :] = block[at : at + size, :].astype(jnp.float32)
    for sub in range(subs):
        put(sub, scratch[pl.ds(sub, total // subs, stride=subs), :])


def lanes_of(sub):
    return slice(sub * LANES, (sub + 1) * LANES)


def route_kernel(devices, capacity, subs, ids_in, weight_in, x_in, g_in, *refs):
    outs, (place_out, mix_out, scratch, ids, weight, x, g, sems) = refs[:devices], refs[devices:]
    pairs = ((ids_in, ids), (weight_in, weight), (x_in, x), (g_in, g))
    copies = [pltpu.make_async_copy(src, dst, sems.at[i]) for i, (src, dst) in enumerate(pairs)]
    for copy in copies:
        copy.start()
    top, tok = ids.shape
    rows = devices * capacity
    order = lax.broadcasted_iota(jnp.int32, (devices, tok), 0)
    half = devices // 2
    bits = jnp.where(order == 0, 0, jnp.where(order <= half, order + half - 1, order - half))
    expert = bits ^ lax.axis_index("expert")
    member = jnp.zeros((devices, tok), jnp.float32)
    mixing = jnp.zeros((devices, tok), jnp.float32)
    copies[0].wait()
    copies[1].wait()
    for route in range(top):
        hit = ids[route : route + 1, :] == expert
        member = jnp.where(hit, 1.0, member)
        mixing = jnp.where(hit, weight[route : route + 1, :], mixing)
    before = lax.broadcasted_iota(jnp.int32, (tok, tok), 0) < lax.broadcasted_iota(jnp.int32, (tok, tok), 1)
    slots = jnp.dot(
        member.astype(jnp.bfloat16),
        jnp.where(before, 1.0, 0.0).astype(jnp.bfloat16),
        preferred_element_type=jnp.float32,
    )
    target = jnp.where(member > 0, slots + capacity * order.astype(jnp.float32), -1.0)
    row = lax.broadcasted_iota(jnp.int32, (rows, tok), 0).astype(jnp.float32)
    place = jnp.zeros((rows, tok), jnp.float32)
    mix = jnp.zeros((rows, tok), jnp.float32)
    for k in range(devices):
        equal = target[k : k + 1, :] == row
        place = jnp.where(equal, 1.0, place)
        mix = jnp.where(equal, mixing[k : k + 1, :], mix)
    row_weight = jnp.broadcast_to(jnp.sum(mix, axis=1, keepdims=True), (rows, LANES))
    low = place.astype(jnp.bfloat16)
    place_out[...] = low
    mix_out[...] = row_weight

    def x_part(sub):
        return jnp.dot(low, x[:, lanes_of(sub)], preferred_element_type=jnp.float32)

    def g_part(sub):
        return jnp.dot(low, g[:, lanes_of(sub)], preferred_element_type=jnp.float32) * row_weight

    copies[2].wait()
    rows_to_blocks(scratch, outs, 0, x_part, subs)
    copies[3].wait()
    rows_to_blocks(scratch, outs, capacity * subs, g_part, subs)


def hold_kernel(source, kept, held, sem):
    copy = pltpu.make_async_copy(source, kept, sem)
    copy.start()
    held[...] = jnp.zeros_like(held)
    copy.wait()


def arrive_kernel(devices, capacity, subs, *refs):
    blocks, (_, x_own, g_own, scratch) = refs[:devices], refs[devices:]

    def put_into(out):
        def put(sub, value):
            out[:, lanes_of(sub)] = value.astype(out.dtype)

        return put

    blocks_to_rows(scratch, blocks, 0, put_into(x_own), subs)
    blocks_to_rows(scratch, blocks, capacity * subs, put_into(g_own), subs)


def leave_kernel(capacity, subs, out_own, out_other, dx_own, dx_other, *refs):
    outs, scratch = refs[:-1], refs[-1]

    def sum_of(own, other):
        def take(sub):
            return own[:, lanes_of(sub)] + other[:, lanes_of(sub)].astype(jnp.float32)

        return take

    rows_to_blocks(scratch, outs, 0, sum_of(out_own, out_other), subs)
    rows_to_blocks(scratch, outs, capacity * subs, sum_of(dx_own, dx_other), subs)


def join_kernel(devices, capacity, subs, place, mix, *refs):
    blocks, (out_tokens, grad_tokens, scratch) = refs[:devices], refs[devices:]

    def put_out(sub, value):
        low = (value * mix[...]).astype(jnp.bfloat16)
        out_tokens[:, lanes_of(sub)] = contract_rows(place[...], low).astype(out_tokens.dtype)

    def put_grad(sub, value):
        grad_tokens[:, lanes_of(sub)] = contract_rows(place[...], value.astype(jnp.bfloat16)).astype(grad_tokens.dtype)

    blocks_to_rows(scratch, blocks, 0, put_out, subs)
    blocks_to_rows(scratch, blocks, capacity * subs, put_grad, subs)


def half_starts(half_width):
    half = lax.axis_index("ffn")
    own = pl.multiple_of(half * half_width, half_width)
    other = pl.multiple_of((1 - half) * half_width, half_width)
    return own, other


def chunk(i, step, base=0):
    return pl.ds(base + pl.multiple_of(i * step, step), step)


def dot(left, right):
    return jnp.dot(left, right, preferred_element_type=jnp.float32)


def stream(step, start, matrices, held, sems):
    copies = []
    for i in range(held[0].shape[0] // step):
        for which, (matrix, kept) in enumerate(zip(matrices, held)):
            copies.append(
                pltpu.make_async_copy(
                    matrix.at[0, chunk(i, step, start), :], kept.at[i * step : (i + 1) * step, :], sems.at[which, i]
                )
            )
    for copy in copies:
        copy.start()
    return copies


def project_own_kernel(step, x_own, w_gate, w_up, gate_part, up_part, gate_held, up_held, sems):
    own, _ = half_starts(x_own.shape[1])
    copies = stream(step, own, (w_gate, w_up), (gate_held, up_held), sems)
    parts = ((gate_part, gate_held), (up_part, up_held))
    for at, copy in enumerate(copies):
        copy.wait()
        here = slice(at // 2 * step, (at // 2 + 1) * step)
        part, held = parts[at % 2]
        term = dot(x_own[:, here], held[here, :])
        part[...] = term if at < 2 else part[...] + term


def forward_kernel(
    step,
    wide,
    x_own,
    x_other,
    gate_part,
    up_part,
    w_gate,
    w_up,
    w_down,
    x_full,
    gate,
    up,
    hidden,
    out_own,
    out_other,
    gate_held,
    up_held,
    gate_sum,
    up_sum,
    sems,
):
    half_width = x_own.shape[1]
    own, other = half_starts(half_width)
    copies = stream(step, other, (w_gate, w_up), (gate_held, up_held), sems)
    x_full[:, pl.ds(own, half_width)] = x_own[...]
    x_full[:, pl.ds(other, half_width)] = x_other[...]
    parts = ((gate_part, gate_sum, gate_held), (up_part, up_sum, up_held))
    for at, copy in enumerate(copies):
        copy.wait()
        here = slice(at // 2 * step, (at // 2 + 1) * step)
        part, total, held = parts[at % 2]
        total[...] = (part if at < 2 else total)[...] + dot(x_other[:, here], held[here, :])
    gate_low = gate_sum[...].astype(jnp.bfloat16)
    up_low = up_sum[...].astype(jnp.bfloat16)
    gate[...] = gate_low
    up[...] = up_low
    value = gate_low.astype(jnp.float32)
    hidden[...] = (value * jax.nn.sigmoid(value) * up_low.astype(jnp.float32)).astype(jnp.bfloat16)

    def spread(i, carry):
        here = chunk(i, wide)
        out_other[:, here] = dot(hidden[...], w_down[0, :, chunk(i, wide, other)]).astype(jnp.bfloat16)
        out_own[:, here] = dot(hidden[...], w_down[0, :, chunk(i, wide, own)])
        return carry

    lax.fori_loop(0, half_width // wide, spread, 0)


def input_term(pre_gate, pre_up, gate_held, up_held, there):
    return contract_cols(pre_gate[...], gate_held[there, :]) + contract_cols(pre_up[...], up_held[there, :])


def backward_kernel(step, g_own, g_other, gate, up, gate_held, up_held, w_down, g_full, pre_gate, pre_up, dx_other):
    half_width = g_own.shape[1]
    own, other = half_starts(half_width)
    g_full[:, pl.ds(own, half_width)] = g_own[...]
    g_full[:, pl.ds(other, half_width)] = g_other[...]

    def pull(i, carry):
        cols = chunk(i, step)
        part = contract_cols(g_full[...], w_down[0, cols, :]).astype(jnp.bfloat16)
        grad_hidden = part.astype(jnp.float32)
        value = gate[:, cols].astype(jnp.float32)
        sig = jax.nn.sigmoid(value)
        pre_gate[:, cols] = (
            grad_hidden * up[:, cols].astype(jnp.float32) * sig * (1.0 + value * (1.0 - sig))
        ).astype(jnp.bfloat16)
        pre_up[:, cols] = (grad_hidden * value * sig).astype(jnp.bfloat16)
        return carry

    lax.fori_loop(0, gate.shape[1] // step, pull, 0)

    def spread(i, carry):
        here = chunk(i, step)
        dx_other[:, here] = input_term(pre_gate, pre_up, gate_held, up_held, here).astype(jnp.bfloat16)
        return carry

    lax.fori_loop(0, half_width // step, spread, 0)


def backward_own_kernel(step, pre_gate, pre_up, gate_held, up_held, dx_own):
    def spread(i, carry):
        here = chunk(i, step)
        dx_own[:, here] = input_term(pre_gate, pre_up, gate_held, up_held, here)
        return carry

    lax.fori_loop(0, dx_own.shape[1] // step, spread, 0)


def gradient_kernel(
    step, x, g, hidden, pre_gate, pre_up, grad_gate, grad_up, grad_down, flipped, tall, wide, tall_sems, wide_sems
):
    width, lanes = x.shape[1], hidden.shape[1]
    count = width // step
    flipped[...] = hidden[...].astype(jnp.float32).T.astype(flipped.dtype)

    def wide_copy(i, slot):
        return pltpu.make_async_copy(wide.at[slot], grad_down.at[0, :, chunk(i, step)], wide_sems.at[slot])

    def tall_copy(which, out, i, slot):
        return pltpu.make_async_copy(tall.at[which, slot], out.at[0, chunk(i, step), :], tall_sems.at[which, slot])

    def down(i, carry):
        slot = i % 2

        @pl.when(i >= 2)
        def _():
            wide_copy(i - 2, slot).wait()

        wide[slot] = dot(flipped[...], g[:, chunk(i, step)]).astype(wide.dtype)
        wide_copy(i, slot).start()
        return carry

    lax.fori_loop(0, count, down, 0)

    def inputs(i, carry):
        slot = i % 2
        for which, (right, out) in enumerate(((pre_gate, grad_gate), (pre_up, grad_up))):

            @pl.when(i >= 2)
            def _():
                tall_copy(which, out, i - 2, slot).wait()

            tall[which, slot] = contract_rows(x[:, chunk(i, step)], right[...]).astype(tall.dtype)
            tall_copy(which, out, i, slot).start()
        return carry

    lax.fori_loop(0, count, inputs, 0)
    for i in range(max(0, count - 2), count):
        wide_copy(i, i % 2).wait()
        tall_copy(0, grad_gate, i, i % 2).wait()
        tall_copy(1, grad_up, i, i % 2).wait()


def partner_bits(count):
    return [0, *range(count // 2, count), *range(1, count // 2)]


def exchange(blocks):
    arrived = []
    for block, bits in zip(blocks, partner_bits(len(blocks))):
        pairs = [(i, i ^ bits) for i in range(len(blocks))]
        arrived.append(lax.ppermute(block, "expert", pairs) if bits else block)
    return arrived


def swap(value):
    return lax.ppermute(value, "ffn", [(0, 1), (1, 0)])


def in_hbm(values):
    return [pltpu.with_memory_space_constraint(value, pltpu.HBM) for value in values]


def one_piece_shards(tokens, grad_out, route_ids, route_weight, gate_weight, up_weight, down_weight):
    tok_dev, sub_width = tokens.shape
    top_count = route_ids.shape[1]
    width, lanes = gate_weight.shape[1:]
    devices = lax.axis_size("expert")
    capacity = max(2, min(tok_dev, (9 * tok_dev * top_count + 8 * EXPERTS - 1) // (8 * EXPERTS)))
    rows = devices * capacity
    subs = sub_width // LANES
    low, full = jnp.bfloat16, jnp.float32
    blocks = [jax.ShapeDtypeStruct((2 * capacity * subs, LANES), low)] * devices
    spread_scratch = [pltpu.VMEM((rows * subs, LANES), full)]
    sizes = (devices, capacity, subs)
    step = 256
    half_flops = 2 * rows * width * lanes // 2

    sources = (route_ids.T, route_weight.T, tokens, grad_out)
    routed = call(
        functools.partial(route_kernel, *sizes),
        blocks + [jax.ShapeDtypeStruct((rows, tok_dev), low), jax.ShapeDtypeStruct((rows, LANES), full)],
        in_hbm(sources),
        in_spaces=[pl.ANY] * 4,
        scratch=spread_scratch
        + [pltpu.VMEM(value.shape, value.dtype) for value in sources]
        + [pltpu.SemaphoreType.DMA((4,))],
        traffic=4 * tok_dev * sub_width,
    )
    place, mix = routed[devices:]
    arrived = exchange(routed[:devices])

    weights = (gate_weight, up_weight, down_weight)
    w_gate, w_up = in_hbm(weights[:2])
    w_down, held = call(
        hold_kernel,
        [vmem(down_weight.shape, low), vmem((8, LANES), full)],
        in_hbm(weights[2:]),
        in_spaces=[pl.ANY],
        scratch=[pltpu.SemaphoreType.DMA],
        traffic=down_weight.size * 2,
    )
    x_own, g_own = call(
        functools.partial(arrive_kernel, *sizes),
        [vmem((rows, sub_width), low)] * 2,
        (*arrived, held),
        scratch=spread_scratch,
        traffic=8 * rows * sub_width,
    )
    x_other = swap(x_own)
    g_other = swap(g_own)
    deep = 512 if sub_width % 512 == 0 else sub_width
    stream_sems = pltpu.SemaphoreType.DMA((2, sub_width // deep))
    gate_part, up_part, gate_own, up_own = call(
        functools.partial(project_own_kernel, deep),
        [vmem((rows, lanes), full)] * 2 + [vmem((sub_width, lanes), low)] * 2,
        (x_own, w_gate, w_up),
        in_spaces=[pltpu.VMEM, pl.ANY, pl.ANY],
        scratch=[stream_sems],
        flops=2 * half_flops,
        traffic=4 * sub_width * lanes,
    )
    x_full, gate, up, hidden, out_own, out_other, gate_other, up_other = call(
        functools.partial(forward_kernel, deep, step),
        [vmem((rows, width), low)]
        + [vmem((rows, lanes), low)] * 3
        + [vmem((rows, sub_width), full), vmem((rows, sub_width), low)]
        + [vmem((sub_width, lanes), low)] * 2,
        (x_own, x_other, gate_part, up_part, w_gate, w_up, w_down),
        in_spaces=[pltpu.VMEM] * 4 + [pl.ANY, pl.ANY, pltpu.VMEM],
        scratch=[pltpu.VMEM((rows, lanes), full)] * 2 + [stream_sems],
        flops=4 * half_flops,
        traffic=4 * sub_width * lanes,
    )
    out_arrived = swap(out_other)
    g_full, pre_gate, pre_up, dx_other = call(
        functools.partial(backward_kernel, step),
        [vmem((rows, width), low)] + [vmem((rows, lanes), low)] * 2 + [vmem((rows, sub_width), low)],
        (g_own, g_other, gate, up, gate_other, up_other, w_down),
        flops=4 * half_flops,
    )
    dx_arrived = swap(dx_other)
    (dx_own,) = call(
        functools.partial(backward_own_kernel, step),
        [vmem((rows, sub_width), full)],
        (pre_gate, pre_up, gate_own, up_own),
        flops=2 * half_flops,
    )
    returned = exchange(
        call(
            functools.partial(leave_kernel, capacity, subs),
            blocks,
            (out_own, out_arrived, dx_own, dx_arrived),
            scratch=spread_scratch,
            traffic=16 * rows * sub_width,
        )
    )
    cut = 1024 if width % 1024 == 0 else width
    grad_gate, grad_up, grad_down = call(
        functools.partial(gradient_kernel, cut),
        [jax.ShapeDtypeStruct(w.shape, low) for w in weights],
        (x_full, g_full, hidden, pre_gate, pre_up),
        out_spaces=[pl.ANY] * 3,
        scratch=[
            pltpu.VMEM((lanes, rows), low),
            pltpu.VMEM((2, 2, cut, lanes), low),
            pltpu.VMEM((2, lanes, cut), low),
            pltpu.SemaphoreType.DMA((2, 2)),
            pltpu.SemaphoreType.DMA((2,)),
        ],
        flops=6 * half_flops,
        traffic=sum(w.size * 2 for w in weights),
        limit=32,
    )
    out_tokens, grad_tokens = call(
        functools.partial(join_kernel, *sizes),
        [jax.ShapeDtypeStruct((tok_dev, sub_width), low)] * 2,
        (place, mix, *returned),
        scratch=spread_scratch,
        traffic=8 * tok_dev * sub_width,
    )
    return out_tokens, grad_tokens, grad_gate, grad_up, grad_down


def shards(*args):
    tokens, gate_weight = args[0], args[4]
    halves = lax.axis_size("ffn")
    devices = lax.axis_size("expert")
    if halves == 2 and devices & (devices - 1) == 0 and tokens.shape[1] * halves == gate_weight.shape[1]:
        return one_piece_shards(*args)
    return general_shards(*args)


def solution(mesh):
    in_specs = (
        P(("groups", "expert"), "ffn"),
        P(("groups", "expert"), "ffn"),
        P(("groups", "expert"), None),
        P(("groups", "expert"), None),
        P("expert", None, "ffn"),
        P("expert", None, "ffn"),
        P("expert", "ffn", None),
    )
    out_specs = (
        P(("groups", "expert"), "ffn"),
        P(("groups", "expert"), "ffn"),
        P(("groups", "expert"), None, "ffn"),
        P(("groups", "expert"), None, "ffn"),
        P(("groups", "expert"), "ffn", None),
    )
    return jax.shard_map(shards, mesh=mesh, in_specs=in_specs, out_specs=out_specs, check_vma=False)
```

```python
import functools

import jax
import jax.numpy as jnp
from jax import lax
from jax.experimental import pallas as pl
from jax.experimental.pallas import tpu as pltpu
from jax.sharding import PartitionSpec as P

EXPERTS = 128
LANES = 128
MIB = 1024 * 1024


def contract_rows(left, right):
    return lax.dot_general(
        left, right, (((0,), (0,)), ((), ())), preferred_element_type=jnp.float32
    )


def contract_cols(left, right):
    return lax.dot_general(
        left, right, (((1,), (1,)), ((), ())), preferred_element_type=jnp.float32
    )


def general_shards(tokens, grad_out, route_ids, route_weight, gate_weight, up_weight, down_weight):
    tokens, grad_out = (
        lax.all_gather(tokens, "ffn", axis=1, tiled=True),
        lax.all_gather(grad_out, "ffn", axis=1, tiled=True),
    )
    tok_dev, width = tokens.shape
    top_count = route_ids.shape[1]
    piece_width = gate_weight.shape[1]
    hidden_half = gate_weight.shape[2]
    pieces = width // piece_width
    devices = lax.axis_size("expert")
    flight = devices // pieces
    halves = lax.axis_size("ffn")
    sub_width = piece_width // halves
    capacity = max(2, min(tok_dev, (9 * tok_dev * top_count + 8 * EXPERTS - 1) // (8 * EXPERTS)))
    total_rows = devices * capacity
    expert_ids = jnp.arange(flight, dtype=jnp.int32)
    member = jnp.zeros((tok_dev, flight), jnp.float32)
    mixing = jnp.zeros((tok_dev, flight), jnp.float32)
    for route in range(top_count):
        hit = (route_ids[:, route : route + 1] == expert_ids[None, :]).astype(jnp.float32)
        member = member + hit
        mixing = mixing + hit * route_weight[:, route : route + 1]
    slots = jnp.cumsum(member, axis=0) - member
    place = member[:, :, None] * (
        slots[:, :, None] == jnp.arange(capacity, dtype=jnp.float32)
    ).astype(jnp.float32)
    weighted = place * mixing[:, :, None]
    place_low = place.astype(jnp.bfloat16)
    x_four = tokens.reshape(tok_dev, halves, pieces, sub_width)
    g_four = grad_out.reshape(tok_dev, halves, pieces, sub_width)
    x_parts = []
    g_parts = []
    for half in range(halves):
        x_parts.append(
            jnp.einsum(
                "Tec,Tjr->ejcr", place_low, x_four[:, half], preferred_element_type=jnp.float32
            )
        )
        g_parts.append(jnp.einsum("Tec,Tjr->ejcr", weighted, g_four[:, half].astype(jnp.float32)))
    x_send = jnp.concatenate(x_parts, axis=3).astype(jnp.bfloat16).reshape(total_rows, piece_width)
    g_send = jnp.concatenate(g_parts, axis=3).astype(jnp.bfloat16).reshape(total_rows, piece_width)

    def return_parts(values):
        arrived = lax.all_to_all(values, "expert", split_axis=0, concat_axis=0, tiled=True)
        lanes = arrived.shape[1]
        return arrived.astype(jnp.float32).reshape(flight, pieces, capacity, lanes).sum(axis=1)

    def spread_rows(values):
        lanes = values.shape[2]
        copies = jnp.broadcast_to(values[:, None], (flight, pieces, capacity, lanes)).reshape(
            total_rows, lanes
        )
        return lax.all_to_all(copies, "expert", split_axis=0, concat_axis=0, tiled=True)

    def finish(term, mix):
        summed = lax.psum_scatter(term, "ffn", scatter_dimension=1, tiled=True)
        back = lax.all_to_all(summed, "expert", split_axis=0, concat_axis=0, tiled=True)
        back = back.reshape(flight, pieces, capacity, sub_width)
        joined = jnp.einsum("Tec,ejcr->Tjr", mix, back)
        return joined.reshape(tok_dev, pieces * sub_width).astype(jnp.bfloat16)

    rows = lax.all_to_all(x_send, "expert", split_axis=0, concat_axis=0, tiled=True)
    w_gate = gate_weight[0]
    w_up = up_weight[0]
    w_down = down_weight[0]
    partial_value = jnp.concatenate(
        [
            jnp.dot(rows, w_gate, preferred_element_type=jnp.float32),
            jnp.dot(rows, w_up, preferred_element_type=jnp.float32),
        ],
        axis=1,
    )
    summed = return_parts(partial_value.astype(jnp.bfloat16))
    gate = summed[:, :, :hidden_half]
    up = summed[:, :, hidden_half:]
    sig = jax.nn.sigmoid(gate)
    act = gate * sig
    hidden = (act * up).astype(jnp.bfloat16)
    h_rows = spread_rows(hidden)
    out_term = jnp.dot(h_rows, w_down, preferred_element_type=jnp.float32)
    out_tokens = finish(out_term, weighted)
    grads = lax.all_to_all(g_send, "expert", split_axis=0, concat_axis=0, tiled=True)
    grad_down = contract_rows(h_rows, grads).astype(jnp.bfloat16)
    hidden_part = contract_cols(grads, w_down).astype(jnp.bfloat16)
    grad_hidden = return_parts(hidden_part)
    pre_gate = (grad_hidden * up * sig * (1.0 + gate * (1.0 - sig))).astype(jnp.bfloat16)
    pre_up = (grad_hidden * act).astype(jnp.bfloat16)
    both = spread_rows(jnp.concatenate([pre_gate, pre_up], axis=2))
    d_gate_rows = both[:, :hidden_half]
    d_up_rows = both[:, hidden_half:]
    grad_gate = contract_rows(rows, d_gate_rows).astype(jnp.bfloat16)
    grad_up = contract_rows(rows, d_up_rows).astype(jnp.bfloat16)
    x_term = contract_cols(d_gate_rows, w_gate) + contract_cols(d_up_rows, w_up)
    grad_tokens = finish(x_term, place)
    return (out_tokens, grad_tokens, grad_gate[None], grad_up[None], grad_down[None])


def vmem(shape, dtype):
    return pltpu.VMEM(shape, dtype)


def call(kernel, out_shape, args, in_spaces=None, out_spaces=None, flops=0, traffic=0, scratch=(), limit=16):
    spaces = in_spaces or [pltpu.VMEM] * len(args)
    outs = out_spaces or [pltpu.VMEM] * len(out_shape)
    return pl.pallas_call(
        kernel,
        out_shape=tuple(out_shape),
        in_specs=[pl.BlockSpec(memory_space=space) for space in spaces],
        out_specs=tuple(pl.BlockSpec(memory_space=space) for space in outs),
        scratch_shapes=list(scratch),
        compiler_params=pltpu.CompilerParams(vmem_limit_bytes=limit * MIB),
        cost_estimate=pl.CostEstimate(flops=flops, bytes_accessed=traffic, transcendentals=0),
    )(*args)


def rows_to_blocks(scratch, outs, at, take, subs):
    total = scratch.shape[0]
    size = total // len(outs)
    for sub in range(subs):
        scratch[pl.ds(sub, total // subs, stride=subs), :] = take(sub)
    for k, out in enumerate(outs):
        out[at : at + size, :] = scratch[k * size : (k + 1) * size, :].astype(out.dtype)


def blocks_to_rows(scratch, blocks, at, put, subs):
    total = scratch.shape[0]
    size = total // len(blocks)
    for k, block in enumerate(blocks):
        scratch[k * size : (k + 1) * size, :] = block[at : at + size, :].astype(jnp.float32)
    for sub in range(subs):
        put(sub, scratch[pl.ds(sub, total // subs, stride=subs), :])


def lanes_of(sub):
    return slice(sub * LANES, (sub + 1) * LANES)


def route_kernel(devices, capacity, subs, ids_in, weight_in, x_in, g_in, *refs):
    outs, (place_out, mix_out, scratch, ids, weight, x, g, sems) = refs[:devices], refs[devices:]
    pairs = ((ids_in, ids), (weight_in, weight), (x_in, x), (g_in, g))
    copies = [pltpu.make_async_copy(src, dst, sems.at[i]) for i, (src, dst) in enumerate(pairs)]
    for copy in copies:
        copy.start()
    top, tok = ids.shape
    rows = devices * capacity
    order = lax.broadcasted_iota(jnp.int32, (devices, tok), 0)
    expert = order ^ lax.axis_index("expert")
    member = jnp.zeros((devices, tok), jnp.float32)
    mixing = jnp.zeros((devices, tok), jnp.float32)
    copies[0].wait()
    copies[1].wait()
    for route in range(top):
        hit = ids[route : route + 1, :] == expert
        member = jnp.where(hit, 1.0, member)
        mixing = jnp.where(hit, weight[route : route + 1, :], mixing)
    before = lax.broadcasted_iota(jnp.int32, (tok, tok), 0) < lax.broadcasted_iota(jnp.int32, (tok, tok), 1)
    slots = jnp.dot(
        member.astype(jnp.bfloat16),
        jnp.where(before, 1.0, 0.0).astype(jnp.bfloat16),
        preferred_element_type=jnp.float32,
    )
    target = jnp.where(member > 0, slots + capacity * order.astype(jnp.float32), -1.0)
    row = lax.broadcasted_iota(jnp.int32, (rows, tok), 0).astype(jnp.float32)
    place = jnp.zeros((rows, tok), jnp.float32)
    mix = jnp.zeros((rows, tok), jnp.float32)
    for k in range(devices):
        equal = target[k : k + 1, :] == row
        place = jnp.where(equal, 1.0, place)
        mix = jnp.where(equal, mixing[k : k + 1, :], mix)
    row_weight = jnp.broadcast_to(jnp.sum(mix, axis=1, keepdims=True), (rows, LANES))
    low = place.astype(jnp.bfloat16)
    place_out[...] = low
    mix_out[...] = row_weight

    def x_part(sub):
        return jnp.dot(low, x[:, lanes_of(sub)], preferred_element_type=jnp.float32)

    def g_part(sub):
        return jnp.dot(low, g[:, lanes_of(sub)], preferred_element_type=jnp.float32) * row_weight

    copies[2].wait()
    rows_to_blocks(scratch, outs, 0, x_part, subs)
    copies[3].wait()
    rows_to_blocks(scratch, outs, capacity * subs, g_part, subs)


def hold_kernel(count, *refs):
    held, sems = refs[2 * count :]
    held[...] = jnp.zeros_like(held)
    copies = [pltpu.make_async_copy(refs[i], refs[count + i], sems.at[i]) for i in range(count)]
    for copy in copies:
        copy.start()
    for copy in copies:
        copy.wait()


def arrive_kernel(devices, capacity, subs, *refs):
    blocks, (_, x_own, g_own, scratch) = refs[:devices], refs[devices:]

    def put_into(out):
        def put(sub, value):
            out[:, lanes_of(sub)] = value.astype(out.dtype)

        return put

    blocks_to_rows(scratch, blocks, 0, put_into(x_own), subs)
    blocks_to_rows(scratch, blocks, capacity * subs, put_into(g_own), subs)


def leave_kernel(capacity, subs, out_own, out_other, dx_own, dx_other, *refs):
    outs, scratch = refs[:-1], refs[-1]

    def sum_of(own, other):
        def take(sub):
            return own[:, lanes_of(sub)] + other[:, lanes_of(sub)].astype(jnp.float32)

        return take

    rows_to_blocks(scratch, outs, 0, sum_of(out_own, out_other), subs)
    rows_to_blocks(scratch, outs, capacity * subs, sum_of(dx_own, dx_other), subs)


def join_kernel(devices, capacity, subs, place, mix, *refs):
    blocks, (out_tokens, grad_tokens, scratch) = refs[:devices], refs[devices:]

    def put_out(sub, value):
        low = (value * mix[...]).astype(jnp.bfloat16)
        out_tokens[:, lanes_of(sub)] = contract_rows(place[...], low).astype(out_tokens.dtype)

    def put_grad(sub, value):
        grad_tokens[:, lanes_of(sub)] = contract_rows(place[...], value.astype(jnp.bfloat16)).astype(grad_tokens.dtype)

    blocks_to_rows(scratch, blocks, 0, put_out, subs)
    blocks_to_rows(scratch, blocks, capacity * subs, put_grad, subs)


def half_starts(half_width):
    half = lax.axis_index("ffn")
    own = pl.multiple_of(half * half_width, half_width)
    other = pl.multiple_of((1 - half) * half_width, half_width)
    return own, other


def chunk(i, step, base=0):
    return pl.ds(base + pl.multiple_of(i * step, step), step)


def dot(left, right):
    return jnp.dot(left, right, preferred_element_type=jnp.float32)


def project_own_kernel(step, x_own, w_gate, w_up, gate_part, up_part):
    half_width = x_own.shape[1]
    own, _ = half_starts(half_width)
    rows = pl.ds(own, half_width)

    def project(i, carry):
        cols = chunk(i, step)
        gate_part[:, cols] = dot(x_own[...], w_gate[0, rows, cols])
        up_part[:, cols] = dot(x_own[...], w_up[0, rows, cols])
        return carry

    lax.fori_loop(0, gate_part.shape[1] // step, project, 0)


def forward_kernel(
    step, x_own, x_other, gate_part, up_part, w_gate, w_up, w_down, x_full, gate, up, hidden, out_own, out_other
):
    half_width = x_own.shape[1]
    own, other = half_starts(half_width)
    x_full[:, pl.ds(own, half_width)] = x_own[...]
    x_full[:, pl.ds(other, half_width)] = x_other[...]
    rows = pl.ds(other, half_width)

    def project(i, carry):
        cols = chunk(i, step)
        gate_low = (gate_part[:, cols] + dot(x_other[...], w_gate[0, rows, cols])).astype(jnp.bfloat16)
        up_low = (up_part[:, cols] + dot(x_other[...], w_up[0, rows, cols])).astype(jnp.bfloat16)
        gate[:, cols] = gate_low
        up[:, cols] = up_low
        value = gate_low.astype(jnp.float32)
        hidden[:, cols] = (value * jax.nn.sigmoid(value) * up_low.astype(jnp.float32)).astype(jnp.bfloat16)
        return carry

    lax.fori_loop(0, gate.shape[1] // step, project, 0)

    def spread(i, carry):
        here = chunk(i, step)
        out_other[:, here] = dot(hidden[...], w_down[0, :, chunk(i, step, other)]).astype(jnp.bfloat16)
        out_own[:, here] = dot(hidden[...], w_down[0, :, chunk(i, step, own)])
        return carry

    lax.fori_loop(0, half_width // step, spread, 0)


def flip(value):
    return value.astype(jnp.float32).T


def input_term(pre_gate, pre_up, w_gate, w_up, there):
    return flip(contract_cols(w_gate[0, there, :], pre_gate[...]) + contract_cols(w_up[0, there, :], pre_up[...]))


def backward_kernel(step, g_own, g_other, gate, up, w_gate, w_up, w_down, g_full, pre_gate, pre_up, dx_other):
    half_width = g_own.shape[1]
    own, other = half_starts(half_width)
    g_full[:, pl.ds(own, half_width)] = g_own[...]
    g_full[:, pl.ds(other, half_width)] = g_other[...]

    def pull(i, carry):
        cols = chunk(i, step)
        part = flip(contract_cols(w_down[0, cols, :], g_full[...])).astype(jnp.bfloat16)
        grad_hidden = part.astype(jnp.float32)
        value = gate[:, cols].astype(jnp.float32)
        sig = jax.nn.sigmoid(value)
        pre_gate[:, cols] = (
            grad_hidden * up[:, cols].astype(jnp.float32) * sig * (1.0 + value * (1.0 - sig))
        ).astype(jnp.bfloat16)
        pre_up[:, cols] = (grad_hidden * value * sig).astype(jnp.bfloat16)
        return carry

    lax.fori_loop(0, gate.shape[1] // step, pull, 0)

    def spread(i, carry):
        dx_other[:, chunk(i, step)] = input_term(pre_gate, pre_up, w_gate, w_up, chunk(i, step, other)).astype(
            jnp.bfloat16
        )
        return carry

    lax.fori_loop(0, half_width // step, spread, 0)


def backward_own_kernel(step, pre_gate, pre_up, w_gate, w_up, dx_own):
    half_width = dx_own.shape[1]
    own, _ = half_starts(half_width)

    def spread(i, carry):
        dx_own[:, chunk(i, step)] = input_term(pre_gate, pre_up, w_gate, w_up, chunk(i, step, own))
        return carry

    lax.fori_loop(0, half_width // step, spread, 0)


def pieces_of(total, size):
    return [slice(at, min(at + size, total)) for at in range(0, total, size)]


def gradient_kernel(
    step, x, g, hidden, pre_gate, pre_up, grad_gate, grad_up, grad_down, flipped, turned, tall, wide, tall_sems, wide_sems
):
    width, lanes = x.shape[1], hidden.shape[1]
    count = width // step
    flipped[...] = flip(hidden[...]).astype(flipped.dtype)

    def wide_copy(i, slot):
        return pltpu.make_async_copy(wide.at[slot], grad_down.at[0, :, chunk(i, step)], wide_sems.at[slot])

    def tall_copy(which, out, i, slot):
        return pltpu.make_async_copy(tall.at[which, slot], out.at[0, chunk(i, step), :], tall_sems.at[which, slot])

    def down(i, carry):
        slot = i % 2

        @pl.when(i >= 2)
        def _():
            wide_copy(i - 2, slot).wait()

        for cut in pieces_of(step, 256):
            right = g[:, chunk(i, step)][:, cut]
            for high in pieces_of(lanes, 256):
                wide[slot, high, cut] = dot(flipped[high, :], right).astype(wide.dtype)
        wide_copy(i, slot).start()
        return carry

    lax.fori_loop(0, count, down, 0)

    def inputs(i, carry):
        slot = i % 2
        turned[...] = flip(x[:, chunk(i, step)]).astype(turned.dtype)
        for which, (right, out) in enumerate(((pre_gate, grad_gate), (pre_up, grad_up))):

            @pl.when(i >= 2)
            def _():
                tall_copy(which, out, i - 2, slot).wait()

            for cut in pieces_of(lanes, 256):
                for high in pieces_of(step, 256):
                    tall[which, slot, high, cut] = dot(turned[high, :], right[:, cut]).astype(tall.dtype)
            tall_copy(which, out, i, slot).start()
        return carry

    lax.fori_loop(0, count, inputs, 0)
    for i in range(max(0, count - 2), count):
        wide_copy(i, i % 2).wait()
        tall_copy(0, grad_gate, i, i % 2).wait()
        tall_copy(1, grad_up, i, i % 2).wait()


def exchange(blocks):
    pairs = [[(i, i ^ k) for i in range(len(blocks))] for k in range(len(blocks))]
    return [blocks[0]] + [lax.ppermute(blocks[k], "expert", pairs[k]) for k in range(1, len(blocks))]


def swap(value):
    return lax.ppermute(value, "ffn", [(0, 1), (1, 0)])


def in_hbm(values):
    return [pltpu.with_memory_space_constraint(value, pltpu.HBM) for value in values]


def one_piece_shards(tokens, grad_out, route_ids, route_weight, gate_weight, up_weight, down_weight):
    tok_dev, sub_width = tokens.shape
    top_count = route_ids.shape[1]
    width, lanes = gate_weight.shape[1:]
    devices = lax.axis_size("expert")
    capacity = max(2, min(tok_dev, (9 * tok_dev * top_count + 8 * EXPERTS - 1) // (8 * EXPERTS)))
    rows = devices * capacity
    subs = sub_width // LANES
    low, full = jnp.bfloat16, jnp.float32
    blocks = [jax.ShapeDtypeStruct((2 * capacity * subs, LANES), low)] * devices
    spread_scratch = [pltpu.VMEM((rows * subs, LANES), full)]
    sizes = (devices, capacity, subs)
    step = 256
    half_flops = 2 * rows * width * lanes // 2

    sources = (route_ids.T, route_weight.T, tokens, grad_out)
    routed = call(
        functools.partial(route_kernel, *sizes),
        blocks + [jax.ShapeDtypeStruct((rows, tok_dev), low), jax.ShapeDtypeStruct((rows, LANES), full)],
        in_hbm(sources),
        in_spaces=[pl.ANY] * 4,
        scratch=spread_scratch
        + [pltpu.VMEM(value.shape, value.dtype) for value in sources]
        + [pltpu.SemaphoreType.DMA((4,))],
        traffic=4 * tok_dev * sub_width,
    )
    place, mix = routed[devices:]
    arrived = exchange(routed[:devices])

    weights = (gate_weight, up_weight, down_weight)
    w_gate, w_up, w_down, held = call(
        functools.partial(hold_kernel, 3),
        [vmem(w.shape, w.dtype) for w in weights] + [vmem((8, LANES), full)],
        in_hbm(weights),
        in_spaces=[pl.ANY] * 3,
        scratch=[pltpu.SemaphoreType.DMA((3,))],
        traffic=sum(w.size * 2 for w in weights),
    )
    x_own, g_own = call(
        functools.partial(arrive_kernel, *sizes),
        [vmem((rows, sub_width), low)] * 2,
        (*arrived, held),
        scratch=spread_scratch,
        traffic=8 * rows * sub_width,
    )
    x_other = swap(x_own)
    g_other = swap(g_own)
    gate_part, up_part = call(
        functools.partial(project_own_kernel, step),
        [vmem((rows, lanes), full)] * 2,
        (x_own, w_gate, w_up),
        flops=2 * half_flops,
    )
    x_full, gate, up, hidden, out_own, out_other = call(
        functools.partial(forward_kernel, step),
        [vmem((rows, width), low)]
        + [vmem((rows, lanes), low)] * 3
        + [vmem((rows, sub_width), full), vmem((rows, sub_width), low)],
        (x_own, x_other, gate_part, up_part, w_gate, w_up, w_down),
        flops=4 * half_flops,
    )
    out_arrived = swap(out_other)
    g_full, pre_gate, pre_up, dx_other = call(
        functools.partial(backward_kernel, step),
        [vmem((rows, width), low)] + [vmem((rows, lanes), low)] * 2 + [vmem((rows, sub_width), low)],
        (g_own, g_other, gate, up, w_gate, w_up, w_down),
        flops=4 * half_flops,
    )
    dx_arrived = swap(dx_other)
    (dx_own,) = call(
        functools.partial(backward_own_kernel, step),
        [vmem((rows, sub_width), full)],
        (pre_gate, pre_up, w_gate, w_up),
        flops=2 * half_flops,
    )
    returned = exchange(
        call(
            functools.partial(leave_kernel, capacity, subs),
            blocks,
            (out_own, out_arrived, dx_own, dx_arrived),
            scratch=spread_scratch,
            traffic=16 * rows * sub_width,
        )
    )
    cut = 1024 if width % 1024 == 0 else width
    grad_gate, grad_up, grad_down = call(
        functools.partial(gradient_kernel, cut),
        [jax.ShapeDtypeStruct(w.shape, low) for w in weights],
        (x_full, g_full, hidden, pre_gate, pre_up),
        out_spaces=[pl.ANY] * 3,
        scratch=[
            pltpu.VMEM((lanes, rows), low),
            pltpu.VMEM((cut, rows), low),
            pltpu.VMEM((2, 2, cut, lanes), low),
            pltpu.VMEM((2, lanes, cut), low),
            pltpu.SemaphoreType.DMA((2, 2)),
            pltpu.SemaphoreType.DMA((2,)),
        ],
        flops=6 * half_flops,
        traffic=sum(w.size * 2 for w in weights),
        limit=32,
    )
    out_tokens, grad_tokens = call(
        functools.partial(join_kernel, *sizes),
        [jax.ShapeDtypeStruct((tok_dev, sub_width), low)] * 2,
        (place, mix, *returned),
        scratch=spread_scratch,
        traffic=8 * tok_dev * sub_width,
    )
    return out_tokens, grad_tokens, grad_gate, grad_up, grad_down


def shards(*args):
    tokens, gate_weight = args[0], args[4]
    halves = lax.axis_size("ffn")
    devices = lax.axis_size("expert")
    if halves == 2 and devices & (devices - 1) == 0 and tokens.shape[1] * halves == gate_weight.shape[1]:
        return one_piece_shards(*args)
    return general_shards(*args)


def solution(mesh):
    in_specs = (
        P(("groups", "expert"), "ffn"),
        P(("groups", "expert"), "ffn"),
        P(("groups", "expert"), None),
        P(("groups", "expert"), None),
        P("expert", None, "ffn"),
        P("expert", None, "ffn"),
        P("expert", "ffn", None),
    )
    out_specs = (
        P(("groups", "expert"), "ffn"),
        P(("groups", "expert"), "ffn"),
        P(("groups", "expert"), None, "ffn"),
        P(("groups", "expert"), None, "ffn"),
        P(("groups", "expert"), "ffn", None),
    )
    return jax.shard_map(shards, mesh=mesh, in_specs=in_specs, out_specs=out_specs, check_vma=False)
```

```python
import functools

import jax
import jax.numpy as jnp
from jax import lax
from jax.experimental import pallas as pl
from jax.experimental.pallas import tpu as pltpu
from jax.sharding import PartitionSpec as P

EXPERTS = 128
LANES = 128
MIB = 1024 * 1024


def contract_rows(left, right):
    return lax.dot_general(
        left, right, (((0,), (0,)), ((), ())), preferred_element_type=jnp.float32
    )


def contract_cols(left, right):
    return lax.dot_general(
        left, right, (((1,), (1,)), ((), ())), preferred_element_type=jnp.float32
    )


def general_shards(tokens, grad_out, route_ids, route_weight, gate_weight, up_weight, down_weight):
    tokens, grad_out = (
        lax.all_gather(tokens, "ffn", axis=1, tiled=True),
        lax.all_gather(grad_out, "ffn", axis=1, tiled=True),
    )
    tok_dev, width = tokens.shape
    top_count = route_ids.shape[1]
    piece_width = gate_weight.shape[1]
    hidden_half = gate_weight.shape[2]
    pieces = width // piece_width
    devices = lax.axis_size("expert")
    flight = devices // pieces
    halves = lax.axis_size("ffn")
    sub_width = piece_width // halves
    capacity = max(2, min(tok_dev, (9 * tok_dev * top_count + 8 * EXPERTS - 1) // (8 * EXPERTS)))
    total_rows = devices * capacity
    expert_ids = jnp.arange(flight, dtype=jnp.int32)
    member = jnp.zeros((tok_dev, flight), jnp.float32)
    mixing = jnp.zeros((tok_dev, flight), jnp.float32)
    for route in range(top_count):
        hit = (route_ids[:, route : route + 1] == expert_ids[None, :]).astype(jnp.float32)
        member = member + hit
        mixing = mixing + hit * route_weight[:, route : route + 1]
    slots = jnp.cumsum(member, axis=0) - member
    place = member[:, :, None] * (
        slots[:, :, None] == jnp.arange(capacity, dtype=jnp.float32)
    ).astype(jnp.float32)
    weighted = place * mixing[:, :, None]
    place_low = place.astype(jnp.bfloat16)
    x_four = tokens.reshape(tok_dev, halves, pieces, sub_width)
    g_four = grad_out.reshape(tok_dev, halves, pieces, sub_width)
    x_parts = []
    g_parts = []
    for half in range(halves):
        x_parts.append(
            jnp.einsum(
                "Tec,Tjr->ejcr", place_low, x_four[:, half], preferred_element_type=jnp.float32
            )
        )
        g_parts.append(jnp.einsum("Tec,Tjr->ejcr", weighted, g_four[:, half].astype(jnp.float32)))
    x_send = jnp.concatenate(x_parts, axis=3).astype(jnp.bfloat16).reshape(total_rows, piece_width)
    g_send = jnp.concatenate(g_parts, axis=3).astype(jnp.bfloat16).reshape(total_rows, piece_width)

    def return_parts(values):
        arrived = lax.all_to_all(values, "expert", split_axis=0, concat_axis=0, tiled=True)
        lanes = arrived.shape[1]
        return arrived.astype(jnp.float32).reshape(flight, pieces, capacity, lanes).sum(axis=1)

    def spread_rows(values):
        lanes = values.shape[2]
        copies = jnp.broadcast_to(values[:, None], (flight, pieces, capacity, lanes)).reshape(
            total_rows, lanes
        )
        return lax.all_to_all(copies, "expert", split_axis=0, concat_axis=0, tiled=True)

    def finish(term, mix):
        summed = lax.psum_scatter(term, "ffn", scatter_dimension=1, tiled=True)
        back = lax.all_to_all(summed, "expert", split_axis=0, concat_axis=0, tiled=True)
        back = back.reshape(flight, pieces, capacity, sub_width)
        joined = jnp.einsum("Tec,ejcr->Tjr", mix, back)
        return joined.reshape(tok_dev, pieces * sub_width).astype(jnp.bfloat16)

    rows = lax.all_to_all(x_send, "expert", split_axis=0, concat_axis=0, tiled=True)
    w_gate = gate_weight[0]
    w_up = up_weight[0]
    w_down = down_weight[0]
    partial_value = jnp.concatenate(
        [
            jnp.dot(rows, w_gate, preferred_element_type=jnp.float32),
            jnp.dot(rows, w_up, preferred_element_type=jnp.float32),
        ],
        axis=1,
    )
    summed = return_parts(partial_value.astype(jnp.bfloat16))
    gate = summed[:, :, :hidden_half]
    up = summed[:, :, hidden_half:]
    sig = jax.nn.sigmoid(gate)
    act = gate * sig
    hidden = (act * up).astype(jnp.bfloat16)
    h_rows = spread_rows(hidden)
    out_term = jnp.dot(h_rows, w_down, preferred_element_type=jnp.float32)
    out_tokens = finish(out_term, weighted)
    grads = lax.all_to_all(g_send, "expert", split_axis=0, concat_axis=0, tiled=True)
    grad_down = contract_rows(h_rows, grads).astype(jnp.bfloat16)
    hidden_part = contract_cols(grads, w_down).astype(jnp.bfloat16)
    grad_hidden = return_parts(hidden_part)
    pre_gate = (grad_hidden * up * sig * (1.0 + gate * (1.0 - sig))).astype(jnp.bfloat16)
    pre_up = (grad_hidden * act).astype(jnp.bfloat16)
    both = spread_rows(jnp.concatenate([pre_gate, pre_up], axis=2))
    d_gate_rows = both[:, :hidden_half]
    d_up_rows = both[:, hidden_half:]
    grad_gate = contract_rows(rows, d_gate_rows).astype(jnp.bfloat16)
    grad_up = contract_rows(rows, d_up_rows).astype(jnp.bfloat16)
    x_term = contract_cols(d_gate_rows, w_gate) + contract_cols(d_up_rows, w_up)
    grad_tokens = finish(x_term, place)
    return (out_tokens, grad_tokens, grad_gate[None], grad_up[None], grad_down[None])


def vmem(shape, dtype):
    return pltpu.VMEM(shape, dtype)


def call(kernel, out_shape, args, in_spaces=None, out_spaces=None, flops=0, traffic=0, scratch=(), limit=16):
    spaces = in_spaces or [pltpu.VMEM] * len(args)
    outs = out_spaces or [pltpu.VMEM] * len(out_shape)
    return pl.pallas_call(
        kernel,
        out_shape=tuple(out_shape),
        in_specs=[pl.BlockSpec(memory_space=space) for space in spaces],
        out_specs=tuple(pl.BlockSpec(memory_space=space) for space in outs),
        scratch_shapes=list(scratch),
        compiler_params=pltpu.CompilerParams(vmem_limit_bytes=limit * MIB),
        cost_estimate=pl.CostEstimate(flops=flops, bytes_accessed=traffic, transcendentals=0),
    )(*args)


def blocks_to_rows(scratch, blocks, put, subs):
    size = blocks[0].shape[0]
    for p, block in enumerate(blocks):
        scratch[p * size : (p + 1) * size, :] = block[...].astype(jnp.float32)
    for sub in range(subs):
        put(sub, scratch[pl.ds(sub, len(blocks) * size // subs, stride=subs), :])


def spread_lanes(scratch, sub, subs, value):
    scratch[pl.ds(sub, value.shape[0], stride=subs), :] = value


def part(ref, start, count):
    return ref.at[start : start + count, :]


def lanes_of(sub):
    return slice(sub * LANES, (sub + 1) * LANES)


def even_masks(count):
    return [*range(count // 2, count, 2), *range(2, count // 2, 2)]


def route_kernel(devices, capacity, subs, ids_in, weight_in, x_in, g_in, *refs):
    mine, theirs, near, here, place_out, mix_out, scratch, ids, weight, x, g, sems = refs
    pairs = ((ids_in, ids), (weight_in, weight), (x_in, x), (g_in, g))
    copies = [pltpu.make_async_copy(src, dst, sems.at[i]) for i, (src, dst) in enumerate(pairs)]
    for copy in copies:
        copy.start()
    top, tok = ids.shape
    rows = devices * capacity
    core = lax.axis_index("ffn")
    masks = even_masks(devices)
    masks = [mask + core for mask in masks] + [mask + 1 - core for mask in masks] + [1, 0]
    order = lax.broadcasted_iota(jnp.int32, (devices, tok), 0)
    bits = jnp.zeros((devices, tok), jnp.int32)
    for p, mask in enumerate(masks):
        bits = jnp.where(order == p, mask, bits)
    expert = bits ^ lax.axis_index("expert")
    member = jnp.zeros((devices, tok), jnp.float32)
    mixing = jnp.zeros((devices, tok), jnp.float32)
    copies[0].wait()
    copies[1].wait()
    for route in range(top):
        hit = ids[route : route + 1, :] == expert
        member = jnp.where(hit, 1.0, member)
        mixing = jnp.where(hit, weight[route : route + 1, :], mixing)
    before = lax.broadcasted_iota(jnp.int32, (tok, tok), 0) < lax.broadcasted_iota(jnp.int32, (tok, tok), 1)
    slots = dot(member.astype(jnp.bfloat16), jnp.where(before, 1.0, 0.0).astype(jnp.bfloat16))
    target = jnp.where(member > 0, slots + capacity * order.astype(jnp.float32), -1.0)
    row = lax.broadcasted_iota(jnp.int32, (rows, tok), 0).astype(jnp.float32)
    place = jnp.zeros((rows, tok), jnp.float32)
    mix = jnp.zeros((rows, tok), jnp.float32)
    for p in range(devices):
        equal = target[p : p + 1, :] == row
        place = jnp.where(equal, 1.0, place)
        mix = jnp.where(equal, mixing[p : p + 1, :], mix)
    row_weight = jnp.broadcast_to(jnp.sum(mix, axis=1, keepdims=True), (rows, LANES))
    low = place.astype(jnp.bfloat16)
    place_out[...] = low
    mix_out[...] = row_weight
    size = capacity * subs
    count = devices // 2 - 1

    def write(at):
        def block(p):
            return scratch[p * size : (p + 1) * size, :].astype(mine.dtype)

        for j in range(count):
            part(mine, 2 * j * size + at, size)[...] = block(j)
            part(theirs, 2 * j * size + at, size)[...] = block(count + j)
        part(near, at, size)[...] = block(2 * count)
        part(here, at, size)[...] = block(2 * count + 1)

    copies[2].wait()
    for sub in range(subs):
        spread_lanes(scratch, sub, subs, dot(low, x[:, lanes_of(sub)]))
    write(0)
    copies[3].wait()
    for sub in range(subs):
        spread_lanes(scratch, sub, subs, dot(low, g[:, lanes_of(sub)]) * row_weight)
    write(size)


def pack_kernel(size, mine, swapped, *outs):
    for j, out in enumerate(outs):
        part(out, 0, 2 * size)[...] = part(mine, 2 * j * size, 2 * size)[...]
        part(out, 2 * size, 2 * size)[...] = part(swapped, 2 * j * size, 2 * size)[...]


def gather_kernel(size, *refs):
    blocks, (near, here, _, x_out, g_out) = refs[:-5], refs[-5:]
    for at, out in ((0, x_out), (size, g_out)):
        for j, block in enumerate(blocks):
            part(out, 2 * j * size, size)[...] = part(block, at, size)[...]
            part(out, (2 * j + 1) * size, size)[...] = part(block, 2 * size + at, size)[...]
        part(out, 2 * len(blocks) * size, size)[...] = part(near, at, size)[...]
        part(out, (2 * len(blocks) + 1) * size, size)[...] = part(here, at, size)[...]


def full_rows(devices, subs, scratch, own_sent, other_sent, out):
    size = own_sent.shape[0] // devices
    count = devices // 2 - 1
    own, other = half_starts(out.shape[1] // 2)
    first, second, last = range(0, 2 * count, 2), range(1, 2 * count, 2), range(2 * count, devices)
    layouts = (
        (own, [(own_sent, i) for i in first] + [(other_sent, i) for i in second] + [(own_sent, i) for i in last]),
        (other, [(own_sent, i) for i in second] + [(other_sent, i) for i in first] + [(other_sent, i) for i in last]),
    )
    for start, layout in layouts:

        def put(sub, value):
            out[:, pl.ds(start + sub * LANES, LANES)] = value.astype(out.dtype)

        blocks_to_rows(scratch, [part(ref, i * size, size) for ref, i in layout], put, subs)


def split_terms(count, size, scratch, own_half, keep, send):
    keep[0 : count * size, :] = scratch[0 : count * size, :]
    send[0 : count * size, :] = scratch[count * size : 2 * count * size, :].astype(send.dtype)
    rest = scratch[2 * count * size :, :]
    if own_half:
        keep[count * size :, :] = rest
    else:
        send[count * size :, :] = rest.astype(send.dtype)


def hold_kernel(count, *refs):
    held, sems = refs[2 * count :]
    held[...] = jnp.zeros_like(held)
    copies = [pltpu.make_async_copy(refs[i], refs[count + i], sems.at[i]) for i in range(count)]
    for copy in copies:
        copy.start()
    for copy in copies:
        copy.wait()


def leave_kernel(size, *refs):
    terms, outs = (refs[:4], refs[4:8]), refs[8:]
    count = len(outs) - 2
    for at, (keep_own, keep_other, came_own, came_other) in zip((0, size), terms):

        def own(p):
            total = part(keep_own, p * size, size)[...] + part(came_own, p * size, size)[...].astype(jnp.float32)
            return total.astype(outs[0].dtype)

        for j, out in enumerate(outs[:count]):
            part(out, at, size)[...] = own(j)
            total = part(keep_other, j * size, size)[...] + part(came_other, j * size, size)[...].astype(jnp.float32)
            part(out, 2 * size + at, size)[...] = total.astype(out.dtype)
        part(outs[count], at, size)[...] = own(count)
        part(outs[count + 1], at, size)[...] = own(count + 1)


def share_kernel(size, *refs):
    blocks, (_, _, out) = refs[:-3], refs[-3:]
    for j, block in enumerate(blocks):
        part(out, 2 * j * size, 2 * size)[...] = part(block, 2 * size, 2 * size)[...]


def join_kernel(count, subs, place, mix, *refs):
    blocks, (near, here, shared, out_tokens, grad_tokens, scratch) = refs[:count], refs[count:]
    size = near.shape[0] // 2

    def layout(at):
        first = [part(block, at, size) for block in blocks]
        second = [part(shared, 2 * j * size + at, size) for j in range(count)]
        return first + second + [part(near, at, size), part(here, at, size)]

    def put_out(sub, value):
        low = (value * mix[...]).astype(jnp.bfloat16)
        out_tokens[:, lanes_of(sub)] = contract_rows(place[...], low).astype(out_tokens.dtype)

    def put_grad(sub, value):
        grad_tokens[:, lanes_of(sub)] = contract_rows(place[...], value.astype(jnp.bfloat16)).astype(grad_tokens.dtype)

    blocks_to_rows(scratch, layout(0), put_out, subs)
    blocks_to_rows(scratch, layout(size), put_grad, subs)


def half_starts(half_width):
    half = lax.axis_index("ffn")
    own = pl.multiple_of(half * half_width, half_width)
    other = pl.multiple_of((1 - half) * half_width, half_width)
    return own, other


def chunk(i, step, base=0):
    return pl.ds(base + pl.multiple_of(i * step, step), step)


def dot(left, right):
    return jnp.dot(left, right, preferred_element_type=jnp.float32)


def halves_of_output(devices, subs, step, scratch, own_half, term, keep, send):
    size = scratch.shape[0] // devices
    for at in range(0, subs * LANES, step):
        value = term(at)
        for i in range(step // LANES):
            spread_lanes(scratch, at // LANES + i, subs, value[:, lanes_of(i)])
    split_terms(devices // 2 - 1, size, scratch, own_half, keep, send)


def forward_kernel(
    devices,
    subs,
    step,
    x_sent,
    x_swapped,
    w_gate,
    w_up,
    w_down,
    x_full,
    gate,
    up,
    hidden,
    keep_own,
    keep_other,
    send_own,
    send_other,
    scratch,
):
    own, other = half_starts(subs * LANES)
    full_rows(devices, subs, scratch, x_sent, x_swapped, x_full)

    def project(i, carry):
        cols = chunk(i, step)
        gate_low = dot(x_full[...], w_gate[0, :, cols]).astype(jnp.bfloat16)
        up_low = dot(x_full[...], w_up[0, :, cols]).astype(jnp.bfloat16)
        gate[:, cols] = gate_low
        up[:, cols] = up_low
        value = gate_low.astype(jnp.float32)
        hidden[:, cols] = (value * jax.nn.sigmoid(value) * up_low.astype(jnp.float32)).astype(jnp.bfloat16)
        return carry

    lax.fori_loop(0, gate.shape[1] // step, project, 0)

    def term(start):
        return lambda at: dot(hidden[...], w_down[0, :, pl.ds(start + at, step)])

    halves_of_output(devices, subs, step, scratch, False, term(other), keep_other, send_other)
    halves_of_output(devices, subs, step, scratch, True, term(own), keep_own, send_own)


def input_term(step, pre_gate, pre_up, w_gate, w_up, start):
    def term(at):
        there = pl.ds(start + at, step)
        return contract_cols(pre_gate[...], w_gate[0, there, :]) + contract_cols(pre_up[...], w_up[0, there, :])

    return term


def backward_kernel(
    devices,
    subs,
    step,
    g_sent,
    g_swapped,
    gate,
    up,
    w_gate,
    w_up,
    w_down,
    g_full,
    pre_gate,
    pre_up,
    keep_other,
    send_other,
    scratch,
):
    _, other = half_starts(subs * LANES)
    full_rows(devices, subs, scratch, g_sent, g_swapped, g_full)

    def pull(i, carry):
        cols = chunk(i, step)
        low = contract_cols(g_full[...], w_down[0, cols, :]).astype(jnp.bfloat16)
        grad_hidden = low.astype(jnp.float32)
        value = gate[:, cols].astype(jnp.float32)
        sig = jax.nn.sigmoid(value)
        pre_gate[:, cols] = (
            grad_hidden * up[:, cols].astype(jnp.float32) * sig * (1.0 + value * (1.0 - sig))
        ).astype(jnp.bfloat16)
        pre_up[:, cols] = (grad_hidden * value * sig).astype(jnp.bfloat16)
        return carry

    lax.fori_loop(0, gate.shape[1] // step, pull, 0)
    term = input_term(step, pre_gate, pre_up, w_gate, w_up, other)
    halves_of_output(devices, subs, step, scratch, False, term, keep_other, send_other)


def backward_own_kernel(devices, subs, step, pre_gate, pre_up, w_gate, w_up, keep_own, send_own, scratch):
    own, _ = half_starts(subs * LANES)
    term = input_term(step, pre_gate, pre_up, w_gate, w_up, own)
    halves_of_output(devices, subs, step, scratch, True, term, keep_own, send_own)


def flip(value):
    return value.astype(jnp.float32).T


def pieces_of(total, size):
    return [slice(at, min(at + size, total)) for at in range(0, total, size)]


def gradient_kernel(
    step,
    x,
    g,
    hidden,
    pre_gate,
    pre_up,
    grad_gate,
    grad_up,
    grad_down,
    written,
    flipped,
    turned,
    tall,
    wide,
    tall_sems,
    wide_sems,
):
    written[...] = jnp.zeros_like(written)
    width, lanes = x.shape[1], hidden.shape[1]
    count = width // step
    flipped[...] = flip(hidden[...]).astype(flipped.dtype)

    def wide_copy(i, slot):
        return pltpu.make_async_copy(wide.at[slot], grad_down.at[0, :, chunk(i, step)], wide_sems.at[slot])

    def tall_copy(which, out, i, slot):
        return pltpu.make_async_copy(tall.at[which, slot], out.at[0, chunk(i, step), :], tall_sems.at[which, slot])

    def down(i, carry):
        slot = i % 2

        @pl.when(i >= 2)
        def _():
            wide_copy(i - 2, slot).wait()

        for cut in pieces_of(step, 256):
            right = g[:, chunk(i, step)][:, cut]
            for high in pieces_of(lanes, 256):
                wide[slot, high, cut] = dot(flipped[high, :], right).astype(wide.dtype)
        wide_copy(i, slot).start()
        return carry

    lax.fori_loop(0, count, down, 0)

    def inputs(i, carry):
        slot = i % 2
        turned[...] = flip(x[:, chunk(i, step)]).astype(turned.dtype)
        for which, (right, out) in enumerate(((pre_gate, grad_gate), (pre_up, grad_up))):

            @pl.when(i >= 2)
            def _():
                tall_copy(which, out, i - 2, slot).wait()

            for cut in pieces_of(lanes, 256):
                for high in pieces_of(step, 256):
                    tall[which, slot, high, cut] = dot(turned[high, :], right[:, cut]).astype(tall.dtype)
            tall_copy(which, out, i, slot).start()
        return carry

    lax.fori_loop(0, count, inputs, 0)
    for i in range(max(0, count - 2), count):
        wide_copy(i, i % 2).wait()
        tall_copy(0, grad_gate, i, i % 2).wait()
        tall_copy(1, grad_up, i, i % 2).wait()


def exchange(blocks, near, devices):
    arrived = []
    for block, mask in zip(blocks, even_masks(devices)):
        pairs = [(2 * i + core, 2 * (i ^ (mask + core)) + core) for i in range(devices) for core in range(2)]
        arrived.append(lax.ppermute(block, ("expert", "ffn"), pairs))
    return arrived, lax.ppermute(near, "expert", [(i, i ^ 1) for i in range(devices)])


def swap(value):
    return lax.ppermute(value, "ffn", [(0, 1), (1, 0)])


def in_hbm(values):
    return [pltpu.with_memory_space_constraint(value, pltpu.HBM) for value in values]


def one_piece_shards(tokens, grad_out, route_ids, route_weight, gate_weight, up_weight, down_weight):
    tok_dev, sub_width = tokens.shape
    top_count = route_ids.shape[1]
    width, lanes = gate_weight.shape[1:]
    devices = lax.axis_size("expert")
    capacity = max(2, min(tok_dev, (9 * tok_dev * top_count + 8 * EXPERTS - 1) // (8 * EXPERTS)))
    rows = devices * capacity
    subs = sub_width // LANES
    low, full = jnp.bfloat16, jnp.float32
    size = capacity * subs
    count = devices // 2 - 1
    spread_scratch = [pltpu.VMEM((devices * size, LANES), full)]
    step = 256
    half_flops = 2 * rows * width * lanes // 2

    def lines(number, dtype=low):
        return jax.ShapeDtypeStruct((number * size, LANES), dtype)

    def lines_in_vmem(number, dtype=low):
        return vmem((number * size, LANES), dtype)

    sources = (route_ids.T, route_weight.T, tokens, grad_out)
    mine, theirs, near, here, place, mix = call(
        functools.partial(route_kernel, devices, capacity, subs),
        [lines(2 * count), lines(2 * count), lines(2), lines(2)]
        + [jax.ShapeDtypeStruct((rows, tok_dev), low), jax.ShapeDtypeStruct((rows, LANES), full)],
        in_hbm(sources),
        in_spaces=[pl.ANY] * 4,
        scratch=spread_scratch
        + [pltpu.VMEM(value.shape, value.dtype) for value in sources]
        + [pltpu.SemaphoreType.DMA((4,))],
        traffic=4 * tok_dev * sub_width,
    )
    packed = call(functools.partial(pack_kernel, size), [lines(4)] * count, (mine, swap(theirs)))
    arrived, near = exchange(packed, near, devices)

    weights = (gate_weight, up_weight, down_weight)
    w_gate, w_up, w_down, held = call(
        functools.partial(hold_kernel, 3),
        [vmem(w.shape, w.dtype) for w in weights] + [vmem((8, LANES), full)],
        in_hbm(weights),
        in_spaces=[pl.ANY] * 3,
        scratch=[pltpu.SemaphoreType.DMA((3,))],
        traffic=sum(w.size * 2 for w in weights),
    )
    x_sent, g_sent = call(
        functools.partial(gather_kernel, size), [lines(devices)] * 2, (*arrived, near, here, held)
    )
    x_swapped = swap(x_sent)
    g_swapped = swap(g_sent)
    terms = [
        lines_in_vmem(count + 2, full),
        lines_in_vmem(count, full),
        lines_in_vmem(count),
        lines_in_vmem(count + 2),
    ]
    x_full, gate, up, hidden, out_own, out_other, send_own, send_other = call(
        functools.partial(forward_kernel, devices, subs, step),
        [vmem((rows, width), low)] + [vmem((rows, lanes), low)] * 3 + terms,
        (x_sent, x_swapped, w_gate, w_up, w_down),
        scratch=spread_scratch,
        flops=6 * half_flops,
    )
    out_terms = (out_own, out_other, swap(send_other), swap(send_own))
    g_full, pre_gate, pre_up, dx_other, send_other = call(
        functools.partial(backward_kernel, devices, subs, step),
        [vmem((rows, width), low)] + [vmem((rows, lanes), low)] * 2 + [terms[1], terms[3]],
        (g_sent, g_swapped, gate, up, w_gate, w_up, w_down),
        scratch=spread_scratch,
        flops=4 * half_flops,
    )
    came_own = swap(send_other)
    dx_own, send_own = call(
        functools.partial(backward_own_kernel, devices, subs, step),
        [terms[0], terms[2]],
        (pre_gate, pre_up, w_gate, w_up),
        scratch=spread_scratch,
        flops=2 * half_flops,
    )
    dx_terms = (dx_own, dx_other, came_own, swap(send_own))
    *leaving, near, here = call(
        functools.partial(leave_kernel, size),
        [lines(4)] * count + [lines(2)] * 2,
        (*out_terms, *dx_terms),
    )
    returned, near = exchange(leaving, near, devices)
    cut = 1024 if width % 1024 == 0 else width
    grad_gate, grad_up, grad_down, written = call(
        functools.partial(gradient_kernel, cut),
        [jax.ShapeDtypeStruct(w.shape, low) for w in weights] + [vmem((8, LANES), full)],
        (x_full, g_full, hidden, pre_gate, pre_up),
        out_spaces=[pl.ANY] * 3 + [pltpu.VMEM],
        scratch=[
            pltpu.VMEM((lanes, rows), low),
            pltpu.VMEM((cut, rows), low),
            pltpu.VMEM((2, 2, cut, lanes), low),
            pltpu.VMEM((2, lanes, cut), low),
            pltpu.SemaphoreType.DMA((2, 2)),
            pltpu.SemaphoreType.DMA((2,)),
        ],
        flops=6 * half_flops,
        traffic=sum(w.size * 2 for w in weights),
        limit=32,
    )
    (sharing,) = call(functools.partial(share_kernel, size), [lines(2 * count)], (*returned, near, written))
    out_tokens, grad_tokens = call(
        functools.partial(join_kernel, count, subs),
        [jax.ShapeDtypeStruct((tok_dev, sub_width), low)] * 2,
        (place, mix, *returned, near, here, swap(sharing)),
        scratch=spread_scratch,
        traffic=8 * tok_dev * sub_width,
    )
    return out_tokens, grad_tokens, grad_gate, grad_up, grad_down


def shards(*args):
    tokens, gate_weight = args[0], args[4]
    halves = lax.axis_size("ffn")
    devices = lax.axis_size("expert")
    if halves == 2 and devices >= 4 and devices & (devices - 1) == 0 and tokens.shape[1] * halves == gate_weight.shape[1]:
        return one_piece_shards(*args)
    return general_shards(*args)


def solution(mesh):
    in_specs = (
        P(("groups", "expert"), "ffn"),
        P(("groups", "expert"), "ffn"),
        P(("groups", "expert"), None),
        P(("groups", "expert"), None),
        P("expert", None, "ffn"),
        P("expert", None, "ffn"),
        P("expert", "ffn", None),
    )
    out_specs = (
        P(("groups", "expert"), "ffn"),
        P(("groups", "expert"), "ffn"),
        P(("groups", "expert"), None, "ffn"),
        P(("groups", "expert"), None, "ffn"),
        P(("groups", "expert"), "ffn", None),
    )
    return jax.shard_map(shards, mesh=mesh, in_specs=in_specs, out_specs=out_specs, check_vma=False)
```

```python
import functools

import jax
import jax.numpy as jnp
from jax import lax
from jax.experimental import pallas as pl
from jax.experimental.pallas import tpu as pltpu
from jax.sharding import PartitionSpec as P

EXPERTS = 128
LANES = 128
MIB = 1024 * 1024


def contract_rows(left, right):
    return lax.dot_general(
        left, right, (((0,), (0,)), ((), ())), preferred_element_type=jnp.float32
    )


def contract_cols(left, right):
    return lax.dot_general(
        left, right, (((1,), (1,)), ((), ())), preferred_element_type=jnp.float32
    )


def general_shards(tokens, grad_out, route_ids, route_weight, gate_weight, up_weight, down_weight):
    tokens, grad_out = (
        lax.all_gather(tokens, "ffn", axis=1, tiled=True),
        lax.all_gather(grad_out, "ffn", axis=1, tiled=True),
    )
    tok_dev, width = tokens.shape
    top_count = route_ids.shape[1]
    piece_width = gate_weight.shape[1]
    hidden_half = gate_weight.shape[2]
    pieces = width // piece_width
    devices = lax.axis_size("expert")
    flight = devices // pieces
    halves = lax.axis_size("ffn")
    sub_width = piece_width // halves
    capacity = max(2, min(tok_dev, (9 * tok_dev * top_count + 8 * EXPERTS - 1) // (8 * EXPERTS)))
    total_rows = devices * capacity
    expert_ids = jnp.arange(flight, dtype=jnp.int32)
    member = jnp.zeros((tok_dev, flight), jnp.float32)
    mixing = jnp.zeros((tok_dev, flight), jnp.float32)
    for route in range(top_count):
        hit = (route_ids[:, route : route + 1] == expert_ids[None, :]).astype(jnp.float32)
        member = member + hit
        mixing = mixing + hit * route_weight[:, route : route + 1]
    slots = jnp.cumsum(member, axis=0) - member
    place = member[:, :, None] * (
        slots[:, :, None] == jnp.arange(capacity, dtype=jnp.float32)
    ).astype(jnp.float32)
    weighted = place * mixing[:, :, None]
    place_low = place.astype(jnp.bfloat16)
    x_four = tokens.reshape(tok_dev, halves, pieces, sub_width)
    g_four = grad_out.reshape(tok_dev, halves, pieces, sub_width)
    x_parts = []
    g_parts = []
    for half in range(halves):
        x_parts.append(
            jnp.einsum(
                "Tec,Tjr->ejcr", place_low, x_four[:, half], preferred_element_type=jnp.float32
            )
        )
        g_parts.append(jnp.einsum("Tec,Tjr->ejcr", weighted, g_four[:, half].astype(jnp.float32)))
    x_send = jnp.concatenate(x_parts, axis=3).astype(jnp.bfloat16).reshape(total_rows, piece_width)
    g_send = jnp.concatenate(g_parts, axis=3).astype(jnp.bfloat16).reshape(total_rows, piece_width)

    def return_parts(values):
        arrived = lax.all_to_all(values, "expert", split_axis=0, concat_axis=0, tiled=True)
        lanes = arrived.shape[1]
        return arrived.astype(jnp.float32).reshape(flight, pieces, capacity, lanes).sum(axis=1)

    def spread_rows(values):
        lanes = values.shape[2]
        copies = jnp.broadcast_to(values[:, None], (flight, pieces, capacity, lanes)).reshape(
            total_rows, lanes
        )
        return lax.all_to_all(copies, "expert", split_axis=0, concat_axis=0, tiled=True)

    def finish(term, mix):
        summed = lax.psum_scatter(term, "ffn", scatter_dimension=1, tiled=True)
        back = lax.all_to_all(summed, "expert", split_axis=0, concat_axis=0, tiled=True)
        back = back.reshape(flight, pieces, capacity, sub_width)
        joined = jnp.einsum("Tec,ejcr->Tjr", mix, back)
        return joined.reshape(tok_dev, pieces * sub_width).astype(jnp.bfloat16)

    rows = lax.all_to_all(x_send, "expert", split_axis=0, concat_axis=0, tiled=True)
    w_gate = gate_weight[0]
    w_up = up_weight[0]
    w_down = down_weight[0]
    partial_value = jnp.concatenate(
        [
            jnp.dot(rows, w_gate, preferred_element_type=jnp.float32),
            jnp.dot(rows, w_up, preferred_element_type=jnp.float32),
        ],
        axis=1,
    )
    summed = return_parts(partial_value.astype(jnp.bfloat16))
    gate = summed[:, :, :hidden_half]
    up = summed[:, :, hidden_half:]
    sig = jax.nn.sigmoid(gate)
    act = gate * sig
    hidden = (act * up).astype(jnp.bfloat16)
    h_rows = spread_rows(hidden)
    out_term = jnp.dot(h_rows, w_down, preferred_element_type=jnp.float32)
    out_tokens = finish(out_term, weighted)
    grads = lax.all_to_all(g_send, "expert", split_axis=0, concat_axis=0, tiled=True)
    grad_down = contract_rows(h_rows, grads).astype(jnp.bfloat16)
    hidden_part = contract_cols(grads, w_down).astype(jnp.bfloat16)
    grad_hidden = return_parts(hidden_part)
    pre_gate = (grad_hidden * up * sig * (1.0 + gate * (1.0 - sig))).astype(jnp.bfloat16)
    pre_up = (grad_hidden * act).astype(jnp.bfloat16)
    both = spread_rows(jnp.concatenate([pre_gate, pre_up], axis=2))
    d_gate_rows = both[:, :hidden_half]
    d_up_rows = both[:, hidden_half:]
    grad_gate = contract_rows(rows, d_gate_rows).astype(jnp.bfloat16)
    grad_up = contract_rows(rows, d_up_rows).astype(jnp.bfloat16)
    x_term = contract_cols(d_gate_rows, w_gate) + contract_cols(d_up_rows, w_up)
    grad_tokens = finish(x_term, place)
    return (out_tokens, grad_tokens, grad_gate[None], grad_up[None], grad_down[None])


def vmem(shape, dtype):
    return pltpu.VMEM(shape, dtype)


def call(kernel, out_shape, args, in_spaces=None, out_spaces=None, flops=0, traffic=0, scratch=(), limit=16):
    spaces = in_spaces or [pltpu.VMEM] * len(args)
    outs = out_spaces or [pltpu.VMEM] * len(out_shape)
    return pl.pallas_call(
        kernel,
        out_shape=tuple(out_shape),
        in_specs=[pl.BlockSpec(memory_space=space) for space in spaces],
        out_specs=tuple(pl.BlockSpec(memory_space=space) for space in outs),
        scratch_shapes=list(scratch),
        compiler_params=pltpu.CompilerParams(vmem_limit_bytes=limit * MIB),
        cost_estimate=pl.CostEstimate(flops=flops, bytes_accessed=traffic, transcendentals=0),
    )(*args)


def blocks_to_rows(scratch, blocks, put, subs):
    size = blocks[0].shape[0]
    for p, block in enumerate(blocks):
        scratch[p * size : (p + 1) * size, :] = block[...].astype(jnp.float32)
    for sub in range(subs):
        put(sub, scratch[pl.ds(sub, len(blocks) * size // subs, stride=subs), :])


def spread_lanes(scratch, sub, subs, value):
    scratch[pl.ds(sub, value.shape[0], stride=subs), :] = value


def part(ref, start, count):
    return ref.at[start : start + count, :]


def lanes_of(sub):
    return slice(sub * LANES, (sub + 1) * LANES)


def even_masks(count):
    return [*range(count // 2, count, 2), *range(2, count // 2, 2)]


def route_kernel(devices, capacity, subs, ids_in, weight_in, x_in, g_in, *refs):
    (*outs, theirs, place_out, mix_out, scratch, ids, weight, x, g, sems) = refs
    pairs = ((ids_in, ids), (weight_in, weight), (x_in, x), (g_in, g))
    copies = [pltpu.make_async_copy(src, dst, sems.at[i]) for i, (src, dst) in enumerate(pairs)]
    for copy in copies:
        copy.start()
    top, tok = ids.shape
    rows = devices * capacity
    core = lax.axis_index("ffn")
    masks = even_masks(devices)
    masks = [mask + core for mask in masks] + [mask + 1 - core for mask in masks] + [1, 0]
    order = lax.broadcasted_iota(jnp.int32, (devices, tok), 0)
    bits = jnp.zeros((devices, tok), jnp.int32)
    for p, mask in enumerate(masks):
        bits = jnp.where(order == p, mask, bits)
    expert = bits ^ lax.axis_index("expert")
    member = jnp.zeros((devices, tok), jnp.float32)
    mixing = jnp.zeros((devices, tok), jnp.float32)
    copies[0].wait()
    copies[1].wait()
    for route in range(top):
        hit = ids[route : route + 1, :] == expert
        member = jnp.where(hit, 1.0, member)
        mixing = jnp.where(hit, weight[route : route + 1, :], mixing)
    before = lax.broadcasted_iota(jnp.int32, (tok, tok), 0) < lax.broadcasted_iota(jnp.int32, (tok, tok), 1)
    slots = dot(member.astype(jnp.bfloat16), jnp.where(before, 1.0, 0.0).astype(jnp.bfloat16))
    target = jnp.where(member > 0, slots + capacity * order.astype(jnp.float32), -1.0)
    row = lax.broadcasted_iota(jnp.int32, (rows, tok), 0).astype(jnp.float32)
    place = jnp.zeros((rows, tok), jnp.float32)
    mix = jnp.zeros((rows, tok), jnp.float32)
    for p in range(devices):
        equal = target[p : p + 1, :] == row
        place = jnp.where(equal, 1.0, place)
        mix = jnp.where(equal, mixing[p : p + 1, :], mix)
    row_weight = jnp.broadcast_to(jnp.sum(mix, axis=1, keepdims=True), (rows, LANES))
    low = place.astype(jnp.bfloat16)
    place_out[...] = low
    mix_out[...] = row_weight
    size = capacity * subs
    count = devices // 2 - 1

    def write(mine, near, here, at):
        def block(p):
            return scratch[p * size : (p + 1) * size, :].astype(mine.dtype)

        for j in range(count):
            part(mine, j * size, size)[...] = block(j)
            part(theirs, (at + j) * size, size)[...] = block(count + j)
        near[...] = block(2 * count)
        here[...] = block(2 * count + 1)

    copies[2].wait()
    for sub in range(subs):
        spread_lanes(scratch, sub, subs, dot(low, x[:, lanes_of(sub)]))
    write(*outs[:3], 0)
    copies[3].wait()
    for sub in range(subs):
        spread_lanes(scratch, sub, subs, dot(low, g[:, lanes_of(sub)]) * row_weight)
    write(*outs[3:], count)


def pack_kernel(size, x_mine, g_mine, swapped, *outs):
    count = len(outs) // 2
    for i, out in enumerate(outs):
        mine = x_mine if i < count else g_mine
        part(out, 0, size)[...] = part(mine, i % count * size, size)[...]
        part(out, size, size)[...] = part(swapped, i * size, size)[...]


def gather_kernel(size, *refs):
    blocks, (near, here, _, out) = refs[:-4], refs[-4:]
    for j, block in enumerate(blocks):
        part(out, 2 * j * size, 2 * size)[...] = block[...]
    part(out, 2 * len(blocks) * size, size)[...] = near[...]
    part(out, (2 * len(blocks) + 1) * size, size)[...] = here[...]


def full_rows(devices, subs, scratch, own_sent, other_sent, out):
    size = own_sent.shape[0] // devices
    count = devices // 2 - 1
    own, other = half_starts(out.shape[1] // 2)
    first, second, last = range(0, 2 * count, 2), range(1, 2 * count, 2), range(2 * count, devices)
    layouts = (
        (own, [(own_sent, i) for i in first] + [(other_sent, i) for i in second] + [(own_sent, i) for i in last]),
        (other, [(own_sent, i) for i in second] + [(other_sent, i) for i in first] + [(other_sent, i) for i in last]),
    )
    for start, layout in layouts:

        def put(sub, value):
            out[:, pl.ds(start + sub * LANES, LANES)] = value.astype(out.dtype)

        blocks_to_rows(scratch, [part(ref, i * size, size) for ref, i in layout], put, subs)


def split_terms(count, size, scratch, own_half, keep, send):
    keep[0 : count * size, :] = scratch[0 : count * size, :]
    send[0 : count * size, :] = scratch[count * size : 2 * count * size, :].astype(send.dtype)
    rest = scratch[2 * count * size :, :]
    if own_half:
        keep[count * size :, :] = rest
    else:
        send[count * size :, :] = rest.astype(send.dtype)


def leave_kernel(size, *refs):
    terms, outs = (refs[:4], refs[4:8]), refs[8:]
    count = len(outs) - 2
    for at, (keep_own, keep_other, came_own, came_other) in zip((0, size), terms):

        def own(p):
            total = part(keep_own, p * size, size)[...] + part(came_own, p * size, size)[...].astype(jnp.float32)
            return total.astype(outs[0].dtype)

        for j, out in enumerate(outs[:count]):
            part(out, at, size)[...] = own(j)
            total = part(keep_other, j * size, size)[...] + part(came_other, j * size, size)[...].astype(jnp.float32)
            part(out, 2 * size + at, size)[...] = total.astype(out.dtype)
        part(outs[count], at, size)[...] = own(count)
        part(outs[count + 1], at, size)[...] = own(count + 1)


def share_kernel(size, *refs):
    blocks, (_, _, out) = refs[:-3], refs[-3:]
    for j, block in enumerate(blocks):
        part(out, 2 * j * size, 2 * size)[...] = part(block, 2 * size, 2 * size)[...]


def join_kernel(count, subs, place, mix, *refs):
    blocks, (near, here, shared, out_tokens, grad_tokens, scratch) = refs[:count], refs[count:]
    size = near.shape[0] // 2

    def layout(at):
        first = [part(block, at, size) for block in blocks]
        second = [part(shared, 2 * j * size + at, size) for j in range(count)]
        return first + second + [part(near, at, size), part(here, at, size)]

    def put_out(sub, value):
        low = (value * mix[...]).astype(jnp.bfloat16)
        out_tokens[:, lanes_of(sub)] = contract_rows(place[...], low).astype(out_tokens.dtype)

    def put_grad(sub, value):
        grad_tokens[:, lanes_of(sub)] = contract_rows(place[...], value.astype(jnp.bfloat16)).astype(grad_tokens.dtype)

    blocks_to_rows(scratch, layout(0), put_out, subs)
    blocks_to_rows(scratch, layout(size), put_grad, subs)


def half_starts(half_width):
    half = lax.axis_index("ffn")
    own = pl.multiple_of(half * half_width, half_width)
    other = pl.multiple_of((1 - half) * half_width, half_width)
    return own, other


def chunk(i, step, base=0):
    return pl.ds(base + pl.multiple_of(i * step, step), step)


def dot(left, right):
    return jnp.dot(left, right, preferred_element_type=jnp.float32)


def halves_of_output(devices, subs, step, scratch, own_half, term, keep, send):
    size = scratch.shape[0] // devices
    for at in range(0, subs * LANES, step):
        value = term(at)
        for i in range(step // LANES):
            spread_lanes(scratch, at // LANES + i, subs, value[:, lanes_of(i)])
    split_terms(devices // 2 - 1, size, scratch, own_half, keep, send)


def forward_kernel(devices, subs, step, x_sent, x_swapped, w_gate, w_up, x_full, gate, up, hidden, scratch):
    full_rows(devices, subs, scratch, x_sent, x_swapped, x_full)
    for cols in pieces_of(gate.shape[1], step):
        gate_low = dot(x_full[...], w_gate[0, :, cols]).astype(jnp.bfloat16)
        up_low = dot(x_full[...], w_up[0, :, cols]).astype(jnp.bfloat16)
        gate[:, cols] = gate_low
        up[:, cols] = up_low
        value = gate_low.astype(jnp.float32)
        hidden[:, cols] = (value * jax.nn.sigmoid(value) * up_low.astype(jnp.float32)).astype(jnp.bfloat16)


def output_kernel(devices, subs, step, hidden, w_down, keep_own, keep_other, send_own, send_other, scratch):
    own, other = half_starts(subs * LANES)

    def term(start):
        return lambda at: dot(hidden[...], w_down[0, :, pl.ds(start + at, step)])

    halves_of_output(devices, subs, step, scratch, False, term(other), keep_other, send_other)
    halves_of_output(devices, subs, step, scratch, True, term(own), keep_own, send_own)


def input_term(step, pre_gate, pre_up, w_gate, w_up, start):
    def term(at):
        there = pl.ds(start + at, step)
        return contract_cols(pre_gate[...], w_gate[0, there, :]) + contract_cols(pre_up[...], w_up[0, there, :])

    return term


def backward_kernel(
    devices,
    subs,
    step,
    g_sent,
    g_swapped,
    gate,
    up,
    w_gate,
    w_up,
    w_down,
    g_full,
    pre_gate,
    pre_up,
    keep_other,
    send_other,
    scratch,
):
    _, other = half_starts(subs * LANES)
    full_rows(devices, subs, scratch, g_sent, g_swapped, g_full)

    def pull(i, carry):
        cols = chunk(i, step)
        low = contract_cols(g_full[...], w_down[0, cols, :]).astype(jnp.bfloat16)
        grad_hidden = low.astype(jnp.float32)
        value = gate[:, cols].astype(jnp.float32)
        sig = jax.nn.sigmoid(value)
        pre_gate[:, cols] = (
            grad_hidden * up[:, cols].astype(jnp.float32) * sig * (1.0 + value * (1.0 - sig))
        ).astype(jnp.bfloat16)
        pre_up[:, cols] = (grad_hidden * value * sig).astype(jnp.bfloat16)
        return carry

    lax.fori_loop(0, gate.shape[1] // step, pull, 0)
    term = input_term(step, pre_gate, pre_up, w_gate, w_up, other)
    halves_of_output(devices, subs, step, scratch, False, term, keep_other, send_other)


def backward_own_kernel(devices, subs, step, pre_gate, pre_up, w_gate, w_up, keep_own, send_own, scratch):
    own, _ = half_starts(subs * LANES)
    term = input_term(step, pre_gate, pre_up, w_gate, w_up, own)
    halves_of_output(devices, subs, step, scratch, True, term, keep_own, send_own)


def flip(value):
    return value.astype(jnp.float32).T


def pieces_of(total, size):
    return [slice(at, min(at + size, total)) for at in range(0, total, size)]


def gradient_kernel(
    step,
    x,
    g,
    hidden,
    pre_gate,
    pre_up,
    grad_gate,
    grad_up,
    grad_down,
    written,
    flipped,
    turned,
    tall,
    wide,
    tall_sems,
    wide_sems,
):
    written[...] = jnp.zeros_like(written)
    width, lanes = x.shape[1], hidden.shape[1]
    count = width // step
    flipped[...] = flip(hidden[...]).astype(flipped.dtype)

    def wide_copy(i, slot):
        return pltpu.make_async_copy(wide.at[slot], grad_down.at[0, :, chunk(i, step)], wide_sems.at[slot])

    def tall_copy(which, out, i, slot):
        return pltpu.make_async_copy(tall.at[which, slot], out.at[0, chunk(i, step), :], tall_sems.at[which, slot])

    def down(i, carry):
        slot = i % 2

        @pl.when(i >= 2)
        def _():
            wide_copy(i - 2, slot).wait()

        for cut in pieces_of(step, 256):
            right = g[:, chunk(i, step)][:, cut]
            for high in pieces_of(lanes, 256):
                wide[slot, high, cut] = dot(flipped[high, :], right).astype(wide.dtype)
        wide_copy(i, slot).start()
        return carry

    lax.fori_loop(0, count, down, 0)

    def inputs(i, carry):
        slot = i % 2
        turned[...] = flip(x[:, chunk(i, step)]).astype(turned.dtype)
        for which, (right, out) in enumerate(((pre_gate, grad_gate), (pre_up, grad_up))):

            @pl.when(i >= 2)
            def _():
                tall_copy(which, out, i - 2, slot).wait()

            for cut in pieces_of(lanes, 256):
                for high in pieces_of(step, 256):
                    tall[which, slot, high, cut] = dot(turned[high, :], right[:, cut]).astype(tall.dtype)
            tall_copy(which, out, i, slot).start()
        return carry

    lax.fori_loop(0, count, inputs, 0)
    for i in range(max(0, count - 2), count):
        wide_copy(i, i % 2).wait()
        tall_copy(0, grad_gate, i, i % 2).wait()
        tall_copy(1, grad_up, i, i % 2).wait()


def exchange(blocks, near, devices):
    arrived = []
    for block, mask in zip(blocks, even_masks(devices)):
        pairs = [(2 * i + core, 2 * (i ^ (mask + core)) + core) for i in range(devices) for core in range(2)]
        arrived.append(lax.ppermute(block, ("expert", "ffn"), pairs))
    return arrived, lax.ppermute(near, "expert", [(i, i ^ 1) for i in range(devices)])


def swap(value):
    return lax.ppermute(value, "ffn", [(0, 1), (1, 0)])


def in_hbm(values):
    return [pltpu.with_memory_space_constraint(value, pltpu.HBM) for value in values]


def one_piece_shards(tokens, grad_out, route_ids, route_weight, gate_weight, up_weight, down_weight):
    tok_dev, sub_width = tokens.shape
    top_count = route_ids.shape[1]
    width, lanes = gate_weight.shape[1:]
    devices = lax.axis_size("expert")
    capacity = max(2, min(tok_dev, (9 * tok_dev * top_count + 8 * EXPERTS - 1) // (8 * EXPERTS)))
    rows = devices * capacity
    subs = sub_width // LANES
    low, full = jnp.bfloat16, jnp.float32
    size = capacity * subs
    count = devices // 2 - 1
    spread_scratch = [pltpu.VMEM((devices * size, LANES), full)]
    step = 256
    half_flops = 2 * rows * width * lanes // 2

    def lines(number, dtype=low):
        return jax.ShapeDtypeStruct((number * size, LANES), dtype)

    def lines_in_vmem(number, dtype=low):
        return vmem((number * size, LANES), dtype)

    sources = (route_ids.T, route_weight.T, tokens, grad_out)
    x_mine, x_near, x_here, g_mine, g_near, g_here, theirs, place, mix = call(
        functools.partial(route_kernel, devices, capacity, subs),
        [lines(count), lines(1), lines(1)] * 2
        + [lines(2 * count), jax.ShapeDtypeStruct((rows, tok_dev), low), jax.ShapeDtypeStruct((rows, LANES), full)],
        in_hbm(sources),
        in_spaces=[pl.ANY] * 4,
        scratch=spread_scratch
        + [pltpu.VMEM(value.shape, value.dtype) for value in sources]
        + [pltpu.SemaphoreType.DMA((4,))],
        traffic=4 * tok_dev * sub_width,
    )
    packed = call(
        functools.partial(pack_kernel, size),
        [lines(2)] * (2 * count),
        (x_mine, g_mine, swap(theirs)),
        flops=24 * half_flops,
    )
    x_arrived, x_near = exchange(packed[:count], x_near, devices)
    g_arrived, g_near = exchange(packed[count:], g_near, devices)

    weights = (gate_weight, up_weight, down_weight)
    w_gate, w_up, w_down = [pltpu.with_memory_space_constraint(w, pltpu.VMEM) for w in weights]

    def gather(arrived, near, here, after):
        return call(functools.partial(gather_kernel, size), [lines(devices)], (*arrived, near, here, after))[0]

    x_sent = gather(x_arrived, x_near, x_here, mix)
    x_swapped = swap(x_sent)
    terms = [
        lines_in_vmem(count + 2, full),
        lines_in_vmem(count, full),
        lines_in_vmem(count),
        lines_in_vmem(count + 2),
    ]
    x_full, gate, up, hidden = call(
        functools.partial(forward_kernel, devices, subs, step),
        [vmem((rows, width), low)] + [vmem((rows, lanes), low)] * 3,
        (x_sent, x_swapped, w_gate, w_up),
        scratch=spread_scratch,
        flops=4 * half_flops,
    )
    g_sent = gather(g_arrived, g_near, g_here, hidden)
    g_swapped = swap(g_sent)
    out_own, out_other, send_own, send_other = call(
        functools.partial(output_kernel, devices, subs, step),
        terms,
        (hidden, w_down),
        scratch=spread_scratch,
        flops=2 * half_flops,
    )
    out_terms = (out_own, out_other, swap(send_other), swap(send_own))
    g_full, pre_gate, pre_up, dx_other, send_other = call(
        functools.partial(backward_kernel, devices, subs, step),
        [vmem((rows, width), low)] + [vmem((rows, lanes), low)] * 2 + [terms[1], terms[3]],
        (g_sent, g_swapped, gate, up, w_gate, w_up, w_down),
        scratch=spread_scratch,
        flops=4 * half_flops,
    )
    came_own = swap(send_other)
    dx_own, send_own = call(
        functools.partial(backward_own_kernel, devices, subs, step),
        [terms[0], terms[2]],
        (pre_gate, pre_up, w_gate, w_up),
        scratch=spread_scratch,
        flops=2 * half_flops,
    )
    dx_terms = (dx_own, dx_other, came_own, swap(send_own))
    *leaving, near, here = call(
        functools.partial(leave_kernel, size),
        [lines(4)] * count + [lines(2)] * 2,
        (*out_terms, *dx_terms),
    )
    returned, near = exchange(leaving, near, devices)
    cut = 1024 if width % 1024 == 0 else width
    grad_gate, grad_up, grad_down, written = call(
        functools.partial(gradient_kernel, cut),
        [jax.ShapeDtypeStruct(w.shape, low) for w in weights] + [vmem((8, LANES), full)],
        (x_full, g_full, hidden, pre_gate, pre_up),
        out_spaces=[pl.ANY] * 3 + [pltpu.VMEM],
        scratch=[
            pltpu.VMEM((lanes, rows), low),
            pltpu.VMEM((cut, rows), low),
            pltpu.VMEM((2, 2, cut, lanes), low),
            pltpu.VMEM((2, lanes, cut), low),
            pltpu.SemaphoreType.DMA((2, 2)),
            pltpu.SemaphoreType.DMA((2,)),
        ],
        flops=6 * half_flops,
        traffic=sum(w.size * 2 for w in weights),
        limit=32,
    )
    (sharing,) = call(functools.partial(share_kernel, size), [lines(2 * count)], (*returned, near, written))
    out_tokens, grad_tokens = call(
        functools.partial(join_kernel, count, subs),
        [jax.ShapeDtypeStruct((tok_dev, sub_width), low)] * 2,
        (place, mix, *returned, near, here, swap(sharing)),
        scratch=spread_scratch,
        traffic=8 * tok_dev * sub_width,
    )
    return out_tokens, grad_tokens, grad_gate, grad_up, grad_down


def shards(*args):
    tokens, gate_weight = args[0], args[4]
    halves = lax.axis_size("ffn")
    devices = lax.axis_size("expert")
    if halves == 2 and devices >= 4 and devices & (devices - 1) == 0 and tokens.shape[1] * halves == gate_weight.shape[1]:
        return one_piece_shards(*args)
    return general_shards(*args)


def solution(mesh):
    in_specs = (
        P(("groups", "expert"), "ffn"),
        P(("groups", "expert"), "ffn"),
        P(("groups", "expert"), None),
        P(("groups", "expert"), None),
        P("expert", None, "ffn"),
        P("expert", None, "ffn"),
        P("expert", "ffn", None),
    )
    out_specs = (
        P(("groups", "expert"), "ffn"),
        P(("groups", "expert"), "ffn"),
        P(("groups", "expert"), None, "ffn"),
        P(("groups", "expert"), None, "ffn"),
        P(("groups", "expert"), "ffn", None),
    )
    return jax.shard_map(shards, mesh=mesh, in_specs=in_specs, out_specs=out_specs, check_vma=False)
```

```python
import functools

import jax
import jax.numpy as jnp
from jax import lax
from jax.experimental import pallas as pl
from jax.experimental.pallas import tpu as pltpu
from jax.sharding import PartitionSpec as P

EXPERTS = 128
LANES = 128
MIB = 1024 * 1024


def contract_rows(left, right):
    return lax.dot_general(
        left, right, (((0,), (0,)), ((), ())), preferred_element_type=jnp.float32
    )


def contract_cols(left, right):
    return lax.dot_general(
        left, right, (((1,), (1,)), ((), ())), preferred_element_type=jnp.float32
    )


def general_shards(tokens, grad_out, route_ids, route_weight, gate_weight, up_weight, down_weight):
    tokens, grad_out = (
        lax.all_gather(tokens, "ffn", axis=1, tiled=True),
        lax.all_gather(grad_out, "ffn", axis=1, tiled=True),
    )
    tok_dev, width = tokens.shape
    top_count = route_ids.shape[1]
    piece_width = gate_weight.shape[1]
    hidden_half = gate_weight.shape[2]
    pieces = width // piece_width
    devices = lax.axis_size("expert")
    flight = devices // pieces
    halves = lax.axis_size("ffn")
    sub_width = piece_width // halves
    capacity = max(2, min(tok_dev, (9 * tok_dev * top_count + 8 * EXPERTS - 1) // (8 * EXPERTS)))
    total_rows = devices * capacity
    expert_ids = jnp.arange(flight, dtype=jnp.int32)
    member = jnp.zeros((tok_dev, flight), jnp.float32)
    mixing = jnp.zeros((tok_dev, flight), jnp.float32)
    for route in range(top_count):
        hit = (route_ids[:, route : route + 1] == expert_ids[None, :]).astype(jnp.float32)
        member = member + hit
        mixing = mixing + hit * route_weight[:, route : route + 1]
    slots = jnp.cumsum(member, axis=0) - member
    place = member[:, :, None] * (
        slots[:, :, None] == jnp.arange(capacity, dtype=jnp.float32)
    ).astype(jnp.float32)
    weighted = place * mixing[:, :, None]
    place_low = place.astype(jnp.bfloat16)
    x_four = tokens.reshape(tok_dev, halves, pieces, sub_width)
    g_four = grad_out.reshape(tok_dev, halves, pieces, sub_width)
    x_parts = []
    g_parts = []
    for half in range(halves):
        x_parts.append(
            jnp.einsum(
                "Tec,Tjr->ejcr", place_low, x_four[:, half], preferred_element_type=jnp.float32
            )
        )
        g_parts.append(jnp.einsum("Tec,Tjr->ejcr", weighted, g_four[:, half].astype(jnp.float32)))
    x_send = jnp.concatenate(x_parts, axis=3).astype(jnp.bfloat16).reshape(total_rows, piece_width)
    g_send = jnp.concatenate(g_parts, axis=3).astype(jnp.bfloat16).reshape(total_rows, piece_width)

    def return_parts(values):
        arrived = lax.all_to_all(values, "expert", split_axis=0, concat_axis=0, tiled=True)
        lanes = arrived.shape[1]
        return arrived.astype(jnp.float32).reshape(flight, pieces, capacity, lanes).sum(axis=1)

    def spread_rows(values):
        lanes = values.shape[2]
        copies = jnp.broadcast_to(values[:, None], (flight, pieces, capacity, lanes)).reshape(
            total_rows, lanes
        )
        return lax.all_to_all(copies, "expert", split_axis=0, concat_axis=0, tiled=True)

    def finish(term, mix):
        summed = lax.psum_scatter(term, "ffn", scatter_dimension=1, tiled=True)
        back = lax.all_to_all(summed, "expert", split_axis=0, concat_axis=0, tiled=True)
        back = back.reshape(flight, pieces, capacity, sub_width)
        joined = jnp.einsum("Tec,ejcr->Tjr", mix, back)
        return joined.reshape(tok_dev, pieces * sub_width).astype(jnp.bfloat16)

    rows = lax.all_to_all(x_send, "expert", split_axis=0, concat_axis=0, tiled=True)
    w_gate = gate_weight[0]
    w_up = up_weight[0]
    w_down = down_weight[0]
    partial_value = jnp.concatenate(
        [
            jnp.dot(rows, w_gate, preferred_element_type=jnp.float32),
            jnp.dot(rows, w_up, preferred_element_type=jnp.float32),
        ],
        axis=1,
    )
    summed = return_parts(partial_value.astype(jnp.bfloat16))
    gate = summed[:, :, :hidden_half]
    up = summed[:, :, hidden_half:]
    sig = jax.nn.sigmoid(gate)
    act = gate * sig
    hidden = (act * up).astype(jnp.bfloat16)
    h_rows = spread_rows(hidden)
    out_term = jnp.dot(h_rows, w_down, preferred_element_type=jnp.float32)
    out_tokens = finish(out_term, weighted)
    grads = lax.all_to_all(g_send, "expert", split_axis=0, concat_axis=0, tiled=True)
    grad_down = contract_rows(h_rows, grads).astype(jnp.bfloat16)
    hidden_part = contract_cols(grads, w_down).astype(jnp.bfloat16)
    grad_hidden = return_parts(hidden_part)
    pre_gate = (grad_hidden * up * sig * (1.0 + gate * (1.0 - sig))).astype(jnp.bfloat16)
    pre_up = (grad_hidden * act).astype(jnp.bfloat16)
    both = spread_rows(jnp.concatenate([pre_gate, pre_up], axis=2))
    d_gate_rows = both[:, :hidden_half]
    d_up_rows = both[:, hidden_half:]
    grad_gate = contract_rows(rows, d_gate_rows).astype(jnp.bfloat16)
    grad_up = contract_rows(rows, d_up_rows).astype(jnp.bfloat16)
    x_term = contract_cols(d_gate_rows, w_gate) + contract_cols(d_up_rows, w_up)
    grad_tokens = finish(x_term, place)
    return (out_tokens, grad_tokens, grad_gate[None], grad_up[None], grad_down[None])


def vmem(shape, dtype):
    return pltpu.VMEM(shape, dtype)


def call(kernel, out_shape, args, in_spaces=None, out_spaces=None, flops=0, traffic=0, scratch=(), limit=16):
    spaces = in_spaces or [pltpu.VMEM] * len(args)
    outs = out_spaces or [pltpu.VMEM] * len(out_shape)
    return pl.pallas_call(
        kernel,
        out_shape=tuple(out_shape),
        in_specs=[pl.BlockSpec(memory_space=space) for space in spaces],
        out_specs=tuple(pl.BlockSpec(memory_space=space) for space in outs),
        scratch_shapes=list(scratch),
        compiler_params=pltpu.CompilerParams(vmem_limit_bytes=limit * MIB),
        cost_estimate=pl.CostEstimate(flops=flops, bytes_accessed=traffic, transcendentals=0),
    )(*args)


def blocks_to_rows(scratch, blocks, put, subs):
    size = blocks[0].shape[0]
    for p, block in enumerate(blocks):
        scratch[p * size : (p + 1) * size, :] = block[...].astype(jnp.float32)
    for sub in range(subs):
        put(sub, scratch[pl.ds(sub, len(blocks) * size // subs, stride=subs), :])


def spread_lanes(scratch, sub, subs, value):
    scratch[pl.ds(sub, value.shape[0], stride=subs), :] = value


def part(ref, start, count):
    return ref.at[start : start + count, :]


def lanes_of(sub):
    return slice(sub * LANES, (sub + 1) * LANES)


def even_masks(count):
    return [*range(count // 2, count, 2), *range(2, count // 2, 2)]


def route_kernel(devices, capacity, subs, ids_in, weight_in, x_in, g_in, *refs):
    x_mine, g_mine, near, here, theirs, place_out, mix_out, scratch, ids, weight, x, g, sems = refs
    pairs = ((ids_in, ids), (weight_in, weight), (x_in, x), (g_in, g))
    copies = [pltpu.make_async_copy(src, dst, sems.at[i]) for i, (src, dst) in enumerate(pairs)]
    for copy in copies:
        copy.start()
    top, tok = ids.shape
    rows = devices * capacity
    core = lax.axis_index("ffn")
    masks = even_masks(devices)
    masks = [mask + core for mask in masks] + [mask + 1 - core for mask in masks] + [1, 0]
    order = lax.broadcasted_iota(jnp.int32, (devices, tok), 0)
    bits = jnp.zeros((devices, tok), jnp.int32)
    for p, mask in enumerate(masks):
        bits = jnp.where(order == p, mask, bits)
    expert = bits ^ lax.axis_index("expert")
    member = jnp.zeros((devices, tok), jnp.float32)
    mixing = jnp.zeros((devices, tok), jnp.float32)
    copies[0].wait()
    copies[1].wait()
    for route in range(top):
        hit = ids[route : route + 1, :] == expert
        member = jnp.where(hit, 1.0, member)
        mixing = jnp.where(hit, weight[route : route + 1, :], mixing)
    before = lax.broadcasted_iota(jnp.int32, (tok, tok), 0) < lax.broadcasted_iota(jnp.int32, (tok, tok), 1)
    slots = dot(member.astype(jnp.bfloat16), jnp.where(before, 1.0, 0.0).astype(jnp.bfloat16))
    target = jnp.where(member > 0, slots + capacity * order.astype(jnp.float32), -1.0)
    row = lax.broadcasted_iota(jnp.int32, (rows, tok), 0).astype(jnp.float32)
    place = jnp.zeros((rows, tok), jnp.float32)
    mix = jnp.zeros((rows, tok), jnp.float32)
    for p in range(devices):
        equal = target[p : p + 1, :] == row
        place = jnp.where(equal, 1.0, place)
        mix = jnp.where(equal, mixing[p : p + 1, :], mix)
    row_weight = jnp.broadcast_to(jnp.sum(mix, axis=1, keepdims=True), (rows, LANES))
    low = place.astype(jnp.bfloat16)
    place_out[...] = low
    mix_out[...] = row_weight
    size = capacity * subs
    count = devices // 2 - 1

    def write(mine, at):
        def block(p):
            return scratch[p * size : (p + 1) * size, :].astype(theirs.dtype)

        for j in range(count):
            part(mine, j * size, size)[...] = block(j)
            part(theirs, (at + j) * size, size)[...] = block(count + j)
        start = size if at else 0
        part(near, start, size)[...] = block(2 * count)
        part(here, start, size)[...] = block(2 * count + 1)

    copies[2].wait()
    for sub in range(subs):
        spread_lanes(scratch, sub, subs, dot(low, x[:, lanes_of(sub)]))
    write(x_mine, 0)
    copies[3].wait()
    for sub in range(subs):
        spread_lanes(scratch, sub, subs, dot(low, g[:, lanes_of(sub)]) * row_weight)
    write(g_mine, count)


def pack_kernel(size, late, x_mine, g_mine, swapped, *outs):
    count = len(outs) - len(late)

    def put(out, at, mine, j, i):
        part(out, at, size)[...] = part(mine, j * size, size)[...]
        part(out, at + size, size)[...] = part(swapped, i * size, size)[...]

    for j, out in enumerate(outs[:count]):
        put(out, 0, x_mine, j, j)
        if j not in late:
            put(out, 2 * size, g_mine, j, count + j)
    for j, out in zip(late, outs[count:]):
        put(out, 0, g_mine, j, count + j)


def gather_kernel(size, at, *refs):
    blocks, (near, here, _, out) = refs[:-4], refs[-4:]
    for j, block in enumerate(blocks):
        start = block.shape[0] - 2 * size if at else 0
        part(out, 2 * j * size, 2 * size)[...] = part(block, start, 2 * size)[...]
    part(out, 2 * len(blocks) * size, size)[...] = part(near, at, size)[...]
    part(out, (2 * len(blocks) + 1) * size, size)[...] = part(here, at, size)[...]


def full_rows(devices, subs, scratch, own_sent, other_sent, out):
    size = own_sent.shape[0] // devices
    count = devices // 2 - 1
    own, other = half_starts(out.shape[1] // 2)
    first, second, last = range(0, 2 * count, 2), range(1, 2 * count, 2), range(2 * count, devices)
    layouts = (
        (own, [(own_sent, i) for i in first] + [(other_sent, i) for i in second] + [(own_sent, i) for i in last]),
        (other, [(own_sent, i) for i in second] + [(other_sent, i) for i in first] + [(other_sent, i) for i in last]),
    )
    for start, layout in layouts:

        def put(sub, value):
            out[:, pl.ds(start + sub * LANES, LANES)] = value.astype(out.dtype)

        blocks_to_rows(scratch, [part(ref, i * size, size) for ref, i in layout], put, subs)


def split_terms(count, size, scratch, own_half, keep, send):
    keep[0 : count * size, :] = scratch[0 : count * size, :]
    send[0 : count * size, :] = scratch[count * size : 2 * count * size, :].astype(send.dtype)
    rest = scratch[2 * count * size :, :]
    if own_half:
        keep[count * size :, :] = rest
    else:
        send[count * size :, :] = rest.astype(send.dtype)


def leave_kernel(size, *refs):
    terms, outs = (refs[:4], refs[4:8]), refs[8:]
    count = len(outs) - 2
    for at, (keep_own, keep_other, came_own, came_other) in zip((0, size), terms):

        def own(p):
            total = part(keep_own, p * size, size)[...] + part(came_own, p * size, size)[...].astype(jnp.float32)
            return total.astype(outs[0].dtype)

        for j, out in enumerate(outs[:count]):
            part(out, at, size)[...] = own(j)
            total = part(keep_other, j * size, size)[...] + part(came_other, j * size, size)[...].astype(jnp.float32)
            part(out, 2 * size + at, size)[...] = total.astype(out.dtype)
        part(outs[count], at, size)[...] = own(count)
        part(outs[count + 1], at, size)[...] = own(count + 1)


def share_kernel(size, *refs):
    blocks, (_, _, out) = refs[:-3], refs[-3:]
    for j, block in enumerate(blocks):
        part(out, 2 * j * size, 2 * size)[...] = part(block, 2 * size, 2 * size)[...]


def join_kernel(count, subs, place, mix, *refs):
    blocks, (near, here, shared, out_tokens, grad_tokens, scratch) = refs[:count], refs[count:]
    size = near.shape[0] // 2

    def layout(at):
        first = [part(block, at, size) for block in blocks]
        second = [part(shared, 2 * j * size + at, size) for j in range(count)]
        return first + second + [part(near, at, size), part(here, at, size)]

    def put_out(sub, value):
        low = (value * mix[...]).astype(jnp.bfloat16)
        out_tokens[:, lanes_of(sub)] = contract_rows(place[...], low).astype(out_tokens.dtype)

    def put_grad(sub, value):
        grad_tokens[:, lanes_of(sub)] = contract_rows(place[...], value.astype(jnp.bfloat16)).astype(grad_tokens.dtype)

    blocks_to_rows(scratch, layout(0), put_out, subs)
    blocks_to_rows(scratch, layout(size), put_grad, subs)


def half_starts(half_width):
    half = lax.axis_index("ffn")
    own = pl.multiple_of(half * half_width, half_width)
    other = pl.multiple_of((1 - half) * half_width, half_width)
    return own, other


def chunk(i, step, base=0):
    return pl.ds(base + pl.multiple_of(i * step, step), step)


def dot(left, right):
    return jnp.dot(left, right, preferred_element_type=jnp.float32)


def halves_of_output(devices, subs, step, scratch, own_half, term, keep, send):
    size = scratch.shape[0] // devices
    for at in range(0, subs * LANES, step):
        value = term(at)
        for i in range(step // LANES):
            spread_lanes(scratch, at // LANES + i, subs, value[:, lanes_of(i)])
    split_terms(devices // 2 - 1, size, scratch, own_half, keep, send)


def forward_kernel(devices, subs, step, x_sent, x_swapped, w_gate, w_up, x_full, gate, up, hidden, scratch):
    full_rows(devices, subs, scratch, x_sent, x_swapped, x_full)
    for cols in pieces_of(gate.shape[1], step):
        gate_low = dot(x_full[...], w_gate[0, :, cols]).astype(jnp.bfloat16)
        up_low = dot(x_full[...], w_up[0, :, cols]).astype(jnp.bfloat16)
        gate[:, cols] = gate_low
        up[:, cols] = up_low
        value = gate_low.astype(jnp.float32)
        hidden[:, cols] = (value * jax.nn.sigmoid(value) * up_low.astype(jnp.float32)).astype(jnp.bfloat16)


def output_kernel(devices, subs, step, hidden, w_down, keep_own, keep_other, send_own, send_other, scratch):
    own, other = half_starts(subs * LANES)

    def term(start):
        return lambda at: dot(hidden[...], w_down[0, :, pl.ds(start + at, step)])

    halves_of_output(devices, subs, step, scratch, False, term(other), keep_other, send_other)
    halves_of_output(devices, subs, step, scratch, True, term(own), keep_own, send_own)


def input_term(step, pre_gate, pre_up, w_gate, w_up, start):
    def term(at):
        there = pl.ds(start + at, step)
        return contract_cols(pre_gate[...], w_gate[0, there, :]) + contract_cols(pre_up[...], w_up[0, there, :])

    return term


def backward_kernel(
    devices,
    subs,
    step,
    g_sent,
    g_swapped,
    gate,
    up,
    w_gate,
    w_up,
    w_down,
    g_full,
    pre_gate,
    pre_up,
    keep_other,
    send_other,
    scratch,
):
    _, other = half_starts(subs * LANES)
    full_rows(devices, subs, scratch, g_sent, g_swapped, g_full)

    def pull(i, carry):
        cols = chunk(i, step)
        low = contract_cols(g_full[...], w_down[0, cols, :]).astype(jnp.bfloat16)
        grad_hidden = low.astype(jnp.float32)
        value = gate[:, cols].astype(jnp.float32)
        sig = jax.nn.sigmoid(value)
        pre_gate[:, cols] = (
            grad_hidden * up[:, cols].astype(jnp.float32) * sig * (1.0 + value * (1.0 - sig))
        ).astype(jnp.bfloat16)
        pre_up[:, cols] = (grad_hidden * value * sig).astype(jnp.bfloat16)
        return carry

    lax.fori_loop(0, gate.shape[1] // step, pull, 0)
    term = input_term(step, pre_gate, pre_up, w_gate, w_up, other)
    halves_of_output(devices, subs, step, scratch, False, term, keep_other, send_other)


def backward_own_kernel(devices, subs, step, pre_gate, pre_up, w_gate, w_up, keep_own, send_own, scratch):
    own, _ = half_starts(subs * LANES)
    term = input_term(step, pre_gate, pre_up, w_gate, w_up, own)
    halves_of_output(devices, subs, step, scratch, True, term, keep_own, send_own)


def flip(value):
    return value.astype(jnp.float32).T


def pieces_of(total, size):
    return [slice(at, min(at + size, total)) for at in range(0, total, size)]


def gradient_kernel(
    step,
    x,
    g,
    hidden,
    pre_gate,
    pre_up,
    grad_gate,
    grad_up,
    grad_down,
    written,
    flipped,
    turned,
    tall,
    wide,
    tall_sems,
    wide_sems,
):
    written[...] = jnp.zeros_like(written)
    width, lanes = x.shape[1], hidden.shape[1]
    count = width // step
    flipped[...] = flip(hidden[...]).astype(flipped.dtype)

    def wide_copy(i, slot):
        return pltpu.make_async_copy(wide.at[slot], grad_down.at[0, :, chunk(i, step)], wide_sems.at[slot])

    def tall_copy(which, out, i, slot):
        return pltpu.make_async_copy(tall.at[which, slot], out.at[0, chunk(i, step), :], tall_sems.at[which, slot])

    def down(i, carry):
        slot = i % 2

        @pl.when(i >= 2)
        def _():
            wide_copy(i - 2, slot).wait()

        for cut in pieces_of(step, 256):
            right = g[:, chunk(i, step)][:, cut]
            for high in pieces_of(lanes, 256):
                wide[slot, high, cut] = dot(flipped[high, :], right).astype(wide.dtype)
        wide_copy(i, slot).start()
        return carry

    lax.fori_loop(0, count, down, 0)

    def inputs(i, carry):
        slot = i % 2
        turned[...] = flip(x[:, chunk(i, step)]).astype(turned.dtype)
        for which, (right, out) in enumerate(((pre_gate, grad_gate), (pre_up, grad_up))):

            @pl.when(i >= 2)
            def _():
                tall_copy(which, out, i - 2, slot).wait()

            for cut in pieces_of(lanes, 256):
                for high in pieces_of(step, 256):
                    tall[which, slot, high, cut] = dot(turned[high, :], right[:, cut]).astype(tall.dtype)
            tall_copy(which, out, i, slot).start()
        return carry

    lax.fori_loop(0, count, inputs, 0)
    for i in range(max(0, count - 2), count):
        wide_copy(i, i % 2).wait()
        tall_copy(0, grad_gate, i, i % 2).wait()
        tall_copy(1, grad_up, i, i % 2).wait()


def exchange(blocks, masks, devices):
    arrived = []
    for block, mask in zip(blocks, masks):
        pairs = [(2 * i + core, 2 * (i ^ (mask + core)) + core) for i in range(devices) for core in range(2)]
        arrived.append(lax.ppermute(block, ("expert", "ffn"), pairs))
    return arrived


def exchange_near(block, devices):
    return lax.ppermute(block, "expert", [(i, i ^ 1) for i in range(devices)])


def swap(value):
    return lax.ppermute(value, "ffn", [(0, 1), (1, 0)])


def in_hbm(values):
    return [pltpu.with_memory_space_constraint(value, pltpu.HBM) for value in values]


def one_piece_shards(tokens, grad_out, route_ids, route_weight, gate_weight, up_weight, down_weight):
    tok_dev, sub_width = tokens.shape
    top_count = route_ids.shape[1]
    width, lanes = gate_weight.shape[1:]
    devices = lax.axis_size("expert")
    capacity = max(2, min(tok_dev, (9 * tok_dev * top_count + 8 * EXPERTS - 1) // (8 * EXPERTS)))
    rows = devices * capacity
    subs = sub_width // LANES
    low, full = jnp.bfloat16, jnp.float32
    size = capacity * subs
    count = devices // 2 - 1
    spread_scratch = [pltpu.VMEM((devices * size, LANES), full)]
    step = 256
    half_flops = 2 * rows * width * lanes // 2

    def lines(number, dtype=low):
        return jax.ShapeDtypeStruct((number * size, LANES), dtype)

    def lines_in_vmem(number, dtype=low):
        return vmem((number * size, LANES), dtype)

    sources = (route_ids.T, route_weight.T, tokens, grad_out)
    x_mine, g_mine, near, here, theirs, place, mix = call(
        functools.partial(route_kernel, devices, capacity, subs),
        [lines(count), lines(count), lines(2), lines(2)]
        + [lines(2 * count), jax.ShapeDtypeStruct((rows, tok_dev), low), jax.ShapeDtypeStruct((rows, LANES), full)],
        in_hbm(sources),
        in_spaces=[pl.ANY] * 4,
        scratch=spread_scratch
        + [pltpu.VMEM(value.shape, value.dtype) for value in sources]
        + [pltpu.SemaphoreType.DMA((4,))],
        traffic=4 * tok_dev * sub_width,
    )
    masks = even_masks(devices)
    late = list(range(devices // 8, devices // 4))
    packed = call(
        functools.partial(pack_kernel, size, late),
        [lines(2 if j in late else 4) for j in range(count)] + [lines(2)] * len(late),
        (x_mine, g_mine, swap(theirs)),
        flops=24 * half_flops,
    )
    x_arrived = exchange(packed[:count], masks, devices)
    near = exchange_near(near, devices)
    g_arrived = list(x_arrived)
    g_arrived[late[0] : late[-1] + 1] = exchange(packed[count:], [masks[j] for j in late], devices)

    weights = (gate_weight, up_weight, down_weight)
    w_gate, w_up, w_down = [pltpu.with_memory_space_constraint(w, pltpu.VMEM) for w in weights]

    def gather(arrived, at, after):
        kernel = functools.partial(gather_kernel, size, at)
        return call(kernel, [lines(devices)], (*arrived, near, here, after))[0]

    x_sent = gather(x_arrived, 0, mix)
    x_swapped = swap(x_sent)
    terms = [
        lines_in_vmem(count + 2, full),
        lines_in_vmem(count, full),
        lines_in_vmem(count),
        lines_in_vmem(count + 2),
    ]
    x_full, gate, up, hidden = call(
        functools.partial(forward_kernel, devices, subs, step),
        [vmem((rows, width), low)] + [vmem((rows, lanes), low)] * 3,
        (x_sent, x_swapped, w_gate, w_up),
        scratch=spread_scratch,
        flops=4 * half_flops,
    )
    g_sent = gather(g_arrived, size, hidden)
    g_swapped = swap(g_sent)
    out_own, out_other, send_own, send_other = call(
        functools.partial(output_kernel, devices, subs, step),
        terms,
        (hidden, w_down),
        scratch=spread_scratch,
        flops=2 * half_flops,
    )
    out_terms = (out_own, out_other, swap(send_other), swap(send_own))
    g_full, pre_gate, pre_up, dx_other, send_other = call(
        functools.partial(backward_kernel, devices, subs, step),
        [vmem((rows, width), low)] + [vmem((rows, lanes), low)] * 2 + [terms[1], terms[3]],
        (g_sent, g_swapped, gate, up, w_gate, w_up, w_down),
        scratch=spread_scratch,
        flops=4 * half_flops,
    )
    came_own = swap(send_other)
    dx_own, send_own = call(
        functools.partial(backward_own_kernel, devices, subs, step),
        [terms[0], terms[2]],
        (pre_gate, pre_up, w_gate, w_up),
        scratch=spread_scratch,
        flops=2 * half_flops,
    )
    dx_terms = (dx_own, dx_other, came_own, swap(send_own))
    *leaving, back, kept = call(
        functools.partial(leave_kernel, size),
        [lines(4)] * count + [lines(2)] * 2,
        (*out_terms, *dx_terms),
    )
    returned = exchange(leaving, masks, devices)
    back = exchange_near(back, devices)
    cut = 1024 if width % 1024 == 0 else width
    grad_gate, grad_up, grad_down, written = call(
        functools.partial(gradient_kernel, cut),
        [jax.ShapeDtypeStruct(w.shape, low) for w in weights] + [vmem((8, LANES), full)],
        (x_full, g_full, hidden, pre_gate, pre_up),
        out_spaces=[pl.ANY] * 3 + [pltpu.VMEM],
        scratch=[
            pltpu.VMEM((lanes, rows), low),
            pltpu.VMEM((cut, rows), low),
            pltpu.VMEM((2, 2, cut, lanes), low),
            pltpu.VMEM((2, lanes, cut), low),
            pltpu.SemaphoreType.DMA((2, 2)),
            pltpu.SemaphoreType.DMA((2,)),
        ],
        flops=6 * half_flops,
        traffic=sum(w.size * 2 for w in weights),
        limit=32,
    )
    (sharing,) = call(functools.partial(share_kernel, size), [lines(2 * count)], (*returned, back, written))
    out_tokens, grad_tokens = call(
        functools.partial(join_kernel, count, subs),
        [jax.ShapeDtypeStruct((tok_dev, sub_width), low)] * 2,
        (place, mix, *returned, back, kept, swap(sharing)),
        scratch=spread_scratch,
        traffic=8 * tok_dev * sub_width,
    )
    return out_tokens, grad_tokens, grad_gate, grad_up, grad_down


def shards(*args):
    tokens, gate_weight = args[0], args[4]
    halves = lax.axis_size("ffn")
    devices = lax.axis_size("expert")
    if halves == 2 and devices >= 4 and devices & (devices - 1) == 0 and tokens.shape[1] * halves == gate_weight.shape[1]:
        return one_piece_shards(*args)
    return general_shards(*args)


def solution(mesh):
    in_specs = (
        P(("groups", "expert"), "ffn"),
        P(("groups", "expert"), "ffn"),
        P(("groups", "expert"), None),
        P(("groups", "expert"), None),
        P("expert", None, "ffn"),
        P("expert", None, "ffn"),
        P("expert", "ffn", None),
    )
    out_specs = (
        P(("groups", "expert"), "ffn"),
        P(("groups", "expert"), "ffn"),
        P(("groups", "expert"), None, "ffn"),
        P(("groups", "expert"), None, "ffn"),
        P(("groups", "expert"), "ffn", None),
    )
    return jax.shard_map(shards, mesh=mesh, in_specs=in_specs, out_specs=out_specs, check_vma=False)
```

```python
import functools

import jax
import jax.numpy as jnp
from jax import lax
from jax.experimental import pallas as pl
from jax.experimental.pallas import tpu as pltpu
from jax.sharding import PartitionSpec as P

EXPERTS = 128
LANES = 128
MIB = 1024 * 1024


def contract_rows(left, right):
    return lax.dot_general(
        left, right, (((0,), (0,)), ((), ())), preferred_element_type=jnp.float32
    )


def contract_cols(left, right):
    return lax.dot_general(
        left, right, (((1,), (1,)), ((), ())), preferred_element_type=jnp.float32
    )


def general_shards(tokens, grad_out, route_ids, route_weight, gate_weight, up_weight, down_weight):
    tokens, grad_out = (
        lax.all_gather(tokens, "ffn", axis=1, tiled=True),
        lax.all_gather(grad_out, "ffn", axis=1, tiled=True),
    )
    tok_dev, width = tokens.shape
    top_count = route_ids.shape[1]
    piece_width = gate_weight.shape[1]
    hidden_half = gate_weight.shape[2]
    pieces = width // piece_width
    devices = lax.axis_size("expert")
    flight = devices // pieces
    halves = lax.axis_size("ffn")
    sub_width = piece_width // halves
    capacity = max(2, min(tok_dev, (9 * tok_dev * top_count + 8 * EXPERTS - 1) // (8 * EXPERTS)))
    total_rows = devices * capacity
    expert_ids = jnp.arange(flight, dtype=jnp.int32)
    member = jnp.zeros((tok_dev, flight), jnp.float32)
    mixing = jnp.zeros((tok_dev, flight), jnp.float32)
    for route in range(top_count):
        hit = (route_ids[:, route : route + 1] == expert_ids[None, :]).astype(jnp.float32)
        member = member + hit
        mixing = mixing + hit * route_weight[:, route : route + 1]
    slots = jnp.cumsum(member, axis=0) - member
    place = member[:, :, None] * (
        slots[:, :, None] == jnp.arange(capacity, dtype=jnp.float32)
    ).astype(jnp.float32)
    weighted = place * mixing[:, :, None]
    place_low = place.astype(jnp.bfloat16)
    x_four = tokens.reshape(tok_dev, halves, pieces, sub_width)
    g_four = grad_out.reshape(tok_dev, halves, pieces, sub_width)
    x_parts = []
    g_parts = []
    for half in range(halves):
        x_parts.append(
            jnp.einsum(
                "Tec,Tjr->ejcr", place_low, x_four[:, half], preferred_element_type=jnp.float32
            )
        )
        g_parts.append(jnp.einsum("Tec,Tjr->ejcr", weighted, g_four[:, half].astype(jnp.float32)))
    x_send = jnp.concatenate(x_parts, axis=3).astype(jnp.bfloat16).reshape(total_rows, piece_width)
    g_send = jnp.concatenate(g_parts, axis=3).astype(jnp.bfloat16).reshape(total_rows, piece_width)

    def return_parts(values):
        arrived = lax.all_to_all(values, "expert", split_axis=0, concat_axis=0, tiled=True)
        lanes = arrived.shape[1]
        return arrived.astype(jnp.float32).reshape(flight, pieces, capacity, lanes).sum(axis=1)

    def spread_rows(values):
        lanes = values.shape[2]
        copies = jnp.broadcast_to(values[:, None], (flight, pieces, capacity, lanes)).reshape(
            total_rows, lanes
        )
        return lax.all_to_all(copies, "expert", split_axis=0, concat_axis=0, tiled=True)

    def finish(term, mix):
        summed = lax.psum_scatter(term, "ffn", scatter_dimension=1, tiled=True)
        back = lax.all_to_all(summed, "expert", split_axis=0, concat_axis=0, tiled=True)
        back = back.reshape(flight, pieces, capacity, sub_width)
        joined = jnp.einsum("Tec,ejcr->Tjr", mix, back)
        return joined.reshape(tok_dev, pieces * sub_width).astype(jnp.bfloat16)

    rows = lax.all_to_all(x_send, "expert", split_axis=0, concat_axis=0, tiled=True)
    w_gate = gate_weight[0]
    w_up = up_weight[0]
    w_down = down_weight[0]
    partial_value = jnp.concatenate(
        [
            jnp.dot(rows, w_gate, preferred_element_type=jnp.float32),
            jnp.dot(rows, w_up, preferred_element_type=jnp.float32),
        ],
        axis=1,
    )
    summed = return_parts(partial_value.astype(jnp.bfloat16))
    gate = summed[:, :, :hidden_half]
    up = summed[:, :, hidden_half:]
    sig = jax.nn.sigmoid(gate)
    act = gate * sig
    hidden = (act * up).astype(jnp.bfloat16)
    h_rows = spread_rows(hidden)
    out_term = jnp.dot(h_rows, w_down, preferred_element_type=jnp.float32)
    out_tokens = finish(out_term, weighted)
    grads = lax.all_to_all(g_send, "expert", split_axis=0, concat_axis=0, tiled=True)
    grad_down = contract_rows(h_rows, grads).astype(jnp.bfloat16)
    hidden_part = contract_cols(grads, w_down).astype(jnp.bfloat16)
    grad_hidden = return_parts(hidden_part)
    pre_gate = (grad_hidden * up * sig * (1.0 + gate * (1.0 - sig))).astype(jnp.bfloat16)
    pre_up = (grad_hidden * act).astype(jnp.bfloat16)
    both = spread_rows(jnp.concatenate([pre_gate, pre_up], axis=2))
    d_gate_rows = both[:, :hidden_half]
    d_up_rows = both[:, hidden_half:]
    grad_gate = contract_rows(rows, d_gate_rows).astype(jnp.bfloat16)
    grad_up = contract_rows(rows, d_up_rows).astype(jnp.bfloat16)
    x_term = contract_cols(d_gate_rows, w_gate) + contract_cols(d_up_rows, w_up)
    grad_tokens = finish(x_term, place)
    return (out_tokens, grad_tokens, grad_gate[None], grad_up[None], grad_down[None])


def vmem(shape, dtype):
    return pltpu.VMEM(shape, dtype)


def call(kernel, out_shape, args, in_spaces=None, out_spaces=None, flops=0, traffic=0, scratch=(), limit=16):
    spaces = in_spaces or [pltpu.VMEM] * len(args)
    outs = out_spaces or [pltpu.VMEM] * len(out_shape)
    return pl.pallas_call(
        kernel,
        out_shape=tuple(out_shape),
        in_specs=[pl.BlockSpec(memory_space=space) for space in spaces],
        out_specs=tuple(pl.BlockSpec(memory_space=space) for space in outs),
        scratch_shapes=list(scratch),
        compiler_params=pltpu.CompilerParams(vmem_limit_bytes=limit * MIB),
        cost_estimate=pl.CostEstimate(flops=flops, bytes_accessed=traffic, transcendentals=0),
    )(*args)


def blocks_to_rows(scratch, blocks, put, subs):
    size = blocks[0].shape[0]
    for p, block in enumerate(blocks):
        scratch[p * size : (p + 1) * size, :] = block[...].astype(jnp.float32)
    for sub in range(subs):
        put(sub, scratch[pl.ds(sub, len(blocks) * size // subs, stride=subs), :])


def spread_lanes(scratch, sub, subs, value):
    scratch[pl.ds(sub, value.shape[0], stride=subs), :] = value


def part(ref, start, count):
    return ref.at[start : start + count, :]


def lanes_of(sub):
    return slice(sub * LANES, (sub + 1) * LANES)


def even_masks(count):
    return [*range(count // 2, count, 2), *range(2, count // 2, 2)]


def route_kernel(devices, capacity, subs, ids_in, weight_in, x_in, g_in, *refs):
    x_mine, g_mine, near, here, theirs, place_out, mix_out, scratch, ids, weight, x, g, sems = refs
    pairs = ((ids_in, ids), (weight_in, weight), (x_in, x), (g_in, g))
    copies = [pltpu.make_async_copy(src, dst, sems.at[i]) for i, (src, dst) in enumerate(pairs)]
    for copy in copies:
        copy.start()
    top, tok = ids.shape
    rows = devices * capacity
    core = lax.axis_index("ffn")
    masks = even_masks(devices)
    masks = [mask + core for mask in masks] + [mask + 1 - core for mask in masks] + [1, 0]
    order = lax.broadcasted_iota(jnp.int32, (devices, tok), 0)
    bits = jnp.zeros((devices, tok), jnp.int32)
    for p, mask in enumerate(masks):
        bits = jnp.where(order == p, mask, bits)
    expert = bits ^ lax.axis_index("expert")
    member = jnp.zeros((devices, tok), jnp.float32)
    mixing = jnp.zeros((devices, tok), jnp.float32)
    copies[0].wait()
    copies[1].wait()
    for route in range(top):
        hit = ids[route : route + 1, :] == expert
        member = jnp.where(hit, 1.0, member)
        mixing = jnp.where(hit, weight[route : route + 1, :], mixing)
    before = lax.broadcasted_iota(jnp.int32, (tok, tok), 0) < lax.broadcasted_iota(jnp.int32, (tok, tok), 1)
    slots = dot(member.astype(jnp.bfloat16), jnp.where(before, 1.0, 0.0).astype(jnp.bfloat16))
    target = jnp.where(member > 0, slots + capacity * order.astype(jnp.float32), -1.0)
    row = lax.broadcasted_iota(jnp.int32, (rows, tok), 0).astype(jnp.float32)
    place = jnp.zeros((rows, tok), jnp.float32)
    mix = jnp.zeros((rows, tok), jnp.float32)
    for p in range(devices):
        equal = target[p : p + 1, :] == row
        place = jnp.where(equal, 1.0, place)
        mix = jnp.where(equal, mixing[p : p + 1, :], mix)
    row_weight = jnp.broadcast_to(jnp.sum(mix, axis=1, keepdims=True), (rows, LANES))
    low = place.astype(jnp.bfloat16)
    place_out[...] = low
    mix_out[...] = row_weight
    size = capacity * subs
    count = devices // 2 - 1

    def write(mine, at):
        def block(p):
            return scratch[p * size : (p + 1) * size, :].astype(theirs.dtype)

        for j in range(count):
            part(mine, j * size, size)[...] = block(j)
            part(theirs, (at + j) * size, size)[...] = block(count + j)
        start = size if at else 0
        part(near, start, size)[...] = block(2 * count)
        part(here, start, size)[...] = block(2 * count + 1)

    copies[2].wait()
    for sub in range(subs):
        spread_lanes(scratch, sub, subs, dot(low, x[:, lanes_of(sub)]))
    write(x_mine, 0)
    copies[3].wait()
    for sub in range(subs):
        spread_lanes(scratch, sub, subs, dot(low, g[:, lanes_of(sub)]) * row_weight)
    write(g_mine, count)


def pack_kernel(size, late, x_mine, g_mine, swapped, *outs):
    count = len(outs) - len(late)

    def put(out, at, mine, j, i):
        part(out, at, size)[...] = part(mine, j * size, size)[...]
        part(out, at + size, size)[...] = part(swapped, i * size, size)[...]

    for j, out in enumerate(outs[:count]):
        put(out, 0, x_mine, j, j)
        if j not in late:
            put(out, 2 * size, g_mine, j, count + j)
    for j, out in zip(late, outs[count:]):
        put(out, 0, g_mine, j, count + j)


def gather_kernel(size, at, *refs):
    blocks, (near, here, _, out) = refs[:-4], refs[-4:]
    for j, block in enumerate(blocks):
        start = block.shape[0] - 2 * size if at else 0
        part(out, 2 * j * size, 2 * size)[...] = part(block, start, 2 * size)[...]
    part(out, 2 * len(blocks) * size, size)[...] = part(near, at, size)[...]
    part(out, (2 * len(blocks) + 1) * size, size)[...] = part(here, at, size)[...]


def full_rows(devices, subs, scratch, own_sent, other_sent, out):
    size = own_sent.shape[0] // devices
    count = devices // 2 - 1
    own, other = half_starts(out.shape[1] // 2)
    first, second, last = range(0, 2 * count, 2), range(1, 2 * count, 2), range(2 * count, devices)
    layouts = (
        (own, [(own_sent, i) for i in first] + [(other_sent, i) for i in second] + [(own_sent, i) for i in last]),
        (other, [(own_sent, i) for i in second] + [(other_sent, i) for i in first] + [(other_sent, i) for i in last]),
    )
    for start, layout in layouts:

        def put(sub, value):
            out[:, pl.ds(start + sub * LANES, LANES)] = value.astype(out.dtype)

        blocks_to_rows(scratch, [part(ref, i * size, size) for ref, i in layout], put, subs)


def split_terms(count, size, scratch, own_half, keep, send):
    keep[0 : count * size, :] = scratch[0 : count * size, :]
    send[0 : count * size, :] = scratch[count * size : 2 * count * size, :].astype(send.dtype)
    rest = scratch[2 * count * size :, :]
    if own_half:
        keep[count * size :, :] = rest
    else:
        send[count * size :, :] = rest.astype(send.dtype)


def leave_kernel(size, *refs):
    terms, outs = (refs[:4], refs[4:8]), refs[8:]
    count = len(outs) - 2
    for at, (keep_own, keep_other, came_own, came_other) in zip((0, size), terms):

        def own(p):
            total = part(keep_own, p * size, size)[...] + part(came_own, p * size, size)[...].astype(jnp.float32)
            return total.astype(outs[0].dtype)

        for j, out in enumerate(outs[:count]):
            part(out, at, size)[...] = own(j)
            total = part(keep_other, j * size, size)[...] + part(came_other, j * size, size)[...].astype(jnp.float32)
            part(out, 2 * size + at, size)[...] = total.astype(out.dtype)
        part(outs[count], at, size)[...] = own(count)
        part(outs[count + 1], at, size)[...] = own(count + 1)


def share_kernel(size, *refs):
    blocks, (_, _, out) = refs[:-3], refs[-3:]
    for j, block in enumerate(blocks):
        part(out, 2 * j * size, 2 * size)[...] = part(block, 2 * size, 2 * size)[...]


def join_kernel(count, subs, place, mix, *refs):
    blocks, (near, here, shared, out_tokens, grad_tokens, scratch) = refs[:count], refs[count:]
    size = near.shape[0] // 2

    def layout(at):
        first = [part(block, at, size) for block in blocks]
        second = [part(shared, 2 * j * size + at, size) for j in range(count)]
        return first + second + [part(near, at, size), part(here, at, size)]

    def put_out(sub, value):
        low = (value * mix[...]).astype(jnp.bfloat16)
        out_tokens[:, lanes_of(sub)] = contract_rows(place[...], low).astype(out_tokens.dtype)

    def put_grad(sub, value):
        grad_tokens[:, lanes_of(sub)] = contract_rows(place[...], value.astype(jnp.bfloat16)).astype(grad_tokens.dtype)

    blocks_to_rows(scratch, layout(0), put_out, subs)
    blocks_to_rows(scratch, layout(size), put_grad, subs)


def half_starts(half_width):
    half = lax.axis_index("ffn")
    own = pl.multiple_of(half * half_width, half_width)
    other = pl.multiple_of((1 - half) * half_width, half_width)
    return own, other


def chunk(i, step, base=0):
    return pl.ds(base + pl.multiple_of(i * step, step), step)


def dot(left, right):
    return jnp.dot(left, right, preferred_element_type=jnp.float32)


def halves_of_output(devices, subs, step, scratch, own_half, term, keep, send):
    size = scratch.shape[0] // devices
    for at in range(0, subs * LANES, step):
        value = term(at)
        for i in range(step // LANES):
            spread_lanes(scratch, at // LANES + i, subs, value[:, lanes_of(i)])
    split_terms(devices // 2 - 1, size, scratch, own_half, keep, send)


def forward_kernel(devices, subs, step, x_sent, x_swapped, w_gate, w_up, x_full, gate, up, hidden, scratch):
    full_rows(devices, subs, scratch, x_sent, x_swapped, x_full)
    for cols in pieces_of(gate.shape[1], 768):
        gate_low = dot(x_full[...], w_gate[0, :, cols]).astype(jnp.bfloat16)
        up_low = dot(x_full[...], w_up[0, :, cols]).astype(jnp.bfloat16)
        gate[:, cols] = gate_low
        up[:, cols] = up_low
        value = gate_low.astype(jnp.float32)
        hidden[:, cols] = (value * jax.nn.sigmoid(value) * up_low.astype(jnp.float32)).astype(jnp.bfloat16)


def output_kernel(devices, subs, step, hidden, w_down, keep_own, keep_other, send_own, send_other, scratch):
    own, other = half_starts(subs * LANES)

    def term(start):
        return lambda at: dot(hidden[...], w_down[0, :, pl.ds(start + at, step)])

    halves_of_output(devices, subs, step, scratch, False, term(other), keep_other, send_other)
    halves_of_output(devices, subs, step, scratch, True, term(own), keep_own, send_own)


def input_term(step, pre_gate, pre_up, w_gate, w_up, start):
    def term(at):
        there = pl.ds(start + at, step)
        return contract_cols(pre_gate[...], w_gate[0, there, :]) + contract_cols(pre_up[...], w_up[0, there, :])

    return term


def backward_kernel(
    devices,
    subs,
    step,
    g_sent,
    g_swapped,
    gate,
    up,
    w_gate,
    w_up,
    w_down,
    g_full,
    pre_gate,
    pre_up,
    keep_other,
    send_other,
    scratch,
):
    _, other = half_starts(subs * LANES)
    full_rows(devices, subs, scratch, g_sent, g_swapped, g_full)

    for cols in pieces_of(gate.shape[1], 768):
        low = contract_cols(g_full[...], w_down[0, cols, :]).astype(jnp.bfloat16)
        grad_hidden = low.astype(jnp.float32)
        value = gate[:, cols].astype(jnp.float32)
        sig = jax.nn.sigmoid(value)
        pre_gate[:, cols] = (
            grad_hidden * up[:, cols].astype(jnp.float32) * sig * (1.0 + value * (1.0 - sig))
        ).astype(jnp.bfloat16)
        pre_up[:, cols] = (grad_hidden * value * sig).astype(jnp.bfloat16)
    term = input_term(step, pre_gate, pre_up, w_gate, w_up, other)
    halves_of_output(devices, subs, step, scratch, False, term, keep_other, send_other)


def backward_own_kernel(devices, subs, step, pre_gate, pre_up, w_gate, w_up, keep_own, send_own, scratch):
    own, _ = half_starts(subs * LANES)
    term = input_term(step, pre_gate, pre_up, w_gate, w_up, own)
    halves_of_output(devices, subs, step, scratch, True, term, keep_own, send_own)


def flip(value):
    return value.astype(jnp.float32).T


def pieces_of(total, size):
    return [slice(at, min(at + size, total)) for at in range(0, total, size)]


def gradient_kernel(
    step,
    x,
    g,
    hidden,
    pre_gate,
    pre_up,
    grad_gate,
    grad_up,
    grad_down,
    written,
    flipped,
    turned,
    both,
    tall,
    wide,
    tall_sems,
    wide_sems,
):
    width, lanes = x.shape[1], hidden.shape[1]
    count = width // step
    written[...] = jnp.zeros_like(written)
    flipped[...] = flip(hidden[...]).astype(flipped.dtype)
    both[:, :lanes] = pre_gate[...]
    both[:, lanes:] = pre_up[...]

    def wide_copy(i):
        return pltpu.make_async_copy(wide.at[i], grad_down.at[0, :, chunk(i, step)], wide_sems.at[i])

    def tall_copy(which, i):
        out = (grad_gate, grad_up)[which]
        return pltpu.make_async_copy(tall.at[which, i], out.at[0, chunk(i, step), :], tall_sems.at[which, i])

    def down(i, carry):
        right = g[:, chunk(i, step)]
        for high in pieces_of(lanes, 128):
            wide[i, high, :] = dot(flipped[high, :], right).astype(wide.dtype)
        wide_copy(i).start()
        return carry

    lax.fori_loop(0, count, down, 0)

    def inputs(i, carry):
        turned[...] = flip(x[:, chunk(i, step)]).astype(turned.dtype)
        for cut in pieces_of(2 * lanes, 512):
            for high in pieces_of(step, 128):
                value = dot(turned[high, :], both[:, cut]).astype(tall.dtype)
                split = max(0, min(lanes, cut.stop) - cut.start)
                if split:
                    tall[0, i, high, cut.start : cut.start + split] = value[:, :split]
                if split < cut.stop - cut.start:
                    tall[1, i, high, cut.start + split - lanes : cut.stop - lanes] = value[:, split:]
        tall_copy(0, i).start()
        tall_copy(1, i).start()
        return carry

    lax.fori_loop(0, count, inputs, 0)
    for i in range(count):
        wide_copy(i).wait()
        tall_copy(0, i).wait()
        tall_copy(1, i).wait()


def exchange(blocks, masks, devices):
    arrived = []
    for block, mask in zip(blocks, masks):
        pairs = [(2 * i + core, 2 * (i ^ (mask + core)) + core) for i in range(devices) for core in range(2)]
        arrived.append(lax.ppermute(block, ("expert", "ffn"), pairs))
    return arrived


def exchange_near(block, devices):
    return lax.ppermute(block, "expert", [(i, i ^ 1) for i in range(devices)])


def swap(value):
    return lax.ppermute(value, "ffn", [(0, 1), (1, 0)])


def in_hbm(values):
    return [pltpu.with_memory_space_constraint(value, pltpu.HBM) for value in values]


def one_piece_shards(tokens, grad_out, route_ids, route_weight, gate_weight, up_weight, down_weight):
    tok_dev, sub_width = tokens.shape
    top_count = route_ids.shape[1]
    width, lanes = gate_weight.shape[1:]
    devices = lax.axis_size("expert")
    capacity = max(2, min(tok_dev, (9 * tok_dev * top_count + 8 * EXPERTS - 1) // (8 * EXPERTS)))
    rows = devices * capacity
    subs = sub_width // LANES
    low, full = jnp.bfloat16, jnp.float32
    size = capacity * subs
    count = devices // 2 - 1
    spread_scratch = [pltpu.VMEM((devices * size, LANES), full)]
    step = 512 if sub_width % 512 == 0 else LANES
    half_flops = 2 * rows * width * lanes // 2

    def lines(number, dtype=low):
        return jax.ShapeDtypeStruct((number * size, LANES), dtype)

    def lines_in_vmem(number, dtype=low):
        return vmem((number * size, LANES), dtype)

    sources = (route_ids.T, route_weight.T, tokens, grad_out)
    x_mine, g_mine, near, here, theirs, place, mix = call(
        functools.partial(route_kernel, devices, capacity, subs),
        [lines(count), lines(count), lines(2), lines(2)]
        + [lines(2 * count), jax.ShapeDtypeStruct((rows, tok_dev), low), jax.ShapeDtypeStruct((rows, LANES), full)],
        in_hbm(sources),
        in_spaces=[pl.ANY] * 4,
        scratch=spread_scratch
        + [pltpu.VMEM(value.shape, value.dtype) for value in sources]
        + [pltpu.SemaphoreType.DMA((4,))],
        traffic=4 * tok_dev * sub_width,
    )
    masks = even_masks(devices)
    late = list(range(devices // 8, devices // 4))
    packed = call(
        functools.partial(pack_kernel, size, late),
        [lines(2 if j in late else 4) for j in range(count)] + [lines(2)] * len(late),
        (x_mine, g_mine, swap(theirs)),
        flops=24 * half_flops,
    )
    x_arrived = exchange(packed[:count], masks, devices)
    near = exchange_near(near, devices)
    g_arrived = list(x_arrived)
    g_arrived[late[0] : late[-1] + 1] = exchange(packed[count:], [masks[j] for j in late], devices)

    weights = (gate_weight, up_weight, down_weight)
    w_gate, w_up, w_down = [pltpu.with_memory_space_constraint(w, pltpu.VMEM) for w in weights]

    def gather(arrived, at, after):
        kernel = functools.partial(gather_kernel, size, at)
        return call(kernel, [lines(devices)], (*arrived, near, here, after))[0]

    x_sent = gather(x_arrived, 0, mix)
    x_swapped = swap(x_sent)
    terms = [
        lines_in_vmem(count + 2, full),
        lines_in_vmem(count, full),
        lines_in_vmem(count),
        lines_in_vmem(count + 2),
    ]
    x_full, gate, up, hidden = call(
        functools.partial(forward_kernel, devices, subs, step),
        [vmem((rows, width), low)] + [vmem((rows, lanes), low)] * 3,
        (x_sent, x_swapped, w_gate, w_up),
        scratch=spread_scratch,
        flops=4 * half_flops,
    )
    g_sent = gather(g_arrived, size, hidden)
    g_swapped = swap(g_sent)
    out_own, out_other, send_own, send_other = call(
        functools.partial(output_kernel, devices, subs, step),
        terms,
        (hidden, w_down),
        scratch=spread_scratch,
        flops=2 * half_flops,
    )
    out_terms = (out_own, out_other, swap(send_other), swap(send_own))
    g_full, pre_gate, pre_up, dx_other, send_other = call(
        functools.partial(backward_kernel, devices, subs, step),
        [vmem((rows, width), low)] + [vmem((rows, lanes), low)] * 2 + [terms[1], terms[3]],
        (g_sent, g_swapped, gate, up, w_gate, w_up, w_down),
        scratch=spread_scratch,
        flops=4 * half_flops,
    )
    came_own = swap(send_other)
    dx_own, send_own = call(
        functools.partial(backward_own_kernel, devices, subs, step),
        [terms[0], terms[2]],
        (pre_gate, pre_up, w_gate, w_up),
        scratch=spread_scratch,
        flops=2 * half_flops,
    )
    dx_terms = (dx_own, dx_other, came_own, swap(send_own))
    *leaving, back, kept = call(
        functools.partial(leave_kernel, size),
        [lines(4)] * count + [lines(2)] * 2,
        (*out_terms, *dx_terms),
    )
    returned = exchange(leaving, masks, devices)
    back = exchange_near(back, devices)
    cut = 512 if width % 512 == 0 else width
    grad_gate, grad_up, grad_down, written = call(
        functools.partial(gradient_kernel, cut),
        [jax.ShapeDtypeStruct(w.shape, low) for w in weights] + [vmem((8, LANES), full)],
        (x_full, g_full, hidden, pre_gate, pre_up),
        out_spaces=[pl.ANY] * 3 + [pltpu.VMEM],
        scratch=[
            pltpu.VMEM((lanes, rows), low),
            pltpu.VMEM((cut, rows), low),
            pltpu.VMEM((rows, 2 * lanes), low),
            pltpu.VMEM((2, width // cut, cut, lanes), low),
            pltpu.VMEM((width // cut, lanes, cut), low),
            pltpu.SemaphoreType.DMA((2, width // cut)),
            pltpu.SemaphoreType.DMA((width // cut,)),
        ],
        flops=6 * half_flops,
        traffic=sum(w.size * 2 for w in weights),
        limit=40,
    )
    (sharing,) = call(functools.partial(share_kernel, size), [lines(2 * count)], (*returned, back, written))
    out_tokens, grad_tokens = call(
        functools.partial(join_kernel, count, subs),
        [jax.ShapeDtypeStruct((tok_dev, sub_width), low)] * 2,
        (place, mix, *returned, back, kept, swap(sharing)),
        scratch=spread_scratch,
        traffic=8 * tok_dev * sub_width,
    )
    return out_tokens, grad_tokens, grad_gate, grad_up, grad_down


def shards(*args):
    tokens, gate_weight = args[0], args[4]
    halves = lax.axis_size("ffn")
    devices = lax.axis_size("expert")
    if halves == 2 and devices >= 4 and devices & (devices - 1) == 0 and tokens.shape[1] * halves == gate_weight.shape[1]:
        return one_piece_shards(*args)
    return general_shards(*args)


def solution(mesh):
    in_specs = (
        P(("groups", "expert"), "ffn"),
        P(("groups", "expert"), "ffn"),
        P(("groups", "expert"), None),
        P(("groups", "expert"), None),
        P("expert", None, "ffn"),
        P("expert", None, "ffn"),
        P("expert", "ffn", None),
    )
    out_specs = (
        P(("groups", "expert"), "ffn"),
        P(("groups", "expert"), "ffn"),
        P(("groups", "expert"), None, "ffn"),
        P(("groups", "expert"), None, "ffn"),
        P(("groups", "expert"), "ffn", None),
    )
    return jax.shard_map(shards, mesh=mesh, in_specs=in_specs, out_specs=out_specs, check_vma=False)
```

```python
import functools

import jax
import jax.numpy as jnp
from jax import lax
from jax.experimental import pallas as pl
from jax.experimental.pallas import tpu as pltpu
from jax.sharding import PartitionSpec as P

EXPERTS = 128
LANES = 128
MIB = 1024 * 1024


def contract_rows(left, right):
    return lax.dot_general(
        left, right, (((0,), (0,)), ((), ())), preferred_element_type=jnp.float32
    )


def contract_cols(left, right):
    return lax.dot_general(
        left, right, (((1,), (1,)), ((), ())), preferred_element_type=jnp.float32
    )


def general_shards(tokens, grad_out, route_ids, route_weight, gate_weight, up_weight, down_weight):
    tokens, grad_out = (
        lax.all_gather(tokens, "ffn", axis=1, tiled=True),
        lax.all_gather(grad_out, "ffn", axis=1, tiled=True),
    )
    tok_dev, width = tokens.shape
    top_count = route_ids.shape[1]
    piece_width = gate_weight.shape[1]
    hidden_half = gate_weight.shape[2]
    pieces = width // piece_width
    devices = lax.axis_size("expert")
    flight = devices // pieces
    halves = lax.axis_size("ffn")
    sub_width = piece_width // halves
    capacity = max(2, min(tok_dev, (9 * tok_dev * top_count + 8 * EXPERTS - 1) // (8 * EXPERTS)))
    total_rows = devices * capacity
    expert_ids = jnp.arange(flight, dtype=jnp.int32)
    member = jnp.zeros((tok_dev, flight), jnp.float32)
    mixing = jnp.zeros((tok_dev, flight), jnp.float32)
    for route in range(top_count):
        hit = (route_ids[:, route : route + 1] == expert_ids[None, :]).astype(jnp.float32)
        member = member + hit
        mixing = mixing + hit * route_weight[:, route : route + 1]
    slots = jnp.cumsum(member, axis=0) - member
    place = member[:, :, None] * (
        slots[:, :, None] == jnp.arange(capacity, dtype=jnp.float32)
    ).astype(jnp.float32)
    weighted = place * mixing[:, :, None]
    place_low = place.astype(jnp.bfloat16)
    x_four = tokens.reshape(tok_dev, halves, pieces, sub_width)
    g_four = grad_out.reshape(tok_dev, halves, pieces, sub_width)
    x_parts = []
    g_parts = []
    for half in range(halves):
        x_parts.append(
            jnp.einsum(
                "Tec,Tjr->ejcr", place_low, x_four[:, half], preferred_element_type=jnp.float32
            )
        )
        g_parts.append(jnp.einsum("Tec,Tjr->ejcr", weighted, g_four[:, half].astype(jnp.float32)))
    x_send = jnp.concatenate(x_parts, axis=3).astype(jnp.bfloat16).reshape(total_rows, piece_width)
    g_send = jnp.concatenate(g_parts, axis=3).astype(jnp.bfloat16).reshape(total_rows, piece_width)

    def return_parts(values):
        arrived = lax.all_to_all(values, "expert", split_axis=0, concat_axis=0, tiled=True)
        lanes = arrived.shape[1]
        return arrived.astype(jnp.float32).reshape(flight, pieces, capacity, lanes).sum(axis=1)

    def spread_rows(values):
        lanes = values.shape[2]
        copies = jnp.broadcast_to(values[:, None], (flight, pieces, capacity, lanes)).reshape(
            total_rows, lanes
        )
        return lax.all_to_all(copies, "expert", split_axis=0, concat_axis=0, tiled=True)

    def finish(term, mix):
        summed = lax.psum_scatter(term, "ffn", scatter_dimension=1, tiled=True)
        back = lax.all_to_all(summed, "expert", split_axis=0, concat_axis=0, tiled=True)
        back = back.reshape(flight, pieces, capacity, sub_width)
        joined = jnp.einsum("Tec,ejcr->Tjr", mix, back)
        return joined.reshape(tok_dev, pieces * sub_width).astype(jnp.bfloat16)

    rows = lax.all_to_all(x_send, "expert", split_axis=0, concat_axis=0, tiled=True)
    w_gate = gate_weight[0]
    w_up = up_weight[0]
    w_down = down_weight[0]
    partial_value = jnp.concatenate(
        [
            jnp.dot(rows, w_gate, preferred_element_type=jnp.float32),
            jnp.dot(rows, w_up, preferred_element_type=jnp.float32),
        ],
        axis=1,
    )
    summed = return_parts(partial_value.astype(jnp.bfloat16))
    gate = summed[:, :, :hidden_half]
    up = summed[:, :, hidden_half:]
    sig = jax.nn.sigmoid(gate)
    act = gate * sig
    hidden = (act * up).astype(jnp.bfloat16)
    h_rows = spread_rows(hidden)
    out_term = jnp.dot(h_rows, w_down, preferred_element_type=jnp.float32)
    out_tokens = finish(out_term, weighted)
    grads = lax.all_to_all(g_send, "expert", split_axis=0, concat_axis=0, tiled=True)
    grad_down = contract_rows(h_rows, grads).astype(jnp.bfloat16)
    hidden_part = contract_cols(grads, w_down).astype(jnp.bfloat16)
    grad_hidden = return_parts(hidden_part)
    pre_gate = (grad_hidden * up * sig * (1.0 + gate * (1.0 - sig))).astype(jnp.bfloat16)
    pre_up = (grad_hidden * act).astype(jnp.bfloat16)
    both = spread_rows(jnp.concatenate([pre_gate, pre_up], axis=2))
    d_gate_rows = both[:, :hidden_half]
    d_up_rows = both[:, hidden_half:]
    grad_gate = contract_rows(rows, d_gate_rows).astype(jnp.bfloat16)
    grad_up = contract_rows(rows, d_up_rows).astype(jnp.bfloat16)
    x_term = contract_cols(d_gate_rows, w_gate) + contract_cols(d_up_rows, w_up)
    grad_tokens = finish(x_term, place)
    return (out_tokens, grad_tokens, grad_gate[None], grad_up[None], grad_down[None])


def vmem(shape, dtype):
    return pltpu.VMEM(shape, dtype)


def call(kernel, out_shape, args, in_spaces=None, out_spaces=None, flops=0, traffic=0, scratch=(), limit=16):
    spaces = in_spaces or [pltpu.VMEM] * len(args)
    outs = out_spaces or [pltpu.VMEM] * len(out_shape)
    return pl.pallas_call(
        kernel,
        out_shape=tuple(out_shape),
        in_specs=[pl.BlockSpec(memory_space=space) for space in spaces],
        out_specs=tuple(pl.BlockSpec(memory_space=space) for space in outs),
        scratch_shapes=list(scratch),
        compiler_params=pltpu.CompilerParams(vmem_limit_bytes=limit * MIB),
        cost_estimate=pl.CostEstimate(flops=flops, bytes_accessed=traffic, transcendentals=0),
    )(*args)


def blocks_to_rows(scratch, blocks, put, subs):
    size = blocks[0].shape[0]
    for p, block in enumerate(blocks):
        scratch[p * size : (p + 1) * size, :] = block[...].astype(jnp.float32)
    for sub in range(subs):
        put(sub, scratch[pl.ds(sub, len(blocks) * size // subs, stride=subs), :])


def spread_lanes(scratch, sub, subs, value):
    scratch[pl.ds(sub, value.shape[0], stride=subs), :] = value


def part(ref, start, count):
    return ref.at[start : start + count, :]


def lanes_of(sub):
    return slice(sub * LANES, (sub + 1) * LANES)


def even_masks(count):
    return [*range(count // 2 + 2, count, 2), *range(2, count // 2, 2)]


def both_masks(count):
    return [count // 2, count // 2 + 1, 1, 0]


def route_kernel(devices, capacity, subs, ids_in, weight_in, x_in, g_in, *refs):
    mine, theirs, *both, place_out, mix_out, scratch, ids, weight, x, g, sems = refs
    pairs = ((ids_in, ids), (weight_in, weight), (x_in, x), (g_in, g))
    copies = [pltpu.make_async_copy(src, dst, sems.at[i]) for i, (src, dst) in enumerate(pairs)]
    for copy in copies:
        copy.start()
    top, tok = ids.shape
    rows = devices * capacity
    core = lax.axis_index("ffn")
    masks = even_masks(devices)
    count = len(masks)
    masks = [mask + core for mask in masks] + [mask + 1 - core for mask in masks] + both_masks(devices)
    order = lax.broadcasted_iota(jnp.int32, (devices, tok), 0)
    bits = jnp.zeros((devices, tok), jnp.int32)
    for p, mask in enumerate(masks):
        bits = jnp.where(order == p, mask, bits)
    expert = bits ^ lax.axis_index("expert")
    member = jnp.zeros((devices, tok), jnp.float32)
    mixing = jnp.zeros((devices, tok), jnp.float32)
    copies[0].wait()
    copies[1].wait()
    for route in range(top):
        hit = ids[route : route + 1, :] == expert
        member = jnp.where(hit, 1.0, member)
        mixing = jnp.where(hit, weight[route : route + 1, :], mixing)
    before = lax.broadcasted_iota(jnp.int32, (tok, tok), 0) < lax.broadcasted_iota(jnp.int32, (tok, tok), 1)
    slots = dot(member.astype(jnp.bfloat16), jnp.where(before, 1.0, 0.0).astype(jnp.bfloat16))
    target = jnp.where(member > 0, slots + capacity * order.astype(jnp.float32), -1.0)
    row = lax.broadcasted_iota(jnp.int32, (rows, tok), 0).astype(jnp.float32)
    place = jnp.zeros((rows, tok), jnp.float32)
    mix = jnp.zeros((rows, tok), jnp.float32)
    for p in range(devices):
        equal = target[p : p + 1, :] == row
        place = jnp.where(equal, 1.0, place)
        mix = jnp.where(equal, mixing[p : p + 1, :], mix)
    row_weight = jnp.broadcast_to(jnp.sum(mix, axis=1, keepdims=True), (rows, LANES))
    low = place.astype(jnp.bfloat16)
    place_out[...] = low
    mix_out[...] = row_weight
    size = capacity * subs

    def write(at):
        def block(p):
            return scratch[p * size : (p + 1) * size, :].astype(theirs.dtype)

        for j in range(count):
            part(mine, 2 * j * size + at, size)[...] = block(j)
            part(theirs, 2 * j * size + at, size)[...] = block(count + j)
        for i, out in enumerate(both):
            part(out, at, size)[...] = block(2 * count + i)

    copies[2].wait()
    for sub in range(subs):
        spread_lanes(scratch, sub, subs, dot(low, x[:, lanes_of(sub)]))
    write(0)
    copies[3].wait()
    for sub in range(subs):
        spread_lanes(scratch, sub, subs, dot(low, g[:, lanes_of(sub)]) * row_weight)
    write(size)


def pack_kernel(size, mine, swapped, *outs):
    for j, out in enumerate(outs):
        part(out, 0, 2 * size)[...] = part(mine, 2 * j * size, 2 * size)[...]
        part(out, 2 * size, 2 * size)[...] = part(swapped, 2 * j * size, 2 * size)[...]


def gather_kernel(size, count, *refs):
    blocks, both, (x_out, g_out) = refs[:count], refs[count:-2], refs[-2:]
    for at, out in ((0, x_out), (size, g_out)):
        for j, block in enumerate(blocks):
            part(out, 2 * j * size, size)[...] = part(block, at, size)[...]
            part(out, (2 * j + 1) * size, size)[...] = part(block, 2 * size + at, size)[...]
        for i, block in enumerate(both):
            part(out, (2 * count + i) * size, size)[...] = part(block, at, size)[...]


def full_rows(devices, subs, scratch, own_sent, other_sent, out):
    size = own_sent.shape[0] // devices
    count = len(even_masks(devices))
    own, other = half_starts(out.shape[1] // 2)
    first, second, last = range(0, 2 * count, 2), range(1, 2 * count, 2), range(2 * count, devices)
    layouts = (
        (own, [(own_sent, i) for i in first] + [(other_sent, i) for i in second] + [(own_sent, i) for i in last]),
        (other, [(own_sent, i) for i in second] + [(other_sent, i) for i in first] + [(other_sent, i) for i in last]),
    )
    for start, layout in layouts:

        def put(sub, value):
            out[:, pl.ds(start + sub * LANES, LANES)] = value.astype(out.dtype)

        blocks_to_rows(scratch, [part(ref, i * size, size) for ref, i in layout], put, subs)


def split_terms(count, size, scratch, own_half, keep, send):
    keep[0 : count * size, :] = scratch[0 : count * size, :]
    send[0 : count * size, :] = scratch[count * size : 2 * count * size, :].astype(send.dtype)
    rest = scratch[2 * count * size :, :]
    if own_half:
        keep[count * size :, :] = rest
    else:
        send[count * size :, :] = rest.astype(send.dtype)


def leave_kernel(size, count, *refs):
    terms, outs = (refs[:4], refs[4:8]), refs[8:]
    for at, (keep_own, keep_other, came_own, came_other) in zip((0, size), terms):

        def own(p):
            total = part(keep_own, p * size, size)[...] + part(came_own, p * size, size)[...].astype(jnp.float32)
            return total.astype(outs[0].dtype)

        for p, out in enumerate(outs):
            part(out, at, size)[...] = own(p)
        for j, out in enumerate(outs[:count]):
            total = part(keep_other, j * size, size)[...] + part(came_other, j * size, size)[...].astype(jnp.float32)
            part(out, 2 * size + at, size)[...] = total.astype(out.dtype)


def share_kernel(size, count, *refs):
    for j, block in enumerate(refs[:count]):
        part(refs[-1], 2 * j * size, 2 * size)[...] = part(block, 2 * size, 2 * size)[...]


def token_sums(subs, place, mix, scratch, rows, blocks, out, before):
    size = scratch.shape[0] // len(blocks)
    for p, block in enumerate(blocks):
        here = slice(p * size, (p + 1) * size)
        scratch[here, :] = jnp.zeros((size, LANES), jnp.float32) if block is None else block[...].astype(jnp.float32)
    for sub in range(subs):
        value = scratch[pl.ds(sub, rows.shape[0], stride=subs), :]
        if mix is not None:
            value = value * mix[...]
        rows[:, lanes_of(sub)] = value.astype(rows.dtype)
    for cut in pieces_of(subs * LANES, 512):
        total = contract_rows(place[...], rows[:, cut])
        if before is not None:
            total = total + before[:, cut]
        out[:, cut] = total.astype(out.dtype)


def join_kernel(count, subs, place, mix, *refs):
    blocks, both, (out_sum, grad_sum, scratch, rows) = refs[:count], refs[count:-4], refs[-4:]
    size = both[0].shape[0] // 2
    for at, scale, out in ((0, mix, out_sum), (size, None, grad_sum)):
        first = [part(block, at, size) for block in blocks]
        last = [part(block, at, size) for block in both]
        token_sums(subs, place, scale, scratch, rows, first + [None] * count + last, out, None)


def finish_kernel(count, subs, place, mix, shared, out_sum, grad_sum, out_tokens, grad_tokens, scratch, rows):
    size = shared.shape[0] // (2 * count)
    rest = scratch.shape[0] // size - 2 * count
    for at, scale, before, out in ((0, mix, out_sum, out_tokens), (size, None, grad_sum, grad_tokens)):
        blocks = [part(shared, 2 * j * size + at, size) for j in range(count)]
        token_sums(subs, place, scale, scratch, rows, [None] * count + blocks + [None] * rest, out, before)


def half_starts(half_width):
    half = lax.axis_index("ffn")
    own = pl.multiple_of(half * half_width, half_width)
    other = pl.multiple_of((1 - half) * half_width, half_width)
    return own, other


def chunk(i, step, base=0):
    return pl.ds(base + pl.multiple_of(i * step, step), step)


def dot(left, right):
    return jnp.dot(left, right, preferred_element_type=jnp.float32)


def halves_of_output(devices, subs, step, scratch, own_half, term, keep, send):
    size = scratch.shape[0] // devices
    for at in range(0, subs * LANES, step):
        value = term(at)
        for i in range(step // LANES):
            spread_lanes(scratch, at // LANES + i, subs, value[:, lanes_of(i)])
    split_terms(len(even_masks(devices)), size, scratch, own_half, keep, send)


def forward_kernel(devices, subs, step, x_sent, x_swapped, w_gate, w_up, x_full, gate, up, hidden, scratch):
    full_rows(devices, subs, scratch, x_sent, x_swapped, x_full)
    for cols in pieces_of(gate.shape[1], step):
        gate_low = dot(x_full[...], w_gate[0, :, cols]).astype(jnp.bfloat16)
        up_low = dot(x_full[...], w_up[0, :, cols]).astype(jnp.bfloat16)
        gate[:, cols] = gate_low
        up[:, cols] = up_low
        value = gate_low.astype(jnp.float32)
        hidden[:, cols] = (value * jax.nn.sigmoid(value) * up_low.astype(jnp.float32)).astype(jnp.bfloat16)


def output_kernel(devices, subs, step, hidden, w_down, keep_own, keep_other, send_own, send_other, scratch):
    own, other = half_starts(subs * LANES)

    def term(start):
        return lambda at: dot(hidden[...], w_down[0, :, pl.ds(start + at, step)])

    halves_of_output(devices, subs, step, scratch, False, term(other), keep_other, send_other)
    halves_of_output(devices, subs, step, scratch, True, term(own), keep_own, send_own)


def input_term(step, pre_gate, pre_up, w_gate, w_up, start):
    def term(at):
        there = pl.ds(start + at, step)
        return contract_cols(pre_gate[...], w_gate[0, there, :]) + contract_cols(pre_up[...], w_up[0, there, :])

    return term


def backward_kernel(
    devices,
    subs,
    step,
    g_sent,
    g_swapped,
    gate,
    up,
    w_gate,
    w_up,
    w_down,
    g_full,
    pre_gate,
    pre_up,
    keep_other,
    send_other,
    scratch,
):
    _, other = half_starts(subs * LANES)
    full_rows(devices, subs, scratch, g_sent, g_swapped, g_full)

    def pull(i, carry):
        cols = chunk(i, step)
        low = contract_cols(g_full[...], w_down[0, cols, :]).astype(jnp.bfloat16)
        grad_hidden = low.astype(jnp.float32)
        value = gate[:, cols].astype(jnp.float32)
        sig = jax.nn.sigmoid(value)
        pre_gate[:, cols] = (
            grad_hidden * up[:, cols].astype(jnp.float32) * sig * (1.0 + value * (1.0 - sig))
        ).astype(jnp.bfloat16)
        pre_up[:, cols] = (grad_hidden * value * sig).astype(jnp.bfloat16)
        return carry

    lax.fori_loop(0, gate.shape[1] // step, pull, 0)
    term = input_term(step, pre_gate, pre_up, w_gate, w_up, other)
    halves_of_output(devices, subs, step, scratch, False, term, keep_other, send_other)


def backward_own_kernel(devices, subs, step, pre_gate, pre_up, w_gate, w_up, keep_own, send_own, scratch):
    own, _ = half_starts(subs * LANES)
    term = input_term(step, pre_gate, pre_up, w_gate, w_up, own)
    halves_of_output(devices, subs, step, scratch, True, term, keep_own, send_own)


def flip(value):
    return value.astype(jnp.float32).T


def pieces_of(total, size):
    return [slice(at, min(at + size, total)) for at in range(0, total, size)]


def gradient_kernel(
    step,
    x,
    g,
    hidden,
    pre_gate,
    pre_up,
    grad_gate,
    grad_up,
    grad_down,
    written,
    flipped,
    turned,
    tall,
    wide,
    tall_sems,
    wide_sems,
):
    written[...] = jnp.zeros_like(written)
    width, lanes = x.shape[1], hidden.shape[1]
    count = width // step
    flipped[...] = flip(hidden[...]).astype(flipped.dtype)

    def wide_copy(i, slot):
        return pltpu.make_async_copy(wide.at[slot], grad_down.at[0, :, chunk(i, step)], wide_sems.at[slot])

    def tall_copy(which, out, i, slot):
        return pltpu.make_async_copy(tall.at[which, slot], out.at[0, chunk(i, step), :], tall_sems.at[which, slot])

    def down(i, carry):
        slot = i % 2

        @pl.when(i >= 2)
        def _():
            wide_copy(i - 2, slot).wait()

        for cut in pieces_of(step, 256):
            right = g[:, chunk(i, step)][:, cut]
            for high in pieces_of(lanes, 256):
                wide[slot, high, cut] = dot(flipped[high, :], right).astype(wide.dtype)
        wide_copy(i, slot).start()
        return carry

    lax.fori_loop(0, count, down, 0)

    def inputs(i, carry):
        slot = i % 2
        turned[...] = flip(x[:, chunk(i, step)]).astype(turned.dtype)
        for which, (right, out) in enumerate(((pre_gate, grad_gate), (pre_up, grad_up))):

            @pl.when(i >= 2)
            def _():
                tall_copy(which, out, i - 2, slot).wait()

            for cut in pieces_of(lanes, 256):
                for high in pieces_of(step, 256):
                    tall[which, slot, high, cut] = dot(turned[high, :], right[:, cut]).astype(tall.dtype)
            tall_copy(which, out, i, slot).start()
        return carry

    lax.fori_loop(0, count, inputs, 0)
    for i in range(max(0, count - 2), count):
        wide_copy(i, i % 2).wait()
        tall_copy(0, grad_gate, i, i % 2).wait()
        tall_copy(1, grad_up, i, i % 2).wait()


def exchange(blocks, masks, devices):
    arrived = []
    for block, mask in zip(blocks, masks):
        pairs = [(2 * i + core, 2 * (i ^ (mask + core)) + core) for i in range(devices) for core in range(2)]
        arrived.append(lax.ppermute(block, ("expert", "ffn"), pairs))
    return arrived


def exchange_both(blocks, devices):
    arrived = []
    for block, mask in zip(blocks, both_masks(devices)):
        arrived.append(lax.ppermute(block, "expert", [(i, i ^ mask) for i in range(devices)]) if mask else block)
    return arrived


def swap(value):
    return lax.ppermute(value, "ffn", [(0, 1), (1, 0)])


def in_hbm(values):
    return [pltpu.with_memory_space_constraint(value, pltpu.HBM) for value in values]


def one_piece_shards(tokens, grad_out, route_ids, route_weight, gate_weight, up_weight, down_weight):
    tok_dev, sub_width = tokens.shape
    top_count = route_ids.shape[1]
    width, lanes = gate_weight.shape[1:]
    devices = lax.axis_size("expert")
    capacity = max(2, min(tok_dev, (9 * tok_dev * top_count + 8 * EXPERTS - 1) // (8 * EXPERTS)))
    rows = devices * capacity
    subs = sub_width // LANES
    low, full = jnp.bfloat16, jnp.float32
    size = capacity * subs
    masks = even_masks(devices)
    count, shared_count = len(masks), len(both_masks(devices))
    spread_scratch = [pltpu.VMEM((devices * size, LANES), full)]
    step = 256
    half_flops = 2 * rows * width * lanes // 2

    def lines(number, dtype=low):
        return jax.ShapeDtypeStruct((number * size, LANES), dtype)

    def lines_in_vmem(number, dtype=low):
        return vmem((number * size, LANES), dtype)

    sources = (route_ids.T, route_weight.T, tokens, grad_out)
    mine, theirs, *both, place, mix = call(
        functools.partial(route_kernel, devices, capacity, subs),
        [lines(2 * count)] * 2
        + [lines(2)] * shared_count
        + [jax.ShapeDtypeStruct((rows, tok_dev), low), jax.ShapeDtypeStruct((rows, LANES), full)],
        in_hbm(sources),
        in_spaces=[pl.ANY] * 4,
        scratch=spread_scratch
        + [pltpu.VMEM(value.shape, value.dtype) for value in sources]
        + [pltpu.SemaphoreType.DMA((4,))],
        traffic=4 * tok_dev * sub_width,
    )
    both = exchange_both(both, devices)
    packed = call(
        functools.partial(pack_kernel, size), [lines(4)] * count, (mine, swap(theirs)), flops=24 * half_flops
    )
    arrived = exchange(packed, masks, devices)

    weights = (gate_weight, up_weight, down_weight)
    w_gate, w_up, w_down = [pltpu.with_memory_space_constraint(w, pltpu.VMEM) for w in weights]

    x_sent, g_sent = call(
        functools.partial(gather_kernel, size, count), [lines(devices)] * 2, (*arrived, *both)
    )
    x_swapped = swap(x_sent)
    g_swapped = swap(g_sent)
    terms = [
        lines_in_vmem(count + shared_count, full),
        lines_in_vmem(count, full),
        lines_in_vmem(count),
        lines_in_vmem(count + shared_count),
    ]
    x_full, gate, up, hidden = call(
        functools.partial(forward_kernel, devices, subs, step),
        [vmem((rows, width), low)] + [vmem((rows, lanes), low)] * 3,
        (x_sent, x_swapped, w_gate, w_up),
        scratch=spread_scratch,
        flops=4 * half_flops,
    )
    out_own, out_other, send_own, send_other = call(
        functools.partial(output_kernel, devices, subs, 2 * step),
        terms,
        (hidden, w_down),
        scratch=spread_scratch,
        flops=2 * half_flops,
    )
    out_terms = (out_own, out_other, swap(send_other), swap(send_own))
    g_full, pre_gate, pre_up, dx_other, send_other = call(
        functools.partial(backward_kernel, devices, subs, step),
        [vmem((rows, width), low)] + [vmem((rows, lanes), low)] * 2 + [terms[1], terms[3]],
        (g_sent, g_swapped, gate, up, w_gate, w_up, w_down),
        scratch=spread_scratch,
        flops=4 * half_flops,
    )
    came_own = swap(send_other)
    dx_own, send_own = call(
        functools.partial(backward_own_kernel, devices, subs, step),
        [terms[0], terms[2]],
        (pre_gate, pre_up, w_gate, w_up),
        scratch=spread_scratch,
        flops=2 * half_flops,
    )
    dx_terms = (dx_own, dx_other, came_own, swap(send_own))
    leaving = call(
        functools.partial(leave_kernel, size, count),
        [lines(4)] * count + [lines(2)] * shared_count,
        (*out_terms, *dx_terms),
    )
    returned = exchange(leaving[:count], masks, devices)
    both = exchange_both(leaving[count:], devices)
    cut = 1024 if width % 1024 == 0 else width
    grad_gate, grad_up, grad_down, written = call(
        functools.partial(gradient_kernel, cut),
        [jax.ShapeDtypeStruct(w.shape, low) for w in weights] + [vmem((8, LANES), full)],
        (x_full, g_full, hidden, pre_gate, pre_up),
        out_spaces=[pl.ANY] * 3 + [pltpu.VMEM],
        scratch=[
            pltpu.VMEM((lanes, rows), low),
            pltpu.VMEM((cut, rows), low),
            pltpu.VMEM((2, 2, cut, lanes), low),
            pltpu.VMEM((2, lanes, cut), low),
            pltpu.SemaphoreType.DMA((2, 2)),
            pltpu.SemaphoreType.DMA((2,)),
        ],
        flops=6 * half_flops,
        traffic=sum(w.size * 2 for w in weights),
        limit=32,
    )
    (sharing,) = call(
        functools.partial(share_kernel, size, count), [lines(2 * count)], (*returned, *both, written)
    )
    shared = swap(sharing)
    rows_scratch = [pltpu.VMEM((rows, sub_width), low)]
    sums = call(
        functools.partial(join_kernel, count, subs),
        [vmem((tok_dev, sub_width), full)] * 2,
        (place, mix, *returned, *both),
        scratch=spread_scratch + rows_scratch,
        flops=4 * rows * tok_dev * sub_width,
    )
    out_tokens, grad_tokens = call(
        functools.partial(finish_kernel, count, subs),
        [jax.ShapeDtypeStruct((tok_dev, sub_width), low)] * 2,
        (place, mix, shared, *sums),
        scratch=spread_scratch + rows_scratch,
        traffic=8 * tok_dev * sub_width,
    )
    return out_tokens, grad_tokens, grad_gate, grad_up, grad_down


def shards(*args):
    tokens, gate_weight = args[0], args[4]
    halves = lax.axis_size("ffn")
    devices = lax.axis_size("expert")
    if halves == 2 and devices >= 8 and devices & (devices - 1) == 0 and tokens.shape[1] * halves == gate_weight.shape[1]:
        return one_piece_shards(*args)
    return general_shards(*args)


def solution(mesh):
    in_specs = (
        P(("groups", "expert"), "ffn"),
        P(("groups", "expert"), "ffn"),
        P(("groups", "expert"), None),
        P(("groups", "expert"), None),
        P("expert", None, "ffn"),
        P("expert", None, "ffn"),
        P("expert", "ffn", None),
    )
    out_specs = (
        P(("groups", "expert"), "ffn"),
        P(("groups", "expert"), "ffn"),
        P(("groups", "expert"), None, "ffn"),
        P(("groups", "expert"), None, "ffn"),
        P(("groups", "expert"), "ffn", None),
    )
    return jax.shard_map(shards, mesh=mesh, in_specs=in_specs, out_specs=out_specs, check_vma=False)
```

```python
import functools

import jax
import jax.numpy as jnp
from jax import lax
from jax.experimental import pallas as pl
from jax.experimental.pallas import tpu as pltpu
from jax.sharding import PartitionSpec as P

EXPERTS = 128
LANES = 128
MIB = 1024 * 1024


def contract_rows(left, right):
    return lax.dot_general(
        left, right, (((0,), (0,)), ((), ())), preferred_element_type=jnp.float32
    )


def contract_cols(left, right):
    return lax.dot_general(
        left, right, (((1,), (1,)), ((), ())), preferred_element_type=jnp.float32
    )


def general_shards(tokens, grad_out, route_ids, route_weight, gate_weight, up_weight, down_weight):
    tokens, grad_out = (
        lax.all_gather(tokens, "ffn", axis=1, tiled=True),
        lax.all_gather(grad_out, "ffn", axis=1, tiled=True),
    )
    tok_dev, width = tokens.shape
    top_count = route_ids.shape[1]
    piece_width = gate_weight.shape[1]
    hidden_half = gate_weight.shape[2]
    pieces = width // piece_width
    devices = lax.axis_size("expert")
    flight = devices // pieces
    halves = lax.axis_size("ffn")
    sub_width = piece_width // halves
    capacity = max(2, min(tok_dev, (9 * tok_dev * top_count + 8 * EXPERTS - 1) // (8 * EXPERTS)))
    total_rows = devices * capacity
    expert_ids = jnp.arange(flight, dtype=jnp.int32)
    member = jnp.zeros((tok_dev, flight), jnp.float32)
    mixing = jnp.zeros((tok_dev, flight), jnp.float32)
    for route in range(top_count):
        hit = (route_ids[:, route : route + 1] == expert_ids[None, :]).astype(jnp.float32)
        member = member + hit
        mixing = mixing + hit * route_weight[:, route : route + 1]
    slots = jnp.cumsum(member, axis=0) - member
    place = member[:, :, None] * (
        slots[:, :, None] == jnp.arange(capacity, dtype=jnp.float32)
    ).astype(jnp.float32)
    weighted = place * mixing[:, :, None]
    place_low = place.astype(jnp.bfloat16)
    x_four = tokens.reshape(tok_dev, halves, pieces, sub_width)
    g_four = grad_out.reshape(tok_dev, halves, pieces, sub_width)
    x_parts = []
    g_parts = []
    for half in range(halves):
        x_parts.append(
            jnp.einsum(
                "Tec,Tjr->ejcr", place_low, x_four[:, half], preferred_element_type=jnp.float32
            )
        )
        g_parts.append(jnp.einsum("Tec,Tjr->ejcr", weighted, g_four[:, half].astype(jnp.float32)))
    x_send = jnp.concatenate(x_parts, axis=3).astype(jnp.bfloat16).reshape(total_rows, piece_width)
    g_send = jnp.concatenate(g_parts, axis=3).astype(jnp.bfloat16).reshape(total_rows, piece_width)

    def return_parts(values):
        arrived = lax.all_to_all(values, "expert", split_axis=0, concat_axis=0, tiled=True)
        lanes = arrived.shape[1]
        return arrived.astype(jnp.float32).reshape(flight, pieces, capacity, lanes).sum(axis=1)

    def spread_rows(values):
        lanes = values.shape[2]
        copies = jnp.broadcast_to(values[:, None], (flight, pieces, capacity, lanes)).reshape(
            total_rows, lanes
        )
        return lax.all_to_all(copies, "expert", split_axis=0, concat_axis=0, tiled=True)

    def finish(term, mix):
        summed = lax.psum_scatter(term, "ffn", scatter_dimension=1, tiled=True)
        back = lax.all_to_all(summed, "expert", split_axis=0, concat_axis=0, tiled=True)
        back = back.reshape(flight, pieces, capacity, sub_width)
        joined = jnp.einsum("Tec,ejcr->Tjr", mix, back)
        return joined.reshape(tok_dev, pieces * sub_width).astype(jnp.bfloat16)

    rows = lax.all_to_all(x_send, "expert", split_axis=0, concat_axis=0, tiled=True)
    w_gate = gate_weight[0]
    w_up = up_weight[0]
    w_down = down_weight[0]
    partial_value = jnp.concatenate(
        [
            jnp.dot(rows, w_gate, preferred_element_type=jnp.float32),
            jnp.dot(rows, w_up, preferred_element_type=jnp.float32),
        ],
        axis=1,
    )
    summed = return_parts(partial_value.astype(jnp.bfloat16))
    gate = summed[:, :, :hidden_half]
    up = summed[:, :, hidden_half:]
    sig = jax.nn.sigmoid(gate)
    act = gate * sig
    hidden = (act * up).astype(jnp.bfloat16)
    h_rows = spread_rows(hidden)
    out_term = jnp.dot(h_rows, w_down, preferred_element_type=jnp.float32)
    out_tokens = finish(out_term, weighted)
    grads = lax.all_to_all(g_send, "expert", split_axis=0, concat_axis=0, tiled=True)
    grad_down = contract_rows(h_rows, grads).astype(jnp.bfloat16)
    hidden_part = contract_cols(grads, w_down).astype(jnp.bfloat16)
    grad_hidden = return_parts(hidden_part)
    pre_gate = (grad_hidden * up * sig * (1.0 + gate * (1.0 - sig))).astype(jnp.bfloat16)
    pre_up = (grad_hidden * act).astype(jnp.bfloat16)
    both = spread_rows(jnp.concatenate([pre_gate, pre_up], axis=2))
    d_gate_rows = both[:, :hidden_half]
    d_up_rows = both[:, hidden_half:]
    grad_gate = contract_rows(rows, d_gate_rows).astype(jnp.bfloat16)
    grad_up = contract_rows(rows, d_up_rows).astype(jnp.bfloat16)
    x_term = contract_cols(d_gate_rows, w_gate) + contract_cols(d_up_rows, w_up)
    grad_tokens = finish(x_term, place)
    return (out_tokens, grad_tokens, grad_gate[None], grad_up[None], grad_down[None])


def vmem(shape, dtype):
    return pltpu.VMEM(shape, dtype)


def call(kernel, out_shape, args, in_spaces=None, out_spaces=None, flops=0, traffic=0, scratch=(), limit=16):
    spaces = in_spaces or [pltpu.VMEM] * len(args)
    outs = out_spaces or [pltpu.VMEM] * len(out_shape)
    return pl.pallas_call(
        kernel,
        out_shape=tuple(out_shape),
        in_specs=[pl.BlockSpec(memory_space=space) for space in spaces],
        out_specs=tuple(pl.BlockSpec(memory_space=space) for space in outs),
        scratch_shapes=list(scratch),
        compiler_params=pltpu.CompilerParams(vmem_limit_bytes=limit * MIB),
        cost_estimate=pl.CostEstimate(flops=flops, bytes_accessed=traffic, transcendentals=0),
    )(*args)


def blocks_to_rows(scratch, blocks, put, subs):
    size = blocks[0].shape[0]
    for p, block in enumerate(blocks):
        scratch[p * size : (p + 1) * size, :] = block[...].astype(jnp.float32)
    for sub in range(subs):
        put(sub, scratch[pl.ds(sub, len(blocks) * size // subs, stride=subs), :])


def spread_lanes(scratch, sub, subs, value):
    scratch[pl.ds(sub, value.shape[0], stride=subs), :] = value


def part(ref, start, count):
    return ref.at[start : start + count, :]


def lanes_of(sub):
    return slice(sub * LANES, (sub + 1) * LANES)


def even_masks(count):
    return [*range(count // 2, count, 2), *range(2, count // 2, 2)]


def route_kernel(devices, capacity, subs, ids_in, weight_in, x_in, g_in, *refs):
    x_mine, g_mine, near, here, theirs, place_out, mix_out, place_other, mix_other, scratch, ids, weight, x, g, sems = refs
    pairs = ((ids_in, ids), (weight_in, weight), (x_in, x), (g_in, g))
    copies = [pltpu.make_async_copy(src, dst, sems.at[i]) for i, (src, dst) in enumerate(pairs)]
    for copy in copies:
        copy.start()
    top, tok = ids.shape
    rows = devices * capacity
    core = lax.axis_index("ffn")
    masks = even_masks(devices)
    masks = [mask + core for mask in masks] + [mask + 1 - core for mask in masks] + [1, 0]
    order = lax.broadcasted_iota(jnp.int32, (devices, tok), 0)
    bits = jnp.zeros((devices, tok), jnp.int32)
    for p, mask in enumerate(masks):
        bits = jnp.where(order == p, mask, bits)
    expert = bits ^ lax.axis_index("expert")
    member = jnp.zeros((devices, tok), jnp.float32)
    mixing = jnp.zeros((devices, tok), jnp.float32)
    copies[0].wait()
    copies[1].wait()
    for route in range(top):
        hit = ids[route : route + 1, :] == expert
        member = jnp.where(hit, 1.0, member)
        mixing = jnp.where(hit, weight[route : route + 1, :], mixing)
    before = lax.broadcasted_iota(jnp.int32, (tok, tok), 0) < lax.broadcasted_iota(jnp.int32, (tok, tok), 1)
    slots = dot(member.astype(jnp.bfloat16), jnp.where(before, 1.0, 0.0).astype(jnp.bfloat16))
    target = jnp.where(member > 0, slots + capacity * order.astype(jnp.float32), -1.0)
    count = devices // 2 - 1

    def placed(first, number):
        row = lax.broadcasted_iota(jnp.int32, (number, tok), 0).astype(jnp.float32) + first
        place = jnp.zeros((number, tok), jnp.float32)
        mix = jnp.zeros((number, tok), jnp.float32)
        for p in range(devices):
            equal = target[p : p + 1, :] == row
            place = jnp.where(equal, 1.0, place)
            mix = jnp.where(equal, mixing[p : p + 1, :], mix)
        row_weight = jnp.broadcast_to(jnp.sum(mix, axis=1, keepdims=True), (number, LANES))
        return place.astype(jnp.bfloat16), row_weight

    low, row_weight = placed(0, rows)
    place_out[...] = low
    mix_out[...] = row_weight
    place_other[...], mix_other[...] = placed(count * capacity, count * capacity)
    size = capacity * subs

    def write(mine, at):
        def block(p):
            return scratch[p * size : (p + 1) * size, :].astype(theirs.dtype)

        for j in range(count):
            part(mine, j * size, size)[...] = block(j)
            part(theirs, (at + j) * size, size)[...] = block(count + j)
        start = size if at else 0
        part(near, start, size)[...] = block(2 * count)
        part(here, start, size)[...] = block(2 * count + 1)

    copies[2].wait()
    for sub in range(subs):
        spread_lanes(scratch, sub, subs, dot(low, x[:, lanes_of(sub)]))
    write(x_mine, 0)
    copies[3].wait()
    for sub in range(subs):
        spread_lanes(scratch, sub, subs, dot(low, g[:, lanes_of(sub)]) * row_weight)
    write(g_mine, count)


def pack_kernel(size, x_mine, g_mine, swapped, *outs):
    count = len(outs)
    for j, out in enumerate(outs):
        for i, mine in enumerate((x_mine, g_mine)):
            part(out, 2 * i * size, size)[...] = part(mine, j * size, size)[...]
            part(out, (2 * i + 1) * size, size)[...] = part(swapped, (i * count + j) * size, size)[...]


def gather_kernel(size, at, *refs):
    blocks, (near, here, out) = refs[:-3], refs[-3:]
    for j, block in enumerate(blocks):
        part(out, 2 * j * size, 2 * size)[...] = part(block, 2 * at, 2 * size)[...]
    part(out, 2 * len(blocks) * size, size)[...] = part(near, at, size)[...]
    part(out, (2 * len(blocks) + 1) * size, size)[...] = part(here, at, size)[...]


def full_rows(devices, subs, scratch, own_sent, other_sent, out):
    size = own_sent.shape[0] // devices
    count = devices // 2 - 1
    own, other = half_starts(out.shape[1] // 2)
    first, second, last = range(0, 2 * count, 2), range(1, 2 * count, 2), range(2 * count, devices)
    layouts = (
        (own, [(own_sent, i) for i in first] + [(other_sent, i) for i in second] + [(own_sent, i) for i in last]),
        (other, [(own_sent, i) for i in second] + [(other_sent, i) for i in first] + [(other_sent, i) for i in last]),
    )
    for start, layout in layouts:

        def put(sub, value):
            out[:, pl.ds(start + sub * LANES, LANES)] = value.astype(out.dtype)

        blocks_to_rows(scratch, [part(ref, i * size, size) for ref, i in layout], put, subs)


def split_terms(count, size, scratch, own_half, keep, send):
    keep[0 : count * size, :] = scratch[0 : count * size, :]
    send[0 : count * size, :] = scratch[count * size : 2 * count * size, :].astype(send.dtype)
    rest = scratch[2 * count * size :, :]
    if own_half:
        keep[count * size :, :] = rest
    else:
        send[count * size :, :] = rest.astype(send.dtype)


def leave_kernel(size, *refs):
    terms, outs = (refs[:4], refs[4:8]), refs[8:]
    count = len(outs) - 2
    for at, (keep_own, keep_other, came_own, came_other) in zip((0, size), terms):

        def own(p):
            total = part(keep_own, p * size, size)[...] + part(came_own, p * size, size)[...].astype(jnp.float32)
            return total.astype(outs[0].dtype)

        for j, out in enumerate(outs[:count]):
            part(out, at, size)[...] = own(j)
            total = part(keep_other, j * size, size)[...] + part(came_other, j * size, size)[...].astype(jnp.float32)
            part(out, 2 * size + at, size)[...] = total.astype(out.dtype)
        part(outs[count], at, size)[...] = own(count)
        part(outs[count + 1], at, size)[...] = own(count + 1)


def share_kernel(size, *refs):
    blocks, (_, _, out) = refs[:-3], refs[-3:]
    for j, block in enumerate(blocks):
        part(out, 2 * j * size, 2 * size)[...] = part(block, 2 * size, 2 * size)[...]


def token_sums(subs, place, mix, scratch, rows, blocks, put):
    size = scratch.shape[0] // len(blocks)
    for p, block in enumerate(blocks):
        here = slice(p * size, (p + 1) * size)
        scratch[here, :] = jnp.zeros((size, LANES), jnp.float32) if block is None else block[...].astype(jnp.float32)
    for sub in range(subs):
        value = scratch[pl.ds(sub, rows.shape[0], stride=subs), :]
        if mix is not None:
            value = value * mix[...]
        rows[:, lanes_of(sub)] = value.astype(rows.dtype)
    for cut in pieces_of(subs * LANES, 512):
        put(cut, contract_rows(place[...], rows[:, cut]))


def join_kernel(count, subs, place, mix, *refs):
    blocks, (near, here, out_sum, grad_sum, scratch, rows) = refs[:count], refs[count:]
    size = near.shape[0] // 2
    for at, scale, out in ((0, mix, out_sum), (size, None, grad_sum)):

        def put(cut, total):
            out[:, cut] = total

        first = [part(block, at, size) for block in blocks]
        last = [part(near, at, size), part(here, at, size)]
        token_sums(subs, place, scale, scratch, rows, first + [None] * count + last, put)


def finish_kernel(
    count, subs, place, mix, shared, out_sum, grad_sum, out_tokens, grad_tokens, scratch, rows, low, sems
):
    size = shared.shape[0] // (2 * count)
    copies = []
    work = ((0, mix, out_sum, out_tokens), (size, None, grad_sum, grad_tokens))
    for i, (at, scale, before, out) in enumerate(work):

        def put(cut, total):
            low[i, :, cut] = (before[:, cut] + total).astype(low.dtype)

        blocks = [part(shared, 2 * j * size + at, size) for j in range(count)]
        token_sums(subs, place, scale, scratch, rows, blocks, put)
        copies.append(pltpu.make_async_copy(low.at[i], out, sems.at[i]))
        copies[-1].start()
    for copy in copies:
        copy.wait()


def half_starts(half_width):
    half = lax.axis_index("ffn")
    own = pl.multiple_of(half * half_width, half_width)
    other = pl.multiple_of((1 - half) * half_width, half_width)
    return own, other


def chunk(i, step, base=0):
    return pl.ds(base + pl.multiple_of(i * step, step), step)


def dot(left, right):
    return jnp.dot(left, right, preferred_element_type=jnp.float32)


def halves_of_output(devices, subs, step, scratch, own_half, term, keep, send):
    size = scratch.shape[0] // devices
    for at in range(0, subs * LANES, step):
        value = term(at)
        for i in range(step // LANES):
            spread_lanes(scratch, at // LANES + i, subs, value[:, lanes_of(i)])
    split_terms(devices // 2 - 1, size, scratch, own_half, keep, send)


def forward_kernel(devices, subs, step, x_sent, x_swapped, w_gate, w_up, x_full, gate, up, hidden, scratch):
    full_rows(devices, subs, scratch, x_sent, x_swapped, x_full)
    for cols in pieces_of(gate.shape[1], step):
        gate_low = dot(x_full[...], w_gate[0, :, cols]).astype(jnp.bfloat16)
        up_low = dot(x_full[...], w_up[0, :, cols]).astype(jnp.bfloat16)
        gate[:, cols] = gate_low
        up[:, cols] = up_low
        value = gate_low.astype(jnp.float32)
        hidden[:, cols] = (value * jax.nn.sigmoid(value) * up_low.astype(jnp.float32)).astype(jnp.bfloat16)


def output_kernel(devices, subs, step, hidden, w_down, keep_own, keep_other, send_own, send_other, scratch):
    own, other = half_starts(subs * LANES)

    def term(start):
        return lambda at: dot(hidden[...], w_down[0, :, pl.ds(start + at, step)])

    halves_of_output(devices, subs, step, scratch, False, term(other), keep_other, send_other)
    halves_of_output(devices, subs, step, scratch, True, term(own), keep_own, send_own)


def input_term(step, pre_gate, pre_up, w_gate, w_up, start):
    def term(at):
        there = pl.ds(start + at, step)
        return contract_cols(pre_gate[...], w_gate[0, there, :]) + contract_cols(pre_up[...], w_up[0, there, :])

    return term


def backward_kernel(
    devices,
    subs,
    step,
    g_sent,
    g_swapped,
    gate,
    up,
    w_gate,
    w_up,
    w_down,
    g_full,
    pre_gate,
    pre_up,
    keep_other,
    send_other,
    scratch,
):
    _, other = half_starts(subs * LANES)
    full_rows(devices, subs, scratch, g_sent, g_swapped, g_full)

    def pull(i, carry):
        cols = chunk(i, step)
        low = contract_cols(g_full[...], w_down[0, cols, :]).astype(jnp.bfloat16)
        grad_hidden = low.astype(jnp.float32)
        value = gate[:, cols].astype(jnp.float32)
        sig = jax.nn.sigmoid(value)
        pre_gate[:, cols] = (
            grad_hidden * up[:, cols].astype(jnp.float32) * sig * (1.0 + value * (1.0 - sig))
        ).astype(jnp.bfloat16)
        pre_up[:, cols] = (grad_hidden * value * sig).astype(jnp.bfloat16)
        return carry

    lax.fori_loop(0, gate.shape[1] // step, pull, 0)
    term = input_term(step, pre_gate, pre_up, w_gate, w_up, other)
    halves_of_output(devices, subs, step, scratch, False, term, keep_other, send_other)


def backward_own_kernel(devices, subs, step, pre_gate, pre_up, w_gate, w_up, keep_own, send_own, scratch):
    own, _ = half_starts(subs * LANES)
    term = input_term(step, pre_gate, pre_up, w_gate, w_up, own)
    halves_of_output(devices, subs, step, scratch, True, term, keep_own, send_own)


def flip(value):
    return value.astype(jnp.float32).T


def pieces_of(total, size):
    return [slice(at, min(at + size, total)) for at in range(0, total, size)]


def gradient_kernel(
    step,
    x,
    g,
    hidden,
    pre_gate,
    pre_up,
    grad_gate,
    grad_up,
    grad_down,
    written,
    flipped,
    turned,
    tall,
    wide,
    tall_sems,
    wide_sems,
):
    written[...] = jnp.zeros_like(written)
    width, lanes = x.shape[1], hidden.shape[1]
    count = width // step
    flipped[...] = flip(hidden[...]).astype(flipped.dtype)

    def wide_copy(i, slot):
        return pltpu.make_async_copy(wide.at[slot], grad_down.at[0, :, chunk(i, step)], wide_sems.at[slot])

    def tall_copy(which, out, i, slot):
        return pltpu.make_async_copy(tall.at[which, slot], out.at[0, chunk(i, step), :], tall_sems.at[which, slot])

    def down(i, carry):
        slot = i % 2

        @pl.when(i >= 2)
        def _():
            wide_copy(i - 2, slot).wait()

        for cut in pieces_of(step, 256):
            right = g[:, chunk(i, step)][:, cut]
            for high in pieces_of(lanes, 256):
                wide[slot, high, cut] = dot(flipped[high, :], right).astype(wide.dtype)
        wide_copy(i, slot).start()
        return carry

    lax.fori_loop(0, count, down, 0)

    def inputs(i, carry):
        slot = i % 2
        turned[...] = flip(x[:, chunk(i, step)]).astype(turned.dtype)
        for which, (right, out) in enumerate(((pre_gate, grad_gate), (pre_up, grad_up))):

            @pl.when(i >= 2)
            def _():
                tall_copy(which, out, i - 2, slot).wait()

            for cut in pieces_of(lanes, 256):
                for high in pieces_of(step, 256):
                    tall[which, slot, high, cut] = dot(turned[high, :], right[:, cut]).astype(tall.dtype)
            tall_copy(which, out, i, slot).start()
        return carry

    lax.fori_loop(0, count, inputs, 0)
    for i in range(max(0, count - 2), count):
        wide_copy(i, i % 2).wait()
        tall_copy(0, grad_gate, i, i % 2).wait()
        tall_copy(1, grad_up, i, i % 2).wait()


def exchange(blocks, masks, devices):
    arrived = []
    for block, mask in zip(blocks, masks):
        pairs = [(2 * i + core, 2 * (i ^ (mask + core)) + core) for i in range(devices) for core in range(2)]
        arrived.append(lax.ppermute(block, ("expert", "ffn"), pairs))
    return arrived


def exchange_near(block, devices):
    return lax.ppermute(block, "expert", [(i, i ^ 1) for i in range(devices)])


def swap(value):
    return lax.ppermute(value, "ffn", [(0, 1), (1, 0)])


def in_hbm(values):
    return [pltpu.with_memory_space_constraint(value, pltpu.HBM) for value in values]


def one_piece_shards(tokens, grad_out, route_ids, route_weight, gate_weight, up_weight, down_weight):
    tok_dev, sub_width = tokens.shape
    top_count = route_ids.shape[1]
    width, lanes = gate_weight.shape[1:]
    devices = lax.axis_size("expert")
    capacity = max(2, min(tok_dev, (9 * tok_dev * top_count + 8 * EXPERTS - 1) // (8 * EXPERTS)))
    rows = devices * capacity
    subs = sub_width // LANES
    low, full = jnp.bfloat16, jnp.float32
    size = capacity * subs
    count = devices // 2 - 1
    spread_scratch = [pltpu.VMEM((devices * size, LANES), full)]
    step = 256
    half_flops = 2 * rows * width * lanes // 2

    def lines(number, dtype=low):
        return jax.ShapeDtypeStruct((number * size, LANES), dtype)

    def lines_in_vmem(number, dtype=low):
        return vmem((number * size, LANES), dtype)

    sources = (route_ids.T, route_weight.T, tokens, grad_out)
    other_rows = count * capacity
    x_mine, g_mine, near, here, theirs, place, mix, place_other, mix_other = call(
        functools.partial(route_kernel, devices, capacity, subs),
        [lines(count), lines(count), lines(2), lines(2)]
        + [lines(2 * count)]
        + [jax.ShapeDtypeStruct((rows, tok_dev), low), jax.ShapeDtypeStruct((rows, LANES), full)]
        + [jax.ShapeDtypeStruct((other_rows, tok_dev), low), jax.ShapeDtypeStruct((other_rows, LANES), full)],
        in_hbm(sources),
        in_spaces=[pl.ANY] * 4,
        scratch=spread_scratch
        + [pltpu.VMEM(value.shape, value.dtype) for value in sources]
        + [pltpu.SemaphoreType.DMA((4,))],
        traffic=4 * tok_dev * sub_width,
    )
    masks = even_masks(devices)
    packed = call(
        functools.partial(pack_kernel, size),
        [lines(4)] * count,
        (x_mine, g_mine, swap(theirs)),
        flops=24 * half_flops,
    )
    arrived = exchange(packed, masks, devices)
    near = exchange_near(near, devices)

    weights = (gate_weight, up_weight, down_weight)
    w_gate, w_up, w_down = [pltpu.with_memory_space_constraint(w, pltpu.VMEM) for w in weights]

    def gather(at):
        return call(functools.partial(gather_kernel, size, at), [lines(devices)], (*arrived, near, here))[0]

    x_sent = gather(0)
    x_swapped = swap(x_sent)
    g_sent = gather(size)
    g_swapped = swap(g_sent)
    terms = [
        lines_in_vmem(count + 2, full),
        lines_in_vmem(count, full),
        lines_in_vmem(count),
        lines_in_vmem(count + 2),
    ]
    x_full, gate, up, hidden = call(
        functools.partial(forward_kernel, devices, subs, step),
        [vmem((rows, width), low)] + [vmem((rows, lanes), low)] * 3,
        (x_sent, x_swapped, w_gate, w_up),
        scratch=spread_scratch,
        flops=4 * half_flops,
    )
    out_own, out_other, send_own, send_other = call(
        functools.partial(output_kernel, devices, subs, 2 * step),
        terms,
        (hidden, w_down),
        scratch=spread_scratch,
        flops=2 * half_flops,
    )
    out_terms = (out_own, out_other, swap(send_other), swap(send_own))
    g_full, pre_gate, pre_up, dx_other, send_other = call(
        functools.partial(backward_kernel, devices, subs, step),
        [vmem((rows, width), low)] + [vmem((rows, lanes), low)] * 2 + [terms[1], terms[3]],
        (g_sent, g_swapped, gate, up, w_gate, w_up, w_down),
        scratch=spread_scratch,
        flops=4 * half_flops,
    )
    came_own = swap(send_other)
    dx_own, send_own = call(
        functools.partial(backward_own_kernel, devices, subs, step),
        [terms[0], terms[2]],
        (pre_gate, pre_up, w_gate, w_up),
        scratch=spread_scratch,
        flops=2 * half_flops,
    )
    dx_terms = (dx_own, dx_other, came_own, swap(send_own))
    *leaving, back, kept = call(
        functools.partial(leave_kernel, size),
        [lines(4)] * count + [lines(2)] * 2,
        (*out_terms, *dx_terms),
    )
    returned = exchange(leaving, masks, devices)
    back = exchange_near(back, devices)
    cut = 1024 if width % 1024 == 0 else width
    grad_gate, grad_up, grad_down, written = call(
        functools.partial(gradient_kernel, cut),
        [jax.ShapeDtypeStruct(w.shape, low) for w in weights] + [vmem((8, LANES), full)],
        (x_full, g_full, hidden, pre_gate, pre_up),
        out_spaces=[pl.ANY] * 3 + [pltpu.VMEM],
        scratch=[
            pltpu.VMEM((lanes, rows), low),
            pltpu.VMEM((cut, rows), low),
            pltpu.VMEM((2, 2, cut, lanes), low),
            pltpu.VMEM((2, lanes, cut), low),
            pltpu.SemaphoreType.DMA((2, 2)),
            pltpu.SemaphoreType.DMA((2,)),
        ],
        flops=6 * half_flops,
        traffic=sum(w.size * 2 for w in weights),
        limit=32,
    )
    (sharing,) = call(functools.partial(share_kernel, size), [lines(2 * count)], (*returned, back, written))
    shared = swap(sharing)
    sums = call(
        functools.partial(join_kernel, count, subs),
        [vmem((tok_dev, sub_width), full)] * 2,
        (place, mix, *returned, back, kept),
        scratch=spread_scratch + [pltpu.VMEM((rows, sub_width), low)],
        flops=4 * rows * tok_dev * sub_width,
    )
    out_tokens, grad_tokens = call(
        functools.partial(finish_kernel, count, subs),
        [jax.ShapeDtypeStruct((tok_dev, sub_width), low)] * 2,
        (place_other, mix_other, shared, *sums),
        out_spaces=[pl.ANY] * 2,
        scratch=[
            pltpu.VMEM((count * size, LANES), full),
            pltpu.VMEM((other_rows, sub_width), low),
            pltpu.VMEM((2, tok_dev, sub_width), low),
            pltpu.SemaphoreType.DMA((2,)),
        ],
        traffic=8 * tok_dev * sub_width,
    )
    return out_tokens, grad_tokens, grad_gate, grad_up, grad_down


def shards(*args):
    tokens, gate_weight = args[0], args[4]
    halves = lax.axis_size("ffn")
    devices = lax.axis_size("expert")
    if halves == 2 and devices >= 4 and devices & (devices - 1) == 0 and tokens.shape[1] * halves == gate_weight.shape[1]:
        return one_piece_shards(*args)
    return general_shards(*args)


def solution(mesh):
    in_specs = (
        P(("groups", "expert"), "ffn"),
        P(("groups", "expert"), "ffn"),
        P(("groups", "expert"), None),
        P(("groups", "expert"), None),
        P("expert", None, "ffn"),
        P("expert", None, "ffn"),
        P("expert", "ffn", None),
    )
    out_specs = (
        P(("groups", "expert"), "ffn"),
        P(("groups", "expert"), "ffn"),
        P(("groups", "expert"), None, "ffn"),
        P(("groups", "expert"), None, "ffn"),
        P(("groups", "expert"), "ffn", None),
    )
    return jax.shard_map(shards, mesh=mesh, in_specs=in_specs, out_specs=out_specs, check_vma=False)
```

```python
import functools

import jax
import jax.numpy as jnp
from jax import lax
from jax.experimental import pallas as pl
from jax.experimental.pallas import tpu as pltpu
from jax.sharding import PartitionSpec as P

EXPERTS = 128
LANES = 128
MIB = 1024 * 1024


def contract_rows(left, right):
    return lax.dot_general(
        left, right, (((0,), (0,)), ((), ())), preferred_element_type=jnp.float32
    )


def contract_cols(left, right):
    return lax.dot_general(
        left, right, (((1,), (1,)), ((), ())), preferred_element_type=jnp.float32
    )


def general_shards(tokens, grad_out, route_ids, route_weight, gate_weight, up_weight, down_weight):
    tokens, grad_out = (
        lax.all_gather(tokens, "ffn", axis=1, tiled=True),
        lax.all_gather(grad_out, "ffn", axis=1, tiled=True),
    )
    tok_dev, width = tokens.shape
    top_count = route_ids.shape[1]
    piece_width = gate_weight.shape[1]
    hidden_half = gate_weight.shape[2]
    pieces = width // piece_width
    devices = lax.axis_size("expert")
    flight = devices // pieces
    halves = lax.axis_size("ffn")
    sub_width = piece_width // halves
    capacity = max(2, min(tok_dev, (9 * tok_dev * top_count + 8 * EXPERTS - 1) // (8 * EXPERTS)))
    total_rows = devices * capacity
    expert_ids = jnp.arange(flight, dtype=jnp.int32)
    member = jnp.zeros((tok_dev, flight), jnp.float32)
    mixing = jnp.zeros((tok_dev, flight), jnp.float32)
    for route in range(top_count):
        hit = (route_ids[:, route : route + 1] == expert_ids[None, :]).astype(jnp.float32)
        member = member + hit
        mixing = mixing + hit * route_weight[:, route : route + 1]
    slots = jnp.cumsum(member, axis=0) - member
    place = member[:, :, None] * (
        slots[:, :, None] == jnp.arange(capacity, dtype=jnp.float32)
    ).astype(jnp.float32)
    weighted = place * mixing[:, :, None]
    place_low = place.astype(jnp.bfloat16)
    x_four = tokens.reshape(tok_dev, halves, pieces, sub_width)
    g_four = grad_out.reshape(tok_dev, halves, pieces, sub_width)
    x_parts = []
    g_parts = []
    for half in range(halves):
        x_parts.append(
            jnp.einsum(
                "Tec,Tjr->ejcr", place_low, x_four[:, half], preferred_element_type=jnp.float32
            )
        )
        g_parts.append(jnp.einsum("Tec,Tjr->ejcr", weighted, g_four[:, half].astype(jnp.float32)))
    x_send = jnp.concatenate(x_parts, axis=3).astype(jnp.bfloat16).reshape(total_rows, piece_width)
    g_send = jnp.concatenate(g_parts, axis=3).astype(jnp.bfloat16).reshape(total_rows, piece_width)

    def return_parts(values):
        arrived = lax.all_to_all(values, "expert", split_axis=0, concat_axis=0, tiled=True)
        lanes = arrived.shape[1]
        return arrived.astype(jnp.float32).reshape(flight, pieces, capacity, lanes).sum(axis=1)

    def spread_rows(values):
        lanes = values.shape[2]
        copies = jnp.broadcast_to(values[:, None], (flight, pieces, capacity, lanes)).reshape(
            total_rows, lanes
        )
        return lax.all_to_all(copies, "expert", split_axis=0, concat_axis=0, tiled=True)

    def finish(term, mix):
        summed = lax.psum_scatter(term, "ffn", scatter_dimension=1, tiled=True)
        back = lax.all_to_all(summed, "expert", split_axis=0, concat_axis=0, tiled=True)
        back = back.reshape(flight, pieces, capacity, sub_width)
        joined = jnp.einsum("Tec,ejcr->Tjr", mix, back)
        return joined.reshape(tok_dev, pieces * sub_width).astype(jnp.bfloat16)

    rows = lax.all_to_all(x_send, "expert", split_axis=0, concat_axis=0, tiled=True)
    w_gate = gate_weight[0]
    w_up = up_weight[0]
    w_down = down_weight[0]
    partial_value = jnp.concatenate(
        [
            jnp.dot(rows, w_gate, preferred_element_type=jnp.float32),
            jnp.dot(rows, w_up, preferred_element_type=jnp.float32),
        ],
        axis=1,
    )
    summed = return_parts(partial_value.astype(jnp.bfloat16))
    gate = summed[:, :, :hidden_half]
    up = summed[:, :, hidden_half:]
    sig = jax.nn.sigmoid(gate)
    act = gate * sig
    hidden = (act * up).astype(jnp.bfloat16)
    h_rows = spread_rows(hidden)
    out_term = jnp.dot(h_rows, w_down, preferred_element_type=jnp.float32)
    out_tokens = finish(out_term, weighted)
    grads = lax.all_to_all(g_send, "expert", split_axis=0, concat_axis=0, tiled=True)
    grad_down = contract_rows(h_rows, grads).astype(jnp.bfloat16)
    hidden_part = contract_cols(grads, w_down).astype(jnp.bfloat16)
    grad_hidden = return_parts(hidden_part)
    pre_gate = (grad_hidden * up * sig * (1.0 + gate * (1.0 - sig))).astype(jnp.bfloat16)
    pre_up = (grad_hidden * act).astype(jnp.bfloat16)
    both = spread_rows(jnp.concatenate([pre_gate, pre_up], axis=2))
    d_gate_rows = both[:, :hidden_half]
    d_up_rows = both[:, hidden_half:]
    grad_gate = contract_rows(rows, d_gate_rows).astype(jnp.bfloat16)
    grad_up = contract_rows(rows, d_up_rows).astype(jnp.bfloat16)
    x_term = contract_cols(d_gate_rows, w_gate) + contract_cols(d_up_rows, w_up)
    grad_tokens = finish(x_term, place)
    return (out_tokens, grad_tokens, grad_gate[None], grad_up[None], grad_down[None])


def vmem(shape, dtype):
    return pltpu.VMEM(shape, dtype)


def call(kernel, out_shape, args, in_spaces=None, out_spaces=None, flops=0, traffic=0, scratch=(), limit=16):
    spaces = in_spaces or [pltpu.VMEM] * len(args)
    outs = out_spaces or [pltpu.VMEM] * len(out_shape)
    return pl.pallas_call(
        kernel,
        out_shape=tuple(out_shape),
        in_specs=[pl.BlockSpec(memory_space=space) for space in spaces],
        out_specs=tuple(pl.BlockSpec(memory_space=space) for space in outs),
        scratch_shapes=list(scratch),
        compiler_params=pltpu.CompilerParams(vmem_limit_bytes=limit * MIB),
        cost_estimate=pl.CostEstimate(flops=flops, bytes_accessed=traffic, transcendentals=0),
    )(*args)


def blocks_to_rows(scratch, blocks, put, subs):
    size = blocks[0].shape[0]
    for p, block in enumerate(blocks):
        scratch[p * size : (p + 1) * size, :] = block[...].astype(jnp.float32)
    for sub in range(subs):
        put(sub, scratch[pl.ds(sub, len(blocks) * size // subs, stride=subs), :])


def spread_lanes(scratch, sub, subs, value):
    scratch[pl.ds(sub, value.shape[0], stride=subs), :] = value


def part(ref, start, count):
    return ref.at[start : start + count, :]


def lanes_of(sub):
    return slice(sub * LANES, (sub + 1) * LANES)


def even_masks(count):
    return [*range(count // 2, count, 2), *range(2, count // 2, 2)]


def route_kernel(devices, capacity, subs, ids_in, weight_in, x_in, g_in, *refs):
    x_mine, g_mine, near, here, theirs, place_out, mix_out, place_other, mix_other, scratch, ids, weight, x, g, sems = refs
    pairs = ((ids_in, ids), (weight_in, weight), (x_in, x), (g_in, g))
    copies = [pltpu.make_async_copy(src, dst, sems.at[i]) for i, (src, dst) in enumerate(pairs)]
    for copy in copies:
        copy.start()
    top, tok = ids.shape
    rows = devices * capacity
    core = lax.axis_index("ffn")
    masks = even_masks(devices)
    masks = [mask + core for mask in masks] + [mask + 1 - core for mask in masks] + [1, 0]
    order = lax.broadcasted_iota(jnp.int32, (devices, tok), 0)
    bits = jnp.zeros((devices, tok), jnp.int32)
    for p, mask in enumerate(masks):
        bits = jnp.where(order == p, mask, bits)
    expert = bits ^ lax.axis_index("expert")
    member = jnp.zeros((devices, tok), jnp.float32)
    mixing = jnp.zeros((devices, tok), jnp.float32)
    copies[0].wait()
    copies[1].wait()
    for route in range(top):
        hit = ids[route : route + 1, :] == expert
        member = jnp.where(hit, 1.0, member)
        mixing = jnp.where(hit, weight[route : route + 1, :], mixing)
    before = lax.broadcasted_iota(jnp.int32, (tok, tok), 0) < lax.broadcasted_iota(jnp.int32, (tok, tok), 1)
    slots = dot(member.astype(jnp.bfloat16), jnp.where(before, 1.0, 0.0).astype(jnp.bfloat16))
    target = jnp.where(member > 0, slots + capacity * order.astype(jnp.float32), -1.0)
    count = devices // 2 - 1

    def placed(first, number):
        row = lax.broadcasted_iota(jnp.int32, (number, tok), 0).astype(jnp.float32) + first
        place = jnp.zeros((number, tok), jnp.float32)
        mix = jnp.zeros((number, tok), jnp.float32)
        for p in range(devices):
            equal = target[p : p + 1, :] == row
            place = jnp.where(equal, 1.0, place)
            mix = jnp.where(equal, mixing[p : p + 1, :], mix)
        row_weight = jnp.broadcast_to(jnp.sum(mix, axis=1, keepdims=True), (number, LANES))
        return place.astype(jnp.bfloat16), row_weight

    low, row_weight = placed(0, rows)
    place_out[...] = low
    mix_out[...] = row_weight
    place_other[...], mix_other[...] = placed(count * capacity, count * capacity)
    size = capacity * subs

    def write(mine, at):
        def block(p):
            return scratch[p * size : (p + 1) * size, :].astype(theirs.dtype)

        for j in range(count):
            part(mine, j * size, size)[...] = block(j)
            part(theirs, (at + j) * size, size)[...] = block(count + j)
        start = size if at else 0
        part(near, start, size)[...] = block(2 * count)
        part(here, start, size)[...] = block(2 * count + 1)

    copies[2].wait()
    for sub in range(subs):
        spread_lanes(scratch, sub, subs, dot(low, x[:, lanes_of(sub)]))
    write(x_mine, 0)
    copies[3].wait()
    for sub in range(subs):
        spread_lanes(scratch, sub, subs, dot(low, g[:, lanes_of(sub)]) * row_weight)
    write(g_mine, count)


def pack_kernel(size, x_mine, g_mine, swapped, *outs):
    count = len(outs)
    for j, out in enumerate(outs):
        for i, mine in enumerate((x_mine, g_mine)):
            part(out, 2 * i * size, size)[...] = part(mine, j * size, size)[...]
            part(out, (2 * i + 1) * size, size)[...] = part(swapped, (i * count + j) * size, size)[...]


def gather_kernel(size, at, *refs):
    blocks, (near, here, out) = refs[:-3], refs[-3:]
    for j, block in enumerate(blocks):
        part(out, 2 * j * size, 2 * size)[...] = part(block, 2 * at, 2 * size)[...]
    part(out, 2 * len(blocks) * size, size)[...] = part(near, at, size)[...]
    part(out, (2 * len(blocks) + 1) * size, size)[...] = part(here, at, size)[...]


def full_rows(devices, subs, scratch, own_sent, other_sent, out):
    size = own_sent.shape[0] // devices
    count = devices // 2 - 1
    own, other = half_starts(out.shape[1] // 2)
    first, second, last = range(0, 2 * count, 2), range(1, 2 * count, 2), range(2 * count, devices)
    layouts = (
        (own, [(own_sent, i) for i in first] + [(other_sent, i) for i in second] + [(own_sent, i) for i in last]),
        (other, [(own_sent, i) for i in second] + [(other_sent, i) for i in first] + [(other_sent, i) for i in last]),
    )
    for start, layout in layouts:

        def put(sub, value):
            out[:, pl.ds(start + sub * LANES, LANES)] = value.astype(out.dtype)

        blocks_to_rows(scratch, [part(ref, i * size, size) for ref, i in layout], put, subs)


def split_terms(count, size, scratch, own_half, keep, send):
    keep[0 : count * size, :] = scratch[0 : count * size, :]
    for j in range(count):
        value = scratch[(count + j) * size : (count + j + 1) * size, :].astype(jnp.bfloat16)
        if isinstance(send, list):
            send[j][...] = value
        else:
            part(send, j * size, size)[...] = value
    rest = scratch[2 * count * size :, :]
    if own_half:
        keep[count * size :, :] = rest
    else:
        send[count * size :, :] = rest.astype(send.dtype)


def early_kernel(size, keep_own, keep_other, came_own, came_other, out):
    for at, keep, came in ((0, keep_own, came_own), (size, keep_other, came_other)):
        total = part(keep, 0, size)[...] + part(came, 0, size)[...].astype(jnp.float32)
        part(out, at, size)[...] = total.astype(out.dtype)


def leave_kernel(size, count, *refs):
    terms, outs = (refs[:4], refs[4 : 7 + count]), refs[8 + count :]
    for which, (keep_own, keep_other, came_own, *came_other) in enumerate(terms):

        def total(keep, came, p):
            return (keep[p * size : (p + 1) * size, :] + came.astype(jnp.float32)).astype(jnp.bfloat16)

        def own(p):
            return total(keep_own, part(came_own, p * size, size)[...], p)

        for j, out in enumerate(outs[:count]):
            if j == 0 and which == 0:
                continue
            at = 2 * size if j and which else 0
            part(out, at, size)[...] = own(j)
            came = came_other[j][...] if which else part(came_other[0], j * size, size)[...]
            part(out, at + size, size)[...] = total(keep_other, came, j)
        part(outs[count], which * size, size)[...] = own(count)
        part(outs[count + 1], which * size, size)[...] = own(count + 1)


def returned_parts(size, early, blocks, which):
    if which:
        return [part(block, 2 * size if j else 0, 2 * size) for j, block in enumerate(blocks)]
    return [part(block, 0, 2 * size) for block in (early, *blocks[1:])]


def share_kernel(size, count, early, *refs):
    blocks, out = refs[:count], refs[-1]
    for which in range(2):
        for j, both in enumerate(returned_parts(size, early, blocks, which)):
            part(out, (2 * j + which) * size, size)[...] = part(both, size, size)[...]


def token_sums(subs, place, mix, scratch, rows, blocks, put):
    size = scratch.shape[0] // len(blocks)
    for p, block in enumerate(blocks):
        here = slice(p * size, (p + 1) * size)
        scratch[here, :] = jnp.zeros((size, LANES), jnp.float32) if block is None else block[...].astype(jnp.float32)
    for sub in range(subs):
        value = scratch[pl.ds(sub, rows.shape[0], stride=subs), :]
        if mix is not None:
            value = value * mix[...]
        rows[:, lanes_of(sub)] = value.astype(rows.dtype)
    for cut in pieces_of(subs * LANES, 512):
        put(cut, contract_rows(place[...], rows[:, cut]))


def join_kernel(count, subs, place, mix, early, *refs):
    blocks, (near, here, out_sum, grad_sum, scratch, rows) = refs[:count], refs[count:]
    size = near.shape[0] // 2
    for which, scale, out in ((0, mix, out_sum), (1, None, grad_sum)):

        def put(cut, total):
            out[:, cut] = total

        first = [part(both, 0, size) for both in returned_parts(size, early, blocks, which)]
        last = [part(near, which * size, size), part(here, which * size, size)]
        token_sums(subs, place, scale, scratch, rows, first + [None] * count + last, put)


def finish_kernel(
    count, subs, place, mix, shared, out_sum, grad_sum, out_tokens, grad_tokens, scratch, rows, low, sems
):
    size = shared.shape[0] // (2 * count)
    copies = []
    work = ((0, mix, out_sum, out_tokens), (size, None, grad_sum, grad_tokens))
    for i, (at, scale, before, out) in enumerate(work):

        def put(cut, total):
            low[i, :, cut] = (before[:, cut] + total).astype(low.dtype)

        blocks = [part(shared, 2 * j * size + at, size) for j in range(count)]
        token_sums(subs, place, scale, scratch, rows, blocks, put)
        copies.append(pltpu.make_async_copy(low.at[i], out, sems.at[i]))
        copies[-1].start()
    for copy in copies:
        copy.wait()


def half_starts(half_width):
    half = lax.axis_index("ffn")
    own = pl.multiple_of(half * half_width, half_width)
    other = pl.multiple_of((1 - half) * half_width, half_width)
    return own, other


def chunk(i, step, base=0):
    return pl.ds(base + pl.multiple_of(i * step, step), step)


def dot(left, right):
    return jnp.dot(left, right, preferred_element_type=jnp.float32)


def halves_of_output(devices, subs, step, scratch, own_half, term, keep, send):
    size = scratch.shape[0] // devices
    for at in range(0, subs * LANES, step):
        value = term(at)
        for i in range(step // LANES):
            spread_lanes(scratch, at // LANES + i, subs, value[:, lanes_of(i)])
    split_terms(devices // 2 - 1, size, scratch, own_half, keep, send)


def forward_kernel(devices, subs, step, x_sent, x_swapped, w_gate, w_up, x_full, gate, up, hidden, scratch):
    full_rows(devices, subs, scratch, x_sent, x_swapped, x_full)
    for cols in pieces_of(gate.shape[1], step):
        gate_low = dot(x_full[...], w_gate[0, :, cols]).astype(jnp.bfloat16)
        up_low = dot(x_full[...], w_up[0, :, cols]).astype(jnp.bfloat16)
        gate[:, cols] = gate_low
        up[:, cols] = up_low
        value = gate_low.astype(jnp.float32)
        hidden[:, cols] = (value * jax.nn.sigmoid(value) * up_low.astype(jnp.float32)).astype(jnp.bfloat16)


def output_kernel(devices, subs, step, hidden, w_down, keep_own, keep_other, send_own, send_other, scratch):
    own, other = half_starts(subs * LANES)

    def term(start):
        return lambda at: dot(hidden[...], w_down[0, :, pl.ds(start + at, step)])

    halves_of_output(devices, subs, step, scratch, False, term(other), keep_other, send_other)
    halves_of_output(devices, subs, step, scratch, True, term(own), keep_own, send_own)


def input_term(step, pre_gate, pre_up, w_gate, w_up, start):
    def term(at):
        there = pl.ds(start + at, step)
        return contract_cols(pre_gate[...], w_gate[0, there, :]) + contract_cols(pre_up[...], w_up[0, there, :])

    return term


def backward_kernel(
    devices,
    subs,
    step,
    g_sent,
    g_swapped,
    gate,
    up,
    w_gate,
    w_up,
    w_down,
    g_full,
    pre_gate,
    pre_up,
    keep_other,
    send_other,
    scratch,
):
    _, other = half_starts(subs * LANES)
    full_rows(devices, subs, scratch, g_sent, g_swapped, g_full)

    def pull(i, carry):
        cols = chunk(i, step)
        low = contract_cols(g_full[...], w_down[0, cols, :]).astype(jnp.bfloat16)
        grad_hidden = low.astype(jnp.float32)
        value = gate[:, cols].astype(jnp.float32)
        sig = jax.nn.sigmoid(value)
        pre_gate[:, cols] = (
            grad_hidden * up[:, cols].astype(jnp.float32) * sig * (1.0 + value * (1.0 - sig))
        ).astype(jnp.bfloat16)
        pre_up[:, cols] = (grad_hidden * value * sig).astype(jnp.bfloat16)
        return carry

    lax.fori_loop(0, gate.shape[1] // step, pull, 0)
    term = input_term(step, pre_gate, pre_up, w_gate, w_up, other)
    halves_of_output(devices, subs, step, scratch, False, term, keep_other, send_other)


def backward_own_kernel(devices, subs, step, pre_gate, pre_up, w_gate, w_up, keep_own, *refs):
    send_own, scratch = list(refs[:-1]), refs[-1]
    own, _ = half_starts(subs * LANES)
    term = input_term(step, pre_gate, pre_up, w_gate, w_up, own)
    halves_of_output(devices, subs, step, scratch, True, term, keep_own, send_own)


def flip(value):
    return value.astype(jnp.float32).T


def pieces_of(total, size):
    return [slice(at, min(at + size, total)) for at in range(0, total, size)]


def gradient_kernel(
    step,
    x,
    g,
    hidden,
    pre_gate,
    pre_up,
    grad_gate,
    grad_up,
    grad_down,
    written,
    flipped,
    turned,
    tall,
    wide,
    tall_sems,
    wide_sems,
):
    written[...] = jnp.zeros_like(written)
    width, lanes = x.shape[1], hidden.shape[1]
    count = width // step
    flipped[...] = flip(hidden[...]).astype(flipped.dtype)

    def wide_copy(i, slot):
        return pltpu.make_async_copy(wide.at[slot], grad_down.at[0, :, chunk(i, step)], wide_sems.at[slot])

    def tall_copy(which, out, i, slot):
        return pltpu.make_async_copy(tall.at[which, slot], out.at[0, chunk(i, step), :], tall_sems.at[which, slot])

    def down(i, carry):
        slot = i % 2

        @pl.when(i >= 2)
        def _():
            wide_copy(i - 2, slot).wait()

        for cut in pieces_of(step, 256):
            right = g[:, chunk(i, step)][:, cut]
            for high in pieces_of(lanes, 256):
                wide[slot, high, cut] = dot(flipped[high, :], right).astype(wide.dtype)
        wide_copy(i, slot).start()
        return carry

    lax.fori_loop(0, count, down, 0)

    def inputs(i, carry):
        slot = i % 2
        turned[...] = flip(x[:, chunk(i, step)]).astype(turned.dtype)
        for which, (right, out) in enumerate(((pre_gate, grad_gate), (pre_up, grad_up))):

            @pl.when(i >= 2)
            def _():
                tall_copy(which, out, i - 2, slot).wait()

            for cut in pieces_of(lanes, 256):
                for high in pieces_of(step, 256):
                    tall[which, slot, high, cut] = dot(turned[high, :], right[:, cut]).astype(tall.dtype)
            tall_copy(which, out, i, slot).start()
        return carry

    lax.fori_loop(0, count, inputs, 0)
    for i in range(max(0, count - 2), count):
        wide_copy(i, i % 2).wait()
        tall_copy(0, grad_gate, i, i % 2).wait()
        tall_copy(1, grad_up, i, i % 2).wait()


def exchange(blocks, masks, devices):
    arrived = []
    for block, mask in zip(blocks, masks):
        pairs = [(2 * i + core, 2 * (i ^ (mask + core)) + core) for i in range(devices) for core in range(2)]
        arrived.append(lax.ppermute(block, ("expert", "ffn"), pairs))
    return arrived


def exchange_near(block, devices):
    return lax.ppermute(block, "expert", [(i, i ^ 1) for i in range(devices)])


def swap(value):
    return lax.ppermute(value, "ffn", [(0, 1), (1, 0)])


def in_hbm(values):
    return [pltpu.with_memory_space_constraint(value, pltpu.HBM) for value in values]


def one_piece_shards(tokens, grad_out, route_ids, route_weight, gate_weight, up_weight, down_weight):
    tok_dev, sub_width = tokens.shape
    top_count = route_ids.shape[1]
    width, lanes = gate_weight.shape[1:]
    devices = lax.axis_size("expert")
    capacity = max(2, min(tok_dev, (9 * tok_dev * top_count + 8 * EXPERTS - 1) // (8 * EXPERTS)))
    rows = devices * capacity
    subs = sub_width // LANES
    low, full = jnp.bfloat16, jnp.float32
    size = capacity * subs
    count = devices // 2 - 1
    spread_scratch = [pltpu.VMEM((devices * size, LANES), full)]
    step = 256
    half_flops = 2 * rows * width * lanes // 2

    def lines(number, dtype=low):
        return jax.ShapeDtypeStruct((number * size, LANES), dtype)

    def lines_in_vmem(number, dtype=low):
        return vmem((number * size, LANES), dtype)

    sources = (route_ids.T, route_weight.T, tokens, grad_out)
    other_rows = count * capacity
    x_mine, g_mine, near, here, theirs, place, mix, place_other, mix_other = call(
        functools.partial(route_kernel, devices, capacity, subs),
        [lines(count), lines(count), lines(2), lines(2)]
        + [lines(2 * count)]
        + [jax.ShapeDtypeStruct((rows, tok_dev), low), jax.ShapeDtypeStruct((rows, LANES), full)]
        + [jax.ShapeDtypeStruct((other_rows, tok_dev), low), jax.ShapeDtypeStruct((other_rows, LANES), full)],
        in_hbm(sources),
        in_spaces=[pl.ANY] * 4,
        scratch=spread_scratch
        + [pltpu.VMEM(value.shape, value.dtype) for value in sources]
        + [pltpu.SemaphoreType.DMA((4,))],
        traffic=4 * tok_dev * sub_width,
    )
    masks = even_masks(devices)
    packed = call(
        functools.partial(pack_kernel, size),
        [lines(4)] * count,
        (x_mine, g_mine, swap(theirs)),
        flops=24 * half_flops,
    )
    arrived = exchange(packed, masks, devices)
    near = exchange_near(near, devices)

    weights = (gate_weight, up_weight, down_weight)
    w_gate, w_up, w_down = [pltpu.with_memory_space_constraint(w, pltpu.VMEM) for w in weights]

    def gather(at):
        return call(functools.partial(gather_kernel, size, at), [lines(devices)], (*arrived, near, here))[0]

    x_sent = gather(0)
    x_swapped = swap(x_sent)
    g_sent = gather(size)
    g_swapped = swap(g_sent)
    terms = [
        lines_in_vmem(count + 2, full),
        lines_in_vmem(count, full),
        lines_in_vmem(count),
        lines_in_vmem(count + 2),
    ]
    x_full, gate, up, hidden = call(
        functools.partial(forward_kernel, devices, subs, step),
        [vmem((rows, width), low)] + [vmem((rows, lanes), low)] * 3,
        (x_sent, x_swapped, w_gate, w_up),
        scratch=spread_scratch,
        flops=4 * half_flops,
    )
    out_own, out_other, send_own, send_other = call(
        functools.partial(output_kernel, devices, subs, 2 * step),
        terms,
        (hidden, w_down),
        scratch=spread_scratch,
        flops=2 * half_flops,
    )
    out_terms = (out_own, out_other, swap(send_other), swap(send_own))
    (early,) = call(functools.partial(early_kernel, size), [lines(2)], out_terms)
    (early,) = exchange([early], masks, devices)
    g_full, pre_gate, pre_up, dx_other, send_other = call(
        functools.partial(backward_kernel, devices, subs, step),
        [vmem((rows, width), low)] + [vmem((rows, lanes), low)] * 2 + [terms[1], terms[3]],
        (g_sent, g_swapped, gate, up, w_gate, w_up, w_down),
        scratch=spread_scratch,
        flops=4 * half_flops,
    )
    came_own = swap(send_other)
    dx_own, *send_own = call(
        functools.partial(backward_own_kernel, devices, subs, step),
        [terms[0]] + [lines_in_vmem(1)] * count,
        (pre_gate, pre_up, w_gate, w_up),
        scratch=spread_scratch,
        flops=2 * half_flops,
    )
    dx_terms = (dx_own, dx_other, came_own, *[swap(value) for value in send_own])
    *leaving, back, kept = call(
        functools.partial(leave_kernel, size, count),
        [lines(2)] + [lines(4)] * (count - 1) + [lines(2)] * 2,
        (*out_terms, *dx_terms, early),
    )
    returned = exchange(leaving, masks, devices)
    back = exchange_near(back, devices)
    cut = 1024 if width % 1024 == 0 else width
    grad_gate, grad_up, grad_down, written = call(
        functools.partial(gradient_kernel, cut),
        [jax.ShapeDtypeStruct(w.shape, low) for w in weights] + [vmem((8, LANES), full)],
        (x_full, g_full, hidden, pre_gate, pre_up),
        out_spaces=[pl.ANY] * 3 + [pltpu.VMEM],
        scratch=[
            pltpu.VMEM((lanes, rows), low),
            pltpu.VMEM((cut, rows), low),
            pltpu.VMEM((2, 2, cut, lanes), low),
            pltpu.VMEM((2, lanes, cut), low),
            pltpu.SemaphoreType.DMA((2, 2)),
            pltpu.SemaphoreType.DMA((2,)),
        ],
        flops=6 * half_flops,
        traffic=sum(w.size * 2 for w in weights),
        limit=32,
    )
    (sharing,) = call(
        functools.partial(share_kernel, size, count), [lines(2 * count)], (early, *returned, back, written)
    )
    shared = swap(sharing)
    sums = call(
        functools.partial(join_kernel, count, subs),
        [vmem((tok_dev, sub_width), full)] * 2,
        (place, mix, early, *returned, back, kept),
        scratch=spread_scratch + [pltpu.VMEM((rows, sub_width), low)],
        flops=4 * rows * tok_dev * sub_width,
    )
    out_tokens, grad_tokens = call(
        functools.partial(finish_kernel, count, subs),
        [jax.ShapeDtypeStruct((tok_dev, sub_width), low)] * 2,
        (place_other, mix_other, shared, *sums),
        out_spaces=[pl.ANY] * 2,
        scratch=[
            pltpu.VMEM((count * size, LANES), full),
            pltpu.VMEM((other_rows, sub_width), low),
            pltpu.VMEM((2, tok_dev, sub_width), low),
            pltpu.SemaphoreType.DMA((2,)),
        ],
        traffic=8 * tok_dev * sub_width,
    )
    return out_tokens, grad_tokens, grad_gate, grad_up, grad_down


def shards(*args):
    tokens, gate_weight = args[0], args[4]
    halves = lax.axis_size("ffn")
    devices = lax.axis_size("expert")
    if halves == 2 and devices >= 4 and devices & (devices - 1) == 0 and tokens.shape[1] * halves == gate_weight.shape[1]:
        return one_piece_shards(*args)
    return general_shards(*args)


def solution(mesh):
    in_specs = (
        P(("groups", "expert"), "ffn"),
        P(("groups", "expert"), "ffn"),
        P(("groups", "expert"), None),
        P(("groups", "expert"), None),
        P("expert", None, "ffn"),
        P("expert", None, "ffn"),
        P("expert", "ffn", None),
    )
    out_specs = (
        P(("groups", "expert"), "ffn"),
        P(("groups", "expert"), "ffn"),
        P(("groups", "expert"), None, "ffn"),
        P(("groups", "expert"), None, "ffn"),
        P(("groups", "expert"), "ffn", None),
    )
    return jax.shard_map(shards, mesh=mesh, in_specs=in_specs, out_specs=out_specs, check_vma=False)
```

```python
import functools

import jax
import jax.numpy as jnp
from jax import lax
from jax.experimental import pallas as pl
from jax.experimental.pallas import tpu as pltpu
from jax.sharding import PartitionSpec as P

EXPERTS = 128
LANES = 128
MIB = 1024 * 1024


def contract_rows(left, right):
    return lax.dot_general(
        left, right, (((0,), (0,)), ((), ())), preferred_element_type=jnp.float32
    )


def contract_cols(left, right):
    return lax.dot_general(
        left, right, (((1,), (1,)), ((), ())), preferred_element_type=jnp.float32
    )


def general_shards(tokens, grad_out, route_ids, route_weight, gate_weight, up_weight, down_weight):
    tokens, grad_out = (
        lax.all_gather(tokens, "ffn", axis=1, tiled=True),
        lax.all_gather(grad_out, "ffn", axis=1, tiled=True),
    )
    tok_dev, width = tokens.shape
    top_count = route_ids.shape[1]
    piece_width = gate_weight.shape[1]
    hidden_half = gate_weight.shape[2]
    pieces = width // piece_width
    devices = lax.axis_size("expert")
    flight = devices // pieces
    halves = lax.axis_size("ffn")
    sub_width = piece_width // halves
    capacity = max(2, min(tok_dev, (9 * tok_dev * top_count + 8 * EXPERTS - 1) // (8 * EXPERTS)))
    total_rows = devices * capacity
    expert_ids = jnp.arange(flight, dtype=jnp.int32)
    member = jnp.zeros((tok_dev, flight), jnp.float32)
    mixing = jnp.zeros((tok_dev, flight), jnp.float32)
    for route in range(top_count):
        hit = (route_ids[:, route : route + 1] == expert_ids[None, :]).astype(jnp.float32)
        member = member + hit
        mixing = mixing + hit * route_weight[:, route : route + 1]
    slots = jnp.cumsum(member, axis=0) - member
    place = member[:, :, None] * (
        slots[:, :, None] == jnp.arange(capacity, dtype=jnp.float32)
    ).astype(jnp.float32)
    weighted = place * mixing[:, :, None]
    place_low = place.astype(jnp.bfloat16)
    x_four = tokens.reshape(tok_dev, halves, pieces, sub_width)
    g_four = grad_out.reshape(tok_dev, halves, pieces, sub_width)
    x_parts = []
    g_parts = []
    for half in range(halves):
        x_parts.append(
            jnp.einsum(
                "Tec,Tjr->ejcr", place_low, x_four[:, half], preferred_element_type=jnp.float32
            )
        )
        g_parts.append(jnp.einsum("Tec,Tjr->ejcr", weighted, g_four[:, half].astype(jnp.float32)))
    x_send = jnp.concatenate(x_parts, axis=3).astype(jnp.bfloat16).reshape(total_rows, piece_width)
    g_send = jnp.concatenate(g_parts, axis=3).astype(jnp.bfloat16).reshape(total_rows, piece_width)

    def return_parts(values):
        arrived = lax.all_to_all(values, "expert", split_axis=0, concat_axis=0, tiled=True)
        lanes = arrived.shape[1]
        return arrived.astype(jnp.float32).reshape(flight, pieces, capacity, lanes).sum(axis=1)

    def spread_rows(values):
        lanes = values.shape[2]
        copies = jnp.broadcast_to(values[:, None], (flight, pieces, capacity, lanes)).reshape(
            total_rows, lanes
        )
        return lax.all_to_all(copies, "expert", split_axis=0, concat_axis=0, tiled=True)

    def finish(term, mix):
        summed = lax.psum_scatter(term, "ffn", scatter_dimension=1, tiled=True)
        back = lax.all_to_all(summed, "expert", split_axis=0, concat_axis=0, tiled=True)
        back = back.reshape(flight, pieces, capacity, sub_width)
        joined = jnp.einsum("Tec,ejcr->Tjr", mix, back)
        return joined.reshape(tok_dev, pieces * sub_width).astype(jnp.bfloat16)

    rows = lax.all_to_all(x_send, "expert", split_axis=0, concat_axis=0, tiled=True)
    w_gate = gate_weight[0]
    w_up = up_weight[0]
    w_down = down_weight[0]
    partial_value = jnp.concatenate(
        [
            jnp.dot(rows, w_gate, preferred_element_type=jnp.float32),
            jnp.dot(rows, w_up, preferred_element_type=jnp.float32),
        ],
        axis=1,
    )
    summed = return_parts(partial_value.astype(jnp.bfloat16))
    gate = summed[:, :, :hidden_half]
    up = summed[:, :, hidden_half:]
    sig = jax.nn.sigmoid(gate)
    act = gate * sig
    hidden = (act * up).astype(jnp.bfloat16)
    h_rows = spread_rows(hidden)
    out_term = jnp.dot(h_rows, w_down, preferred_element_type=jnp.float32)
    out_tokens = finish(out_term, weighted)
    grads = lax.all_to_all(g_send, "expert", split_axis=0, concat_axis=0, tiled=True)
    grad_down = contract_rows(h_rows, grads).astype(jnp.bfloat16)
    hidden_part = contract_cols(grads, w_down).astype(jnp.bfloat16)
    grad_hidden = return_parts(hidden_part)
    pre_gate = (grad_hidden * up * sig * (1.0 + gate * (1.0 - sig))).astype(jnp.bfloat16)
    pre_up = (grad_hidden * act).astype(jnp.bfloat16)
    both = spread_rows(jnp.concatenate([pre_gate, pre_up], axis=2))
    d_gate_rows = both[:, :hidden_half]
    d_up_rows = both[:, hidden_half:]
    grad_gate = contract_rows(rows, d_gate_rows).astype(jnp.bfloat16)
    grad_up = contract_rows(rows, d_up_rows).astype(jnp.bfloat16)
    x_term = contract_cols(d_gate_rows, w_gate) + contract_cols(d_up_rows, w_up)
    grad_tokens = finish(x_term, place)
    return (out_tokens, grad_tokens, grad_gate[None], grad_up[None], grad_down[None])


def vmem(shape, dtype):
    return pltpu.VMEM(shape, dtype)


def call(kernel, out_shape, args, in_spaces=None, out_spaces=None, flops=0, traffic=0, scratch=(), limit=16):
    spaces = in_spaces or [pltpu.VMEM] * len(args)
    outs = out_spaces or [pltpu.VMEM] * len(out_shape)
    return pl.pallas_call(
        kernel,
        out_shape=tuple(out_shape),
        in_specs=[pl.BlockSpec(memory_space=space) for space in spaces],
        out_specs=tuple(pl.BlockSpec(memory_space=space) for space in outs),
        scratch_shapes=list(scratch),
        compiler_params=pltpu.CompilerParams(vmem_limit_bytes=limit * MIB),
        cost_estimate=pl.CostEstimate(flops=flops, bytes_accessed=traffic, transcendentals=0),
    )(*args)


def blocks_to_rows(scratch, blocks, put, subs):
    size = blocks[0].shape[0]
    for p, block in enumerate(blocks):
        scratch[p * size : (p + 1) * size, :] = block[...].astype(jnp.float32)
    for sub in range(subs):
        put(sub, scratch[pl.ds(sub, len(blocks) * size // subs, stride=subs), :])


def spread_lanes(scratch, sub, subs, value):
    scratch[pl.ds(sub, value.shape[0], stride=subs), :] = value


def part(ref, start, count):
    return ref.at[start : start + count, :]


def lanes_of(sub):
    return slice(sub * LANES, (sub + 1) * LANES)


def even_masks(count):
    return [*range(count // 2, count, 2), *range(2, count // 2, 2)]


def route_kernel(devices, capacity, subs, ids_in, weight_in, x_in, g_in, *refs):
    x_mine, g_mine, near, here, theirs, place_out, mix_out, place_other, mix_other, scratch, ids, weight, x, g, sems = refs
    pairs = ((ids_in, ids), (weight_in, weight), (x_in, x), (g_in, g))
    copies = [pltpu.make_async_copy(src, dst, sems.at[i]) for i, (src, dst) in enumerate(pairs)]
    for copy in copies:
        copy.start()
    top, tok = ids.shape
    rows = devices * capacity
    core = lax.axis_index("ffn")
    masks = even_masks(devices)
    masks = [mask + core for mask in masks] + [mask + 1 - core for mask in masks] + [1, 0]
    order = lax.broadcasted_iota(jnp.int32, (devices, tok), 0)
    bits = jnp.zeros((devices, tok), jnp.int32)
    for p, mask in enumerate(masks):
        bits = jnp.where(order == p, mask, bits)
    expert = bits ^ lax.axis_index("expert")
    member = jnp.zeros((devices, tok), jnp.float32)
    mixing = jnp.zeros((devices, tok), jnp.float32)
    copies[0].wait()
    copies[1].wait()
    for route in range(top):
        hit = ids[route : route + 1, :] == expert
        member = jnp.where(hit, 1.0, member)
        mixing = jnp.where(hit, weight[route : route + 1, :], mixing)
    before = lax.broadcasted_iota(jnp.int32, (tok, tok), 0) < lax.broadcasted_iota(jnp.int32, (tok, tok), 1)
    slots = dot(member.astype(jnp.bfloat16), jnp.where(before, 1.0, 0.0).astype(jnp.bfloat16))
    target = jnp.where(member > 0, slots + capacity * order.astype(jnp.float32), -1.0)
    count = devices // 2 - 1

    def placed(first, number):
        row = lax.broadcasted_iota(jnp.int32, (number, tok), 0).astype(jnp.float32) + first
        place = jnp.zeros((number, tok), jnp.float32)
        mix = jnp.zeros((number, tok), jnp.float32)
        for p in range(devices):
            equal = target[p : p + 1, :] == row
            place = jnp.where(equal, 1.0, place)
            mix = jnp.where(equal, mixing[p : p + 1, :], mix)
        row_weight = jnp.broadcast_to(jnp.sum(mix, axis=1, keepdims=True), (number, LANES))
        return place.astype(jnp.bfloat16), row_weight

    low, row_weight = placed(0, rows)
    place_out[...] = low
    mix_out[...] = row_weight
    place_other[...], mix_other[...] = placed(count * capacity, count * capacity)
    size = capacity * subs

    def write(mine, at):
        def block(p):
            return scratch[p * size : (p + 1) * size, :].astype(theirs.dtype)

        for j in range(count):
            part(mine, j * size, size)[...] = block(j)
            part(theirs, (at + j) * size, size)[...] = block(count + j)
        start = size if at else 0
        part(near, start, size)[...] = block(2 * count)
        part(here, start, size)[...] = block(2 * count + 1)

    copies[2].wait()
    for sub in range(subs):
        spread_lanes(scratch, sub, subs, dot(low, x[:, lanes_of(sub)]))
    write(x_mine, 0)
    copies[3].wait()
    for sub in range(subs):
        spread_lanes(scratch, sub, subs, dot(low, g[:, lanes_of(sub)]) * row_weight)
    write(g_mine, count)


def pack_kernel(size, late, x_mine, g_mine, swapped, *outs):
    count = len(outs) - len(late)
    lates = dict(zip(late, outs[count:]))
    for j, out in enumerate(outs[:count]):
        places = ((out, 0), (lates.get(j, out), 0 if j in late else 2 * size))
        for i, (mine, (to, at)) in enumerate(zip((x_mine, g_mine), places)):
            part(to, at, size)[...] = part(mine, j * size, size)[...]
            part(to, at + size, size)[...] = part(swapped, (i * count + j) * size, size)[...]
    for out in lates.values():
        rest = part(out, 2 * size, out.shape[0] - 2 * size)
        rest[...] = jnp.zeros(rest.shape, rest.dtype)


def gather_x_kernel(size, *refs):
    count = (len(refs) - 3) // 2
    blocks, (near, here), outs = refs[:count], refs[count : count + 2], refs[count + 2 :]
    for block, out in zip(blocks, outs):
        out[...] = part(block, 0, 2 * size)[...]
    part(outs[-1], 0, size)[...] = part(near, 0, size)[...]
    part(outs[-1], size, size)[...] = part(here, 0, size)[...]


def gather_g_kernel(size, late, *refs):
    blocks, (near, here, _, out) = refs[:-4], refs[-4:]
    for j, block in enumerate(blocks):
        start = 0 if j in late else 2 * size
        part(out, 2 * j * size, 2 * size)[...] = part(block, start, 2 * size)[...]
    part(out, 2 * len(blocks) * size, size)[...] = part(near, size, size)[...]
    part(out, (2 * len(blocks) + 1) * size, size)[...] = part(here, size, size)[...]


def full_rows(devices, subs, scratch, own_sent, other_sent, out):
    per = devices // len(own_sent)
    size = own_sent[0].shape[0] // per
    count = devices // 2 - 1
    own, other = half_starts(out.shape[1] // 2)
    first, second, last = range(0, 2 * count, 2), range(1, 2 * count, 2), range(2 * count, devices)
    layouts = (
        (own, [(own_sent, i) for i in first] + [(other_sent, i) for i in second] + [(own_sent, i) for i in last]),
        (other, [(own_sent, i) for i in second] + [(other_sent, i) for i in first] + [(other_sent, i) for i in last]),
    )
    for start, layout in layouts:

        def put(sub, value):
            out[:, pl.ds(start + sub * LANES, LANES)] = value.astype(out.dtype)

        blocks_to_rows(scratch, [part(refs[i // per], i % per * size, size) for refs, i in layout], put, subs)


def split_terms(count, size, scratch, own_half, keep, send):
    keep[0 : count * size, :] = scratch[0 : count * size, :]
    send[0 : count * size, :] = scratch[count * size : 2 * count * size, :].astype(send.dtype)
    rest = scratch[2 * count * size :, :]
    if own_half:
        keep[count * size :, :] = rest
    else:
        send[count * size :, :] = rest.astype(send.dtype)


def leave_kernel(size, *refs):
    terms, outs = (refs[:4], refs[4:8]), refs[8:]
    count = len(outs) - 2
    for at, (keep_own, keep_other, came_own, came_other) in zip((0, size), terms):

        def own(p):
            total = part(keep_own, p * size, size)[...] + part(came_own, p * size, size)[...].astype(jnp.float32)
            return total.astype(outs[0].dtype)

        for j, out in enumerate(outs[:count]):
            part(out, at, size)[...] = own(j)
            total = part(keep_other, j * size, size)[...] + part(came_other, j * size, size)[...].astype(jnp.float32)
            part(out, 2 * size + at, size)[...] = total.astype(out.dtype)
        part(outs[count], at, size)[...] = own(count)
        part(outs[count + 1], at, size)[...] = own(count + 1)


def share_kernel(size, *refs):
    blocks, (_, _, out) = refs[:-3], refs[-3:]
    for j, block in enumerate(blocks):
        part(out, 2 * j * size, 2 * size)[...] = part(block, 2 * size, 2 * size)[...]


def token_sums(subs, place, mix, scratch, rows, blocks, put):
    size = scratch.shape[0] // len(blocks)
    for p, block in enumerate(blocks):
        here = slice(p * size, (p + 1) * size)
        scratch[here, :] = jnp.zeros((size, LANES), jnp.float32) if block is None else block[...].astype(jnp.float32)
    for sub in range(subs):
        value = scratch[pl.ds(sub, rows.shape[0], stride=subs), :]
        if mix is not None:
            value = value * mix[...]
        rows[:, lanes_of(sub)] = value.astype(rows.dtype)
    for cut in pieces_of(subs * LANES, 512):
        put(cut, contract_rows(place[...], rows[:, cut]))


def join_kernel(count, subs, place, mix, *refs):
    blocks, (near, here, out_sum, grad_sum, scratch, rows) = refs[:count], refs[count:]
    size = near.shape[0] // 2
    for at, scale, out in ((0, mix, out_sum), (size, None, grad_sum)):

        def put(cut, total):
            out[:, cut] = total

        first = [part(block, at, size) for block in blocks]
        last = [part(near, at, size), part(here, at, size)]
        token_sums(subs, place, scale, scratch, rows, first + [None] * count + last, put)


def finish_kernel(
    count, subs, place, mix, shared, out_sum, grad_sum, out_tokens, grad_tokens, scratch, rows, low, sems
):
    size = shared.shape[0] // (2 * count)
    copies = []
    work = ((0, mix, out_sum, out_tokens), (size, None, grad_sum, grad_tokens))
    for i, (at, scale, before, out) in enumerate(work):

        def put(cut, total):
            low[i, :, cut] = (before[:, cut] + total).astype(low.dtype)

        blocks = [part(shared, 2 * j * size + at, size) for j in range(count)]
        token_sums(subs, place, scale, scratch, rows, blocks, put)
        copies.append(pltpu.make_async_copy(low.at[i], out, sems.at[i]))
        copies[-1].start()
    for copy in copies:
        copy.wait()


def half_starts(half_width):
    half = lax.axis_index("ffn")
    own = pl.multiple_of(half * half_width, half_width)
    other = pl.multiple_of((1 - half) * half_width, half_width)
    return own, other


def chunk(i, step, base=0):
    return pl.ds(base + pl.multiple_of(i * step, step), step)


def dot(left, right):
    return jnp.dot(left, right, preferred_element_type=jnp.float32)


def halves_of_output(devices, subs, step, scratch, own_half, term, keep, send):
    size = scratch.shape[0] // devices
    for at in range(0, subs * LANES, step):
        value = term(at)
        for i in range(step // LANES):
            spread_lanes(scratch, at // LANES + i, subs, value[:, lanes_of(i)])
    split_terms(devices // 2 - 1, size, scratch, own_half, keep, send)


def forward_kernel(devices, subs, step, *refs):
    half = devices // 2
    x_sent, x_swapped = refs[:half], refs[half : 2 * half]
    w_gate, w_up, x_full, gate, up, hidden, scratch = refs[2 * half :]
    full_rows(devices, subs, scratch, x_sent, x_swapped, x_full)
    for cols in pieces_of(gate.shape[1], step):
        gate_low = dot(x_full[...], w_gate[0, :, cols]).astype(jnp.bfloat16)
        up_low = dot(x_full[...], w_up[0, :, cols]).astype(jnp.bfloat16)
        gate[:, cols] = gate_low
        up[:, cols] = up_low
        value = gate_low.astype(jnp.float32)
        hidden[:, cols] = (value * jax.nn.sigmoid(value) * up_low.astype(jnp.float32)).astype(jnp.bfloat16)


def output_kernel(devices, subs, step, hidden, w_down, keep_own, keep_other, send_own, send_other, scratch):
    own, other = half_starts(subs * LANES)

    def term(start):
        return lambda at: dot(hidden[...], w_down[0, :, pl.ds(start + at, step)])

    halves_of_output(devices, subs, step, scratch, False, term(other), keep_other, send_other)
    halves_of_output(devices, subs, step, scratch, True, term(own), keep_own, send_own)


def input_term(step, pre_gate, pre_up, w_gate, w_up, start):
    def term(at):
        there = pl.ds(start + at, step)
        return contract_cols(pre_gate[...], w_gate[0, there, :]) + contract_cols(pre_up[...], w_up[0, there, :])

    return term


def backward_kernel(
    devices,
    subs,
    step,
    g_sent,
    g_swapped,
    gate,
    up,
    w_gate,
    w_up,
    w_down,
    g_full,
    pre_gate,
    pre_up,
    keep_other,
    send_other,
    scratch,
):
    _, other = half_starts(subs * LANES)
    full_rows(devices, subs, scratch, [g_sent], [g_swapped], g_full)

    def pull(i, carry):
        cols = chunk(i, step)
        low = contract_cols(g_full[...], w_down[0, cols, :]).astype(jnp.bfloat16)
        grad_hidden = low.astype(jnp.float32)
        value = gate[:, cols].astype(jnp.float32)
        sig = jax.nn.sigmoid(value)
        pre_gate[:, cols] = (
            grad_hidden * up[:, cols].astype(jnp.float32) * sig * (1.0 + value * (1.0 - sig))
        ).astype(jnp.bfloat16)
        pre_up[:, cols] = (grad_hidden * value * sig).astype(jnp.bfloat16)
        return carry

    lax.fori_loop(0, gate.shape[1] // step, pull, 0)
    term = input_term(step, pre_gate, pre_up, w_gate, w_up, other)
    halves_of_output(devices, subs, step, scratch, False, term, keep_other, send_other)


def backward_own_kernel(devices, subs, step, pre_gate, pre_up, w_gate, w_up, keep_own, send_own, scratch):
    own, _ = half_starts(subs * LANES)
    term = input_term(step, pre_gate, pre_up, w_gate, w_up, own)
    halves_of_output(devices, subs, step, scratch, True, term, keep_own, send_own)


def flip(value):
    return value.astype(jnp.float32).T


def pieces_of(total, size):
    return [slice(at, min(at + size, total)) for at in range(0, total, size)]


def gradient_kernel(
    step,
    x,
    g,
    hidden,
    pre_gate,
    pre_up,
    grad_gate,
    grad_up,
    grad_down,
    written,
    flipped,
    turned,
    tall,
    wide,
    tall_sems,
    wide_sems,
):
    written[...] = jnp.zeros_like(written)
    width, lanes = x.shape[1], hidden.shape[1]
    count = width // step
    flipped[...] = flip(hidden[...]).astype(flipped.dtype)

    def wide_copy(i, slot):
        return pltpu.make_async_copy(wide.at[slot], grad_down.at[0, :, chunk(i, step)], wide_sems.at[slot])

    def tall_copy(which, out, i, slot):
        return pltpu.make_async_copy(tall.at[which, slot], out.at[0, chunk(i, step), :], tall_sems.at[which, slot])

    def down(i, carry):
        slot = i % 2

        @pl.when(i >= 2)
        def _():
            wide_copy(i - 2, slot).wait()

        for cut in pieces_of(step, 256):
            right = g[:, chunk(i, step)][:, cut]
            for high in pieces_of(lanes, 256):
                wide[slot, high, cut] = dot(flipped[high, :], right).astype(wide.dtype)
        wide_copy(i, slot).start()
        return carry

    lax.fori_loop(0, count, down, 0)

    def inputs(i, carry):
        slot = i % 2
        turned[...] = flip(x[:, chunk(i, step)]).astype(turned.dtype)
        for which, (right, out) in enumerate(((pre_gate, grad_gate), (pre_up, grad_up))):

            @pl.when(i >= 2)
            def _():
                tall_copy(which, out, i - 2, slot).wait()

            for cut in pieces_of(lanes, 256):
                for high in pieces_of(step, 256):
                    tall[which, slot, high, cut] = dot(turned[high, :], right[:, cut]).astype(tall.dtype)
            tall_copy(which, out, i, slot).start()
        return carry

    lax.fori_loop(0, count, inputs, 0)
    for i in range(max(0, count - 2), count):
        wide_copy(i, i % 2).wait()
        tall_copy(0, grad_gate, i, i % 2).wait()
        tall_copy(1, grad_up, i, i % 2).wait()


def exchange(blocks, masks, devices):
    arrived = []
    for block, mask in zip(blocks, masks):
        pairs = [(2 * i + core, 2 * (i ^ (mask + core)) + core) for i in range(devices) for core in range(2)]
        arrived.append(lax.ppermute(block, ("expert", "ffn"), pairs))
    return arrived


def exchange_near(block, devices):
    return lax.ppermute(block, "expert", [(i, i ^ 1) for i in range(devices)])


def swap(value):
    return lax.ppermute(value, "ffn", [(0, 1), (1, 0)])


def in_hbm(values):
    return [pltpu.with_memory_space_constraint(value, pltpu.HBM) for value in values]


def one_piece_shards(tokens, grad_out, route_ids, route_weight, gate_weight, up_weight, down_weight):
    tok_dev, sub_width = tokens.shape
    top_count = route_ids.shape[1]
    width, lanes = gate_weight.shape[1:]
    devices = lax.axis_size("expert")
    capacity = max(2, min(tok_dev, (9 * tok_dev * top_count + 8 * EXPERTS - 1) // (8 * EXPERTS)))
    rows = devices * capacity
    subs = sub_width // LANES
    low, full = jnp.bfloat16, jnp.float32
    size = capacity * subs
    count = devices // 2 - 1
    spread_scratch = [pltpu.VMEM((devices * size, LANES), full)]
    step = 256
    half_flops = 2 * rows * width * lanes // 2

    def lines(number, dtype=low):
        return jax.ShapeDtypeStruct((number * size, LANES), dtype)

    def lines_in_vmem(number, dtype=low):
        return vmem((number * size, LANES), dtype)

    sources = (route_ids.T, route_weight.T, tokens, grad_out)
    other_rows = count * capacity
    x_mine, g_mine, near, here, theirs, place, mix, place_other, mix_other = call(
        functools.partial(route_kernel, devices, capacity, subs),
        [lines(count), lines(count), lines(2), lines(2)]
        + [lines(2 * count)]
        + [jax.ShapeDtypeStruct((rows, tok_dev), low), jax.ShapeDtypeStruct((rows, LANES), full)]
        + [jax.ShapeDtypeStruct((other_rows, tok_dev), low), jax.ShapeDtypeStruct((other_rows, LANES), full)],
        in_hbm(sources),
        in_spaces=[pl.ANY] * 4,
        scratch=spread_scratch
        + [pltpu.VMEM(value.shape, value.dtype) for value in sources]
        + [pltpu.SemaphoreType.DMA((4,))],
        traffic=4 * tok_dev * sub_width,
    )
    masks = even_masks(devices)
    late = [devices // 4 - 1]
    late_block = jax.ShapeDtypeStruct((2 * size + 16, LANES), low)
    packed = call(
        functools.partial(pack_kernel, size, late),
        [lines(2 if j in late else 4) for j in range(count)] + [late_block] * len(late),
        (x_mine, g_mine, swap(theirs)),
        flops=24 * half_flops,
    )
    x_arrived = exchange(packed[:count], masks, devices)
    g_arrived = list(x_arrived)
    for j, block in zip(late, packed[count:]):
        (g_arrived[j],) = exchange([block], masks[j:], devices)
    near = exchange_near(near, devices)

    weights = (gate_weight, up_weight, down_weight)
    w_gate, w_up, w_down = [pltpu.with_memory_space_constraint(w, pltpu.VMEM) for w in weights]

    x_sent = call(
        functools.partial(gather_x_kernel, size), [lines(2)] * (count + 1), (*x_arrived, near, here)
    )
    x_swapped = [swap(value) for value in x_sent]
    terms = [
        lines_in_vmem(count + 2, full),
        lines_in_vmem(count, full),
        lines_in_vmem(count),
        lines_in_vmem(count + 2),
    ]
    x_full, gate, up, hidden = call(
        functools.partial(forward_kernel, devices, subs, step),
        [vmem((rows, width), low)] + [vmem((rows, lanes), low)] * 3,
        (*x_sent, *x_swapped, w_gate, w_up),
        scratch=spread_scratch,
    )
    (g_sent,) = call(
        functools.partial(gather_g_kernel, size, late), [lines(devices)], (*g_arrived, near, here, hidden)
    )
    g_swapped = swap(g_sent)
    out_own, out_other, send_own, send_other = call(
        functools.partial(output_kernel, devices, subs, 2 * step),
        terms,
        (hidden, w_down),
        scratch=spread_scratch,
        flops=2 * half_flops,
    )
    out_terms = (out_own, out_other, swap(send_other), swap(send_own))
    g_full, pre_gate, pre_up, dx_other, send_other = call(
        functools.partial(backward_kernel, devices, subs, step),
        [vmem((rows, width), low)] + [vmem((rows, lanes), low)] * 2 + [terms[1], terms[3]],
        (g_sent, g_swapped, gate, up, w_gate, w_up, w_down),
        scratch=spread_scratch,
        flops=4 * half_flops,
    )
    came_own = swap(send_other)
    dx_own, send_own = call(
        functools.partial(backward_own_kernel, devices, subs, step),
        [terms[0], terms[2]],
        (pre_gate, pre_up, w_gate, w_up),
        scratch=spread_scratch,
        flops=2 * half_flops,
    )
    dx_terms = (dx_own, dx_other, came_own, swap(send_own))
    *leaving, back, kept = call(
        functools.partial(leave_kernel, size),
        [lines(4)] * count + [lines(2)] * 2,
        (*out_terms, *dx_terms),
    )
    returned = exchange(leaving, masks, devices)
    back = exchange_near(back, devices)
    cut = 1024 if width % 1024 == 0 else width
    grad_gate, grad_up, grad_down, written = call(
        functools.partial(gradient_kernel, cut),
        [jax.ShapeDtypeStruct(w.shape, low) for w in weights] + [vmem((8, LANES), full)],
        (x_full, g_full, hidden, pre_gate, pre_up),
        out_spaces=[pl.ANY] * 3 + [pltpu.VMEM],
        scratch=[
            pltpu.VMEM((lanes, rows), low),
            pltpu.VMEM((cut, rows), low),
            pltpu.VMEM((2, 2, cut, lanes), low),
            pltpu.VMEM((2, lanes, cut), low),
            pltpu.SemaphoreType.DMA((2, 2)),
            pltpu.SemaphoreType.DMA((2,)),
        ],
        flops=6 * half_flops,
        traffic=sum(w.size * 2 for w in weights),
        limit=32,
    )
    (sharing,) = call(functools.partial(share_kernel, size), [lines(2 * count)], (*returned, back, written))
    shared = swap(sharing)
    sums = call(
        functools.partial(join_kernel, count, subs),
        [vmem((tok_dev, sub_width), full)] * 2,
        (place, mix, *returned, back, kept),
        scratch=spread_scratch + [pltpu.VMEM((rows, sub_width), low)],
        flops=4 * rows * tok_dev * sub_width,
    )
    out_tokens, grad_tokens = call(
        functools.partial(finish_kernel, count, subs),
        [jax.ShapeDtypeStruct((tok_dev, sub_width), low)] * 2,
        (place_other, mix_other, shared, *sums),
        out_spaces=[pl.ANY] * 2,
        scratch=[
            pltpu.VMEM((count * size, LANES), full),
            pltpu.VMEM((other_rows, sub_width), low),
            pltpu.VMEM((2, tok_dev, sub_width), low),
            pltpu.SemaphoreType.DMA((2,)),
        ],
        traffic=8 * tok_dev * sub_width,
    )
    return out_tokens, grad_tokens, grad_gate, grad_up, grad_down


def shards(*args):
    tokens, gate_weight = args[0], args[4]
    halves = lax.axis_size("ffn")
    devices = lax.axis_size("expert")
    if halves == 2 and devices >= 4 and devices & (devices - 1) == 0 and tokens.shape[1] * halves == gate_weight.shape[1]:
        return one_piece_shards(*args)
    return general_shards(*args)


def solution(mesh):
    in_specs = (
        P(("groups", "expert"), "ffn"),
        P(("groups", "expert"), "ffn"),
        P(("groups", "expert"), None),
        P(("groups", "expert"), None),
        P("expert", None, "ffn"),
        P("expert", None, "ffn"),
        P("expert", "ffn", None),
    )
    out_specs = (
        P(("groups", "expert"), "ffn"),
        P(("groups", "expert"), "ffn"),
        P(("groups", "expert"), None, "ffn"),
        P(("groups", "expert"), None, "ffn"),
        P(("groups", "expert"), "ffn", None),
    )
    return jax.shard_map(shards, mesh=mesh, in_specs=in_specs, out_specs=out_specs, check_vma=False)
```

```python
import functools

import jax
import jax.numpy as jnp
from jax import lax
from jax.experimental import pallas as pl
from jax.experimental.pallas import tpu as pltpu
from jax.sharding import PartitionSpec as P

EXPERTS = 128
LANES = 128
MIB = 1024 * 1024


def contract_rows(left, right):
    return lax.dot_general(
        left, right, (((0,), (0,)), ((), ())), preferred_element_type=jnp.float32
    )


def contract_cols(left, right):
    return lax.dot_general(
        left, right, (((1,), (1,)), ((), ())), preferred_element_type=jnp.float32
    )


def general_shards(tokens, grad_out, route_ids, route_weight, gate_weight, up_weight, down_weight):
    tokens, grad_out = (
        lax.all_gather(tokens, "ffn", axis=1, tiled=True),
        lax.all_gather(grad_out, "ffn", axis=1, tiled=True),
    )
    tok_dev, width = tokens.shape
    top_count = route_ids.shape[1]
    piece_width = gate_weight.shape[1]
    hidden_half = gate_weight.shape[2]
    pieces = width // piece_width
    devices = lax.axis_size("expert")
    flight = devices // pieces
    halves = lax.axis_size("ffn")
    sub_width = piece_width // halves
    capacity = max(2, min(tok_dev, (9 * tok_dev * top_count + 8 * EXPERTS - 1) // (8 * EXPERTS)))
    total_rows = devices * capacity
    expert_ids = jnp.arange(flight, dtype=jnp.int32)
    member = jnp.zeros((tok_dev, flight), jnp.float32)
    mixing = jnp.zeros((tok_dev, flight), jnp.float32)
    for route in range(top_count):
        hit = (route_ids[:, route : route + 1] == expert_ids[None, :]).astype(jnp.float32)
        member = member + hit
        mixing = mixing + hit * route_weight[:, route : route + 1]
    slots = jnp.cumsum(member, axis=0) - member
    place = member[:, :, None] * (
        slots[:, :, None] == jnp.arange(capacity, dtype=jnp.float32)
    ).astype(jnp.float32)
    weighted = place * mixing[:, :, None]
    place_low = place.astype(jnp.bfloat16)
    x_four = tokens.reshape(tok_dev, halves, pieces, sub_width)
    g_four = grad_out.reshape(tok_dev, halves, pieces, sub_width)
    x_parts = []
    g_parts = []
    for half in range(halves):
        x_parts.append(
            jnp.einsum(
                "Tec,Tjr->ejcr", place_low, x_four[:, half], preferred_element_type=jnp.float32
            )
        )
        g_parts.append(jnp.einsum("Tec,Tjr->ejcr", weighted, g_four[:, half].astype(jnp.float32)))
    x_send = jnp.concatenate(x_parts, axis=3).astype(jnp.bfloat16).reshape(total_rows, piece_width)
    g_send = jnp.concatenate(g_parts, axis=3).astype(jnp.bfloat16).reshape(total_rows, piece_width)

    def return_parts(values):
        arrived = lax.all_to_all(values, "expert", split_axis=0, concat_axis=0, tiled=True)
        lanes = arrived.shape[1]
        return arrived.astype(jnp.float32).reshape(flight, pieces, capacity, lanes).sum(axis=1)

    def spread_rows(values):
        lanes = values.shape[2]
        copies = jnp.broadcast_to(values[:, None], (flight, pieces, capacity, lanes)).reshape(
            total_rows, lanes
        )
        return lax.all_to_all(copies, "expert", split_axis=0, concat_axis=0, tiled=True)

    def finish(term, mix):
        summed = lax.psum_scatter(term, "ffn", scatter_dimension=1, tiled=True)
        back = lax.all_to_all(summed, "expert", split_axis=0, concat_axis=0, tiled=True)
        back = back.reshape(flight, pieces, capacity, sub_width)
        joined = jnp.einsum("Tec,ejcr->Tjr", mix, back)
        return joined.reshape(tok_dev, pieces * sub_width).astype(jnp.bfloat16)

    rows = lax.all_to_all(x_send, "expert", split_axis=0, concat_axis=0, tiled=True)
    w_gate = gate_weight[0]
    w_up = up_weight[0]
    w_down = down_weight[0]
    partial_value = jnp.concatenate(
        [
            jnp.dot(rows, w_gate, preferred_element_type=jnp.float32),
            jnp.dot(rows, w_up, preferred_element_type=jnp.float32),
        ],
        axis=1,
    )
    summed = return_parts(partial_value.astype(jnp.bfloat16))
    gate = summed[:, :, :hidden_half]
    up = summed[:, :, hidden_half:]
    sig = jax.nn.sigmoid(gate)
    act = gate * sig
    hidden = (act * up).astype(jnp.bfloat16)
    h_rows = spread_rows(hidden)
    out_term = jnp.dot(h_rows, w_down, preferred_element_type=jnp.float32)
    out_tokens = finish(out_term, weighted)
    grads = lax.all_to_all(g_send, "expert", split_axis=0, concat_axis=0, tiled=True)
    grad_down = contract_rows(h_rows, grads).astype(jnp.bfloat16)
    hidden_part = contract_cols(grads, w_down).astype(jnp.bfloat16)
    grad_hidden = return_parts(hidden_part)
    pre_gate = (grad_hidden * up * sig * (1.0 + gate * (1.0 - sig))).astype(jnp.bfloat16)
    pre_up = (grad_hidden * act).astype(jnp.bfloat16)
    both = spread_rows(jnp.concatenate([pre_gate, pre_up], axis=2))
    d_gate_rows = both[:, :hidden_half]
    d_up_rows = both[:, hidden_half:]
    grad_gate = contract_rows(rows, d_gate_rows).astype(jnp.bfloat16)
    grad_up = contract_rows(rows, d_up_rows).astype(jnp.bfloat16)
    x_term = contract_cols(d_gate_rows, w_gate) + contract_cols(d_up_rows, w_up)
    grad_tokens = finish(x_term, place)
    return (out_tokens, grad_tokens, grad_gate[None], grad_up[None], grad_down[None])


def vmem(shape, dtype):
    return pltpu.VMEM(shape, dtype)


def call(kernel, out_shape, args, in_spaces=None, out_spaces=None, flops=0, traffic=0, scratch=(), limit=16):
    spaces = in_spaces or [pltpu.VMEM] * len(args)
    outs = out_spaces or [pltpu.VMEM] * len(out_shape)
    return pl.pallas_call(
        kernel,
        out_shape=tuple(out_shape),
        in_specs=[pl.BlockSpec(memory_space=space) for space in spaces],
        out_specs=tuple(pl.BlockSpec(memory_space=space) for space in outs),
        scratch_shapes=list(scratch),
        compiler_params=pltpu.CompilerParams(vmem_limit_bytes=limit * MIB),
        cost_estimate=pl.CostEstimate(flops=flops, bytes_accessed=traffic, transcendentals=0),
    )(*args)


def blocks_to_rows(scratch, blocks, put, subs):
    size = blocks[0].shape[0]
    for p, block in enumerate(blocks):
        scratch[p * size : (p + 1) * size, :] = block[...].astype(jnp.float32)
    for sub in range(subs):
        put(sub, scratch[pl.ds(sub, len(blocks) * size // subs, stride=subs), :])


def spread_lanes(scratch, sub, subs, value):
    scratch[pl.ds(sub, value.shape[0], stride=subs), :] = value


def part(ref, start, count):
    return ref.at[start : start + count, :]


def lanes_of(sub):
    return slice(sub * LANES, (sub + 1) * LANES)


def even_masks(count):
    return [*reversed(range(count // 2, count, 2)), *range(2, count // 2, 2)]


def route_kernel(devices, capacity, subs, ids_in, weight_in, x_in, g_in, *refs):
    x_mine, g_mine, near, here, theirs, place_out, mix_out, place_other, mix_other, scratch, ids, weight, x, g, sems = refs
    pairs = ((ids_in, ids), (weight_in, weight), (x_in, x), (g_in, g))
    copies = [pltpu.make_async_copy(src, dst, sems.at[i]) for i, (src, dst) in enumerate(pairs)]
    for copy in copies:
        copy.start()
    top, tok = ids.shape
    rows = devices * capacity
    core = lax.axis_index("ffn")
    masks = even_masks(devices)
    masks = [mask + core for mask in masks] + [mask + 1 - core for mask in masks] + [1, 0]
    order = lax.broadcasted_iota(jnp.int32, (devices, tok), 0)
    bits = jnp.zeros((devices, tok), jnp.int32)
    for p, mask in enumerate(masks):
        bits = jnp.where(order == p, mask, bits)
    expert = bits ^ lax.axis_index("expert")
    member = jnp.zeros((devices, tok), jnp.float32)
    mixing = jnp.zeros((devices, tok), jnp.float32)
    copies[0].wait()
    copies[1].wait()
    for route in range(top):
        hit = ids[route : route + 1, :] == expert
        member = jnp.where(hit, 1.0, member)
        mixing = jnp.where(hit, weight[route : route + 1, :], mixing)
    before = lax.broadcasted_iota(jnp.int32, (tok, tok), 0) < lax.broadcasted_iota(jnp.int32, (tok, tok), 1)
    slots = dot(member.astype(jnp.bfloat16), jnp.where(before, 1.0, 0.0).astype(jnp.bfloat16))
    target = jnp.where(member > 0, slots + capacity * order.astype(jnp.float32), -1.0)
    count = devices // 2 - 1

    def placed(first, number):
        row = lax.broadcasted_iota(jnp.int32, (number, tok), 0).astype(jnp.float32) + first
        place = jnp.zeros((number, tok), jnp.float32)
        mix = jnp.zeros((number, tok), jnp.float32)
        for p in range(devices):
            equal = target[p : p + 1, :] == row
            place = jnp.where(equal, 1.0, place)
            mix = jnp.where(equal, mixing[p : p + 1, :], mix)
        row_weight = jnp.broadcast_to(jnp.sum(mix, axis=1, keepdims=True), (number, LANES))
        return place.astype(jnp.bfloat16), row_weight

    low, row_weight = placed(0, rows)
    place_out[...] = low
    mix_out[...] = row_weight
    place_other[...], mix_other[...] = placed(count * capacity, count * capacity)
    size = capacity * subs

    def write(mine, at):
        def block(p):
            return scratch[p * size : (p + 1) * size, :].astype(theirs.dtype)

        for j in range(count):
            part(mine, j * size, size)[...] = block(j)
            part(theirs, (at + j) * size, size)[...] = block(count + j)
        start = size if at else 0
        part(near, start, size)[...] = block(2 * count)
        part(here, start, size)[...] = block(2 * count + 1)

    copies[2].wait()
    for sub in range(subs):
        spread_lanes(scratch, sub, subs, dot(low, x[:, lanes_of(sub)]))
    write(x_mine, 0)
    copies[3].wait()
    for sub in range(subs):
        spread_lanes(scratch, sub, subs, dot(low, g[:, lanes_of(sub)]) * row_weight)
    write(g_mine, count)


def pack_kernel(size, late, x_mine, g_mine, swapped, *outs):
    count = len(outs) - len(late)
    lates = dict(zip(late, outs[count:]))
    for j, out in enumerate(outs[:count]):
        places = ((out, 0), (lates.get(j, out), 0 if j in late else 2 * size))
        for i, (mine, (to, at)) in enumerate(zip((x_mine, g_mine), places)):
            part(to, at, size)[...] = part(mine, j * size, size)[...]
            part(to, at + size, size)[...] = part(swapped, (i * count + j) * size, size)[...]
    for out in [*lates.values(), *[outs[j] for j in late]]:
        rest = part(out, 2 * size, out.shape[0] - 2 * size)
        rest[...] = jnp.zeros(rest.shape, rest.dtype)


def gather_x_kernel(size, *refs):
    count = (len(refs) - 3) // 2
    blocks, (near, here), outs = refs[:count], refs[count : count + 2], refs[count + 2 :]
    for block, out in zip(blocks, outs):
        out[...] = part(block, 0, 2 * size)[...]
    part(outs[-1], 0, size)[...] = part(near, 0, size)[...]
    part(outs[-1], size, size)[...] = part(here, 0, size)[...]


def gather_g_kernel(size, late, *refs):
    blocks, (near, here, _, out) = refs[:-4], refs[-4:]
    for j, block in enumerate(blocks):
        start = 0 if j in late else 2 * size
        part(out, 2 * j * size, 2 * size)[...] = part(block, start, 2 * size)[...]
    part(out, 2 * len(blocks) * size, size)[...] = part(near, size, size)[...]
    part(out, (2 * len(blocks) + 1) * size, size)[...] = part(here, size, size)[...]


def full_rows(devices, subs, scratch, own_sent, other_sent, out):
    per = devices // len(own_sent)
    size = own_sent[0].shape[0] // per
    count = devices // 2 - 1
    own, other = half_starts(out.shape[1] // 2)
    first, second, last = range(0, 2 * count, 2), range(1, 2 * count, 2), range(2 * count, devices)
    layouts = (
        (own, [(own_sent, i) for i in first] + [(other_sent, i) for i in second] + [(own_sent, i) for i in last]),
        (other, [(own_sent, i) for i in second] + [(other_sent, i) for i in first] + [(other_sent, i) for i in last]),
    )
    for start, layout in layouts:

        def put(sub, value):
            out[:, pl.ds(start + sub * LANES, LANES)] = value.astype(out.dtype)

        blocks_to_rows(scratch, [part(refs[i // per], i % per * size, size) for refs, i in layout], put, subs)


def split_terms(count, size, scratch, own_half, keep, send):
    keep[0 : count * size, :] = scratch[0 : count * size, :]
    send[0 : count * size, :] = scratch[count * size : 2 * count * size, :].astype(send.dtype)
    rest = scratch[2 * count * size :, :]
    if own_half:
        keep[count * size :, :] = rest
    else:
        send[count * size :, :] = rest.astype(send.dtype)


def leave_kernel(size, *refs):
    terms, outs = (refs[:4], refs[4:8]), refs[8:]
    count = len(outs) - 2
    for at, (keep_own, keep_other, came_own, came_other) in zip((0, size), terms):

        def own(p):
            total = part(keep_own, p * size, size)[...] + part(came_own, p * size, size)[...].astype(jnp.float32)
            return total.astype(outs[0].dtype)

        for j, out in enumerate(outs[:count]):
            part(out, at, size)[...] = own(j)
            total = part(keep_other, j * size, size)[...] + part(came_other, j * size, size)[...].astype(jnp.float32)
            part(out, 2 * size + at, size)[...] = total.astype(out.dtype)
        part(outs[count], at, size)[...] = own(count)
        part(outs[count + 1], at, size)[...] = own(count + 1)


def share_kernel(size, *refs):
    blocks, (_, _, out) = refs[:-3], refs[-3:]
    for j, block in enumerate(blocks):
        part(out, 2 * j * size, 2 * size)[...] = part(block, 2 * size, 2 * size)[...]


def token_sums(subs, place, mix, scratch, rows, blocks, put):
    size = scratch.shape[0] // len(blocks)
    for p, block in enumerate(blocks):
        here = slice(p * size, (p + 1) * size)
        scratch[here, :] = jnp.zeros((size, LANES), jnp.float32) if block is None else block[...].astype(jnp.float32)
    for sub in range(subs):
        value = scratch[pl.ds(sub, rows.shape[0], stride=subs), :]
        if mix is not None:
            value = value * mix[...]
        rows[:, lanes_of(sub)] = value.astype(rows.dtype)
    for cut in pieces_of(subs * LANES, 512):
        put(cut, contract_rows(place[...], rows[:, cut]))


def join_kernel(count, subs, place, mix, *refs):
    blocks, (near, here, out_sum, grad_sum, scratch, rows) = refs[:count], refs[count:]
    size = near.shape[0] // 2
    for at, scale, out in ((0, mix, out_sum), (size, None, grad_sum)):

        def put(cut, total):
            out[:, cut] = total

        first = [part(block, at, size) for block in blocks]
        last = [part(near, at, size), part(here, at, size)]
        token_sums(subs, place, scale, scratch, rows, first + [None] * count + last, put)


def finish_kernel(
    count, subs, place, mix, shared, out_sum, grad_sum, out_tokens, grad_tokens, scratch, rows, low, sems
):
    size = shared.shape[0] // (2 * count)
    copies = []
    work = ((0, mix, out_sum, out_tokens), (size, None, grad_sum, grad_tokens))
    for i, (at, scale, before, out) in enumerate(work):

        def put(cut, total):
            low[i, :, cut] = (before[:, cut] + total).astype(low.dtype)

        blocks = [part(shared, 2 * j * size + at, size) for j in range(count)]
        token_sums(subs, place, scale, scratch, rows, blocks, put)
        copies.append(pltpu.make_async_copy(low.at[i], out, sems.at[i]))
        copies[-1].start()
    for copy in copies:
        copy.wait()


def half_starts(half_width):
    half = lax.axis_index("ffn")
    own = pl.multiple_of(half * half_width, half_width)
    other = pl.multiple_of((1 - half) * half_width, half_width)
    return own, other


def chunk(i, step, base=0):
    return pl.ds(base + pl.multiple_of(i * step, step), step)


def dot(left, right):
    return jnp.dot(left, right, preferred_element_type=jnp.float32)


def halves_of_output(devices, subs, step, scratch, own_half, term, keep, send):
    size = scratch.shape[0] // devices
    for at in range(0, subs * LANES, step):
        value = term(at)
        for i in range(step // LANES):
            spread_lanes(scratch, at // LANES + i, subs, value[:, lanes_of(i)])
    split_terms(devices // 2 - 1, size, scratch, own_half, keep, send)


def forward_kernel(devices, subs, step, *refs):
    half = devices // 2
    x_sent, x_swapped = refs[:half], refs[half : 2 * half]
    w_gate, w_up, x_full, gate, up, hidden, scratch = refs[2 * half :]
    full_rows(devices, subs, scratch, x_sent, x_swapped, x_full)
    for cols in pieces_of(gate.shape[1], step):
        gate_low = dot(x_full[...], w_gate[0, :, cols]).astype(jnp.bfloat16)
        up_low = dot(x_full[...], w_up[0, :, cols]).astype(jnp.bfloat16)
        gate[:, cols] = gate_low
        up[:, cols] = up_low
        value = gate_low.astype(jnp.float32)
        hidden[:, cols] = (value * jax.nn.sigmoid(value) * up_low.astype(jnp.float32)).astype(jnp.bfloat16)


def output_kernel(devices, subs, step, hidden, w_down, keep_own, keep_other, send_own, send_other, scratch):
    own, other = half_starts(subs * LANES)

    def term(start):
        return lambda at: dot(hidden[...], w_down[0, :, pl.ds(start + at, step)])

    halves_of_output(devices, subs, step, scratch, False, term(other), keep_other, send_other)
    halves_of_output(devices, subs, step, scratch, True, term(own), keep_own, send_own)


def input_term(step, pre_gate, pre_up, w_gate, w_up, start):
    def term(at):
        there = pl.ds(start + at, step)
        return contract_cols(pre_gate[...], w_gate[0, there, :]) + contract_cols(pre_up[...], w_up[0, there, :])

    return term


def backward_kernel(
    devices,
    subs,
    step,
    g_sent,
    g_swapped,
    gate,
    up,
    w_gate,
    w_up,
    w_down,
    g_full,
    pre_gate,
    pre_up,
    keep_other,
    send_other,
    scratch,
):
    _, other = half_starts(subs * LANES)
    full_rows(devices, subs, scratch, [g_sent], [g_swapped], g_full)

    def pull(i, carry):
        cols = chunk(i, step)
        low = contract_cols(g_full[...], w_down[0, cols, :]).astype(jnp.bfloat16)
        grad_hidden = low.astype(jnp.float32)
        value = gate[:, cols].astype(jnp.float32)
        sig = jax.nn.sigmoid(value)
        pre_gate[:, cols] = (
            grad_hidden * up[:, cols].astype(jnp.float32) * sig * (1.0 + value * (1.0 - sig))
        ).astype(jnp.bfloat16)
        pre_up[:, cols] = (grad_hidden * value * sig).astype(jnp.bfloat16)
        return carry

    lax.fori_loop(0, gate.shape[1] // step, pull, 0)
    term = input_term(step, pre_gate, pre_up, w_gate, w_up, other)
    halves_of_output(devices, subs, step, scratch, False, term, keep_other, send_other)


def backward_own_kernel(devices, subs, step, pre_gate, pre_up, w_gate, w_up, keep_own, send_own, scratch):
    own, _ = half_starts(subs * LANES)
    term = input_term(step, pre_gate, pre_up, w_gate, w_up, own)
    halves_of_output(devices, subs, step, scratch, True, term, keep_own, send_own)


def flip(value):
    return value.astype(jnp.float32).T


def pieces_of(total, size):
    return [slice(at, min(at + size, total)) for at in range(0, total, size)]


def gradient_kernel(
    step,
    x,
    g,
    hidden,
    pre_gate,
    pre_up,
    grad_gate,
    grad_up,
    grad_down,
    written,
    flipped,
    turned,
    tall,
    wide,
    tall_sems,
    wide_sems,
):
    written[...] = jnp.zeros_like(written)
    width, lanes = x.shape[1], hidden.shape[1]
    count = width // step
    flipped[...] = flip(hidden[...]).astype(flipped.dtype)

    def wide_copy(i, slot):
        return pltpu.make_async_copy(wide.at[slot], grad_down.at[0, :, chunk(i, step)], wide_sems.at[slot])

    def tall_copy(which, out, i, slot):
        return pltpu.make_async_copy(tall.at[which, slot], out.at[0, chunk(i, step), :], tall_sems.at[which, slot])

    def down(i, carry):
        slot = i % 2

        @pl.when(i >= 2)
        def _():
            wide_copy(i - 2, slot).wait()

        for cut in pieces_of(step, 256):
            right = g[:, chunk(i, step)][:, cut]
            for high in pieces_of(lanes, 256):
                wide[slot, high, cut] = dot(flipped[high, :], right).astype(wide.dtype)
        wide_copy(i, slot).start()
        return carry

    lax.fori_loop(0, count, down, 0)

    def inputs(i, carry):
        slot = i % 2
        turned[...] = flip(x[:, chunk(i, step)]).astype(turned.dtype)
        for which, (right, out) in enumerate(((pre_gate, grad_gate), (pre_up, grad_up))):

            @pl.when(i >= 2)
            def _():
                tall_copy(which, out, i - 2, slot).wait()

            for cut in pieces_of(lanes, 256):
                for high in pieces_of(step, 256):
                    tall[which, slot, high, cut] = dot(turned[high, :], right[:, cut]).astype(tall.dtype)
            tall_copy(which, out, i, slot).start()
        return carry

    lax.fori_loop(0, count, inputs, 0)
    for i in range(max(0, count - 2), count):
        wide_copy(i, i % 2).wait()
        tall_copy(0, grad_gate, i, i % 2).wait()
        tall_copy(1, grad_up, i, i % 2).wait()


def exchange(blocks, masks, devices):
    arrived = []
    for block, mask in zip(blocks, masks):
        pairs = [(2 * i + core, 2 * (i ^ (mask + core)) + core) for i in range(devices) for core in range(2)]
        arrived.append(lax.ppermute(block, ("expert", "ffn"), pairs))
    return arrived


def exchange_near(block, devices):
    return lax.ppermute(block, "expert", [(i, i ^ 1) for i in range(devices)])


def swap(value):
    return lax.ppermute(value, "ffn", [(0, 1), (1, 0)])


def in_hbm(values):
    return [pltpu.with_memory_space_constraint(value, pltpu.HBM) for value in values]


def one_piece_shards(tokens, grad_out, route_ids, route_weight, gate_weight, up_weight, down_weight):
    tok_dev, sub_width = tokens.shape
    top_count = route_ids.shape[1]
    width, lanes = gate_weight.shape[1:]
    devices = lax.axis_size("expert")
    capacity = max(2, min(tok_dev, (9 * tok_dev * top_count + 8 * EXPERTS - 1) // (8 * EXPERTS)))
    rows = devices * capacity
    subs = sub_width // LANES
    low, full = jnp.bfloat16, jnp.float32
    size = capacity * subs
    count = devices // 2 - 1
    spread_scratch = [pltpu.VMEM((devices * size, LANES), full)]
    step = 256
    half_flops = 2 * rows * width * lanes // 2

    def lines(number, dtype=low):
        return jax.ShapeDtypeStruct((number * size, LANES), dtype)

    def lines_in_vmem(number, dtype=low):
        return vmem((number * size, LANES), dtype)

    sources = (route_ids.T, route_weight.T, tokens, grad_out)
    other_rows = count * capacity
    x_mine, g_mine, near, here, theirs, place, mix, place_other, mix_other = call(
        functools.partial(route_kernel, devices, capacity, subs),
        [lines(count), lines(count), lines(2), lines(2)]
        + [lines(2 * count)]
        + [jax.ShapeDtypeStruct((rows, tok_dev), low), jax.ShapeDtypeStruct((rows, LANES), full)]
        + [jax.ShapeDtypeStruct((other_rows, tok_dev), low), jax.ShapeDtypeStruct((other_rows, LANES), full)],
        in_hbm(sources),
        in_spaces=[pl.ANY] * 4,
        scratch=spread_scratch
        + [pltpu.VMEM(value.shape, value.dtype) for value in sources]
        + [pltpu.SemaphoreType.DMA((4,))],
        traffic=4 * tok_dev * sub_width,
    )
    masks = even_masks(devices)
    late = [devices // 4 - 1]
    late_block = jax.ShapeDtypeStruct((2 * size + 16, LANES), low)
    packed = call(
        functools.partial(pack_kernel, size, late),
        [late_block if j in late else lines(4) for j in range(count)] + [late_block] * len(late),
        (x_mine, g_mine, swap(theirs)),
        flops=24 * half_flops,
    )
    x_arrived = exchange(packed[:count], masks, devices)
    g_arrived = list(x_arrived)
    for j, block in zip(late, packed[count:]):
        (g_arrived[j],) = exchange([block], masks[j:], devices)
    near = exchange_near(near, devices)

    weights = (gate_weight, up_weight, down_weight)
    w_gate, w_up, w_down = [pltpu.with_memory_space_constraint(w, pltpu.VMEM) for w in weights]

    x_sent = call(
        functools.partial(gather_x_kernel, size), [lines(2)] * (count + 1), (*x_arrived, near, here)
    )
    x_swapped = [swap(value) for value in x_sent]
    terms = [
        lines_in_vmem(count + 2, full),
        lines_in_vmem(count, full),
        lines_in_vmem(count),
        lines_in_vmem(count + 2),
    ]
    x_full, gate, up, hidden = call(
        functools.partial(forward_kernel, devices, subs, step),
        [vmem((rows, width), low)] + [vmem((rows, lanes), low)] * 3,
        (*x_sent, *x_swapped, w_gate, w_up),
        scratch=spread_scratch,
    )
    (g_sent,) = call(
        functools.partial(gather_g_kernel, size, late), [lines(devices)], (*g_arrived, near, here, hidden)
    )
    g_swapped = swap(g_sent)
    out_own, out_other, send_own, send_other = call(
        functools.partial(output_kernel, devices, subs, 2 * step),
        terms,
        (hidden, w_down),
        scratch=spread_scratch,
        flops=2 * half_flops,
    )
    out_terms = (out_own, out_other, swap(send_other), swap(send_own))
    g_full, pre_gate, pre_up, dx_other, send_other = call(
        functools.partial(backward_kernel, devices, subs, step),
        [vmem((rows, width), low)] + [vmem((rows, lanes), low)] * 2 + [terms[1], terms[3]],
        (g_sent, g_swapped, gate, up, w_gate, w_up, w_down),
        scratch=spread_scratch,
        flops=4 * half_flops,
    )
    came_own = swap(send_other)
    dx_own, send_own = call(
        functools.partial(backward_own_kernel, devices, subs, step),
        [terms[0], terms[2]],
        (pre_gate, pre_up, w_gate, w_up),
        scratch=spread_scratch,
        flops=2 * half_flops,
    )
    dx_terms = (dx_own, dx_other, came_own, swap(send_own))
    *leaving, back, kept = call(
        functools.partial(leave_kernel, size),
        [lines(4)] * count + [lines(2)] * 2,
        (*out_terms, *dx_terms),
    )
    returned = exchange(leaving, masks, devices)
    back = exchange_near(back, devices)
    cut = 1024 if width % 1024 == 0 else width
    grad_gate, grad_up, grad_down, written = call(
        functools.partial(gradient_kernel, cut),
        [jax.ShapeDtypeStruct(w.shape, low) for w in weights] + [vmem((8, LANES), full)],
        (x_full, g_full, hidden, pre_gate, pre_up),
        out_spaces=[pl.ANY] * 3 + [pltpu.VMEM],
        scratch=[
            pltpu.VMEM((lanes, rows), low),
            pltpu.VMEM((cut, rows), low),
            pltpu.VMEM((2, 2, cut, lanes), low),
            pltpu.VMEM((2, lanes, cut), low),
            pltpu.SemaphoreType.DMA((2, 2)),
            pltpu.SemaphoreType.DMA((2,)),
        ],
        flops=6 * half_flops,
        traffic=sum(w.size * 2 for w in weights),
        limit=32,
    )
    (sharing,) = call(functools.partial(share_kernel, size), [lines(2 * count)], (*returned, back, written))
    shared = swap(sharing)
    sums = call(
        functools.partial(join_kernel, count, subs),
        [vmem((tok_dev, sub_width), full)] * 2,
        (place, mix, *returned, back, kept),
        scratch=spread_scratch + [pltpu.VMEM((rows, sub_width), low)],
        flops=4 * rows * tok_dev * sub_width,
    )
    out_tokens, grad_tokens = call(
        functools.partial(finish_kernel, count, subs),
        [jax.ShapeDtypeStruct((tok_dev, sub_width), low)] * 2,
        (place_other, mix_other, shared, *sums),
        out_spaces=[pl.ANY] * 2,
        scratch=[
            pltpu.VMEM((count * size, LANES), full),
            pltpu.VMEM((other_rows, sub_width), low),
            pltpu.VMEM((2, tok_dev, sub_width), low),
            pltpu.SemaphoreType.DMA((2,)),
        ],
        traffic=8 * tok_dev * sub_width,
    )
    return out_tokens, grad_tokens, grad_gate, grad_up, grad_down


def shards(*args):
    tokens, gate_weight = args[0], args[4]
    halves = lax.axis_size("ffn")
    devices = lax.axis_size("expert")
    if halves == 2 and devices >= 4 and devices & (devices - 1) == 0 and tokens.shape[1] * halves == gate_weight.shape[1]:
        return one_piece_shards(*args)
    return general_shards(*args)


def solution(mesh):
    in_specs = (
        P(("groups", "expert"), "ffn"),
        P(("groups", "expert"), "ffn"),
        P(("groups", "expert"), None),
        P(("groups", "expert"), None),
        P("expert", None, "ffn"),
        P("expert", None, "ffn"),
        P("expert", "ffn", None),
    )
    out_specs = (
        P(("groups", "expert"), "ffn"),
        P(("groups", "expert"), "ffn"),
        P(("groups", "expert"), None, "ffn"),
        P(("groups", "expert"), None, "ffn"),
        P(("groups", "expert"), "ffn", None),
    )
    return jax.shard_map(shards, mesh=mesh, in_specs=in_specs, out_specs=out_specs, check_vma=False)
```

```python
import functools

import jax
import jax.numpy as jnp
from jax import lax
from jax.experimental import pallas as pl
from jax.experimental.pallas import tpu as pltpu
from jax.sharding import PartitionSpec as P

EXPERTS = 128
LANES = 128
MIB = 1024 * 1024


def contract_rows(left, right):
    return lax.dot_general(
        left, right, (((0,), (0,)), ((), ())), preferred_element_type=jnp.float32
    )


def contract_cols(left, right):
    return lax.dot_general(
        left, right, (((1,), (1,)), ((), ())), preferred_element_type=jnp.float32
    )


def general_shards(tokens, grad_out, route_ids, route_weight, gate_weight, up_weight, down_weight):
    tokens, grad_out = (
        lax.all_gather(tokens, "ffn", axis=1, tiled=True),
        lax.all_gather(grad_out, "ffn", axis=1, tiled=True),
    )
    tok_dev, width = tokens.shape
    top_count = route_ids.shape[1]
    piece_width = gate_weight.shape[1]
    hidden_half = gate_weight.shape[2]
    pieces = width // piece_width
    devices = lax.axis_size("expert")
    flight = devices // pieces
    halves = lax.axis_size("ffn")
    sub_width = piece_width // halves
    capacity = max(2, min(tok_dev, (9 * tok_dev * top_count + 8 * EXPERTS - 1) // (8 * EXPERTS)))
    total_rows = devices * capacity
    expert_ids = jnp.arange(flight, dtype=jnp.int32)
    member = jnp.zeros((tok_dev, flight), jnp.float32)
    mixing = jnp.zeros((tok_dev, flight), jnp.float32)
    for route in range(top_count):
        hit = (route_ids[:, route : route + 1] == expert_ids[None, :]).astype(jnp.float32)
        member = member + hit
        mixing = mixing + hit * route_weight[:, route : route + 1]
    slots = jnp.cumsum(member, axis=0) - member
    place = member[:, :, None] * (
        slots[:, :, None] == jnp.arange(capacity, dtype=jnp.float32)
    ).astype(jnp.float32)
    weighted = place * mixing[:, :, None]
    place_low = place.astype(jnp.bfloat16)
    x_four = tokens.reshape(tok_dev, halves, pieces, sub_width)
    g_four = grad_out.reshape(tok_dev, halves, pieces, sub_width)
    x_parts = []
    g_parts = []
    for half in range(halves):
        x_parts.append(
            jnp.einsum(
                "Tec,Tjr->ejcr", place_low, x_four[:, half], preferred_element_type=jnp.float32
            )
        )
        g_parts.append(jnp.einsum("Tec,Tjr->ejcr", weighted, g_four[:, half].astype(jnp.float32)))
    x_send = jnp.concatenate(x_parts, axis=3).astype(jnp.bfloat16).reshape(total_rows, piece_width)
    g_send = jnp.concatenate(g_parts, axis=3).astype(jnp.bfloat16).reshape(total_rows, piece_width)

    def return_parts(values):
        arrived = lax.all_to_all(values, "expert", split_axis=0, concat_axis=0, tiled=True)
        lanes = arrived.shape[1]
        return arrived.astype(jnp.float32).reshape(flight, pieces, capacity, lanes).sum(axis=1)

    def spread_rows(values):
        lanes = values.shape[2]
        copies = jnp.broadcast_to(values[:, None], (flight, pieces, capacity, lanes)).reshape(
            total_rows, lanes
        )
        return lax.all_to_all(copies, "expert", split_axis=0, concat_axis=0, tiled=True)

    def finish(term, mix):
        summed = lax.psum_scatter(term, "ffn", scatter_dimension=1, tiled=True)
        back = lax.all_to_all(summed, "expert", split_axis=0, concat_axis=0, tiled=True)
        back = back.reshape(flight, pieces, capacity, sub_width)
        joined = jnp.einsum("Tec,ejcr->Tjr", mix, back)
        return joined.reshape(tok_dev, pieces * sub_width).astype(jnp.bfloat16)

    rows = lax.all_to_all(x_send, "expert", split_axis=0, concat_axis=0, tiled=True)
    w_gate = gate_weight[0]
    w_up = up_weight[0]
    w_down = down_weight[0]
    partial_value = jnp.concatenate(
        [
            jnp.dot(rows, w_gate, preferred_element_type=jnp.float32),
            jnp.dot(rows, w_up, preferred_element_type=jnp.float32),
        ],
        axis=1,
    )
    summed = return_parts(partial_value.astype(jnp.bfloat16))
    gate = summed[:, :, :hidden_half]
    up = summed[:, :, hidden_half:]
    sig = jax.nn.sigmoid(gate)
    act = gate * sig
    hidden = (act * up).astype(jnp.bfloat16)
    h_rows = spread_rows(hidden)
    out_term = jnp.dot(h_rows, w_down, preferred_element_type=jnp.float32)
    out_tokens = finish(out_term, weighted)
    grads = lax.all_to_all(g_send, "expert", split_axis=0, concat_axis=0, tiled=True)
    grad_down = contract_rows(h_rows, grads).astype(jnp.bfloat16)
    hidden_part = contract_cols(grads, w_down).astype(jnp.bfloat16)
    grad_hidden = return_parts(hidden_part)
    pre_gate = (grad_hidden * up * sig * (1.0 + gate * (1.0 - sig))).astype(jnp.bfloat16)
    pre_up = (grad_hidden * act).astype(jnp.bfloat16)
    both = spread_rows(jnp.concatenate([pre_gate, pre_up], axis=2))
    d_gate_rows = both[:, :hidden_half]
    d_up_rows = both[:, hidden_half:]
    grad_gate = contract_rows(rows, d_gate_rows).astype(jnp.bfloat16)
    grad_up = contract_rows(rows, d_up_rows).astype(jnp.bfloat16)
    x_term = contract_cols(d_gate_rows, w_gate) + contract_cols(d_up_rows, w_up)
    grad_tokens = finish(x_term, place)
    return (out_tokens, grad_tokens, grad_gate[None], grad_up[None], grad_down[None])


def vmem(shape, dtype):
    return pltpu.VMEM(shape, dtype)


def call(kernel, out_shape, args, in_spaces=None, out_spaces=None, flops=0, traffic=0, scratch=(), limit=16):
    spaces = in_spaces or [pltpu.VMEM] * len(args)
    outs = out_spaces or [pltpu.VMEM] * len(out_shape)
    return pl.pallas_call(
        kernel,
        out_shape=tuple(out_shape),
        in_specs=[pl.BlockSpec(memory_space=space) for space in spaces],
        out_specs=tuple(pl.BlockSpec(memory_space=space) for space in outs),
        scratch_shapes=list(scratch),
        compiler_params=pltpu.CompilerParams(vmem_limit_bytes=limit * MIB),
        cost_estimate=pl.CostEstimate(flops=flops, bytes_accessed=traffic, transcendentals=0),
    )(*args)


def blocks_to_rows(scratch, blocks, put, subs):
    size = blocks[0].shape[0]
    for p, block in enumerate(blocks):
        scratch[p * size : (p + 1) * size, :] = block[...].astype(jnp.float32)
    for sub in range(subs):
        put(sub, scratch[pl.ds(sub, len(blocks) * size // subs, stride=subs), :])


def spread_lanes(scratch, sub, subs, value):
    scratch[pl.ds(sub, value.shape[0], stride=subs), :] = value


def part(ref, start, count):
    return ref.at[start : start + count, :]


def lanes_of(sub):
    return slice(sub * LANES, (sub + 1) * LANES)


def even_masks(count):
    return [*reversed(range(count // 2, count, 2)), *range(2, count // 2, 2)]


def route_kernel(devices, capacity, subs, ids_in, weight_in, x_in, g_in, *refs):
    x_mine, g_mine, near, here, theirs, place_out, mix_out, place_other, mix_other, scratch, ids, weight, x, g, sems = refs
    pairs = ((ids_in, ids), (weight_in, weight), (x_in, x), (g_in, g))
    copies = [pltpu.make_async_copy(src, dst, sems.at[i]) for i, (src, dst) in enumerate(pairs)]
    for copy in copies:
        copy.start()
    top, tok = ids.shape
    rows = devices * capacity
    core = lax.axis_index("ffn")
    masks = even_masks(devices)
    masks = [mask + core for mask in masks] + [mask + 1 - core for mask in masks] + [1, 0]
    order = lax.broadcasted_iota(jnp.int32, (devices, tok), 0)
    bits = jnp.zeros((devices, tok), jnp.int32)
    for p, mask in enumerate(masks):
        bits = jnp.where(order == p, mask, bits)
    expert = bits ^ lax.axis_index("expert")
    member = jnp.zeros((devices, tok), jnp.float32)
    mixing = jnp.zeros((devices, tok), jnp.float32)
    copies[0].wait()
    copies[1].wait()
    for route in range(top):
        hit = ids[route : route + 1, :] == expert
        member = jnp.where(hit, 1.0, member)
        mixing = jnp.where(hit, weight[route : route + 1, :], mixing)
    before = lax.broadcasted_iota(jnp.int32, (tok, tok), 0) < lax.broadcasted_iota(jnp.int32, (tok, tok), 1)
    slots = dot(member.astype(jnp.bfloat16), jnp.where(before, 1.0, 0.0).astype(jnp.bfloat16))
    target = jnp.where(member > 0, slots + capacity * order.astype(jnp.float32), -1.0)
    count = devices // 2 - 1

    def placed(first, number):
        row = lax.broadcasted_iota(jnp.int32, (number, tok), 0).astype(jnp.float32) + first
        place = jnp.zeros((number, tok), jnp.float32)
        mix = jnp.zeros((number, tok), jnp.float32)
        for p in range(devices):
            equal = target[p : p + 1, :] == row
            place = jnp.where(equal, 1.0, place)
            mix = jnp.where(equal, mixing[p : p + 1, :], mix)
        row_weight = jnp.broadcast_to(jnp.sum(mix, axis=1, keepdims=True), (number, LANES))
        return place.astype(jnp.bfloat16), row_weight

    low, row_weight = placed(0, rows)
    place_out[...] = low
    mix_out[...] = row_weight
    place_other[...], mix_other[...] = placed(count * capacity, count * capacity)
    size = capacity * subs

    def write(mine, at):
        def block(p):
            return scratch[p * size : (p + 1) * size, :].astype(theirs.dtype)

        for j in range(count):
            part(mine, j * size, size)[...] = block(j)
            part(theirs, (at + j) * size, size)[...] = block(count + j)
        start = size if at else 0
        part(near, start, size)[...] = block(2 * count)
        part(here, start, size)[...] = block(2 * count + 1)

    copies[2].wait()
    for sub in range(subs):
        spread_lanes(scratch, sub, subs, dot(low, x[:, lanes_of(sub)]))
    write(x_mine, 0)
    copies[3].wait()
    for sub in range(subs):
        spread_lanes(scratch, sub, subs, dot(low, g[:, lanes_of(sub)]) * row_weight)
    write(g_mine, count)


def pack_kernel(size, late, x_mine, g_mine, swapped, *outs):
    count = len(outs) - len(late)
    lates = dict(zip(late, outs[count:]))
    for j, out in enumerate(outs[:count]):
        places = ((out, 0), (lates.get(j, out), 0 if j in late else 2 * size))
        for i, (mine, (to, at)) in enumerate(zip((x_mine, g_mine), places)):
            part(to, at, size)[...] = part(mine, j * size, size)[...]
            part(to, at + size, size)[...] = part(swapped, (i * count + j) * size, size)[...]
    for out in [*lates.values(), *[outs[j] for j in late]]:
        rest = part(out, 2 * size, out.shape[0] - 2 * size)
        rest[...] = jnp.zeros(rest.shape, rest.dtype)


def gather_x_kernel(size, *refs):
    count = (len(refs) - 3) // 2
    blocks, (near, here), outs = refs[:count], refs[count : count + 2], refs[count + 2 :]
    for block, out in zip(blocks, outs):
        out[...] = part(block, 0, 2 * size)[...]
    part(outs[-1], 0, size)[...] = part(near, 0, size)[...]
    part(outs[-1], size, size)[...] = part(here, 0, size)[...]


def gather_g_kernel(size, late, *refs):
    blocks, (near, here, _, out) = refs[:-4], refs[-4:]
    for j, block in enumerate(blocks):
        start = 0 if j in late else 2 * size
        part(out, 2 * j * size, 2 * size)[...] = part(block, start, 2 * size)[...]
    part(out, 2 * len(blocks) * size, size)[...] = part(near, size, size)[...]
    part(out, (2 * len(blocks) + 1) * size, size)[...] = part(here, size, size)[...]


def full_rows(devices, subs, scratch, own_sent, other_sent, out):
    per = devices // len(own_sent)
    size = own_sent[0].shape[0] // per
    count = devices // 2 - 1
    own, other = half_starts(out.shape[1] // 2)
    first, second, last = range(0, 2 * count, 2), range(1, 2 * count, 2), range(2 * count, devices)
    layouts = (
        (own, [(own_sent, i) for i in first] + [(other_sent, i) for i in second] + [(own_sent, i) for i in last]),
        (other, [(own_sent, i) for i in second] + [(other_sent, i) for i in first] + [(other_sent, i) for i in last]),
    )
    for start, layout in layouts:

        def put(sub, value):
            out[:, pl.ds(start + sub * LANES, LANES)] = value.astype(out.dtype)

        blocks_to_rows(scratch, [part(refs[i // per], i % per * size, size) for refs, i in layout], put, subs)


def split_terms(count, size, scratch, own_half, keep, send):
    keep[0 : count * size, :] = scratch[0 : count * size, :]
    send[0 : count * size, :] = scratch[count * size : 2 * count * size, :].astype(send.dtype)
    rest = scratch[2 * count * size :, :]
    if own_half:
        keep[count * size :, :] = rest
    else:
        send[count * size :, :] = rest.astype(send.dtype)


def leave_kernel(size, *refs):
    terms, outs = (refs[:4], refs[4:8]), refs[9:]
    count = len(outs) - 2
    for at, (keep_own, keep_other, came_own, came_other) in zip((0, size), terms):

        def own(p):
            total = part(keep_own, p * size, size)[...] + part(came_own, p * size, size)[...].astype(jnp.float32)
            return total.astype(outs[0].dtype)

        for j, out in enumerate(outs[:count]):
            part(out, at, size)[...] = own(j)
            total = part(keep_other, j * size, size)[...] + part(came_other, j * size, size)[...].astype(jnp.float32)
            part(out, 2 * size + at, size)[...] = total.astype(out.dtype)
        part(outs[count], at, size)[...] = own(count)
        part(outs[count + 1], at, size)[...] = own(count + 1)


def share_kernel(size, *refs):
    blocks, (_, _, out) = refs[:-3], refs[-3:]
    for j, block in enumerate(blocks):
        part(out, 2 * j * size, 2 * size)[...] = part(block, 2 * size, 2 * size)[...]


def token_sums(subs, place, mix, scratch, rows, blocks, put):
    size = scratch.shape[0] // len(blocks)
    for p, block in enumerate(blocks):
        here = slice(p * size, (p + 1) * size)
        scratch[here, :] = jnp.zeros((size, LANES), jnp.float32) if block is None else block[...].astype(jnp.float32)
    for sub in range(subs):
        value = scratch[pl.ds(sub, rows.shape[0], stride=subs), :]
        if mix is not None:
            value = value * mix[...]
        rows[:, lanes_of(sub)] = value.astype(rows.dtype)
    for cut in pieces_of(subs * LANES, 512):
        put(cut, contract_rows(place[...], rows[:, cut]))


def join_kernel(count, subs, place, mix, *refs):
    blocks, (near, here, out_sum, grad_sum, scratch, rows) = refs[:count], refs[count:]
    size = near.shape[0] // 2
    for at, scale, out in ((0, mix, out_sum), (size, None, grad_sum)):

        def put(cut, total):
            out[:, cut] = total

        first = [part(block, at, size) for block in blocks]
        last = [part(near, at, size), part(here, at, size)]
        token_sums(subs, place, scale, scratch, rows, first + [None] * count + last, put)


def finish_kernel(
    count, subs, place, mix, shared, out_sum, grad_sum, out_tokens, grad_tokens, scratch, rows, low, sems
):
    size = shared.shape[0] // (2 * count)
    copies = []
    work = ((0, mix, out_sum, out_tokens), (size, None, grad_sum, grad_tokens))
    for i, (at, scale, before, out) in enumerate(work):

        def put(cut, total):
            low[i, :, cut] = (before[:, cut] + total).astype(low.dtype)

        blocks = [part(shared, 2 * j * size + at, size) for j in range(count)]
        token_sums(subs, place, scale, scratch, rows, blocks, put)
        copies.append(pltpu.make_async_copy(low.at[i], out, sems.at[i]))
        copies[-1].start()
    for copy in copies:
        copy.wait()


def half_starts(half_width):
    half = lax.axis_index("ffn")
    own = pl.multiple_of(half * half_width, half_width)
    other = pl.multiple_of((1 - half) * half_width, half_width)
    return own, other


def chunk(i, step, base=0):
    return pl.ds(base + pl.multiple_of(i * step, step), step)


def dot(left, right):
    return jnp.dot(left, right, preferred_element_type=jnp.float32)


def halves_of_output(devices, subs, step, scratch, own_half, term, keep, send):
    size = scratch.shape[0] // devices
    for at in range(0, subs * LANES, step):
        value = term(at)
        for i in range(step // LANES):
            spread_lanes(scratch, at // LANES + i, subs, value[:, lanes_of(i)])
    split_terms(devices // 2 - 1, size, scratch, own_half, keep, send)


def forward_kernel(devices, subs, step, *refs):
    half = devices // 2
    x_sent, x_swapped = refs[:half], refs[half : 2 * half]
    w_gate, w_up, x_full, gate, up, hidden, scratch = refs[2 * half :]
    full_rows(devices, subs, scratch, x_sent, x_swapped, x_full)
    for cols in pieces_of(gate.shape[1], step):
        gate_low = dot(x_full[...], w_gate[0, :, cols]).astype(jnp.bfloat16)
        up_low = dot(x_full[...], w_up[0, :, cols]).astype(jnp.bfloat16)
        gate[:, cols] = gate_low
        up[:, cols] = up_low
        value = gate_low.astype(jnp.float32)
        hidden[:, cols] = (value * jax.nn.sigmoid(value) * up_low.astype(jnp.float32)).astype(jnp.bfloat16)


def output_kernel(devices, subs, step, hidden, w_down, keep_own, keep_other, send_own, send_other, scratch):
    own, other = half_starts(subs * LANES)

    def term(start):
        return lambda at: dot(hidden[...], w_down[0, :, pl.ds(start + at, step)])

    halves_of_output(devices, subs, step, scratch, False, term(other), keep_other, send_other)
    halves_of_output(devices, subs, step, scratch, True, term(own), keep_own, send_own)


def input_term(step, pre_gate, pre_up, w_gate, w_up, start):
    def term(at):
        there = pl.ds(start + at, step)
        return contract_cols(pre_gate[...], w_gate[0, there, :]) + contract_cols(pre_up[...], w_up[0, there, :])

    return term


def backward_kernel(
    devices,
    subs,
    step,
    g_sent,
    g_swapped,
    gate,
    up,
    w_gate,
    w_up,
    w_down,
    g_full,
    pre_gate,
    pre_up,
    keep_other,
    send_other,
    scratch,
):
    _, other = half_starts(subs * LANES)
    full_rows(devices, subs, scratch, [g_sent], [g_swapped], g_full)

    def pull(i, carry):
        cols = chunk(i, step)
        low = contract_cols(g_full[...], w_down[0, cols, :]).astype(jnp.bfloat16)
        grad_hidden = low.astype(jnp.float32)
        value = gate[:, cols].astype(jnp.float32)
        sig = jax.nn.sigmoid(value)
        pre_gate[:, cols] = (
            grad_hidden * up[:, cols].astype(jnp.float32) * sig * (1.0 + value * (1.0 - sig))
        ).astype(jnp.bfloat16)
        pre_up[:, cols] = (grad_hidden * value * sig).astype(jnp.bfloat16)
        return carry

    lax.fori_loop(0, gate.shape[1] // step, pull, 0)
    term = input_term(step, pre_gate, pre_up, w_gate, w_up, other)
    halves_of_output(devices, subs, step, scratch, False, term, keep_other, send_other)


def backward_own_kernel(devices, subs, step, pre_gate, pre_up, w_gate, w_up, keep_own, send_own, scratch):
    own, _ = half_starts(subs * LANES)
    term = input_term(step, pre_gate, pre_up, w_gate, w_up, own)
    halves_of_output(devices, subs, step, scratch, True, term, keep_own, send_own)


def flip(value):
    return value.astype(jnp.float32).T


def pieces_of(total, size):
    return [slice(at, min(at + size, total)) for at in range(0, total, size)]


def first_chunk_kernel(hidden, g, turned, out):
    turned[...] = flip(hidden[...]).astype(turned.dtype)
    for cut in pieces_of(out.shape[1], 256):
        out[:, cut] = dot(turned[...], g[:, cut]).astype(out.dtype)


def gradient_kernel(
    step,
    x,
    g,
    hidden_turned,
    first,
    pre_gate,
    pre_up,
    grad_gate,
    grad_up,
    grad_down,
    written,
    turned,
    tall,
    wide,
    tall_sems,
    wide_sems,
    first_sem,
):
    width, lanes = x.shape[1], hidden_turned.shape[0]
    count = width // step
    written[...] = jnp.zeros_like(written)
    first_copy = pltpu.make_async_copy(first, grad_down.at[0, :, 0:step], first_sem)
    first_copy.start()

    def wide_copy(i, slot):
        return pltpu.make_async_copy(wide.at[slot], grad_down.at[0, :, chunk(i, step)], wide_sems.at[slot])

    def tall_copy(which, out, i, slot):
        return pltpu.make_async_copy(tall.at[which, slot], out.at[0, chunk(i, step), :], tall_sems.at[which, slot])

    def down(i, carry):
        slot = i % 2

        @pl.when(i >= 3)
        def _():
            wide_copy(i - 2, slot).wait()

        for cut in pieces_of(step, 256):
            right = g[:, chunk(i, step)][:, cut]
            wide[slot, :, cut] = dot(hidden_turned[...], right).astype(wide.dtype)
        wide_copy(i, slot).start()
        return carry

    lax.fori_loop(1, count, down, 0)

    def inputs(i, carry):
        slot = i % 2
        turned[...] = flip(x[:, chunk(i, step)]).astype(turned.dtype)
        for which, (right, out) in enumerate(((pre_gate, grad_gate), (pre_up, grad_up))):

            @pl.when(i >= 2)
            def _():
                tall_copy(which, out, i - 2, slot).wait()

            for cut in pieces_of(lanes, 256):
                for high in pieces_of(step, 512):
                    tall[which, slot, high, cut] = dot(turned[high, :], right[:, cut]).astype(tall.dtype)
            tall_copy(which, out, i, slot).start()
        return carry

    lax.fori_loop(0, count, inputs, 0)
    first_copy.wait()
    for i in range(max(1, count - 2), count):
        wide_copy(i, i % 2).wait()
    for i in range(max(0, count - 2), count):
        tall_copy(0, grad_gate, i, i % 2).wait()
        tall_copy(1, grad_up, i, i % 2).wait()


def exchange(blocks, masks, devices):
    arrived = []
    for block, mask in zip(blocks, masks):
        pairs = [(2 * i + core, 2 * (i ^ (mask + core)) + core) for i in range(devices) for core in range(2)]
        arrived.append(lax.ppermute(block, ("expert", "ffn"), pairs))
    return arrived


def exchange_near(block, devices):
    return lax.ppermute(block, "expert", [(i, i ^ 1) for i in range(devices)])


def swap(value):
    return lax.ppermute(value, "ffn", [(0, 1), (1, 0)])


def in_hbm(values):
    return [pltpu.with_memory_space_constraint(value, pltpu.HBM) for value in values]


def one_piece_shards(tokens, grad_out, route_ids, route_weight, gate_weight, up_weight, down_weight):
    tok_dev, sub_width = tokens.shape
    top_count = route_ids.shape[1]
    width, lanes = gate_weight.shape[1:]
    devices = lax.axis_size("expert")
    capacity = max(2, min(tok_dev, (9 * tok_dev * top_count + 8 * EXPERTS - 1) // (8 * EXPERTS)))
    rows = devices * capacity
    subs = sub_width // LANES
    low, full = jnp.bfloat16, jnp.float32
    size = capacity * subs
    count = devices // 2 - 1
    spread_scratch = [pltpu.VMEM((devices * size, LANES), full)]
    step = 256
    half_flops = 2 * rows * width * lanes // 2

    def lines(number, dtype=low):
        return jax.ShapeDtypeStruct((number * size, LANES), dtype)

    def lines_in_vmem(number, dtype=low):
        return vmem((number * size, LANES), dtype)

    sources = (route_ids.T, route_weight.T, tokens, grad_out)
    other_rows = count * capacity
    x_mine, g_mine, near, here, theirs, place, mix, place_other, mix_other = call(
        functools.partial(route_kernel, devices, capacity, subs),
        [lines(count), lines(count), lines(2), lines(2)]
        + [lines(2 * count)]
        + [jax.ShapeDtypeStruct((rows, tok_dev), low), jax.ShapeDtypeStruct((rows, LANES), full)]
        + [jax.ShapeDtypeStruct((other_rows, tok_dev), low), jax.ShapeDtypeStruct((other_rows, LANES), full)],
        in_hbm(sources),
        in_spaces=[pl.ANY] * 4,
        scratch=spread_scratch
        + [pltpu.VMEM(value.shape, value.dtype) for value in sources]
        + [pltpu.SemaphoreType.DMA((4,))],
        traffic=4 * tok_dev * sub_width,
    )
    masks = even_masks(devices)
    late = [0]
    late_block = jax.ShapeDtypeStruct((2 * size + 16, LANES), low)
    packed = call(
        functools.partial(pack_kernel, size, late),
        [late_block if j in late else lines(4) for j in range(count)] + [late_block] * len(late),
        (x_mine, g_mine, swap(theirs)),
        flops=24 * half_flops,
    )
    x_arrived = exchange(packed[:count], masks, devices)
    g_arrived = list(x_arrived)
    for j, block in zip(late, packed[count:]):
        (g_arrived[j],) = exchange([block], masks[j:], devices)
    near = exchange_near(near, devices)

    weights = (gate_weight, up_weight, down_weight)
    w_gate, w_up, w_down = [pltpu.with_memory_space_constraint(w, pltpu.VMEM) for w in weights]

    x_sent = call(
        functools.partial(gather_x_kernel, size), [lines(2)] * (count + 1), (*x_arrived, near, here)
    )
    x_swapped = [swap(value) for value in x_sent]
    terms = [
        lines_in_vmem(count + 2, full),
        lines_in_vmem(count, full),
        lines_in_vmem(count),
        lines_in_vmem(count + 2),
    ]
    x_full, gate, up, hidden = call(
        functools.partial(forward_kernel, devices, subs, step),
        [vmem((rows, width), low)] + [vmem((rows, lanes), low)] * 3,
        (*x_sent, *x_swapped, w_gate, w_up),
        scratch=spread_scratch,
    )
    (g_sent,) = call(
        functools.partial(gather_g_kernel, size, late), [lines(devices)], (*g_arrived, near, here, hidden)
    )
    g_swapped = swap(g_sent)
    out_own, out_other, send_own, send_other = call(
        functools.partial(output_kernel, devices, subs, 2 * step),
        terms,
        (hidden, w_down),
        scratch=spread_scratch,
        flops=2 * half_flops,
    )
    out_terms = (out_own, out_other, swap(send_other), swap(send_own))
    g_full, pre_gate, pre_up, dx_other, send_other = call(
        functools.partial(backward_kernel, devices, subs, step),
        [vmem((rows, width), low)] + [vmem((rows, lanes), low)] * 2 + [terms[1], terms[3]],
        (g_sent, g_swapped, gate, up, w_gate, w_up, w_down),
        scratch=spread_scratch,
        flops=4 * half_flops,
    )
    came_own = swap(send_other)
    dx_own, send_own = call(
        functools.partial(backward_own_kernel, devices, subs, step),
        [terms[0], terms[2]],
        (pre_gate, pre_up, w_gate, w_up),
        scratch=spread_scratch,
        flops=2 * half_flops,
    )
    dx_terms = (dx_own, dx_other, came_own, swap(send_own))
    cut = 1024 if width % 1024 == 0 else width
    hidden_turned, first = call(
        first_chunk_kernel,
        [vmem((lanes, rows), low), vmem((lanes, cut), low)],
        (hidden, g_full),
        flops=2 * half_flops * cut // width,
    )
    *leaving, back, kept = call(
        functools.partial(leave_kernel, size),
        [lines(4)] * count + [lines(2)] * 2,
        (*out_terms, *dx_terms, first),
    )
    returned = exchange(leaving, masks, devices)
    back = exchange_near(back, devices)
    grad_gate, grad_up, grad_down, written = call(
        functools.partial(gradient_kernel, cut),
        [jax.ShapeDtypeStruct(w.shape, low) for w in weights] + [vmem((8, LANES), full)],
        (x_full, g_full, hidden_turned, first, pre_gate, pre_up),
        out_spaces=[pl.ANY] * 3 + [pltpu.VMEM],
        scratch=[
            pltpu.VMEM((cut, rows), low),
            pltpu.VMEM((2, 2, cut, lanes), low),
            pltpu.VMEM((2, lanes, cut), low),
            pltpu.SemaphoreType.DMA((2, 2)),
            pltpu.SemaphoreType.DMA((2,)),
            pltpu.SemaphoreType.DMA,
        ],
        flops=6 * half_flops,
        traffic=sum(w.size * 2 for w in weights),
        limit=32,
    )
    (sharing,) = call(functools.partial(share_kernel, size), [lines(2 * count)], (*returned, back, written))
    shared = swap(sharing)
    sums = call(
        functools.partial(join_kernel, count, subs),
        [vmem((tok_dev, sub_width), full)] * 2,
        (place, mix, *returned, back, kept),
        scratch=spread_scratch + [pltpu.VMEM((rows, sub_width), low)],
        flops=4 * rows * tok_dev * sub_width,
    )
    out_tokens, grad_tokens = call(
        functools.partial(finish_kernel, count, subs),
        [jax.ShapeDtypeStruct((tok_dev, sub_width), low)] * 2,
        (place_other, mix_other, shared, *sums),
        out_spaces=[pl.ANY] * 2,
        scratch=[
            pltpu.VMEM((count * size, LANES), full),
            pltpu.VMEM((other_rows, sub_width), low),
            pltpu.VMEM((2, tok_dev, sub_width), low),
            pltpu.SemaphoreType.DMA((2,)),
        ],
        traffic=8 * tok_dev * sub_width,
    )
    return out_tokens, grad_tokens, grad_gate, grad_up, grad_down


def shards(*args):
    tokens, gate_weight = args[0], args[4]
    halves = lax.axis_size("ffn")
    devices = lax.axis_size("expert")
    if halves == 2 and devices >= 4 and devices & (devices - 1) == 0 and tokens.shape[1] * halves == gate_weight.shape[1]:
        return one_piece_shards(*args)
    return general_shards(*args)


def solution(mesh):
    in_specs = (
        P(("groups", "expert"), "ffn"),
        P(("groups", "expert"), "ffn"),
        P(("groups", "expert"), None),
        P(("groups", "expert"), None),
        P("expert", None, "ffn"),
        P("expert", None, "ffn"),
        P("expert", "ffn", None),
    )
    out_specs = (
        P(("groups", "expert"), "ffn"),
        P(("groups", "expert"), "ffn"),
        P(("groups", "expert"), None, "ffn"),
        P(("groups", "expert"), None, "ffn"),
        P(("groups", "expert"), "ffn", None),
    )
    return jax.shard_map(shards, mesh=mesh, in_specs=in_specs, out_specs=out_specs, check_vma=False)
```

```python
import functools

import jax
import jax.numpy as jnp
from jax import lax
from jax.experimental import pallas as pl
from jax.experimental.pallas import tpu as pltpu
from jax.sharding import PartitionSpec as P

EXPERTS = 128
LANES = 128
MIB = 1024 * 1024


def contract_rows(left, right):
    return lax.dot_general(
        left, right, (((0,), (0,)), ((), ())), preferred_element_type=jnp.float32
    )


def contract_cols(left, right):
    return lax.dot_general(
        left, right, (((1,), (1,)), ((), ())), preferred_element_type=jnp.float32
    )


def general_shards(tokens, grad_out, route_ids, route_weight, gate_weight, up_weight, down_weight):
    tokens, grad_out = (
        lax.all_gather(tokens, "ffn", axis=1, tiled=True),
        lax.all_gather(grad_out, "ffn", axis=1, tiled=True),
    )
    tok_dev, width = tokens.shape
    top_count = route_ids.shape[1]
    piece_width = gate_weight.shape[1]
    hidden_half = gate_weight.shape[2]
    pieces = width // piece_width
    devices = lax.axis_size("expert")
    flight = devices // pieces
    halves = lax.axis_size("ffn")
    sub_width = piece_width // halves
    capacity = max(2, min(tok_dev, (9 * tok_dev * top_count + 8 * EXPERTS - 1) // (8 * EXPERTS)))
    total_rows = devices * capacity
    expert_ids = jnp.arange(flight, dtype=jnp.int32)
    member = jnp.zeros((tok_dev, flight), jnp.float32)
    mixing = jnp.zeros((tok_dev, flight), jnp.float32)
    for route in range(top_count):
        hit = (route_ids[:, route : route + 1] == expert_ids[None, :]).astype(jnp.float32)
        member = member + hit
        mixing = mixing + hit * route_weight[:, route : route + 1]
    slots = jnp.cumsum(member, axis=0) - member
    place = member[:, :, None] * (
        slots[:, :, None] == jnp.arange(capacity, dtype=jnp.float32)
    ).astype(jnp.float32)
    weighted = place * mixing[:, :, None]
    place_low = place.astype(jnp.bfloat16)
    x_four = tokens.reshape(tok_dev, halves, pieces, sub_width)
    g_four = grad_out.reshape(tok_dev, halves, pieces, sub_width)
    x_parts = []
    g_parts = []
    for half in range(halves):
        x_parts.append(
            jnp.einsum(
                "Tec,Tjr->ejcr", place_low, x_four[:, half], preferred_element_type=jnp.float32
            )
        )
        g_parts.append(jnp.einsum("Tec,Tjr->ejcr", weighted, g_four[:, half].astype(jnp.float32)))
    x_send = jnp.concatenate(x_parts, axis=3).astype(jnp.bfloat16).reshape(total_rows, piece_width)
    g_send = jnp.concatenate(g_parts, axis=3).astype(jnp.bfloat16).reshape(total_rows, piece_width)

    def return_parts(values):
        arrived = lax.all_to_all(values, "expert", split_axis=0, concat_axis=0, tiled=True)
        lanes = arrived.shape[1]
        return arrived.astype(jnp.float32).reshape(flight, pieces, capacity, lanes).sum(axis=1)

    def spread_rows(values):
        lanes = values.shape[2]
        copies = jnp.broadcast_to(values[:, None], (flight, pieces, capacity, lanes)).reshape(
            total_rows, lanes
        )
        return lax.all_to_all(copies, "expert", split_axis=0, concat_axis=0, tiled=True)

    def finish(term, mix):
        summed = lax.psum_scatter(term, "ffn", scatter_dimension=1, tiled=True)
        back = lax.all_to_all(summed, "expert", split_axis=0, concat_axis=0, tiled=True)
        back = back.reshape(flight, pieces, capacity, sub_width)
        joined = jnp.einsum("Tec,ejcr->Tjr", mix, back)
        return joined.reshape(tok_dev, pieces * sub_width).astype(jnp.bfloat16)

    rows = lax.all_to_all(x_send, "expert", split_axis=0, concat_axis=0, tiled=True)
    w_gate = gate_weight[0]
    w_up = up_weight[0]
    w_down = down_weight[0]
    partial_value = jnp.concatenate(
        [
            jnp.dot(rows, w_gate, preferred_element_type=jnp.float32),
            jnp.dot(rows, w_up, preferred_element_type=jnp.float32),
        ],
        axis=1,
    )
    summed = return_parts(partial_value.astype(jnp.bfloat16))
    gate = summed[:, :, :hidden_half]
    up = summed[:, :, hidden_half:]
    sig = jax.nn.sigmoid(gate)
    act = gate * sig
    hidden = (act * up).astype(jnp.bfloat16)
    h_rows = spread_rows(hidden)
    out_term = jnp.dot(h_rows, w_down, preferred_element_type=jnp.float32)
    out_tokens = finish(out_term, weighted)
    grads = lax.all_to_all(g_send, "expert", split_axis=0, concat_axis=0, tiled=True)
    grad_down = contract_rows(h_rows, grads).astype(jnp.bfloat16)
    hidden_part = contract_cols(grads, w_down).astype(jnp.bfloat16)
    grad_hidden = return_parts(hidden_part)
    pre_gate = (grad_hidden * up * sig * (1.0 + gate * (1.0 - sig))).astype(jnp.bfloat16)
    pre_up = (grad_hidden * act).astype(jnp.bfloat16)
    both = spread_rows(jnp.concatenate([pre_gate, pre_up], axis=2))
    d_gate_rows = both[:, :hidden_half]
    d_up_rows = both[:, hidden_half:]
    grad_gate = contract_rows(rows, d_gate_rows).astype(jnp.bfloat16)
    grad_up = contract_rows(rows, d_up_rows).astype(jnp.bfloat16)
    x_term = contract_cols(d_gate_rows, w_gate) + contract_cols(d_up_rows, w_up)
    grad_tokens = finish(x_term, place)
    return (out_tokens, grad_tokens, grad_gate[None], grad_up[None], grad_down[None])


def vmem(shape, dtype):
    return pltpu.VMEM(shape, dtype)


def call(kernel, out_shape, args, in_spaces=None, out_spaces=None, flops=0, traffic=0, scratch=(), limit=16):
    spaces = in_spaces or [pltpu.VMEM] * len(args)
    outs = out_spaces or [pltpu.VMEM] * len(out_shape)
    return pl.pallas_call(
        kernel,
        out_shape=tuple(out_shape),
        in_specs=[pl.BlockSpec(memory_space=space) for space in spaces],
        out_specs=tuple(pl.BlockSpec(memory_space=space) for space in outs),
        scratch_shapes=list(scratch),
        compiler_params=pltpu.CompilerParams(vmem_limit_bytes=limit * MIB),
        cost_estimate=pl.CostEstimate(flops=flops, bytes_accessed=traffic, transcendentals=0),
    )(*args)


def blocks_to_rows(scratch, blocks, put, subs):
    size = blocks[0].shape[0]
    for p, block in enumerate(blocks):
        scratch[p * size : (p + 1) * size, :] = block[...].astype(jnp.float32)
    for sub in range(subs):
        put(sub, scratch[pl.ds(sub, len(blocks) * size // subs, stride=subs), :])


def spread_lanes(scratch, sub, subs, value):
    scratch[pl.ds(sub, value.shape[0], stride=subs), :] = value


def part(ref, start, count):
    return ref.at[start : start + count, :]


def lanes_of(sub):
    return slice(sub * LANES, (sub + 1) * LANES)


def even_masks(count):
    return [*reversed(range(count // 2, count, 2)), *range(2, count // 2, 2)]


def route_kernel(devices, capacity, subs, ids_in, weight_in, x_in, g_in, *refs):
    x_mine, g_mine, near, here, theirs, place_out, mix_out, place_other, mix_other, scratch, ids, weight, x, g, sems = refs
    pairs = ((ids_in, ids), (weight_in, weight), (x_in, x), (g_in, g))
    copies = [pltpu.make_async_copy(src, dst, sems.at[i]) for i, (src, dst) in enumerate(pairs)]
    for copy in copies:
        copy.start()
    top, tok = ids.shape
    rows = devices * capacity
    core = lax.axis_index("ffn")
    masks = even_masks(devices)
    masks = [mask + core for mask in masks] + [mask + 1 - core for mask in masks] + [1, 0]
    order = lax.broadcasted_iota(jnp.int32, (devices, tok), 0)
    bits = jnp.zeros((devices, tok), jnp.int32)
    for p, mask in enumerate(masks):
        bits = jnp.where(order == p, mask, bits)
    expert = bits ^ lax.axis_index("expert")
    member = jnp.zeros((devices, tok), jnp.float32)
    mixing = jnp.zeros((devices, tok), jnp.float32)
    copies[0].wait()
    copies[1].wait()
    for route in range(top):
        hit = ids[route : route + 1, :] == expert
        member = jnp.where(hit, 1.0, member)
        mixing = jnp.where(hit, weight[route : route + 1, :], mixing)
    before = lax.broadcasted_iota(jnp.int32, (tok, tok), 0) < lax.broadcasted_iota(jnp.int32, (tok, tok), 1)
    slots = dot(member.astype(jnp.bfloat16), jnp.where(before, 1.0, 0.0).astype(jnp.bfloat16))
    target = jnp.where(member > 0, slots + capacity * order.astype(jnp.float32), -1.0)
    count = devices // 2 - 1

    def placed(first, number):
        row = lax.broadcasted_iota(jnp.int32, (number, tok), 0).astype(jnp.float32) + first
        place = jnp.zeros((number, tok), jnp.float32)
        mix = jnp.zeros((number, tok), jnp.float32)
        for p in range(devices):
            equal = target[p : p + 1, :] == row
            place = jnp.where(equal, 1.0, place)
            mix = jnp.where(equal, mixing[p : p + 1, :], mix)
        row_weight = jnp.broadcast_to(jnp.sum(mix, axis=1, keepdims=True), (number, LANES))
        return place.astype(jnp.bfloat16), row_weight

    low, row_weight = placed(0, rows)
    place_out[...] = low
    mix_out[...] = row_weight
    place_other[...], mix_other[...] = placed(count * capacity, count * capacity)
    size = capacity * subs

    def write(mine, at):
        def block(p):
            return scratch[p * size : (p + 1) * size, :].astype(theirs.dtype)

        for j in range(count):
            part(mine, j * size, size)[...] = block(j)
            part(theirs, (at + j) * size, size)[...] = block(count + j)
        start = size if at else 0
        part(near, start, size)[...] = block(2 * count)
        part(here, start, size)[...] = block(2 * count + 1)

    copies[2].wait()
    for sub in range(subs):
        spread_lanes(scratch, sub, subs, dot(low, x[:, lanes_of(sub)]))
    write(x_mine, 0)
    copies[3].wait()
    for sub in range(subs):
        spread_lanes(scratch, sub, subs, dot(low, g[:, lanes_of(sub)]) * row_weight)
    write(g_mine, count)


def pack_kernel(size, late, x_mine, g_mine, swapped, *outs):
    count = len(outs) - len(late)
    lates = dict(zip(late, outs[count:]))
    for j, out in enumerate(outs[:count]):
        places = ((out, 0), (lates.get(j, out), 0 if j in late else 2 * size))
        for i, (mine, (to, at)) in enumerate(zip((x_mine, g_mine), places)):
            part(to, at, size)[...] = part(mine, j * size, size)[...]
            part(to, at + size, size)[...] = part(swapped, (i * count + j) * size, size)[...]
    for out in [*lates.values(), *[outs[j] for j in late]]:
        rest = part(out, 2 * size, out.shape[0] - 2 * size)
        rest[...] = jnp.zeros(rest.shape, rest.dtype)


def gather_x_kernel(size, *refs):
    count = (len(refs) - 3) // 2
    blocks, (near, here), outs = refs[:count], refs[count : count + 2], refs[count + 2 :]
    for block, out in zip(blocks, outs):
        out[...] = part(block, 0, 2 * size)[...]
    part(outs[-1], 0, size)[...] = part(near, 0, size)[...]
    part(outs[-1], size, size)[...] = part(here, 0, size)[...]


def gather_g_kernel(size, late, *refs):
    blocks, (near, here, _, out) = refs[:-4], refs[-4:]
    for j, block in enumerate(blocks):
        start = 0 if j in late else 2 * size
        part(out, 2 * j * size, 2 * size)[...] = part(block, start, 2 * size)[...]
    part(out, 2 * len(blocks) * size, size)[...] = part(near, size, size)[...]
    part(out, (2 * len(blocks) + 1) * size, size)[...] = part(here, size, size)[...]


def full_rows(devices, subs, scratch, own_sent, other_sent, out):
    per = devices // len(own_sent)
    size = own_sent[0].shape[0] // per
    count = devices // 2 - 1
    own, other = half_starts(out.shape[1] // 2)
    first, second, last = range(0, 2 * count, 2), range(1, 2 * count, 2), range(2 * count, devices)
    layouts = (
        (own, [(own_sent, i) for i in first] + [(other_sent, i) for i in second] + [(own_sent, i) for i in last]),
        (other, [(own_sent, i) for i in second] + [(other_sent, i) for i in first] + [(other_sent, i) for i in last]),
    )
    for start, layout in layouts:

        def put(sub, value):
            out[:, pl.ds(start + sub * LANES, LANES)] = value.astype(out.dtype)

        blocks_to_rows(scratch, [part(refs[i // per], i % per * size, size) for refs, i in layout], put, subs)


def split_terms(count, size, scratch, own_half, keep, send):
    keep[0 : count * size, :] = scratch[0 : count * size, :]
    send[0 : count * size, :] = scratch[count * size : 2 * count * size, :].astype(send.dtype)
    rest = scratch[2 * count * size :, :]
    if own_half:
        keep[count * size :, :] = rest
    else:
        send[count * size :, :] = rest.astype(send.dtype)


def leave_kernel(size, *refs):
    terms, outs = (refs[:4], refs[4:8]), refs[9:]
    count = len(outs) - 2
    for at, (keep_own, keep_other, came_own, came_other) in zip((0, size), terms):

        def own(p):
            total = part(keep_own, p * size, size)[...] + part(came_own, p * size, size)[...].astype(jnp.float32)
            return total.astype(outs[0].dtype)

        for j, out in enumerate(outs[:count]):
            part(out, at, size)[...] = own(j)
            total = part(keep_other, j * size, size)[...] + part(came_other, j * size, size)[...].astype(jnp.float32)
            part(out, 2 * size + at, size)[...] = total.astype(out.dtype)
        part(outs[count], at, size)[...] = own(count)
        part(outs[count + 1], at, size)[...] = own(count + 1)


def share_kernel(size, *refs):
    blocks, (_, _, out) = refs[:-3], refs[-3:]
    for j, block in enumerate(blocks):
        part(out, 2 * j * size, 2 * size)[...] = part(block, 2 * size, 2 * size)[...]


def token_sums(subs, place, mix, scratch, rows, blocks, put):
    size = scratch.shape[0] // len(blocks)
    for p, block in enumerate(blocks):
        here = slice(p * size, (p + 1) * size)
        scratch[here, :] = jnp.zeros((size, LANES), jnp.float32) if block is None else block[...].astype(jnp.float32)
    for sub in range(subs):
        value = scratch[pl.ds(sub, rows.shape[0], stride=subs), :]
        if mix is not None:
            value = value * mix[...]
        rows[:, lanes_of(sub)] = value.astype(rows.dtype)
    for cut in pieces_of(subs * LANES, 512):
        put(cut, contract_rows(place[...], rows[:, cut]))


def join_kernel(count, subs, place, mix, *refs):
    blocks, (near, here, out_sum, grad_sum, scratch, rows) = refs[:count], refs[count:]
    size = near.shape[0] // 2
    for at, scale, out in ((0, mix, out_sum), (size, None, grad_sum)):

        def put(cut, total):
            out[:, cut] = total

        first = [part(block, at, size) for block in blocks]
        last = [part(near, at, size), part(here, at, size)]
        token_sums(subs, place, scale, scratch, rows, first + [None] * count + last, put)


def finish_kernel(
    count, subs, place, mix, shared, out_sum, grad_sum, out_tokens, grad_tokens, scratch, rows, low, sems
):
    size = shared.shape[0] // (2 * count)
    copies = []
    work = ((0, mix, out_sum, out_tokens), (size, None, grad_sum, grad_tokens))
    for i, (at, scale, before, out) in enumerate(work):

        def put(cut, total):
            low[i, :, cut] = (before[:, cut] + total).astype(low.dtype)

        blocks = [part(shared, 2 * j * size + at, size) for j in range(count)]
        token_sums(subs, place, scale, scratch, rows, blocks, put)
        copies.append(pltpu.make_async_copy(low.at[i], out, sems.at[i]))
        copies[-1].start()
    for copy in copies:
        copy.wait()


def half_starts(half_width):
    half = lax.axis_index("ffn")
    own = pl.multiple_of(half * half_width, half_width)
    other = pl.multiple_of((1 - half) * half_width, half_width)
    return own, other


def chunk(i, step, base=0):
    return pl.ds(base + pl.multiple_of(i * step, step), step)


def dot(left, right):
    return jnp.dot(left, right, preferred_element_type=jnp.float32)


def halves_of_output(devices, subs, step, scratch, own_half, term, keep, send):
    size = scratch.shape[0] // devices
    for at in range(0, subs * LANES, step):
        value = term(at)
        for i in range(step // LANES):
            spread_lanes(scratch, at // LANES + i, subs, value[:, lanes_of(i)])
    split_terms(devices // 2 - 1, size, scratch, own_half, keep, send)


def forward_kernel(devices, subs, step, *refs):
    half = devices // 2
    x_sent, x_swapped = refs[:half], refs[half : 2 * half]
    w_gate, w_up, x_full, gate, up, hidden, scratch = refs[2 * half :]
    full_rows(devices, subs, scratch, x_sent, x_swapped, x_full)
    for cols in pieces_of(gate.shape[1], step):
        gate_low = dot(x_full[...], w_gate[0, :, cols]).astype(jnp.bfloat16)
        up_low = dot(x_full[...], w_up[0, :, cols]).astype(jnp.bfloat16)
        gate[:, cols] = gate_low
        up[:, cols] = up_low
        value = gate_low.astype(jnp.float32)
        hidden[:, cols] = (value * jax.nn.sigmoid(value) * up_low.astype(jnp.float32)).astype(jnp.bfloat16)


def output_kernel(devices, subs, step, hidden, w_down, keep_own, keep_other, send_own, send_other, scratch):
    own, other = half_starts(subs * LANES)

    def term(start):
        return lambda at: dot(hidden[...], w_down[0, :, pl.ds(start + at, step)])

    halves_of_output(devices, subs, step, scratch, False, term(other), keep_other, send_other)
    halves_of_output(devices, subs, step, scratch, True, term(own), keep_own, send_own)


def input_term(step, pre_gate, pre_up, w_gate, w_up, start):
    def term(at):
        there = pl.ds(start + at, step)
        return contract_cols(pre_gate[...], w_gate[0, there, :]) + contract_cols(pre_up[...], w_up[0, there, :])

    return term


def backward_kernel(
    devices,
    subs,
    step,
    g_sent,
    g_swapped,
    gate,
    up,
    w_gate,
    w_up,
    w_down,
    g_full,
    pre_gate,
    pre_up,
    keep_other,
    send_other,
    scratch,
):
    _, other = half_starts(subs * LANES)
    full_rows(devices, subs, scratch, [g_sent], [g_swapped], g_full)

    def pull(i, carry):
        cols = chunk(i, step)
        low = contract_cols(g_full[...], w_down[0, cols, :]).astype(jnp.bfloat16)
        grad_hidden = low.astype(jnp.float32)
        value = gate[:, cols].astype(jnp.float32)
        sig = jax.nn.sigmoid(value)
        pre_gate[:, cols] = (
            grad_hidden * up[:, cols].astype(jnp.float32) * sig * (1.0 + value * (1.0 - sig))
        ).astype(jnp.bfloat16)
        pre_up[:, cols] = (grad_hidden * value * sig).astype(jnp.bfloat16)
        return carry

    lax.fori_loop(0, gate.shape[1] // step, pull, 0)
    term = input_term(step, pre_gate, pre_up, w_gate, w_up, other)
    halves_of_output(devices, subs, step, scratch, False, term, keep_other, send_other)


def backward_own_kernel(devices, subs, step, pre_gate, pre_up, w_gate, w_up, keep_own, send_own, scratch):
    own, _ = half_starts(subs * LANES)
    term = input_term(step, pre_gate, pre_up, w_gate, w_up, own)
    halves_of_output(devices, subs, step, scratch, True, term, keep_own, send_own)


def flip(value):
    return value.astype(jnp.float32).T


def pieces_of(total, size):
    return [slice(at, min(at + size, total)) for at in range(0, total, size)]


def first_chunk_kernel(hidden, g, turned, out):
    turned[...] = flip(hidden[...]).astype(turned.dtype)
    for cut in pieces_of(out.shape[1], 256):
        out[:, cut] = dot(turned[...], g[:, cut]).astype(out.dtype)


def gradient_kernel(
    step,
    x,
    g,
    hidden_turned,
    first,
    pre_gate,
    pre_up,
    grad_gate,
    grad_up,
    grad_down,
    written,
    turned,
    tall,
    wide,
    tall_sems,
    wide_sems,
    first_sem,
):
    width, lanes = x.shape[1], hidden_turned.shape[0]
    count = width // step
    written[...] = jnp.zeros_like(written)
    first_copy = pltpu.make_async_copy(first, grad_down.at[0, :, 0:step], first_sem)
    first_copy.start()

    def wide_copy(i, slot):
        return pltpu.make_async_copy(wide.at[slot], grad_down.at[0, :, chunk(i, step)], wide_sems.at[slot])

    def tall_copy(which, out, i, slot):
        return pltpu.make_async_copy(tall.at[which, slot], out.at[0, chunk(i, step), :], tall_sems.at[which, slot])

    def down(i, carry):
        slot = i % 2

        @pl.when(i >= 3)
        def _():
            wide_copy(i - 2, slot).wait()

        for cut in pieces_of(step, 256):
            right = g[:, chunk(i, step)][:, cut]
            wide[slot, :, cut] = dot(hidden_turned[...], right).astype(wide.dtype)
        wide_copy(i, slot).start()
        return carry

    lax.fori_loop(1, count, down, 0)

    def inputs(i, carry):
        slot = i % 2
        turned[...] = flip(x[:, chunk(i, step)]).astype(turned.dtype)
        for which, (right, out) in enumerate(((pre_gate, grad_gate), (pre_up, grad_up))):

            @pl.when(i >= 2)
            def _():
                tall_copy(which, out, i - 2, slot).wait()

            for cut in pieces_of(lanes, 256):
                for high in pieces_of(step, 512):
                    tall[which, slot, high, cut] = dot(turned[high, :], right[:, cut]).astype(tall.dtype)
            tall_copy(which, out, i, slot).start()
        return carry

    lax.fori_loop(0, count, inputs, 0)
    first_copy.wait()
    for i in range(max(1, count - 2), count):
        wide_copy(i, i % 2).wait()
    for i in range(max(0, count - 2), count):
        tall_copy(0, grad_gate, i, i % 2).wait()
        tall_copy(1, grad_up, i, i % 2).wait()


def exchange(blocks, masks, devices):
    arrived = []
    for block, mask in zip(blocks, masks):
        pairs = [(2 * i + core, 2 * (i ^ (mask + core)) + core) for i in range(devices) for core in range(2)]
        arrived.append(lax.ppermute(block, ("expert", "ffn"), pairs))
    return arrived


def exchange_near(block, devices):
    return lax.ppermute(block, "expert", [(i, i ^ 1) for i in range(devices)])


def swap(value):
    return lax.ppermute(value, "ffn", [(0, 1), (1, 0)])


def in_hbm(values):
    return [pltpu.with_memory_space_constraint(value, pltpu.HBM) for value in values]


def one_piece_shards(tokens, grad_out, route_ids, route_weight, gate_weight, up_weight, down_weight):
    tok_dev, sub_width = tokens.shape
    top_count = route_ids.shape[1]
    width, lanes = gate_weight.shape[1:]
    devices = lax.axis_size("expert")
    capacity = max(2, min(tok_dev, (9 * tok_dev * top_count + 8 * EXPERTS - 1) // (8 * EXPERTS)))
    rows = devices * capacity
    subs = sub_width // LANES
    low, full = jnp.bfloat16, jnp.float32
    size = capacity * subs
    count = devices // 2 - 1
    spread_scratch = [pltpu.VMEM((devices * size, LANES), full)]
    step = 256
    half_flops = 2 * rows * width * lanes // 2

    def lines(number, dtype=low):
        return jax.ShapeDtypeStruct((number * size, LANES), dtype)

    def lines_in_vmem(number, dtype=low):
        return vmem((number * size, LANES), dtype)

    sources = (route_ids.T, route_weight.T, tokens, grad_out)
    other_rows = count * capacity
    x_mine, g_mine, near, here, theirs, place, mix, place_other, mix_other = call(
        functools.partial(route_kernel, devices, capacity, subs),
        [lines(count), lines(count), lines(2), lines(2)]
        + [lines(2 * count)]
        + [jax.ShapeDtypeStruct((rows, tok_dev), low), jax.ShapeDtypeStruct((rows, LANES), full)]
        + [jax.ShapeDtypeStruct((other_rows, tok_dev), low), jax.ShapeDtypeStruct((other_rows, LANES), full)],
        in_hbm(sources),
        in_spaces=[pl.ANY] * 4,
        scratch=spread_scratch
        + [pltpu.VMEM(value.shape, value.dtype) for value in sources]
        + [pltpu.SemaphoreType.DMA((4,))],
        traffic=4 * tok_dev * sub_width,
    )
    masks = even_masks(devices)
    late = [devices // 4 - 1]
    late_block = jax.ShapeDtypeStruct((2 * size + 16, LANES), low)
    packed = call(
        functools.partial(pack_kernel, size, late),
        [late_block if j in late else lines(4) for j in range(count)] + [late_block] * len(late),
        (x_mine, g_mine, swap(theirs)),
        flops=24 * half_flops,
    )
    x_arrived = exchange(packed[:count], masks, devices)
    g_arrived = list(x_arrived)
    for j, block in zip(late, packed[count:]):
        (g_arrived[j],) = exchange([block], masks[j:], devices)
    near = exchange_near(near, devices)

    weights = (gate_weight, up_weight, down_weight)
    w_gate, w_up, w_down = [pltpu.with_memory_space_constraint(w, pltpu.VMEM) for w in weights]

    x_sent = call(
        functools.partial(gather_x_kernel, size), [lines(2)] * (count + 1), (*x_arrived, near, here)
    )
    x_swapped = [swap(value) for value in x_sent]
    terms = [
        lines_in_vmem(count + 2, full),
        lines_in_vmem(count, full),
        lines_in_vmem(count),
        lines_in_vmem(count + 2),
    ]
    x_full, gate, up, hidden = call(
        functools.partial(forward_kernel, devices, subs, step),
        [vmem((rows, width), low)] + [vmem((rows, lanes), low)] * 3,
        (*x_sent, *x_swapped, w_gate, w_up),
        scratch=spread_scratch,
    )
    (g_sent,) = call(
        functools.partial(gather_g_kernel, size, late), [lines(devices)], (*g_arrived, near, here, hidden)
    )
    g_swapped = swap(g_sent)
    out_own, out_other, send_own, send_other = call(
        functools.partial(output_kernel, devices, subs, 2 * step),
        terms,
        (hidden, w_down),
        scratch=spread_scratch,
        flops=2 * half_flops,
    )
    out_terms = (out_own, out_other, swap(send_other), swap(send_own))
    g_full, pre_gate, pre_up, dx_other, send_other = call(
        functools.partial(backward_kernel, devices, subs, step),
        [vmem((rows, width), low)] + [vmem((rows, lanes), low)] * 2 + [terms[1], terms[3]],
        (g_sent, g_swapped, gate, up, w_gate, w_up, w_down),
        scratch=spread_scratch,
        flops=4 * half_flops,
    )
    came_own = swap(send_other)
    dx_own, send_own = call(
        functools.partial(backward_own_kernel, devices, subs, step),
        [terms[0], terms[2]],
        (pre_gate, pre_up, w_gate, w_up),
        scratch=spread_scratch,
        flops=2 * half_flops,
    )
    dx_terms = (dx_own, dx_other, came_own, swap(send_own))
    cut = 1024 if width % 1024 == 0 else width
    hidden_turned, first = call(
        first_chunk_kernel,
        [vmem((lanes, rows), low), vmem((lanes, cut), low)],
        (hidden, g_full),
        flops=2 * half_flops * cut // width,
    )
    *leaving, back, kept = call(
        functools.partial(leave_kernel, size),
        [lines(4)] * count + [lines(2)] * 2,
        (*out_terms, *dx_terms, first),
    )
    returned = exchange(leaving, masks, devices)
    back = exchange_near(back, devices)
    grad_gate, grad_up, grad_down, written = call(
        functools.partial(gradient_kernel, cut),
        [jax.ShapeDtypeStruct(w.shape, low) for w in weights] + [vmem((8, LANES), full)],
        (x_full, g_full, hidden_turned, first, pre_gate, pre_up),
        out_spaces=[pl.ANY] * 3 + [pltpu.VMEM],
        scratch=[
            pltpu.VMEM((cut, rows), low),
            pltpu.VMEM((2, 2, cut, lanes), low),
            pltpu.VMEM((2, lanes, cut), low),
            pltpu.SemaphoreType.DMA((2, 2)),
            pltpu.SemaphoreType.DMA((2,)),
            pltpu.SemaphoreType.DMA,
        ],
        flops=6 * half_flops,
        traffic=sum(w.size * 2 for w in weights),
        limit=32,
    )
    (sharing,) = call(functools.partial(share_kernel, size), [lines(2 * count)], (*returned, back, written))
    shared = swap(sharing)
    sums = call(
        functools.partial(join_kernel, count, subs),
        [vmem((tok_dev, sub_width), full)] * 2,
        (place, mix, *returned, back, kept),
        scratch=spread_scratch + [pltpu.VMEM((rows, sub_width), low)],
        flops=4 * rows * tok_dev * sub_width,
    )
    out_tokens, grad_tokens = call(
        functools.partial(finish_kernel, count, subs),
        [jax.ShapeDtypeStruct((tok_dev, sub_width), low)] * 2,
        (place_other, mix_other, shared, *sums),
        out_spaces=[pl.ANY] * 2,
        scratch=[
            pltpu.VMEM((count * size, LANES), full),
            pltpu.VMEM((other_rows, sub_width), low),
            pltpu.VMEM((2, tok_dev, sub_width), low),
            pltpu.SemaphoreType.DMA((2,)),
        ],
        traffic=8 * tok_dev * sub_width,
    )
    return out_tokens, grad_tokens, grad_gate, grad_up, grad_down


def shards(*args):
    tokens, gate_weight = args[0], args[4]
    halves = lax.axis_size("ffn")
    devices = lax.axis_size("expert")
    if halves == 2 and devices >= 4 and devices & (devices - 1) == 0 and tokens.shape[1] * halves == gate_weight.shape[1]:
        return one_piece_shards(*args)
    return general_shards(*args)


def solution(mesh):
    in_specs = (
        P(("groups", "expert"), "ffn"),
        P(("groups", "expert"), "ffn"),
        P(("groups", "expert"), None),
        P(("groups", "expert"), None),
        P("expert", None, "ffn"),
        P("expert", None, "ffn"),
        P("expert", "ffn", None),
    )
    out_specs = (
        P(("groups", "expert"), "ffn"),
        P(("groups", "expert"), "ffn"),
        P(("groups", "expert"), None, "ffn"),
        P(("groups", "expert"), None, "ffn"),
        P(("groups", "expert"), "ffn", None),
    )
    return jax.shard_map(shards, mesh=mesh, in_specs=in_specs, out_specs=out_specs, check_vma=False)
```

```python
import functools

import jax
import jax.numpy as jnp
from jax import lax
from jax.experimental import pallas as pl
from jax.experimental.pallas import tpu as pltpu
from jax.sharding import PartitionSpec as P

EXPERTS = 128
LANES = 128
MIB = 1024 * 1024


def contract_rows(left, right):
    return lax.dot_general(
        left, right, (((0,), (0,)), ((), ())), preferred_element_type=jnp.float32
    )


def contract_cols(left, right):
    return lax.dot_general(
        left, right, (((1,), (1,)), ((), ())), preferred_element_type=jnp.float32
    )


def general_shards(tokens, grad_out, route_ids, route_weight, gate_weight, up_weight, down_weight):
    tokens, grad_out = (
        lax.all_gather(tokens, "ffn", axis=1, tiled=True),
        lax.all_gather(grad_out, "ffn", axis=1, tiled=True),
    )
    tok_dev, width = tokens.shape
    top_count = route_ids.shape[1]
    piece_width = gate_weight.shape[1]
    hidden_half = gate_weight.shape[2]
    pieces = width // piece_width
    devices = lax.axis_size("expert")
    flight = devices // pieces
    halves = lax.axis_size("ffn")
    sub_width = piece_width // halves
    capacity = max(2, min(tok_dev, (9 * tok_dev * top_count + 8 * EXPERTS - 1) // (8 * EXPERTS)))
    total_rows = devices * capacity
    expert_ids = jnp.arange(flight, dtype=jnp.int32)
    member = jnp.zeros((tok_dev, flight), jnp.float32)
    mixing = jnp.zeros((tok_dev, flight), jnp.float32)
    for route in range(top_count):
        hit = (route_ids[:, route : route + 1] == expert_ids[None, :]).astype(jnp.float32)
        member = member + hit
        mixing = mixing + hit * route_weight[:, route : route + 1]
    slots = jnp.cumsum(member, axis=0) - member
    place = member[:, :, None] * (
        slots[:, :, None] == jnp.arange(capacity, dtype=jnp.float32)
    ).astype(jnp.float32)
    weighted = place * mixing[:, :, None]
    place_low = place.astype(jnp.bfloat16)
    x_four = tokens.reshape(tok_dev, halves, pieces, sub_width)
    g_four = grad_out.reshape(tok_dev, halves, pieces, sub_width)
    x_parts = []
    g_parts = []
    for half in range(halves):
        x_parts.append(
            jnp.einsum(
                "Tec,Tjr->ejcr", place_low, x_four[:, half], preferred_element_type=jnp.float32
            )
        )
        g_parts.append(jnp.einsum("Tec,Tjr->ejcr", weighted, g_four[:, half].astype(jnp.float32)))
    x_send = jnp.concatenate(x_parts, axis=3).astype(jnp.bfloat16).reshape(total_rows, piece_width)
    g_send = jnp.concatenate(g_parts, axis=3).astype(jnp.bfloat16).reshape(total_rows, piece_width)

    def return_parts(values):
        arrived = lax.all_to_all(values, "expert", split_axis=0, concat_axis=0, tiled=True)
        lanes = arrived.shape[1]
        return arrived.astype(jnp.float32).reshape(flight, pieces, capacity, lanes).sum(axis=1)

    def spread_rows(values):
        lanes = values.shape[2]
        copies = jnp.broadcast_to(values[:, None], (flight, pieces, capacity, lanes)).reshape(
            total_rows, lanes
        )
        return lax.all_to_all(copies, "expert", split_axis=0, concat_axis=0, tiled=True)

    def finish(term, mix):
        summed = lax.psum_scatter(term, "ffn", scatter_dimension=1, tiled=True)
        back = lax.all_to_all(summed, "expert", split_axis=0, concat_axis=0, tiled=True)
        back = back.reshape(flight, pieces, capacity, sub_width)
        joined = jnp.einsum("Tec,ejcr->Tjr", mix, back)
        return joined.reshape(tok_dev, pieces * sub_width).astype(jnp.bfloat16)

    rows = lax.all_to_all(x_send, "expert", split_axis=0, concat_axis=0, tiled=True)
    w_gate = gate_weight[0]
    w_up = up_weight[0]
    w_down = down_weight[0]
    partial_value = jnp.concatenate(
        [
            jnp.dot(rows, w_gate, preferred_element_type=jnp.float32),
            jnp.dot(rows, w_up, preferred_element_type=jnp.float32),
        ],
        axis=1,
    )
    summed = return_parts(partial_value.astype(jnp.bfloat16))
    gate = summed[:, :, :hidden_half]
    up = summed[:, :, hidden_half:]
    sig = jax.nn.sigmoid(gate)
    act = gate * sig
    hidden = (act * up).astype(jnp.bfloat16)
    h_rows = spread_rows(hidden)
    out_term = jnp.dot(h_rows, w_down, preferred_element_type=jnp.float32)
    out_tokens = finish(out_term, weighted)
    grads = lax.all_to_all(g_send, "expert", split_axis=0, concat_axis=0, tiled=True)
    grad_down = contract_rows(h_rows, grads).astype(jnp.bfloat16)
    hidden_part = contract_cols(grads, w_down).astype(jnp.bfloat16)
    grad_hidden = return_parts(hidden_part)
    pre_gate = (grad_hidden * up * sig * (1.0 + gate * (1.0 - sig))).astype(jnp.bfloat16)
    pre_up = (grad_hidden * act).astype(jnp.bfloat16)
    both = spread_rows(jnp.concatenate([pre_gate, pre_up], axis=2))
    d_gate_rows = both[:, :hidden_half]
    d_up_rows = both[:, hidden_half:]
    grad_gate = contract_rows(rows, d_gate_rows).astype(jnp.bfloat16)
    grad_up = contract_rows(rows, d_up_rows).astype(jnp.bfloat16)
    x_term = contract_cols(d_gate_rows, w_gate) + contract_cols(d_up_rows, w_up)
    grad_tokens = finish(x_term, place)
    return (out_tokens, grad_tokens, grad_gate[None], grad_up[None], grad_down[None])


def vmem(shape, dtype):
    return pltpu.VMEM(shape, dtype)


def call(kernel, out_shape, args, in_spaces=None, out_spaces=None, flops=0, traffic=0, scratch=(), limit=16):
    spaces = in_spaces or [pltpu.VMEM] * len(args)
    outs = out_spaces or [pltpu.VMEM] * len(out_shape)
    return pl.pallas_call(
        kernel,
        out_shape=tuple(out_shape),
        in_specs=[pl.BlockSpec(memory_space=space) for space in spaces],
        out_specs=tuple(pl.BlockSpec(memory_space=space) for space in outs),
        scratch_shapes=list(scratch),
        compiler_params=pltpu.CompilerParams(vmem_limit_bytes=limit * MIB),
        cost_estimate=pl.CostEstimate(flops=flops, bytes_accessed=traffic, transcendentals=0),
    )(*args)


def blocks_to_rows(scratch, blocks, put, subs):
    size = blocks[0].shape[0]
    for p, block in enumerate(blocks):
        scratch[p * size : (p + 1) * size, :] = block[...].astype(jnp.float32)
    for sub in range(subs):
        put(sub, scratch[pl.ds(sub, len(blocks) * size // subs, stride=subs), :])


def spread_lanes(scratch, sub, subs, value):
    scratch[pl.ds(sub, value.shape[0], stride=subs), :] = value


def part(ref, start, count):
    return ref.at[start : start + count, :]


def lanes_of(sub):
    return slice(sub * LANES, (sub + 1) * LANES)


def even_masks(count):
    return [*reversed(range(count // 2, count, 2)), *range(2, count // 2, 2)]


def route_kernel(devices, capacity, subs, ids_in, weight_in, x_in, g_in, *refs):
    x_mine, g_mine, near, here, theirs, place_out, mix_out, place_other, mix_other, scratch, ids, weight, x, g, sems = refs
    pairs = ((ids_in, ids), (weight_in, weight), (x_in, x), (g_in, g))
    copies = [pltpu.make_async_copy(src, dst, sems.at[i]) for i, (src, dst) in enumerate(pairs)]
    for copy in copies:
        copy.start()
    top, tok = ids.shape
    rows = devices * capacity
    core = lax.axis_index("ffn")
    masks = even_masks(devices)
    masks = [mask + core for mask in masks] + [mask + 1 - core for mask in masks] + [1, 0]
    order = lax.broadcasted_iota(jnp.int32, (devices, tok), 0)
    bits = jnp.zeros((devices, tok), jnp.int32)
    for p, mask in enumerate(masks):
        bits = jnp.where(order == p, mask, bits)
    expert = bits ^ lax.axis_index("expert")
    member = jnp.zeros((devices, tok), jnp.float32)
    mixing = jnp.zeros((devices, tok), jnp.float32)
    copies[0].wait()
    copies[1].wait()
    for route in range(top):
        hit = ids[route : route + 1, :] == expert
        member = jnp.where(hit, 1.0, member)
        mixing = jnp.where(hit, weight[route : route + 1, :], mixing)
    before = lax.broadcasted_iota(jnp.int32, (tok, tok), 0) < lax.broadcasted_iota(jnp.int32, (tok, tok), 1)
    slots = dot(member.astype(jnp.bfloat16), jnp.where(before, 1.0, 0.0).astype(jnp.bfloat16))
    target = jnp.where(member > 0, slots + capacity * order.astype(jnp.float32), -1.0)
    count = devices // 2 - 1

    def placed(first, number):
        row = lax.broadcasted_iota(jnp.int32, (number, tok), 0).astype(jnp.float32) + first
        place = jnp.zeros((number, tok), jnp.float32)
        mix = jnp.zeros((number, tok), jnp.float32)
        for p in range(devices):
            equal = target[p : p + 1, :] == row
            place = jnp.where(equal, 1.0, place)
            mix = jnp.where(equal, mixing[p : p + 1, :], mix)
        row_weight = jnp.broadcast_to(jnp.sum(mix, axis=1, keepdims=True), (number, LANES))
        return place.astype(jnp.bfloat16), row_weight

    low, row_weight = placed(0, rows)
    place_out[...] = low
    mix_out[...] = row_weight
    place_other[...], mix_other[...] = placed(count * capacity, count * capacity)
    size = capacity * subs

    def write(mine, at):
        def block(p):
            return scratch[p * size : (p + 1) * size, :].astype(theirs.dtype)

        for j in range(count):
            part(mine, j * size, size)[...] = block(j)
            part(theirs, (at + j) * size, size)[...] = block(count + j)
        start = size if at else 0
        part(near, start, size)[...] = block(2 * count)
        part(here, start, size)[...] = block(2 * count + 1)

    copies[2].wait()
    for sub in range(subs):
        spread_lanes(scratch, sub, subs, dot(low, x[:, lanes_of(sub)]))
    write(x_mine, 0)
    copies[3].wait()
    for sub in range(subs):
        spread_lanes(scratch, sub, subs, dot(low, g[:, lanes_of(sub)]) * row_weight)
    write(g_mine, count)


def pack_kernel(size, late, x_mine, g_mine, swapped, *outs):
    count = len(outs) - len(late)
    lates = dict(zip(late, outs[count:]))
    for j, out in enumerate(outs[:count]):
        places = ((out, 0), (lates.get(j, out), 0 if j in late else 2 * size))
        for i, (mine, (to, at)) in enumerate(zip((x_mine, g_mine), places)):
            part(to, at, size)[...] = part(mine, j * size, size)[...]
            part(to, at + size, size)[...] = part(swapped, (i * count + j) * size, size)[...]
    for out in [*lates.values(), *[outs[j] for j in late]]:
        rest = part(out, 2 * size, out.shape[0] - 2 * size)
        rest[...] = jnp.zeros(rest.shape, rest.dtype)


def gather_x_kernel(size, *refs):
    count = (len(refs) - 3) // 2
    blocks, (near, here), outs = refs[:count], refs[count : count + 2], refs[count + 2 :]
    for block, out in zip(blocks, outs):
        out[...] = part(block, 0, 2 * size)[...]
    part(outs[-1], 0, size)[...] = part(near, 0, size)[...]
    part(outs[-1], size, size)[...] = part(here, 0, size)[...]


def gather_g_kernel(size, late, *refs):
    blocks, (near, here, _, out) = refs[:-4], refs[-4:]
    for j, block in enumerate(blocks):
        start = 0 if j in late else 2 * size
        part(out, 2 * j * size, 2 * size)[...] = part(block, start, 2 * size)[...]
    part(out, 2 * len(blocks) * size, size)[...] = part(near, size, size)[...]
    part(out, (2 * len(blocks) + 1) * size, size)[...] = part(here, size, size)[...]


def full_rows(devices, subs, scratch, own_sent, other_sent, out):
    per = devices // len(own_sent)
    size = own_sent[0].shape[0] // per
    count = devices // 2 - 1
    own, other = half_starts(out.shape[1] // 2)
    first, second, last = range(0, 2 * count, 2), range(1, 2 * count, 2), range(2 * count, devices)
    layouts = (
        (own, [(own_sent, i) for i in first] + [(other_sent, i) for i in second] + [(own_sent, i) for i in last]),
        (other, [(own_sent, i) for i in second] + [(other_sent, i) for i in first] + [(other_sent, i) for i in last]),
    )
    for start, layout in layouts:

        def put(sub, value):
            out[:, pl.ds(start + sub * LANES, LANES)] = value.astype(out.dtype)

        blocks_to_rows(scratch, [part(refs[i // per], i % per * size, size) for refs, i in layout], put, subs)


def split_terms(count, size, scratch, own_half, keep, send):
    keep[0 : count * size, :] = scratch[0 : count * size, :]
    send[0 : count * size, :] = scratch[count * size : 2 * count * size, :].astype(send.dtype)
    rest = scratch[2 * count * size :, :]
    if own_half:
        keep[count * size :, :] = rest
    else:
        send[count * size :, :] = rest.astype(send.dtype)


def leave_kernel(size, *refs):
    terms, outs = (refs[:4], refs[4:8]), refs[9:]
    count = len(outs) - 2
    for at, (keep_own, keep_other, came_own, came_other) in zip((0, size), terms):

        def own(p):
            total = part(keep_own, p * size, size)[...] + part(came_own, p * size, size)[...].astype(jnp.float32)
            return total.astype(outs[0].dtype)

        for j, out in enumerate(outs[:count]):
            part(out, at, size)[...] = own(j)
            total = part(keep_other, j * size, size)[...] + part(came_other, j * size, size)[...].astype(jnp.float32)
            part(out, 2 * size + at, size)[...] = total.astype(out.dtype)
        part(outs[count], at, size)[...] = own(count)
        part(outs[count + 1], at, size)[...] = own(count + 1)


def share_kernel(size, *refs):
    blocks, (_, _, out) = refs[:-3], refs[-3:]
    for j, block in enumerate(blocks):
        part(out, 2 * j * size, 2 * size)[...] = part(block, 2 * size, 2 * size)[...]


def token_sums(subs, place, mix, scratch, rows, blocks, put):
    size = scratch.shape[0] // len(blocks)
    for p, block in enumerate(blocks):
        here = slice(p * size, (p + 1) * size)
        scratch[here, :] = jnp.zeros((size, LANES), jnp.float32) if block is None else block[...].astype(jnp.float32)
    for sub in range(subs):
        value = scratch[pl.ds(sub, rows.shape[0], stride=subs), :]
        if mix is not None:
            value = value * mix[...]
        rows[:, lanes_of(sub)] = value.astype(rows.dtype)
    for cut in pieces_of(subs * LANES, 512):
        put(cut, contract_rows(place[...], rows[:, cut]))


def join_kernel(count, subs, place, mix, *refs):
    blocks, (near, here, out_sum, grad_sum, scratch, rows) = refs[:count], refs[count:]
    size = near.shape[0] // 2
    for at, scale, out in ((0, mix, out_sum), (size, None, grad_sum)):

        def put(cut, total):
            out[:, cut] = total

        first = [part(block, at, size) for block in blocks]
        last = [part(near, at, size), part(here, at, size)]
        token_sums(subs, place, scale, scratch, rows, first + [None] * count + last, put)


def finish_kernel(
    count, subs, place, mix, shared, out_sum, grad_sum, out_tokens, grad_tokens, scratch, rows, low, sems
):
    size = shared.shape[0] // (2 * count)
    copies = []
    work = ((0, mix, out_sum, out_tokens), (size, None, grad_sum, grad_tokens))
    for i, (at, scale, before, out) in enumerate(work):

        def put(cut, total):
            low[i, :, cut] = (before[:, cut] + total).astype(low.dtype)

        blocks = [part(shared, 2 * j * size + at, size) for j in range(count)]
        token_sums(subs, place, scale, scratch, rows, blocks, put)
        copies.append(pltpu.make_async_copy(low.at[i], out, sems.at[i]))
        copies[-1].start()
    for copy in copies:
        copy.wait()


def half_starts(half_width):
    half = lax.axis_index("ffn")
    own = pl.multiple_of(half * half_width, half_width)
    other = pl.multiple_of((1 - half) * half_width, half_width)
    return own, other


def chunk(i, step, base=0):
    return pl.ds(base + pl.multiple_of(i * step, step), step)


def dot(left, right):
    return jnp.dot(left, right, preferred_element_type=jnp.float32)


def halves_of_output(devices, subs, step, scratch, own_half, term, keep, send):
    size = scratch.shape[0] // devices
    for at in range(0, subs * LANES, step):
        value = term(at)
        for i in range(step // LANES):
            spread_lanes(scratch, at // LANES + i, subs, value[:, lanes_of(i)])
    split_terms(devices // 2 - 1, size, scratch, own_half, keep, send)


def forward_kernel(devices, subs, step, *refs):
    half = devices // 2
    x_sent, x_swapped = refs[:half], refs[half : 2 * half]
    w_gate, w_up, x_full, gate, up, hidden, scratch = refs[2 * half :]
    full_rows(devices, subs, scratch, x_sent, x_swapped, x_full)
    for cols in pieces_of(gate.shape[1], step):
        gate_low = dot(x_full[...], w_gate[0, :, cols]).astype(jnp.bfloat16)
        up_low = dot(x_full[...], w_up[0, :, cols]).astype(jnp.bfloat16)
        gate[:, cols] = gate_low
        up[:, cols] = up_low
        value = gate_low.astype(jnp.float32)
        hidden[:, cols] = (value * jax.nn.sigmoid(value) * up_low.astype(jnp.float32)).astype(jnp.bfloat16)


def output_kernel(devices, subs, step, hidden, w_down, keep_own, keep_other, send_own, send_other, scratch):
    own, other = half_starts(subs * LANES)

    def term(start):
        return lambda at: dot(hidden[...], w_down[0, :, pl.ds(start + at, step)])

    halves_of_output(devices, subs, step, scratch, False, term(other), keep_other, send_other)
    halves_of_output(devices, subs, step, scratch, True, term(own), keep_own, send_own)


def input_term(step, pre_gate, pre_up, w_gate, w_up, start):
    def term(at):
        there = pl.ds(start + at, step)
        return contract_cols(pre_gate[...], w_gate[0, there, :]) + contract_cols(pre_up[...], w_up[0, there, :])

    return term


def backward_kernel(
    devices,
    subs,
    step,
    g_sent,
    g_swapped,
    gate,
    up,
    w_gate,
    w_up,
    w_down,
    g_full,
    pre_gate,
    pre_up,
    keep_other,
    send_other,
    scratch,
):
    _, other = half_starts(subs * LANES)
    full_rows(devices, subs, scratch, [g_sent], [g_swapped], g_full)

    def pull(i, carry):
        cols = chunk(i, step)
        low = contract_cols(g_full[...], w_down[0, cols, :]).astype(jnp.bfloat16)
        grad_hidden = low.astype(jnp.float32)
        value = gate[:, cols].astype(jnp.float32)
        sig = jax.nn.sigmoid(value)
        pre_gate[:, cols] = (
            grad_hidden * up[:, cols].astype(jnp.float32) * sig * (1.0 + value * (1.0 - sig))
        ).astype(jnp.bfloat16)
        pre_up[:, cols] = (grad_hidden * value * sig).astype(jnp.bfloat16)
        return carry

    lax.fori_loop(0, gate.shape[1] // step, pull, 0)
    term = input_term(step, pre_gate, pre_up, w_gate, w_up, other)
    halves_of_output(devices, subs, step, scratch, False, term, keep_other, send_other)


def backward_own_kernel(devices, subs, step, pre_gate, pre_up, w_gate, w_up, keep_own, send_own, scratch):
    own, _ = half_starts(subs * LANES)
    term = input_term(step, pre_gate, pre_up, w_gate, w_up, own)
    halves_of_output(devices, subs, step, scratch, True, term, keep_own, send_own)


def flip(value):
    return value.astype(jnp.float32).T


def pieces_of(total, size):
    return [slice(at, min(at + size, total)) for at in range(0, total, size)]


def first_chunk_kernel(hidden, g, turned, out):
    turned[...] = flip(hidden[...]).astype(turned.dtype)
    for cut in pieces_of(out.shape[1], 256):
        out[:, cut] = dot(turned[...], g[:, cut]).astype(out.dtype)


def gradient_kernel(
    step,
    x,
    g,
    hidden_turned,
    first,
    pre_gate,
    pre_up,
    grad_gate,
    grad_up,
    grad_down,
    written,
    turned,
    tall,
    wide,
    tall_sems,
    wide_sems,
    first_sem,
):
    width, lanes = x.shape[1], hidden_turned.shape[0]
    count = width // step
    written[...] = jnp.zeros_like(written)
    first_copy = pltpu.make_async_copy(first, grad_down.at[0, :, 0:step], first_sem)
    first_copy.start()

    cuts = pieces_of(step, 256)

    def wide_copy(i, slot, n):
        there = pl.ds(pl.multiple_of(i * step, step) + cuts[n].start, cuts[n].stop - cuts[n].start)
        return pltpu.make_async_copy(wide.at[slot, :, cuts[n]], grad_down.at[0, :, there], wide_sems.at[slot, n])

    def tall_copy(which, out, i, slot):
        return pltpu.make_async_copy(tall.at[which, slot], out.at[0, chunk(i, step), :], tall_sems.at[which, slot])

    def inputs(i, carry):
        slot = i % 2
        turned[...] = flip(x[:, chunk(i, step)]).astype(turned.dtype)
        for which, (right, out) in enumerate(((pre_gate, grad_gate), (pre_up, grad_up))):

            @pl.when(i >= 2)
            def _():
                tall_copy(which, out, i - 2, slot).wait()

            for cut in pieces_of(lanes, 256):
                for high in pieces_of(step, 1024):
                    tall[which, slot, high, cut] = dot(turned[high, :], right[:, cut]).astype(tall.dtype)
            tall_copy(which, out, i, slot).start()
        return carry

    lax.fori_loop(0, count, inputs, 0)

    def down(i, carry):
        slot = i % 2

        @pl.when(i >= 3)
        def _():
            for n in range(len(cuts)):
                wide_copy(i - 2, slot, n).wait()

        for n, cut in enumerate(cuts):
            right = g[:, chunk(i, step)][:, cut]
            wide[slot, :, cut] = dot(hidden_turned[...], right).astype(wide.dtype)
            wide_copy(i, slot, n).start()
        return carry

    lax.fori_loop(1, count, down, 0)
    first_copy.wait()
    for i in range(max(1, count - 2), count):
        for n in range(len(cuts)):
            wide_copy(i, i % 2, n).wait()
    for i in range(max(0, count - 2), count):
        tall_copy(0, grad_gate, i, i % 2).wait()
        tall_copy(1, grad_up, i, i % 2).wait()


def exchange(blocks, masks, devices):
    arrived = []
    for block, mask in zip(blocks, masks):
        pairs = [(2 * i + core, 2 * (i ^ (mask + core)) + core) for i in range(devices) for core in range(2)]
        arrived.append(lax.ppermute(block, ("expert", "ffn"), pairs))
    return arrived


def exchange_near(block, devices):
    return lax.ppermute(block, "expert", [(i, i ^ 1) for i in range(devices)])


def swap(value):
    return lax.ppermute(value, "ffn", [(0, 1), (1, 0)])


def in_hbm(values):
    return [pltpu.with_memory_space_constraint(value, pltpu.HBM) for value in values]


def one_piece_shards(tokens, grad_out, route_ids, route_weight, gate_weight, up_weight, down_weight):
    tok_dev, sub_width = tokens.shape
    top_count = route_ids.shape[1]
    width, lanes = gate_weight.shape[1:]
    devices = lax.axis_size("expert")
    capacity = max(2, min(tok_dev, (9 * tok_dev * top_count + 8 * EXPERTS - 1) // (8 * EXPERTS)))
    rows = devices * capacity
    subs = sub_width // LANES
    low, full = jnp.bfloat16, jnp.float32
    size = capacity * subs
    count = devices // 2 - 1
    spread_scratch = [pltpu.VMEM((devices * size, LANES), full)]
    step = 256
    half_flops = 2 * rows * width * lanes // 2

    def lines(number, dtype=low):
        return jax.ShapeDtypeStruct((number * size, LANES), dtype)

    def lines_in_vmem(number, dtype=low):
        return vmem((number * size, LANES), dtype)

    sources = (route_ids.T, route_weight.T, tokens, grad_out)
    other_rows = count * capacity
    x_mine, g_mine, near, here, theirs, place, mix, place_other, mix_other = call(
        functools.partial(route_kernel, devices, capacity, subs),
        [lines(count), lines(count), lines(2), lines(2)]
        + [lines(2 * count)]
        + [jax.ShapeDtypeStruct((rows, tok_dev), low), jax.ShapeDtypeStruct((rows, LANES), full)]
        + [jax.ShapeDtypeStruct((other_rows, tok_dev), low), jax.ShapeDtypeStruct((other_rows, LANES), full)],
        in_hbm(sources),
        in_spaces=[pl.ANY] * 4,
        scratch=spread_scratch
        + [pltpu.VMEM(value.shape, value.dtype) for value in sources]
        + [pltpu.SemaphoreType.DMA((4,))],
        traffic=4 * tok_dev * sub_width,
    )
    masks = even_masks(devices)
    late = [devices // 4 - 1]
    late_block = jax.ShapeDtypeStruct((2 * size + 16, LANES), low)
    packed = call(
        functools.partial(pack_kernel, size, late),
        [late_block if j in late else lines(4) for j in range(count)] + [late_block] * len(late),
        (x_mine, g_mine, swap(theirs)),
        flops=24 * half_flops,
    )
    x_arrived = exchange(packed[:count], masks, devices)
    g_arrived = list(x_arrived)
    for j, block in zip(late, packed[count:]):
        (g_arrived[j],) = exchange([block], masks[j:], devices)
    near = exchange_near(near, devices)

    weights = (gate_weight, up_weight, down_weight)
    w_gate, w_up, w_down = [pltpu.with_memory_space_constraint(w, pltpu.VMEM) for w in weights]

    x_sent = call(
        functools.partial(gather_x_kernel, size), [lines(2)] * (count + 1), (*x_arrived, near, here)
    )
    x_swapped = [swap(value) for value in x_sent]
    terms = [
        lines_in_vmem(count + 2, full),
        lines_in_vmem(count, full),
        lines_in_vmem(count),
        lines_in_vmem(count + 2),
    ]
    x_full, gate, up, hidden = call(
        functools.partial(forward_kernel, devices, subs, step),
        [vmem((rows, width), low)] + [vmem((rows, lanes), low)] * 3,
        (*x_sent, *x_swapped, w_gate, w_up),
        scratch=spread_scratch,
    )
    (g_sent,) = call(
        functools.partial(gather_g_kernel, size, late), [lines(devices)], (*g_arrived, near, here, hidden)
    )
    g_swapped = swap(g_sent)
    out_own, out_other, send_own, send_other = call(
        functools.partial(output_kernel, devices, subs, 2 * step),
        terms,
        (hidden, w_down),
        scratch=spread_scratch,
        flops=2 * half_flops,
    )
    out_terms = (out_own, out_other, swap(send_other), swap(send_own))
    g_full, pre_gate, pre_up, dx_other, send_other = call(
        functools.partial(backward_kernel, devices, subs, step),
        [vmem((rows, width), low)] + [vmem((rows, lanes), low)] * 2 + [terms[1], terms[3]],
        (g_sent, g_swapped, gate, up, w_gate, w_up, w_down),
        scratch=spread_scratch,
        flops=4 * half_flops,
    )
    came_own = swap(send_other)
    dx_own, send_own = call(
        functools.partial(backward_own_kernel, devices, subs, step),
        [terms[0], terms[2]],
        (pre_gate, pre_up, w_gate, w_up),
        scratch=spread_scratch,
        flops=2 * half_flops,
    )
    dx_terms = (dx_own, dx_other, came_own, swap(send_own))
    cut = 1024 if width % 1024 == 0 else width
    hidden_turned, first = call(
        first_chunk_kernel,
        [vmem((lanes, rows), low), vmem((lanes, cut), low)],
        (hidden, g_full),
        flops=2 * half_flops * cut // width,
    )
    *leaving, back, kept = call(
        functools.partial(leave_kernel, size),
        [lines(4)] * count + [lines(2)] * 2,
        (*out_terms, *dx_terms, first),
    )
    returned = exchange(leaving, masks, devices)
    back = exchange_near(back, devices)
    grad_gate, grad_up, grad_down, written = call(
        functools.partial(gradient_kernel, cut),
        [jax.ShapeDtypeStruct(w.shape, low) for w in weights] + [vmem((8, LANES), full)],
        (x_full, g_full, hidden_turned, first, pre_gate, pre_up),
        out_spaces=[pl.ANY] * 3 + [pltpu.VMEM],
        scratch=[
            pltpu.VMEM((cut, rows), low),
            pltpu.VMEM((2, 2, cut, lanes), low),
            pltpu.VMEM((2, lanes, cut), low),
            pltpu.SemaphoreType.DMA((2, 2)),
            pltpu.SemaphoreType.DMA((2, -(-cut // 256))),
            pltpu.SemaphoreType.DMA,
        ],
        flops=6 * half_flops,
        traffic=sum(w.size * 2 for w in weights),
        limit=32,
    )
    (sharing,) = call(functools.partial(share_kernel, size), [lines(2 * count)], (*returned, back, written))
    shared = swap(sharing)
    sums = call(
        functools.partial(join_kernel, count, subs),
        [vmem((tok_dev, sub_width), full)] * 2,
        (place, mix, *returned, back, kept),
        scratch=spread_scratch + [pltpu.VMEM((rows, sub_width), low)],
        flops=4 * rows * tok_dev * sub_width,
    )
    out_tokens, grad_tokens = call(
        functools.partial(finish_kernel, count, subs),
        [jax.ShapeDtypeStruct((tok_dev, sub_width), low)] * 2,
        (place_other, mix_other, shared, *sums),
        out_spaces=[pl.ANY] * 2,
        scratch=[
            pltpu.VMEM((count * size, LANES), full),
            pltpu.VMEM((other_rows, sub_width), low),
            pltpu.VMEM((2, tok_dev, sub_width), low),
            pltpu.SemaphoreType.DMA((2,)),
        ],
        traffic=8 * tok_dev * sub_width,
    )
    return out_tokens, grad_tokens, grad_gate, grad_up, grad_down


def shards(*args):
    tokens, gate_weight = args[0], args[4]
    halves = lax.axis_size("ffn")
    devices = lax.axis_size("expert")
    if halves == 2 and devices >= 4 and devices & (devices - 1) == 0 and tokens.shape[1] * halves == gate_weight.shape[1]:
        return one_piece_shards(*args)
    return general_shards(*args)


def solution(mesh):
    in_specs = (
        P(("groups", "expert"), "ffn"),
        P(("groups", "expert"), "ffn"),
        P(("groups", "expert"), None),
        P(("groups", "expert"), None),
        P("expert", None, "ffn"),
        P("expert", None, "ffn"),
        P("expert", "ffn", None),
    )
    out_specs = (
        P(("groups", "expert"), "ffn"),
        P(("groups", "expert"), "ffn"),
        P(("groups", "expert"), None, "ffn"),
        P(("groups", "expert"), None, "ffn"),
        P(("groups", "expert"), "ffn", None),
    )
    return jax.shard_map(shards, mesh=mesh, in_specs=in_specs, out_specs=out_specs, check_vma=False)
```

```python
import functools

import jax
import jax.numpy as jnp
from jax import lax
from jax.experimental import pallas as pl
from jax.experimental.pallas import tpu as pltpu
from jax.sharding import PartitionSpec as P

EXPERTS = 128
LANES = 128
MIB = 1024 * 1024


def contract_rows(left, right):
    return lax.dot_general(
        left, right, (((0,), (0,)), ((), ())), preferred_element_type=jnp.float32
    )


def contract_cols(left, right):
    return lax.dot_general(
        left, right, (((1,), (1,)), ((), ())), preferred_element_type=jnp.float32
    )


def general_shards(tokens, grad_out, route_ids, route_weight, gate_weight, up_weight, down_weight):
    tokens, grad_out = (
        lax.all_gather(tokens, "ffn", axis=1, tiled=True),
        lax.all_gather(grad_out, "ffn", axis=1, tiled=True),
    )
    tok_dev, width = tokens.shape
    top_count = route_ids.shape[1]
    piece_width = gate_weight.shape[1]
    hidden_half = gate_weight.shape[2]
    pieces = width // piece_width
    devices = lax.axis_size("expert")
    flight = devices // pieces
    halves = lax.axis_size("ffn")
    sub_width = piece_width // halves
    capacity = max(2, min(tok_dev, (9 * tok_dev * top_count + 8 * EXPERTS - 1) // (8 * EXPERTS)))
    total_rows = devices * capacity
    expert_ids = jnp.arange(flight, dtype=jnp.int32)
    member = jnp.zeros((tok_dev, flight), jnp.float32)
    mixing = jnp.zeros((tok_dev, flight), jnp.float32)
    for route in range(top_count):
        hit = (route_ids[:, route : route + 1] == expert_ids[None, :]).astype(jnp.float32)
        member = member + hit
        mixing = mixing + hit * route_weight[:, route : route + 1]
    slots = jnp.cumsum(member, axis=0) - member
    place = member[:, :, None] * (
        slots[:, :, None] == jnp.arange(capacity, dtype=jnp.float32)
    ).astype(jnp.float32)
    weighted = place * mixing[:, :, None]
    place_low = place.astype(jnp.bfloat16)
    x_four = tokens.reshape(tok_dev, halves, pieces, sub_width)
    g_four = grad_out.reshape(tok_dev, halves, pieces, sub_width)
    x_parts = []
    g_parts = []
    for half in range(halves):
        x_parts.append(
            jnp.einsum(
                "Tec,Tjr->ejcr", place_low, x_four[:, half], preferred_element_type=jnp.float32
            )
        )
        g_parts.append(jnp.einsum("Tec,Tjr->ejcr", weighted, g_four[:, half].astype(jnp.float32)))
    x_send = jnp.concatenate(x_parts, axis=3).astype(jnp.bfloat16).reshape(total_rows, piece_width)
    g_send = jnp.concatenate(g_parts, axis=3).astype(jnp.bfloat16).reshape(total_rows, piece_width)

    def return_parts(values):
        arrived = lax.all_to_all(values, "expert", split_axis=0, concat_axis=0, tiled=True)
        lanes = arrived.shape[1]
        return arrived.astype(jnp.float32).reshape(flight, pieces, capacity, lanes).sum(axis=1)

    def spread_rows(values):
        lanes = values.shape[2]
        copies = jnp.broadcast_to(values[:, None], (flight, pieces, capacity, lanes)).reshape(
            total_rows, lanes
        )
        return lax.all_to_all(copies, "expert", split_axis=0, concat_axis=0, tiled=True)

    def finish(term, mix):
        summed = lax.psum_scatter(term, "ffn", scatter_dimension=1, tiled=True)
        back = lax.all_to_all(summed, "expert", split_axis=0, concat_axis=0, tiled=True)
        back = back.reshape(flight, pieces, capacity, sub_width)
        joined = jnp.einsum("Tec,ejcr->Tjr", mix, back)
        return joined.reshape(tok_dev, pieces * sub_width).astype(jnp.bfloat16)

    rows = lax.all_to_all(x_send, "expert", split_axis=0, concat_axis=0, tiled=True)
    w_gate = gate_weight[0]
    w_up = up_weight[0]
    w_down = down_weight[0]
    partial_value = jnp.concatenate(
        [
            jnp.dot(rows, w_gate, preferred_element_type=jnp.float32),
            jnp.dot(rows, w_up, preferred_element_type=jnp.float32),
        ],
        axis=1,
    )
    summed = return_parts(partial_value.astype(jnp.bfloat16))
    gate = summed[:, :, :hidden_half]
    up = summed[:, :, hidden_half:]
    sig = jax.nn.sigmoid(gate)
    act = gate * sig
    hidden = (act * up).astype(jnp.bfloat16)
    h_rows = spread_rows(hidden)
    out_term = jnp.dot(h_rows, w_down, preferred_element_type=jnp.float32)
    out_tokens = finish(out_term, weighted)
    grads = lax.all_to_all(g_send, "expert", split_axis=0, concat_axis=0, tiled=True)
    grad_down = contract_rows(h_rows, grads).astype(jnp.bfloat16)
    hidden_part = contract_cols(grads, w_down).astype(jnp.bfloat16)
    grad_hidden = return_parts(hidden_part)
    pre_gate = (grad_hidden * up * sig * (1.0 + gate * (1.0 - sig))).astype(jnp.bfloat16)
    pre_up = (grad_hidden * act).astype(jnp.bfloat16)
    both = spread_rows(jnp.concatenate([pre_gate, pre_up], axis=2))
    d_gate_rows = both[:, :hidden_half]
    d_up_rows = both[:, hidden_half:]
    grad_gate = contract_rows(rows, d_gate_rows).astype(jnp.bfloat16)
    grad_up = contract_rows(rows, d_up_rows).astype(jnp.bfloat16)
    x_term = contract_cols(d_gate_rows, w_gate) + contract_cols(d_up_rows, w_up)
    grad_tokens = finish(x_term, place)
    return (out_tokens, grad_tokens, grad_gate[None], grad_up[None], grad_down[None])


def vmem(shape, dtype):
    return pltpu.VMEM(shape, dtype)


def call(kernel, out_shape, args, in_spaces=None, out_spaces=None, flops=0, traffic=0, scratch=(), limit=16):
    spaces = in_spaces or [pltpu.VMEM] * len(args)
    outs = out_spaces or [pltpu.VMEM] * len(out_shape)
    return pl.pallas_call(
        kernel,
        out_shape=tuple(out_shape),
        in_specs=[pl.BlockSpec(memory_space=space) for space in spaces],
        out_specs=tuple(pl.BlockSpec(memory_space=space) for space in outs),
        scratch_shapes=list(scratch),
        compiler_params=pltpu.CompilerParams(vmem_limit_bytes=limit * MIB),
        cost_estimate=pl.CostEstimate(flops=flops, bytes_accessed=traffic, transcendentals=0),
    )(*args)


def blocks_to_rows(scratch, blocks, put, subs):
    size = blocks[0].shape[0]
    for p, block in enumerate(blocks):
        scratch[p * size : (p + 1) * size, :] = block[...].astype(jnp.float32)
    for sub in range(subs):
        put(sub, scratch[pl.ds(sub, len(blocks) * size // subs, stride=subs), :])


def spread_lanes(scratch, sub, subs, value):
    scratch[pl.ds(sub, value.shape[0], stride=subs), :] = value


def part(ref, start, count):
    return ref.at[start : start + count, :]


def lanes_of(sub):
    return slice(sub * LANES, (sub + 1) * LANES)


def even_masks(count):
    return [*reversed(range(count // 2, count, 2)), *range(2, count // 2, 2)]


def route_kernel(devices, capacity, subs, ids_in, weight_in, x_in, g_in, *refs):
    x_mine, g_mine, near, here, theirs, place_out, mix_out, place_other, mix_other, scratch, ids, weight, x, g, sems = refs
    pairs = ((ids_in, ids), (weight_in, weight), (x_in, x), (g_in, g))
    copies = [pltpu.make_async_copy(src, dst, sems.at[i]) for i, (src, dst) in enumerate(pairs)]
    for copy in copies:
        copy.start()
    top, tok = ids.shape
    rows = devices * capacity
    core = lax.axis_index("ffn")
    masks = even_masks(devices)
    masks = [mask + core for mask in masks] + [mask + 1 - core for mask in masks] + [1, 0]
    order = lax.broadcasted_iota(jnp.int32, (devices, tok), 0)
    bits = jnp.zeros((devices, tok), jnp.int32)
    for p, mask in enumerate(masks):
        bits = jnp.where(order == p, mask, bits)
    expert = bits ^ lax.axis_index("expert")
    member = jnp.zeros((devices, tok), jnp.float32)
    mixing = jnp.zeros((devices, tok), jnp.float32)
    copies[0].wait()
    copies[1].wait()
    for route in range(top):
        hit = ids[route : route + 1, :] == expert
        member = jnp.where(hit, 1.0, member)
        mixing = jnp.where(hit, weight[route : route + 1, :], mixing)
    before = lax.broadcasted_iota(jnp.int32, (tok, tok), 0) < lax.broadcasted_iota(jnp.int32, (tok, tok), 1)
    slots = dot(member.astype(jnp.bfloat16), jnp.where(before, 1.0, 0.0).astype(jnp.bfloat16))
    target = jnp.where(member > 0, slots + capacity * order.astype(jnp.float32), -1.0)
    count = devices // 2 - 1

    def placed(first, number):
        row = lax.broadcasted_iota(jnp.int32, (number, tok), 0).astype(jnp.float32) + first
        place = jnp.zeros((number, tok), jnp.float32)
        mix = jnp.zeros((number, tok), jnp.float32)
        for p in range(devices):
            equal = target[p : p + 1, :] == row
            place = jnp.where(equal, 1.0, place)
            mix = jnp.where(equal, mixing[p : p + 1, :], mix)
        row_weight = jnp.broadcast_to(jnp.sum(mix, axis=1, keepdims=True), (number, LANES))
        return place.astype(jnp.bfloat16), row_weight

    low, row_weight = placed(0, rows)
    place_out[...] = low
    mix_out[...] = row_weight
    place_other[...], mix_other[...] = placed(count * capacity, count * capacity)
    size = capacity * subs

    def write(mine, at):
        def block(p):
            return scratch[p * size : (p + 1) * size, :].astype(theirs.dtype)

        for j in range(count):
            part(mine, j * size, size)[...] = block(j)
            part(theirs, (at + j) * size, size)[...] = block(count + j)
        start = size if at else 0
        part(near, start, size)[...] = block(2 * count)
        part(here, start, size)[...] = block(2 * count + 1)

    copies[2].wait()
    for sub in range(subs):
        spread_lanes(scratch, sub, subs, dot(low, x[:, lanes_of(sub)]))
    write(x_mine, 0)
    copies[3].wait()
    for sub in range(subs):
        spread_lanes(scratch, sub, subs, dot(low, g[:, lanes_of(sub)]) * row_weight)
    write(g_mine, count)


def pack_kernel(size, late, x_mine, g_mine, swapped, *outs):
    count = len(outs) - len(late)
    lates = dict(zip(late, outs[count:]))
    for j, out in enumerate(outs[:count]):
        places = ((out, 0), (lates.get(j, out), 0 if j in late else 2 * size))
        for i, (mine, (to, at)) in enumerate(zip((x_mine, g_mine), places)):
            part(to, at, size)[...] = part(mine, j * size, size)[...]
            part(to, at + size, size)[...] = part(swapped, (i * count + j) * size, size)[...]
    for out in [*lates.values(), *[outs[j] for j in late]]:
        rest = part(out, 2 * size, out.shape[0] - 2 * size)
        rest[...] = jnp.zeros(rest.shape, rest.dtype)


def gather_x_kernel(size, *refs):
    count = (len(refs) - 3) // 2
    blocks, (near, here), outs = refs[:count], refs[count : count + 2], refs[count + 2 :]
    for block, out in zip(blocks, outs):
        out[...] = part(block, 0, 2 * size)[...]
    part(outs[-1], 0, size)[...] = part(near, 0, size)[...]
    part(outs[-1], size, size)[...] = part(here, 0, size)[...]


def gather_g_kernel(size, late, *refs):
    blocks, (near, here, _, out) = refs[:-4], refs[-4:]
    for j, block in enumerate(blocks):
        start = 0 if j in late else 2 * size
        part(out, 2 * j * size, 2 * size)[...] = part(block, start, 2 * size)[...]
    part(out, 2 * len(blocks) * size, size)[...] = part(near, size, size)[...]
    part(out, (2 * len(blocks) + 1) * size, size)[...] = part(here, size, size)[...]


def full_rows(devices, subs, scratch, own_sent, other_sent, out):
    per = devices // len(own_sent)
    size = own_sent[0].shape[0] // per
    count = devices // 2 - 1
    own, other = half_starts(out.shape[1] // 2)
    first, second, last = range(0, 2 * count, 2), range(1, 2 * count, 2), range(2 * count, devices)
    layouts = (
        (own, [(own_sent, i) for i in first] + [(other_sent, i) for i in second] + [(own_sent, i) for i in last]),
        (other, [(own_sent, i) for i in second] + [(other_sent, i) for i in first] + [(other_sent, i) for i in last]),
    )
    for start, layout in layouts:

        def put(sub, value):
            out[:, pl.ds(start + sub * LANES, LANES)] = value.astype(out.dtype)

        blocks_to_rows(scratch, [part(refs[i // per], i % per * size, size) for refs, i in layout], put, subs)


def split_terms(count, size, scratch, own_half, keep, send):
    keep[0 : count * size, :] = scratch[0 : count * size, :]
    send[0 : count * size, :] = scratch[count * size : 2 * count * size, :].astype(send.dtype)
    rest = scratch[2 * count * size :, :]
    if own_half:
        keep[count * size :, :] = rest
    else:
        send[count * size :, :] = rest.astype(send.dtype)


def leave_kernel(size, *refs):
    terms, outs = (refs[:4], refs[4:8]), refs[9:]
    count = len(outs) - 2
    for at, (keep_own, keep_other, came_own, came_other) in zip((0, size), terms):

        def own(p):
            total = part(keep_own, p * size, size)[...] + part(came_own, p * size, size)[...].astype(jnp.float32)
            return total.astype(outs[0].dtype)

        for j, out in enumerate(outs[:count]):
            part(out, at, size)[...] = own(j)
            total = part(keep_other, j * size, size)[...] + part(came_other, j * size, size)[...].astype(jnp.float32)
            part(out, 2 * size + at, size)[...] = total.astype(out.dtype)
        part(outs[count], at, size)[...] = own(count)
        part(outs[count + 1], at, size)[...] = own(count + 1)


def share_kernel(size, *refs):
    blocks, (_, _, out) = refs[:-3], refs[-3:]
    for j, block in enumerate(blocks):
        part(out, 2 * j * size, 2 * size)[...] = part(block, 2 * size, 2 * size)[...]


def token_sums(subs, place, mix, scratch, rows, blocks, put):
    size = scratch.shape[0] // len(blocks)
    for p, block in enumerate(blocks):
        here = slice(p * size, (p + 1) * size)
        scratch[here, :] = jnp.zeros((size, LANES), jnp.float32) if block is None else block[...].astype(jnp.float32)
    for sub in range(subs):
        value = scratch[pl.ds(sub, rows.shape[0], stride=subs), :]
        if mix is not None:
            value = value * mix[...]
        rows[:, lanes_of(sub)] = value.astype(rows.dtype)
    for cut in pieces_of(subs * LANES, 512):
        put(cut, contract_rows(place[...], rows[:, cut]))


def join_kernel(count, subs, place, mix, *refs):
    blocks, (near, here, out_sum, grad_sum, scratch, rows) = refs[:count], refs[count:]
    size = near.shape[0] // 2
    for at, scale, out in ((0, mix, out_sum), (size, None, grad_sum)):

        def put(cut, total):
            out[:, cut] = total

        first = [part(block, at, size) for block in blocks]
        last = [part(near, at, size), part(here, at, size)]
        token_sums(subs, place, scale, scratch, rows, first + [None] * count + last, put)


def finish_kernel(
    count, subs, place, mix, shared, out_sum, grad_sum, out_tokens, grad_tokens, scratch, rows, low, sems
):
    size = shared.shape[0] // (2 * count)
    copies = []
    work = ((0, mix, out_sum, out_tokens), (size, None, grad_sum, grad_tokens))
    for i, (at, scale, before, out) in enumerate(work):

        def put(cut, total):
            low[i, :, cut] = (before[:, cut] + total).astype(low.dtype)

        blocks = [part(shared, 2 * j * size + at, size) for j in range(count)]
        token_sums(subs, place, scale, scratch, rows, blocks, put)
        copies.append(pltpu.make_async_copy(low.at[i], out, sems.at[i]))
        copies[-1].start()
    for copy in copies:
        copy.wait()


def half_starts(half_width):
    half = lax.axis_index("ffn")
    own = pl.multiple_of(half * half_width, half_width)
    other = pl.multiple_of((1 - half) * half_width, half_width)
    return own, other


def chunk(i, step, base=0):
    return pl.ds(base + pl.multiple_of(i * step, step), step)


def dot(left, right):
    return jnp.dot(left, right, preferred_element_type=jnp.float32)


def halves_of_output(devices, subs, step, scratch, own_half, term, keep, send):
    size = scratch.shape[0] // devices
    for at in range(0, subs * LANES, step):
        value = term(at)
        for i in range(step // LANES):
            spread_lanes(scratch, at // LANES + i, subs, value[:, lanes_of(i)])
    split_terms(devices // 2 - 1, size, scratch, own_half, keep, send)


def forward_kernel(devices, subs, step, *refs):
    half = devices // 2
    x_sent, x_swapped = refs[:half], refs[half : 2 * half]
    w_gate, w_up, x_full, gate, up, hidden, scratch = refs[2 * half :]
    full_rows(devices, subs, scratch, x_sent, x_swapped, x_full)
    for cols in pieces_of(gate.shape[1], step):
        gate_low = dot(x_full[...], w_gate[0, :, cols]).astype(jnp.bfloat16)
        up_low = dot(x_full[...], w_up[0, :, cols]).astype(jnp.bfloat16)
        gate[:, cols] = gate_low
        up[:, cols] = up_low
        value = gate_low.astype(jnp.float32)
        hidden[:, cols] = (value * jax.nn.sigmoid(value) * up_low.astype(jnp.float32)).astype(jnp.bfloat16)


def output_kernel(devices, subs, step, hidden, w_down, keep_own, keep_other, send_own, send_other, scratch):
    own, other = half_starts(subs * LANES)

    def term(start):
        return lambda at: dot(hidden[...], w_down[0, :, pl.ds(start + at, step)])

    halves_of_output(devices, subs, step, scratch, False, term(other), keep_other, send_other)
    halves_of_output(devices, subs, step, scratch, True, term(own), keep_own, send_own)


def input_term(step, pre_gate, pre_up, w_gate, w_up, start):
    def term(at):
        there = pl.ds(start + at, step)
        return contract_cols(pre_gate[...], w_gate[0, there, :]) + contract_cols(pre_up[...], w_up[0, there, :])

    return term


def backward_kernel(
    devices,
    subs,
    step,
    g_sent,
    g_swapped,
    gate,
    up,
    w_gate,
    w_up,
    w_down,
    g_full,
    pre_gate,
    pre_up,
    keep_other,
    send_other,
    scratch,
):
    _, other = half_starts(subs * LANES)
    full_rows(devices, subs, scratch, [g_sent], [g_swapped], g_full)

    def pull(i, carry):
        cols = chunk(i, step)
        low = contract_cols(g_full[...], w_down[0, cols, :]).astype(jnp.bfloat16)
        grad_hidden = low.astype(jnp.float32)
        value = gate[:, cols].astype(jnp.float32)
        sig = jax.nn.sigmoid(value)
        pre_gate[:, cols] = (
            grad_hidden * up[:, cols].astype(jnp.float32) * sig * (1.0 + value * (1.0 - sig))
        ).astype(jnp.bfloat16)
        pre_up[:, cols] = (grad_hidden * value * sig).astype(jnp.bfloat16)
        return carry

    lax.fori_loop(0, gate.shape[1] // step, pull, 0)
    term = input_term(step, pre_gate, pre_up, w_gate, w_up, other)
    halves_of_output(devices, subs, step, scratch, False, term, keep_other, send_other)


def backward_own_kernel(devices, subs, step, pre_gate, pre_up, w_gate, w_up, keep_own, send_own, scratch):
    own, _ = half_starts(subs * LANES)
    term = input_term(step, pre_gate, pre_up, w_gate, w_up, own)
    halves_of_output(devices, subs, step, scratch, True, term, keep_own, send_own)


def flip(value):
    return value.astype(jnp.float32).T


def pieces_of(total, size):
    return [slice(at, min(at + size, total)) for at in range(0, total, size)]


def first_chunk_kernel(hidden, g, turned, out):
    turned[...] = flip(hidden[...]).astype(turned.dtype)
    for cut in pieces_of(out.shape[1], 256):
        out[:, cut] = dot(turned[...], g[:, cut]).astype(out.dtype)


def gradient_kernel(
    step,
    x,
    g,
    hidden_turned,
    first,
    pre_gate,
    pre_up,
    grad_gate,
    grad_up,
    grad_down,
    written,
    turned,
    tall,
    wide,
    tall_sems,
    wide_sems,
    first_sem,
):
    width, lanes = x.shape[1], hidden_turned.shape[0]
    count = width // step
    written[...] = jnp.zeros_like(written)
    first_copy = pltpu.make_async_copy(first, grad_down.at[0, :, 0:step], first_sem)
    first_copy.start()

    cuts = pieces_of(step, 256)

    def wide_copy(i, slot, n):
        there = pl.ds(pl.multiple_of(i * step, step) + cuts[n].start, cuts[n].stop - cuts[n].start)
        return pltpu.make_async_copy(wide.at[slot, :, cuts[n]], grad_down.at[0, :, there], wide_sems.at[slot, n])

    def tall_copy(which, out, i, slot):
        return pltpu.make_async_copy(tall.at[which, slot], out.at[0, chunk(i, step), :], tall_sems.at[which, slot])

    def inputs(i, carry):
        slot = i % 2
        turned[...] = flip(x[:, chunk(i, step)]).astype(turned.dtype)
        for which, (right, out) in enumerate(((pre_gate, grad_gate), (pre_up, grad_up))):

            @pl.when(i >= 2)
            def _():
                tall_copy(which, out, i - 2, slot).wait()

            for cut in pieces_of(lanes, 256):
                for high in pieces_of(step, 512):
                    tall[which, slot, high, cut] = dot(turned[high, :], right[:, cut]).astype(tall.dtype)
            tall_copy(which, out, i, slot).start()
        return carry

    lax.fori_loop(0, count, inputs, 0)

    def down(i, carry):
        slot = i % 2

        @pl.when(i >= 3)
        def _():
            for n in range(len(cuts)):
                wide_copy(i - 2, slot, n).wait()

        for n, cut in enumerate(cuts):
            right = g[:, chunk(i, step)][:, cut]
            wide[slot, :, cut] = dot(hidden_turned[...], right).astype(wide.dtype)
            wide_copy(i, slot, n).start()
        return carry

    lax.fori_loop(1, count, down, 0)
    first_copy.wait()
    for i in range(max(1, count - 2), count):
        for n in range(len(cuts)):
            wide_copy(i, i % 2, n).wait()
    for i in range(max(0, count - 2), count):
        tall_copy(0, grad_gate, i, i % 2).wait()
        tall_copy(1, grad_up, i, i % 2).wait()


def exchange(blocks, masks, devices):
    arrived = []
    for block, mask in zip(blocks, masks):
        pairs = [(2 * i + core, 2 * (i ^ (mask + core)) + core) for i in range(devices) for core in range(2)]
        arrived.append(lax.ppermute(block, ("expert", "ffn"), pairs))
    return arrived


def exchange_near(block, devices):
    return lax.ppermute(block, "expert", [(i, i ^ 1) for i in range(devices)])


def swap(value):
    return lax.ppermute(value, "ffn", [(0, 1), (1, 0)])


def in_hbm(values):
    return [pltpu.with_memory_space_constraint(value, pltpu.HBM) for value in values]


def one_piece_shards(tokens, grad_out, route_ids, route_weight, gate_weight, up_weight, down_weight):
    tok_dev, sub_width = tokens.shape
    top_count = route_ids.shape[1]
    width, lanes = gate_weight.shape[1:]
    devices = lax.axis_size("expert")
    capacity = max(2, min(tok_dev, (9 * tok_dev * top_count + 8 * EXPERTS - 1) // (8 * EXPERTS)))
    rows = devices * capacity
    subs = sub_width // LANES
    low, full = jnp.bfloat16, jnp.float32
    size = capacity * subs
    count = devices // 2 - 1
    spread_scratch = [pltpu.VMEM((devices * size, LANES), full)]
    step = 256
    half_flops = 2 * rows * width * lanes // 2

    def lines(number, dtype=low):
        return jax.ShapeDtypeStruct((number * size, LANES), dtype)

    def lines_in_vmem(number, dtype=low):
        return vmem((number * size, LANES), dtype)

    sources = (route_ids.T, route_weight.T, tokens, grad_out)
    other_rows = count * capacity
    x_mine, g_mine, near, here, theirs, place, mix, place_other, mix_other = call(
        functools.partial(route_kernel, devices, capacity, subs),
        [lines(count), lines(count), lines(2), lines(2)]
        + [lines(2 * count)]
        + [jax.ShapeDtypeStruct((rows, tok_dev), low), jax.ShapeDtypeStruct((rows, LANES), full)]
        + [jax.ShapeDtypeStruct((other_rows, tok_dev), low), jax.ShapeDtypeStruct((other_rows, LANES), full)],
        in_hbm(sources),
        in_spaces=[pl.ANY] * 4,
        scratch=spread_scratch
        + [pltpu.VMEM(value.shape, value.dtype) for value in sources]
        + [pltpu.SemaphoreType.DMA((4,))],
        traffic=4 * tok_dev * sub_width,
    )
    masks = even_masks(devices)
    late = [devices // 4 - 1]
    late_block = jax.ShapeDtypeStruct((2 * size + 16, LANES), low)
    packed = call(
        functools.partial(pack_kernel, size, late),
        [late_block if j in late else lines(4) for j in range(count)] + [late_block] * len(late),
        (x_mine, g_mine, swap(theirs)),
        flops=24 * half_flops,
    )
    x_arrived = exchange(packed[:count], masks, devices)
    g_arrived = list(x_arrived)
    for j, block in zip(late, packed[count:]):
        (g_arrived[j],) = exchange([block], masks[j:], devices)
    near = exchange_near(near, devices)

    weights = (gate_weight, up_weight, down_weight)
    w_gate, w_up, w_down = [pltpu.with_memory_space_constraint(w, pltpu.VMEM) for w in weights]

    x_sent = call(
        functools.partial(gather_x_kernel, size), [lines(2)] * (count + 1), (*x_arrived, near, here)
    )
    x_swapped = [swap(value) for value in x_sent]
    terms = [
        lines_in_vmem(count + 2, full),
        lines_in_vmem(count, full),
        lines_in_vmem(count),
        lines_in_vmem(count + 2),
    ]
    x_full, gate, up, hidden = call(
        functools.partial(forward_kernel, devices, subs, step),
        [vmem((rows, width), low)] + [vmem((rows, lanes), low)] * 3,
        (*x_sent, *x_swapped, w_gate, w_up),
        scratch=spread_scratch,
    )
    (g_sent,) = call(
        functools.partial(gather_g_kernel, size, late), [lines(devices)], (*g_arrived, near, here, hidden)
    )
    g_swapped = swap(g_sent)
    out_own, out_other, send_own, send_other = call(
        functools.partial(output_kernel, devices, subs, 2 * step),
        terms,
        (hidden, w_down),
        scratch=spread_scratch,
        flops=2 * half_flops,
    )
    out_terms = (out_own, out_other, swap(send_other), swap(send_own))
    g_full, pre_gate, pre_up, dx_other, send_other = call(
        functools.partial(backward_kernel, devices, subs, step),
        [vmem((rows, width), low)] + [vmem((rows, lanes), low)] * 2 + [terms[1], terms[3]],
        (g_sent, g_swapped, gate, up, w_gate, w_up, w_down),
        scratch=spread_scratch,
        flops=4 * half_flops,
    )
    came_own = swap(send_other)
    dx_own, send_own = call(
        functools.partial(backward_own_kernel, devices, subs, step),
        [terms[0], terms[2]],
        (pre_gate, pre_up, w_gate, w_up),
        scratch=spread_scratch,
        flops=2 * half_flops,
    )
    dx_terms = (dx_own, dx_other, came_own, swap(send_own))
    cut = 1024 if width % 1024 == 0 else width
    hidden_turned, first = call(
        first_chunk_kernel,
        [vmem((lanes, rows), low), vmem((lanes, cut), low)],
        (hidden, g_full),
        flops=2 * half_flops * cut // width,
    )
    *leaving, back, kept = call(
        functools.partial(leave_kernel, size),
        [lines(4)] * count + [lines(2)] * 2,
        (*out_terms, *dx_terms, first),
    )
    returned = exchange(leaving, masks, devices)
    back = exchange_near(back, devices)
    grad_gate, grad_up, grad_down, written = call(
        functools.partial(gradient_kernel, cut),
        [jax.ShapeDtypeStruct(w.shape, low) for w in weights] + [vmem((8, LANES), full)],
        (x_full, g_full, hidden_turned, first, pre_gate, pre_up),
        out_spaces=[pl.ANY] * 3 + [pltpu.VMEM],
        scratch=[
            pltpu.VMEM((cut, rows), low),
            pltpu.VMEM((2, 2, cut, lanes), low),
            pltpu.VMEM((2, lanes, cut), low),
            pltpu.SemaphoreType.DMA((2, 2)),
            pltpu.SemaphoreType.DMA((2, -(-cut // 256))),
            pltpu.SemaphoreType.DMA,
        ],
        flops=6 * half_flops,
        traffic=sum(w.size * 2 for w in weights),
        limit=32,
    )
    (sharing,) = call(functools.partial(share_kernel, size), [lines(2 * count)], (*returned, back, written))
    shared = swap(sharing)
    sums = call(
        functools.partial(join_kernel, count, subs),
        [vmem((tok_dev, sub_width), full)] * 2,
        (place, mix, *returned, back, kept),
        scratch=spread_scratch + [pltpu.VMEM((rows, sub_width), low)],
        flops=4 * rows * tok_dev * sub_width,
    )
    out_tokens, grad_tokens = call(
        functools.partial(finish_kernel, count, subs),
        [jax.ShapeDtypeStruct((tok_dev, sub_width), low)] * 2,
        (place_other, mix_other, shared, *sums),
        out_spaces=[pl.ANY] * 2,
        scratch=[
            pltpu.VMEM((count * size, LANES), full),
            pltpu.VMEM((other_rows, sub_width), low),
            pltpu.VMEM((2, tok_dev, sub_width), low),
            pltpu.SemaphoreType.DMA((2,)),
        ],
        traffic=8 * tok_dev * sub_width,
    )
    return out_tokens, grad_tokens, grad_gate, grad_up, grad_down


def shards(*args):
    tokens, gate_weight = args[0], args[4]
    halves = lax.axis_size("ffn")
    devices = lax.axis_size("expert")
    if halves == 2 and devices >= 4 and devices & (devices - 1) == 0 and tokens.shape[1] * halves == gate_weight.shape[1]:
        return one_piece_shards(*args)
    return general_shards(*args)


def solution(mesh):
    in_specs = (
        P(("groups", "expert"), "ffn"),
        P(("groups", "expert"), "ffn"),
        P(("groups", "expert"), None),
        P(("groups", "expert"), None),
        P("expert", None, "ffn"),
        P("expert", None, "ffn"),
        P("expert", "ffn", None),
    )
    out_specs = (
        P(("groups", "expert"), "ffn"),
        P(("groups", "expert"), "ffn"),
        P(("groups", "expert"), None, "ffn"),
        P(("groups", "expert"), None, "ffn"),
        P(("groups", "expert"), "ffn", None),
    )
    return jax.shard_map(shards, mesh=mesh, in_specs=in_specs, out_specs=out_specs, check_vma=False)
```

```python
import functools

import jax
import jax.numpy as jnp
from jax import lax
from jax.experimental import pallas as pl
from jax.experimental.pallas import tpu as pltpu
from jax.sharding import PartitionSpec as P

EXPERTS = 128
LANES = 128
MIB = 1024 * 1024


def contract_rows(left, right):
    return lax.dot_general(
        left, right, (((0,), (0,)), ((), ())), preferred_element_type=jnp.float32
    )


def contract_cols(left, right):
    return lax.dot_general(
        left, right, (((1,), (1,)), ((), ())), preferred_element_type=jnp.float32
    )


def general_shards(tokens, grad_out, route_ids, route_weight, gate_weight, up_weight, down_weight):
    tokens, grad_out = (
        lax.all_gather(tokens, "ffn", axis=1, tiled=True),
        lax.all_gather(grad_out, "ffn", axis=1, tiled=True),
    )
    tok_dev, width = tokens.shape
    top_count = route_ids.shape[1]
    piece_width = gate_weight.shape[1]
    hidden_half = gate_weight.shape[2]
    pieces = width // piece_width
    devices = lax.axis_size("expert")
    flight = devices // pieces
    halves = lax.axis_size("ffn")
    sub_width = piece_width // halves
    capacity = max(2, min(tok_dev, (9 * tok_dev * top_count + 8 * EXPERTS - 1) // (8 * EXPERTS)))
    total_rows = devices * capacity
    expert_ids = jnp.arange(flight, dtype=jnp.int32)
    member = jnp.zeros((tok_dev, flight), jnp.float32)
    mixing = jnp.zeros((tok_dev, flight), jnp.float32)
    for route in range(top_count):
        hit = (route_ids[:, route : route + 1] == expert_ids[None, :]).astype(jnp.float32)
        member = member + hit
        mixing = mixing + hit * route_weight[:, route : route + 1]
    slots = jnp.cumsum(member, axis=0) - member
    place = member[:, :, None] * (
        slots[:, :, None] == jnp.arange(capacity, dtype=jnp.float32)
    ).astype(jnp.float32)
    weighted = place * mixing[:, :, None]
    place_low = place.astype(jnp.bfloat16)
    x_four = tokens.reshape(tok_dev, halves, pieces, sub_width)
    g_four = grad_out.reshape(tok_dev, halves, pieces, sub_width)
    x_parts = []
    g_parts = []
    for half in range(halves):
        x_parts.append(
            jnp.einsum(
                "Tec,Tjr->ejcr", place_low, x_four[:, half], preferred_element_type=jnp.float32
            )
        )
        g_parts.append(jnp.einsum("Tec,Tjr->ejcr", weighted, g_four[:, half].astype(jnp.float32)))
    x_send = jnp.concatenate(x_parts, axis=3).astype(jnp.bfloat16).reshape(total_rows, piece_width)
    g_send = jnp.concatenate(g_parts, axis=3).astype(jnp.bfloat16).reshape(total_rows, piece_width)

    def return_parts(values):
        arrived = lax.all_to_all(values, "expert", split_axis=0, concat_axis=0, tiled=True)
        lanes = arrived.shape[1]
        return arrived.astype(jnp.float32).reshape(flight, pieces, capacity, lanes).sum(axis=1)

    def spread_rows(values):
        lanes = values.shape[2]
        copies = jnp.broadcast_to(values[:, None], (flight, pieces, capacity, lanes)).reshape(
            total_rows, lanes
        )
        return lax.all_to_all(copies, "expert", split_axis=0, concat_axis=0, tiled=True)

    def finish(term, mix):
        summed = lax.psum_scatter(term, "ffn", scatter_dimension=1, tiled=True)
        back = lax.all_to_all(summed, "expert", split_axis=0, concat_axis=0, tiled=True)
        back = back.reshape(flight, pieces, capacity, sub_width)
        joined = jnp.einsum("Tec,ejcr->Tjr", mix, back)
        return joined.reshape(tok_dev, pieces * sub_width).astype(jnp.bfloat16)

    rows = lax.all_to_all(x_send, "expert", split_axis=0, concat_axis=0, tiled=True)
    w_gate = gate_weight[0]
    w_up = up_weight[0]
    w_down = down_weight[0]
    partial_value = jnp.concatenate(
        [
            jnp.dot(rows, w_gate, preferred_element_type=jnp.float32),
            jnp.dot(rows, w_up, preferred_element_type=jnp.float32),
        ],
        axis=1,
    )
    summed = return_parts(partial_value.astype(jnp.bfloat16))
    gate = summed[:, :, :hidden_half]
    up = summed[:, :, hidden_half:]
    sig = jax.nn.sigmoid(gate)
    act = gate * sig
    hidden = (act * up).astype(jnp.bfloat16)
    h_rows = spread_rows(hidden)
    out_term = jnp.dot(h_rows, w_down, preferred_element_type=jnp.float32)
    out_tokens = finish(out_term, weighted)
    grads = lax.all_to_all(g_send, "expert", split_axis=0, concat_axis=0, tiled=True)
    grad_down = contract_rows(h_rows, grads).astype(jnp.bfloat16)
    hidden_part = contract_cols(grads, w_down).astype(jnp.bfloat16)
    grad_hidden = return_parts(hidden_part)
    pre_gate = (grad_hidden * up * sig * (1.0 + gate * (1.0 - sig))).astype(jnp.bfloat16)
    pre_up = (grad_hidden * act).astype(jnp.bfloat16)
    both = spread_rows(jnp.concatenate([pre_gate, pre_up], axis=2))
    d_gate_rows = both[:, :hidden_half]
    d_up_rows = both[:, hidden_half:]
    grad_gate = contract_rows(rows, d_gate_rows).astype(jnp.bfloat16)
    grad_up = contract_rows(rows, d_up_rows).astype(jnp.bfloat16)
    x_term = contract_cols(d_gate_rows, w_gate) + contract_cols(d_up_rows, w_up)
    grad_tokens = finish(x_term, place)
    return (out_tokens, grad_tokens, grad_gate[None], grad_up[None], grad_down[None])


def vmem(shape, dtype):
    return pltpu.VMEM(shape, dtype)


def call(kernel, out_shape, args, in_spaces=None, out_spaces=None, flops=0, traffic=0, scratch=(), limit=16):
    spaces = in_spaces or [pltpu.VMEM] * len(args)
    outs = out_spaces or [pltpu.VMEM] * len(out_shape)
    return pl.pallas_call(
        kernel,
        out_shape=tuple(out_shape),
        in_specs=[pl.BlockSpec(memory_space=space) for space in spaces],
        out_specs=tuple(pl.BlockSpec(memory_space=space) for space in outs),
        scratch_shapes=list(scratch),
        compiler_params=pltpu.CompilerParams(vmem_limit_bytes=limit * MIB),
        cost_estimate=pl.CostEstimate(flops=flops, bytes_accessed=traffic, transcendentals=0),
    )(*args)


def blocks_to_rows(scratch, blocks, put, subs):
    size = blocks[0].shape[0]
    for p, block in enumerate(blocks):
        scratch[p * size : (p + 1) * size, :] = block[...].astype(jnp.float32)
    for sub in range(subs):
        put(sub, scratch[pl.ds(sub, len(blocks) * size // subs, stride=subs), :])


def spread_lanes(scratch, sub, subs, value):
    scratch[pl.ds(sub, value.shape[0], stride=subs), :] = value


def part(ref, start, count):
    return ref.at[start : start + count, :]


def lanes_of(sub):
    return slice(sub * LANES, (sub + 1) * LANES)


def even_masks(count):
    return [*reversed(range(count // 2, count, 2)), *range(2, count // 2, 2)]


def route_kernel(devices, capacity, subs, ids_in, weight_in, x_in, g_in, *refs):
    x_mine, g_mine, near, here, theirs, place_out, mix_out, place_other, mix_other, scratch, ids, weight, x, g, sems = refs
    pairs = ((ids_in, ids), (weight_in, weight), (x_in, x), (g_in, g))
    copies = [pltpu.make_async_copy(src, dst, sems.at[i]) for i, (src, dst) in enumerate(pairs)]
    for copy in copies:
        copy.start()
    top, tok = ids.shape
    rows = devices * capacity
    core = lax.axis_index("ffn")
    masks = even_masks(devices)
    masks = [mask + core for mask in masks] + [mask + 1 - core for mask in masks] + [1, 0]
    order = lax.broadcasted_iota(jnp.int32, (devices, tok), 0)
    bits = jnp.zeros((devices, tok), jnp.int32)
    for p, mask in enumerate(masks):
        bits = jnp.where(order == p, mask, bits)
    expert = bits ^ lax.axis_index("expert")
    member = jnp.zeros((devices, tok), jnp.float32)
    mixing = jnp.zeros((devices, tok), jnp.float32)
    copies[0].wait()
    copies[1].wait()
    for route in range(top):
        hit = ids[route : route + 1, :] == expert
        member = jnp.where(hit, 1.0, member)
        mixing = jnp.where(hit, weight[route : route + 1, :], mixing)
    before = lax.broadcasted_iota(jnp.int32, (tok, tok), 0) < lax.broadcasted_iota(jnp.int32, (tok, tok), 1)
    slots = dot(member.astype(jnp.bfloat16), jnp.where(before, 1.0, 0.0).astype(jnp.bfloat16))
    target = jnp.where(member > 0, slots + capacity * order.astype(jnp.float32), -1.0)
    count = devices // 2 - 1

    def placed(first, number):
        row = lax.broadcasted_iota(jnp.int32, (number, tok), 0).astype(jnp.float32) + first
        place = jnp.zeros((number, tok), jnp.float32)
        mix = jnp.zeros((number, tok), jnp.float32)
        for p in range(devices):
            equal = target[p : p + 1, :] == row
            place = jnp.where(equal, 1.0, place)
            mix = jnp.where(equal, mixing[p : p + 1, :], mix)
        row_weight = jnp.broadcast_to(jnp.sum(mix, axis=1, keepdims=True), (number, LANES))
        return place.astype(jnp.bfloat16), row_weight

    low, row_weight = placed(0, rows)
    place_out[...] = low
    mix_out[...] = row_weight
    place_other[...], mix_other[...] = placed(count * capacity, count * capacity)
    size = capacity * subs

    def write(mine, at):
        def block(p):
            return scratch[p * size : (p + 1) * size, :].astype(theirs.dtype)

        for j in range(count):
            part(mine, j * size, size)[...] = block(j)
            part(theirs, (at + j) * size, size)[...] = block(count + j)
        start = size if at else 0
        part(near, start, size)[...] = block(2 * count)
        part(here, start, size)[...] = block(2 * count + 1)

    copies[2].wait()
    for cut in pieces_of(subs * LANES, 512):
        value = dot(low, x[:, cut])
        for i in range(value.shape[1] // LANES):
            spread_lanes(scratch, cut.start // LANES + i, subs, value[:, lanes_of(i)])
    write(x_mine, 0)
    copies[3].wait()
    for cut in pieces_of(subs * LANES, 512):
        value = dot(low, g[:, cut])
        for i in range(value.shape[1] // LANES):
            spread_lanes(scratch, cut.start // LANES + i, subs, value[:, lanes_of(i)] * row_weight)
    write(g_mine, count)


def pack_kernel(size, late, x_mine, g_mine, swapped, *outs):
    count = len(outs) - len(late)
    lates = dict(zip(late, outs[count:]))
    for j, out in enumerate(outs[:count]):
        places = ((out, 0), (lates.get(j, out), 0 if j in late else 2 * size))
        for i, (mine, (to, at)) in enumerate(zip((x_mine, g_mine), places)):
            part(to, at, size)[...] = part(mine, j * size, size)[...]
            part(to, at + size, size)[...] = part(swapped, (i * count + j) * size, size)[...]
    for out in [*lates.values(), *[outs[j] for j in late]]:
        rest = part(out, 2 * size, out.shape[0] - 2 * size)
        rest[...] = jnp.zeros(rest.shape, rest.dtype)


def gather_x_kernel(size, *refs):
    count = (len(refs) - 3) // 2
    blocks, (near, here), outs = refs[:count], refs[count : count + 2], refs[count + 2 :]
    for block, out in zip(blocks, outs):
        out[...] = part(block, 0, 2 * size)[...]
    part(outs[-1], 0, size)[...] = part(near, 0, size)[...]
    part(outs[-1], size, size)[...] = part(here, 0, size)[...]


def gather_g_kernel(size, late, *refs):
    blocks, (near, here, _, out) = refs[:-4], refs[-4:]
    for j, block in enumerate(blocks):
        start = 0 if j in late else 2 * size
        part(out, 2 * j * size, 2 * size)[...] = part(block, start, 2 * size)[...]
    part(out, 2 * len(blocks) * size, size)[...] = part(near, size, size)[...]
    part(out, (2 * len(blocks) + 1) * size, size)[...] = part(here, size, size)[...]


def full_rows(devices, subs, scratch, own_sent, other_sent, out):
    per = devices // len(own_sent)
    size = own_sent[0].shape[0] // per
    count = devices // 2 - 1
    own, other = half_starts(out.shape[1] // 2)
    first, second, last = range(0, 2 * count, 2), range(1, 2 * count, 2), range(2 * count, devices)
    layouts = (
        (own, [(own_sent, i) for i in first] + [(other_sent, i) for i in second] + [(own_sent, i) for i in last]),
        (other, [(own_sent, i) for i in second] + [(other_sent, i) for i in first] + [(other_sent, i) for i in last]),
    )
    for start, layout in layouts:

        def put(sub, value):
            out[:, pl.ds(start + sub * LANES, LANES)] = value.astype(out.dtype)

        blocks_to_rows(scratch, [part(refs[i // per], i % per * size, size) for refs, i in layout], put, subs)


def split_terms(count, size, scratch, own_half, keep, send):
    keep[0 : count * size, :] = scratch[0 : count * size, :]
    send[0 : count * size, :] = scratch[count * size : 2 * count * size, :].astype(send.dtype)
    rest = scratch[2 * count * size :, :]
    if own_half:
        keep[count * size :, :] = rest
    else:
        send[count * size :, :] = rest.astype(send.dtype)


def leave_kernel(size, *refs):
    terms, outs = (refs[:4], refs[4:8]), refs[9:]
    count = len(outs) - 2
    for at, (keep_own, keep_other, came_own, came_other) in zip((0, size), terms):

        def own(p):
            total = part(keep_own, p * size, size)[...] + part(came_own, p * size, size)[...].astype(jnp.float32)
            return total.astype(outs[0].dtype)

        for j, out in enumerate(outs[:count]):
            part(out, at, size)[...] = own(j)
            total = part(keep_other, j * size, size)[...] + part(came_other, j * size, size)[...].astype(jnp.float32)
            part(out, 2 * size + at, size)[...] = total.astype(out.dtype)
        part(outs[count], at, size)[...] = own(count)
        part(outs[count + 1], at, size)[...] = own(count + 1)


def share_kernel(size, *refs):
    blocks, (_, _, out) = refs[:-3], refs[-3:]
    for j, block in enumerate(blocks):
        part(out, 2 * j * size, 2 * size)[...] = part(block, 2 * size, 2 * size)[...]


def token_sums(subs, place, mix, scratch, rows, blocks, put):
    size = scratch.shape[0] // len(blocks)
    for p, block in enumerate(blocks):
        here = slice(p * size, (p + 1) * size)
        scratch[here, :] = jnp.zeros((size, LANES), jnp.float32) if block is None else block[...].astype(jnp.float32)
    for sub in range(subs):
        value = scratch[pl.ds(sub, rows.shape[0], stride=subs), :]
        if mix is not None:
            value = value * mix[...]
        rows[:, lanes_of(sub)] = value.astype(rows.dtype)
    for cut in pieces_of(subs * LANES, 512):
        put(cut, contract_rows(place[...], rows[:, cut]))


def join_kernel(count, subs, place, mix, *refs):
    blocks, (near, here, out_sum, grad_sum, scratch, rows) = refs[:count], refs[count:]
    size = near.shape[0] // 2
    for at, scale, out in ((0, mix, out_sum), (size, None, grad_sum)):

        def put(cut, total):
            out[:, cut] = total

        first = [part(block, at, size) for block in blocks]
        last = [part(near, at, size), part(here, at, size)]
        token_sums(subs, place, scale, scratch, rows, first + [None] * count + last, put)


def finish_kernel(
    count, subs, place, mix, shared, out_sum, grad_sum, out_tokens, grad_tokens, scratch, rows, low, sems
):
    size = shared.shape[0] // (2 * count)
    copies = []
    work = ((0, mix, out_sum, out_tokens), (size, None, grad_sum, grad_tokens))
    for i, (at, scale, before, out) in enumerate(work):

        def put(cut, total):
            low[i, :, cut] = (before[:, cut] + total).astype(low.dtype)
            sem = sems.at[i, cut.start // 512]
            copies.append(pltpu.make_async_copy(low.at[i, :, cut], out.at[:, cut], sem))
            copies[-1].start()

        blocks = [part(shared, 2 * j * size + at, size) for j in range(count)]
        token_sums(subs, place, scale, scratch, rows, blocks, put)
    for copy in copies:
        copy.wait()


def half_starts(half_width):
    half = lax.axis_index("ffn")
    own = pl.multiple_of(half * half_width, half_width)
    other = pl.multiple_of((1 - half) * half_width, half_width)
    return own, other


def chunk(i, step, base=0):
    return pl.ds(base + pl.multiple_of(i * step, step), step)


def dot(left, right):
    return jnp.dot(left, right, preferred_element_type=jnp.float32)


def halves_of_output(devices, subs, step, scratch, own_half, term, keep, send):
    size = scratch.shape[0] // devices
    for at in range(0, subs * LANES, step):
        value = term(at)
        for i in range(step // LANES):
            spread_lanes(scratch, at // LANES + i, subs, value[:, lanes_of(i)])
    split_terms(devices // 2 - 1, size, scratch, own_half, keep, send)


def forward_kernel(devices, subs, step, *refs):
    half = devices // 2
    x_sent, x_swapped = refs[:half], refs[half : 2 * half]
    w_gate, w_up, x_full, gate, up, hidden, scratch = refs[2 * half :]
    full_rows(devices, subs, scratch, x_sent, x_swapped, x_full)
    for cols in pieces_of(gate.shape[1], step):
        gate_low = dot(x_full[...], w_gate[0, :, cols]).astype(jnp.bfloat16)
        up_low = dot(x_full[...], w_up[0, :, cols]).astype(jnp.bfloat16)
        gate[:, cols] = gate_low
        up[:, cols] = up_low
        value = gate_low.astype(jnp.float32)
        hidden[:, cols] = (value * jax.nn.sigmoid(value) * up_low.astype(jnp.float32)).astype(jnp.bfloat16)


def output_kernel(devices, subs, step, hidden, w_down, keep_own, keep_other, send_own, send_other, scratch):
    own, other = half_starts(subs * LANES)

    def term(start):
        return lambda at: dot(hidden[...], w_down[0, :, pl.ds(start + at, step)])

    halves_of_output(devices, subs, step, scratch, False, term(other), keep_other, send_other)
    halves_of_output(devices, subs, step, scratch, True, term(own), keep_own, send_own)


def input_term(step, pre_gate, pre_up, w_gate, w_up, start):
    def term(at):
        there = pl.ds(start + at, step)
        return contract_cols(pre_gate[...], w_gate[0, there, :]) + contract_cols(pre_up[...], w_up[0, there, :])

    return term


def backward_kernel(
    devices,
    subs,
    step,
    g_sent,
    g_swapped,
    gate,
    up,
    w_gate,
    w_up,
    w_down,
    g_full,
    pre_gate,
    pre_up,
    keep_other,
    send_other,
    scratch,
):
    _, other = half_starts(subs * LANES)
    full_rows(devices, subs, scratch, [g_sent], [g_swapped], g_full)

    def pull(i, carry):
        cols = chunk(i, step)
        low = contract_cols(g_full[...], w_down[0, cols, :]).astype(jnp.bfloat16)
        grad_hidden = low.astype(jnp.float32)
        value = gate[:, cols].astype(jnp.float32)
        sig = jax.nn.sigmoid(value)
        pre_gate[:, cols] = (
            grad_hidden * up[:, cols].astype(jnp.float32) * sig * (1.0 + value * (1.0 - sig))
        ).astype(jnp.bfloat16)
        pre_up[:, cols] = (grad_hidden * value * sig).astype(jnp.bfloat16)
        return carry

    lax.fori_loop(0, gate.shape[1] // step, pull, 0)
    term = input_term(step, pre_gate, pre_up, w_gate, w_up, other)
    halves_of_output(devices, subs, step, scratch, False, term, keep_other, send_other)


def backward_own_kernel(devices, subs, step, pre_gate, pre_up, w_gate, w_up, keep_own, send_own, scratch):
    own, _ = half_starts(subs * LANES)
    term = input_term(step, pre_gate, pre_up, w_gate, w_up, own)
    halves_of_output(devices, subs, step, scratch, True, term, keep_own, send_own)


def flip(value):
    return value.astype(jnp.float32).T


def pieces_of(total, size):
    return [slice(at, min(at + size, total)) for at in range(0, total, size)]


def first_chunk_kernel(hidden, g, turned, out):
    turned[...] = flip(hidden[...]).astype(turned.dtype)
    for cut in pieces_of(out.shape[1], 256):
        out[:, cut] = dot(turned[...], g[:, cut]).astype(out.dtype)


def gradient_kernel(
    step,
    x,
    g,
    hidden_turned,
    first,
    pre_gate,
    pre_up,
    grad_gate,
    grad_up,
    grad_down,
    written,
    turned,
    tall,
    wide,
    tall_sems,
    wide_sems,
    first_sem,
):
    width, lanes = x.shape[1], hidden_turned.shape[0]
    count = width // step
    written[...] = jnp.zeros_like(written)
    first_copy = pltpu.make_async_copy(first, grad_down.at[0, :, 0:step], first_sem)
    first_copy.start()

    cuts = pieces_of(step, 256)

    def wide_copy(i, slot, n):
        there = pl.ds(pl.multiple_of(i * step, step) + cuts[n].start, cuts[n].stop - cuts[n].start)
        return pltpu.make_async_copy(wide.at[slot, :, cuts[n]], grad_down.at[0, :, there], wide_sems.at[slot, n])

    def tall_copy(which, out, i, slot):
        return pltpu.make_async_copy(tall.at[which, slot], out.at[0, chunk(i, step), :], tall_sems.at[which, slot])

    def inputs(i, carry):
        slot = i % 2
        turned[...] = flip(x[:, chunk(i, step)]).astype(turned.dtype)
        for which, (right, out) in enumerate(((pre_gate, grad_gate), (pre_up, grad_up))):

            @pl.when(i >= 2)
            def _():
                tall_copy(which, out, i - 2, slot).wait()

            for cut in pieces_of(lanes, 256):
                for high in pieces_of(step, 512):
                    tall[which, slot, high, cut] = dot(turned[high, :], right[:, cut]).astype(tall.dtype)
            tall_copy(which, out, i, slot).start()
        return carry

    lax.fori_loop(0, count, inputs, 0)

    def down(i, carry):
        slot = i % 2

        @pl.when(i >= 3)
        def _():
            for n in range(len(cuts)):
                wide_copy(i - 2, slot, n).wait()

        for n, cut in enumerate(cuts):
            right = g[:, chunk(i, step)][:, cut]
            wide[slot, :, cut] = dot(hidden_turned[...], right).astype(wide.dtype)
            wide_copy(i, slot, n).start()
        return carry

    lax.fori_loop(1, count, down, 0)
    first_copy.wait()
    for i in range(max(1, count - 2), count):
        for n in range(len(cuts)):
            wide_copy(i, i % 2, n).wait()
    for i in range(max(0, count - 2), count):
        tall_copy(0, grad_gate, i, i % 2).wait()
        tall_copy(1, grad_up, i, i % 2).wait()


def exchange(blocks, masks, devices):
    arrived = []
    for block, mask in zip(blocks, masks):
        pairs = [(2 * i + core, 2 * (i ^ (mask + core)) + core) for i in range(devices) for core in range(2)]
        arrived.append(lax.ppermute(block, ("expert", "ffn"), pairs))
    return arrived


def exchange_near(block, devices):
    return lax.ppermute(block, "expert", [(i, i ^ 1) for i in range(devices)])


def swap(value):
    return lax.ppermute(value, "ffn", [(0, 1), (1, 0)])


def in_hbm(values):
    return [pltpu.with_memory_space_constraint(value, pltpu.HBM) for value in values]


def one_piece_shards(tokens, grad_out, route_ids, route_weight, gate_weight, up_weight, down_weight):
    tok_dev, sub_width = tokens.shape
    top_count = route_ids.shape[1]
    width, lanes = gate_weight.shape[1:]
    devices = lax.axis_size("expert")
    capacity = max(2, min(tok_dev, (9 * tok_dev * top_count + 8 * EXPERTS - 1) // (8 * EXPERTS)))
    rows = devices * capacity
    subs = sub_width // LANES
    low, full = jnp.bfloat16, jnp.float32
    size = capacity * subs
    count = devices // 2 - 1
    spread_scratch = [pltpu.VMEM((devices * size, LANES), full)]
    step = 256
    half_flops = 2 * rows * width * lanes // 2

    def lines(number, dtype=low):
        return jax.ShapeDtypeStruct((number * size, LANES), dtype)

    def lines_in_vmem(number, dtype=low):
        return vmem((number * size, LANES), dtype)

    sources = (route_ids.T, route_weight.T, tokens, grad_out)
    other_rows = count * capacity
    x_mine, g_mine, near, here, theirs, place, mix, place_other, mix_other = call(
        functools.partial(route_kernel, devices, capacity, subs),
        [lines(count), lines(count), lines(2), lines(2)]
        + [lines(2 * count)]
        + [jax.ShapeDtypeStruct((rows, tok_dev), low), jax.ShapeDtypeStruct((rows, LANES), full)]
        + [jax.ShapeDtypeStruct((other_rows, tok_dev), low), jax.ShapeDtypeStruct((other_rows, LANES), full)],
        in_hbm(sources),
        in_spaces=[pl.ANY] * 4,
        scratch=spread_scratch
        + [pltpu.VMEM(value.shape, value.dtype) for value in sources]
        + [pltpu.SemaphoreType.DMA((4,))],
        traffic=4 * tok_dev * sub_width,
    )
    masks = even_masks(devices)
    late = [devices // 4 - 1]
    late_block = jax.ShapeDtypeStruct((2 * size + 16, LANES), low)
    packed = call(
        functools.partial(pack_kernel, size, late),
        [late_block if j in late else lines(4) for j in range(count)] + [late_block] * len(late),
        (x_mine, g_mine, swap(theirs)),
        flops=24 * half_flops,
    )
    x_arrived = exchange(packed[:count], masks, devices)
    g_arrived = list(x_arrived)
    for j, block in zip(late, packed[count:]):
        (g_arrived[j],) = exchange([block], masks[j:], devices)
    near = exchange_near(near, devices)

    weights = (gate_weight, up_weight, down_weight)
    w_gate, w_up, w_down = [pltpu.with_memory_space_constraint(w, pltpu.VMEM) for w in weights]

    x_sent = call(
        functools.partial(gather_x_kernel, size), [lines(2)] * (count + 1), (*x_arrived, near, here)
    )
    x_swapped = [swap(value) for value in x_sent]
    terms = [
        lines_in_vmem(count + 2, full),
        lines_in_vmem(count, full),
        lines_in_vmem(count),
        lines_in_vmem(count + 2),
    ]
    x_full, gate, up, hidden = call(
        functools.partial(forward_kernel, devices, subs, step),
        [vmem((rows, width), low)] + [vmem((rows, lanes), low)] * 3,
        (*x_sent, *x_swapped, w_gate, w_up),
        scratch=spread_scratch,
    )
    (g_sent,) = call(
        functools.partial(gather_g_kernel, size, late), [lines(devices)], (*g_arrived, near, here, hidden)
    )
    g_swapped = swap(g_sent)
    out_own, out_other, send_own, send_other = call(
        functools.partial(output_kernel, devices, subs, 2 * step),
        terms,
        (hidden, w_down),
        scratch=spread_scratch,
        flops=2 * half_flops,
    )
    out_terms = (out_own, out_other, swap(send_other), swap(send_own))
    g_full, pre_gate, pre_up, dx_other, send_other = call(
        functools.partial(backward_kernel, devices, subs, step),
        [vmem((rows, width), low)] + [vmem((rows, lanes), low)] * 2 + [terms[1], terms[3]],
        (g_sent, g_swapped, gate, up, w_gate, w_up, w_down),
        scratch=spread_scratch,
        flops=4 * half_flops,
    )
    came_own = swap(send_other)
    dx_own, send_own = call(
        functools.partial(backward_own_kernel, devices, subs, step),
        [terms[0], terms[2]],
        (pre_gate, pre_up, w_gate, w_up),
        scratch=spread_scratch,
        flops=2 * half_flops,
    )
    dx_terms = (dx_own, dx_other, came_own, swap(send_own))
    cut = 1024 if width % 1024 == 0 else width
    hidden_turned, first = call(
        first_chunk_kernel,
        [vmem((lanes, rows), low), vmem((lanes, cut), low)],
        (hidden, g_full),
        flops=2 * half_flops * cut // width,
    )
    *leaving, back, kept = call(
        functools.partial(leave_kernel, size),
        [lines(4)] * count + [lines(2)] * 2,
        (*out_terms, *dx_terms, first),
    )
    returned = exchange(leaving, masks, devices)
    back = exchange_near(back, devices)
    grad_gate, grad_up, grad_down, written = call(
        functools.partial(gradient_kernel, cut),
        [jax.ShapeDtypeStruct(w.shape, low) for w in weights] + [vmem((8, LANES), full)],
        (x_full, g_full, hidden_turned, first, pre_gate, pre_up),
        out_spaces=[pl.ANY] * 3 + [pltpu.VMEM],
        scratch=[
            pltpu.VMEM((cut, rows), low),
            pltpu.VMEM((2, 2, cut, lanes), low),
            pltpu.VMEM((2, lanes, cut), low),
            pltpu.SemaphoreType.DMA((2, 2)),
            pltpu.SemaphoreType.DMA((2, -(-cut // 256))),
            pltpu.SemaphoreType.DMA,
        ],
        flops=6 * half_flops,
        traffic=sum(w.size * 2 for w in weights),
        limit=32,
    )
    (sharing,) = call(functools.partial(share_kernel, size), [lines(2 * count)], (*returned, back, written))
    shared = swap(sharing)
    sums = call(
        functools.partial(join_kernel, count, subs),
        [vmem((tok_dev, sub_width), full)] * 2,
        (place, mix, *returned, back, kept),
        scratch=spread_scratch + [pltpu.VMEM((rows, sub_width), low)],
        flops=4 * rows * tok_dev * sub_width,
    )
    out_tokens, grad_tokens = call(
        functools.partial(finish_kernel, count, subs),
        [jax.ShapeDtypeStruct((tok_dev, sub_width), low)] * 2,
        (place_other, mix_other, shared, *sums),
        out_spaces=[pl.ANY] * 2,
        scratch=[
            pltpu.VMEM((count * size, LANES), full),
            pltpu.VMEM((other_rows, sub_width), low),
            pltpu.VMEM((2, tok_dev, sub_width), low),
            pltpu.SemaphoreType.DMA((2, -(-sub_width // 512))),
        ],
        traffic=8 * tok_dev * sub_width,
    )
    return out_tokens, grad_tokens, grad_gate, grad_up, grad_down


def shards(*args):
    tokens, gate_weight = args[0], args[4]
    halves = lax.axis_size("ffn")
    devices = lax.axis_size("expert")
    if halves == 2 and devices >= 4 and devices & (devices - 1) == 0 and tokens.shape[1] * halves == gate_weight.shape[1]:
        return one_piece_shards(*args)
    return general_shards(*args)


def solution(mesh):
    in_specs = (
        P(("groups", "expert"), "ffn"),
        P(("groups", "expert"), "ffn"),
        P(("groups", "expert"), None),
        P(("groups", "expert"), None),
        P("expert", None, "ffn"),
        P("expert", None, "ffn"),
        P("expert", "ffn", None),
    )
    out_specs = (
        P(("groups", "expert"), "ffn"),
        P(("groups", "expert"), "ffn"),
        P(("groups", "expert"), None, "ffn"),
        P(("groups", "expert"), None, "ffn"),
        P(("groups", "expert"), "ffn", None),
    )
    return jax.shard_map(shards, mesh=mesh, in_specs=in_specs, out_specs=out_specs, check_vma=False)
```
